32 devices in a mesh: grp: 4 (over y, x), rep: 8 (over z, core).
Axes of the slice: x: 2, y: 2, z: 4, core: 2. Of those that a mesh axis runs over, the one named last changes fastest.
Arguments:
- embeddings: bfloat16 [512, 256], P('rep')
- labels: int32 [512], replicated, may hold values from 0 to 262143
- class_weights: bfloat16 [262144, 256], P(('rep', 'grp'))
- centroids: bfloat16 [262144, 256], P(('grp', 'rep')), may hold values from -6 to 6
- centroid_class: int32 [262144], P(('grp', 'rep')), may hold values from 0 to 8191, as said below
Outputs:
- loss: float32 [512], P('rep')
- embedding_gradient: float32 [512, 256], P('rep')
- weight_grad: float32 [262144, 256], P(('rep', 'grp'))
- refreshed: bfloat16 [262144, 256], P(('rep', 'grp'))
The draws below stay inside these ranges and needn't reach their ends.
Inputs may be any that keep to these rules, and one draw needn't show every extreme that they name: `centroid_class`: cut every block of 8192 consecutive entries into runs of 256 entries; over the k-th runs of all blocks together, each number of 0 to 8191 appears exactly once.
All inputs are finite; a program needn't handle non-finite values.
Results may differ from the reference program's by a relative error of at most 0.0053.
Values may be sent and summed in bfloat16 or wider, within the bound.
No kernel may reach another device: no remote copies, remote signals or barrier semaphores. Data moves between devices by JAX's collectives and lax.ppermute only.
A program may use at most 128 MiB of HBM per device.

```python
import math
import jax
import jax.numpy as jnp
from jax import lax

D = 256
C_DEV = 8192
BATCH = 512
CLASSES = 262144


def shared_labels(key):
    drawn = jax.random.randint(jax.random.fold_in(key, 4), (BATCH,), 0, CLASSES, dtype=jnp.int32)
    return drawn.at[0].set(0).at[BATCH - 1].set(CLASSES - 1)


def shared_rows(key, class_ids):
    base_key = jax.random.fold_in(key, 5)

    def one_row(class_id):
        row_key = jax.random.fold_in(base_key, class_id)
        noise = jax.random.normal(row_key, (D,), jnp.float32)
        factor = jax.random.normal(jax.random.fold_in(row_key, 1), (), jnp.float32)
        return (noise, factor)
    noise, factor = jax.vmap(one_row)(class_ids)
    direction = jax.random.normal(jax.random.fold_in(key, 6), (D,), jnp.float32)
    rising = 1.0 + 2.0 * class_ids.astype(jnp.float32) / CLASSES
    return (noise + 0.2 * (rising * factor)[:, None] * direction[None, :], direction)


def draw_labels(key, part):
    return shared_labels(key)


def draw_class_weights(key, part):
    rows, _ = shared_rows(key, jnp.arange(CLASSES, dtype=jnp.int32))
    return rows.astype(jnp.bfloat16)


def draw_embeddings(key, part):
    own_key = jax.random.fold_in(key, 23)
    labels = shared_labels(key)
    label_rows, direction = shared_rows(key, labels)
    noise = jax.random.normal(own_key, (BATCH, D), jnp.float32)
    picked = jax.random.uniform(jax.random.fold_in(own_key, 3), (BATCH, 1), jnp.float32)
    strength = jnp.where(picked < 0.15, 6.0, jnp.where(picked < 0.45, 1.0, 0.0))
    values = noise + 0.7 * direction[None, :] + strength * label_rows
    return values.astype(jnp.bfloat16)


def draw_centroid_class(key, part):
    own_key = jax.random.fold_in(key, 24)
    blocks = CLASSES // C_DEV
    per_peer = C_DEV // blocks
    target_perm = jax.vmap(lambda row_key: jax.random.permutation(row_key, C_DEV))(jax.random.split(own_key, blocks))
    shaped = target_perm.reshape(blocks, blocks, per_peer)
    return jnp.transpose(shaped, (1, 0, 2)).reshape(-1).astype(jnp.int32)


def level_of(key, extent, cuts, low, top_value):
    loudness, own = 1.0, jax.random.fold_in(key, 6)
    for axis_at, shards_of in cuts:
        steps = jnp.exp(jax.random.uniform(jax.random.fold_in(own, axis_at), (shards_of,), jnp.float32, low / len(cuts), top_value / len(cuts)))
        loudness = loudness * jnp.repeat(steps, extent[axis_at] // shards_of).reshape([-1 if axis == axis_at else 1 for axis in range(len(extent))])
    return loudness


def gaussian(rng, extent, deviation, limit, cuts=(), held_as=jnp.bfloat16):
    array = jax.random.normal(rng, extent, jnp.float32) * deviation
    if len(cuts) > 0:
        array = level_of(rng, extent, cuts, -0.22, 0.18) * array
    return jnp.clip(array, min=-limit, max=limit).astype(held_as)


def setup_inputs(seed: int = 0) -> dict:
    arg_keys = jax.random.split(jax.random.key(seed), 6)
    embeddings = draw_embeddings(jax.random.fold_in(arg_keys[5], 71), 0)
    labels = draw_labels(jax.random.fold_in(arg_keys[5], 71), 0)
    class_weights = draw_class_weights(jax.random.fold_in(arg_keys[5], 71), 0)
    centroids = gaussian(arg_keys[3], (CLASSES, D), 1.0, 6.0, ((0, 32),))
    centroid_class = draw_centroid_class(jax.random.fold_in(arg_keys[5], 71), 0)
    return {"embeddings": embeddings, "labels": labels, "class_weights": class_weights, "centroids": centroids, "centroid_class": centroid_class}


SCALE = 32.0
MARGIN = 0.2
SIN_FLOOR = 0.09

def unit_length_rows(values):
    wide = values.astype(jnp.float32)
    inv_norm = lax.rsqrt(lax.optimization_barrier(jnp.sum(wide * wide, axis=1, keepdims=True)) + 1e-06)
    return (wide * inv_norm, inv_norm)

def margin_terms(cosine_matrix, is_label):
    label_cos = lax.optimization_barrier(jnp.sum(jnp.where(is_label, cosine_matrix, 0.0), axis=1))
    sine_sq = 1.0 - label_cos * label_cos
    sine = jnp.sqrt(jnp.maximum(sine_sq, SIN_FLOOR))
    margined = label_cos * math.cos(MARGIN) - sine * math.sin(MARGIN)
    margin_slope = math.cos(MARGIN) + jnp.where(sine_sq > SIN_FLOOR, label_cos * math.sin(MARGIN) / sine, 0.0)
    logits = jnp.where(is_label, SCALE * margined[:, None], SCALE * cosine_matrix)
    return (logits, margin_slope)

def reference(embeddings, labels, class_weights, centroids, centroid_class):
    normalized_input_wide, input_inverse_norm = unit_length_rows(embeddings)
    normalized_input = normalized_input_wide.astype(jnp.bfloat16)
    what_wide, w_inv = unit_length_rows(class_weights)
    what = what_wide.astype(jnp.bfloat16)
    block_count = CLASSES // C_DEV
    column_base = jnp.arange(C_DEV, dtype=jnp.int32)
    tiles = jnp.arange(block_count, dtype=jnp.int32)

    def tile_logits(tile):
        first_row = (tile * C_DEV).astype(jnp.int32)
        weight_block = lax.dynamic_slice_in_dim(what, first_row, C_DEV, 0)
        cosine_matrix = lax.dot_general(normalized_input, weight_block, (((1,), (1,)), ((), ())), preferred_element_type=jnp.float32)
        is_label = labels[:, None] == (first_row + column_base)[None, :]
        logits, margin_slope = margin_terms(cosine_matrix, is_label)
        return (logits, margin_slope, is_label, weight_block, first_row)

    def first_pass(tile):
        logits, _, is_label, _, _ = tile_logits(tile)
        return (lax.optimization_barrier(jnp.sum(jnp.exp(logits - SCALE), axis=1)), lax.optimization_barrier(jnp.sum(jnp.where(is_label, logits, 0.0), axis=1)))
    exp_parts, target_parts = lax.map(first_pass, tiles)
    totals = lax.optimization_barrier(jnp.sum(exp_parts, axis=0))
    target = lax.optimization_barrier(jnp.sum(target_parts, axis=0))
    log_total = SCALE + jnp.log(totals)
    loss = log_total - target

    def second_pass(carry, tile):
        logits, margin_slope, is_label, weight_block, first_row = tile_logits(tile)
        probs = jnp.exp(logits - log_total[:, None])
        onehot = is_label.astype(jnp.float32)
        cosine_gradient = (SCALE * (probs - onehot) * jnp.where(is_label, margin_slope[:, None], 1.0)).astype(jnp.bfloat16)
        carry = carry + jnp.dot(cosine_gradient, weight_block, preferred_element_type=jnp.float32)
        unnormalized_input = lax.dot_general(cosine_gradient, normalized_input, (((0,), (0,)), ((), ())), preferred_element_type=jnp.float32)
        wide_tile = lax.dynamic_slice_in_dim(what_wide, first_row, C_DEV, 0)
        inv_tile = lax.dynamic_slice_in_dim(w_inv, first_row, C_DEV, 0)
        grad_tile = (unnormalized_input - wide_tile * lax.optimization_barrier(jnp.sum(wide_tile * unnormalized_input, axis=1, keepdims=True))) * inv_tile
        return (carry, grad_tile)
    normalized_gradient, grad_tiles = lax.scan(second_pass, jnp.zeros((BATCH, D), jnp.float32), tiles)
    weight_grad = grad_tiles.reshape(CLASSES, D)
    embedding_gradient = (normalized_gradient - normalized_input_wide * lax.optimization_barrier(jnp.sum(normalized_input_wide * normalized_gradient, axis=1, keepdims=True))) * input_inverse_norm
    run_length = C_DEV // block_count
    positions = jnp.arange(CLASSES, dtype=jnp.int32)
    target_class = positions % C_DEV // run_length * C_DEV + centroid_class
    relaid = jnp.zeros((CLASSES, D), jnp.bfloat16).at[target_class].set(centroids)
    chat, _ = unit_length_rows(relaid)
    refreshed, _ = unit_length_rows(what_wide + chat)
    return (loss, embedding_gradient, weight_grad, refreshed.astype(jnp.bfloat16))
```

```python
import functools
import math

import jax
import jax.numpy as jnp
from jax import lax
from jax.experimental import pallas as pl
from jax.experimental.pallas import tpu as pltpu
from jax.sharding import PartitionSpec as P

SCALE = 32.0
MARGIN = 0.2
SIN_FLOOR = 0.09
LOG2E = math.log2(math.e)
ALL = ("rep", "grp")
VMEM_BYTES = 50 * 1024 * 1024

NT = (((1,), (1,)), ((), ()))


def unit_rows(wide):
    inv = lax.rsqrt(jnp.sum(wide * wide, axis=1, keepdims=True) + 1e-06)
    return wide * inv, inv


def column_of(row):
    lanes = row.shape[1]
    return jnp.transpose(jnp.broadcast_to(row, (128, lanes)))[:, :1]


def forward_kernel(base_ref, emb_ref, lab_ref, w_ref, a_ref, b_ref, st_ref, xhat_ref, sum_ref, *, classes):
    step = pl.program_id(0)
    tile = w_ref.shape[0]
    batch = emb_ref.shape[0]

    @pl.when(step == 0)
    def _():
        xwide, _ = unit_rows(emb_ref[...].astype(jnp.float32))
        xhat_ref[...] = xwide.astype(jnp.bfloat16)
        sum_ref[...] = jnp.zeros_like(sum_ref)
        a_ref[...] = jnp.zeros_like(a_ref)
        b_ref[...] = jnp.zeros_like(b_ref)

    wwide, _ = unit_rows(w_ref[...].astype(jnp.float32))
    what = wwide.astype(jnp.bfloat16)
    cosine = lax.dot_general(xhat_ref[...], what, NT, preferred_element_type=jnp.float32)
    ids = lax.broadcasted_iota(jnp.int32, (batch, tile), 1)
    is_label = ids == lab_ref[...] - (base_ref[0] + step * tile)
    e = jnp.where(is_label, 0.0, jnp.exp2(cosine * (SCALE * LOG2E) - SCALE * LOG2E))
    partial = e[:, :128]
    for c in range(1, tile // 128):
        partial = partial + e[:, c * 128 : (c + 1) * 128]
    sum_ref[...] += partial
    onehot = jnp.where(is_label, 1.0, 0.0).astype(jnp.bfloat16)
    a_ref[...] += jnp.dot(e.astype(jnp.bfloat16), what, preferred_element_type=jnp.float32)
    b_ref[...] += jnp.dot(onehot, what, preferred_element_type=jnp.float32)

    @pl.when(step == pl.num_programs(0) - 1)
    def _():
        xwide, x_inv = unit_rows(emb_ref[...].astype(jnp.float32))
        label_row = b_ref[...]
        c = jnp.sum(xhat_ref[...].astype(jnp.float32) * label_row, axis=1, keepdims=True)
        offset = lab_ref[...] - base_ref[0]
        has = jnp.where((offset >= 0) & (offset < classes), 1.0, 0.0)
        q = 1.0 - c * c
        sine = jnp.sqrt(jnp.maximum(q, SIN_FLOOR))
        margined = c * math.cos(MARGIN) - sine * math.sin(MARGIN)
        slope = math.cos(MARGIN) + jnp.where(q > SIN_FLOOR, c * math.sin(MARGIN) / sine, 0.0)
        slope = slope * has
        label_e = jnp.exp(SCALE * margined - SCALE) * has
        total = jnp.sum(sum_ref[...], axis=1, keepdims=True) + label_e
        target = SCALE * margined * has
        b = slope * label_row
        a = a_ref[...] + label_e * b
        gain = SCALE * x_inv
        a_ref[...] = (a - xwide * jnp.sum(xwide * a, axis=1, keepdims=True)) * gain
        b_ref[...] = (b - xwide * jnp.sum(xwide * b, axis=1, keepdims=True)) * gain
        lane = lax.broadcasted_iota(jnp.int32, (batch, 128), 1)
        stats = jnp.where(lane == 0, total, 0.0)
        stats = jnp.where(lane == 1, target, stats)
        stats = jnp.where(lane == 2, label_e * slope, stats)
        stats = jnp.where(lane == 3, slope, stats)
        st_ref[...] = jnp.transpose(stats)[:8, :]


def forward(base, emb, labels, weights):
    batch, width = emb.shape
    classes = weights.shape[0]
    tile = math.gcd(classes, 1024)
    whole = lambda i: (0, 0)
    return pl.pallas_call(
        functools.partial(forward_kernel, classes=classes),
        grid=(classes // tile,),
        in_specs=[
            pl.BlockSpec(memory_space=pltpu.SMEM),
            pl.BlockSpec((batch, width), whole),
            pl.BlockSpec((batch, 1), whole),
            pl.BlockSpec((tile, width), lambda i: (i, 0)),
        ],
        out_specs=[
            pl.BlockSpec((batch, width), whole),
            pl.BlockSpec((batch, width), whole),
            pl.BlockSpec((8, batch), whole),
        ],
        out_shape=[
            jax.ShapeDtypeStruct((batch, width), jnp.float32),
            jax.ShapeDtypeStruct((batch, width), jnp.float32),
            jax.ShapeDtypeStruct((8, batch), jnp.float32),
        ],
        scratch_shapes=[pltpu.VMEM((batch, width), jnp.bfloat16), pltpu.VMEM((batch, 128), jnp.float32)],
        compiler_params=pltpu.CompilerParams(
            dimension_semantics=("arbitrary",), vmem_limit_bytes=VMEM_BYTES
        ),
        cost_estimate=pl.CostEstimate(
            flops=6 * batch * classes * width,
            bytes_accessed=classes * width * 2,
            transcendentals=batch * classes,
        ),
        name="forward_sums",
    )(base, emb, labels.reshape(batch, 1), weights)


def weight_kernel(base_ref, emb_ref, lab_ref, st_ref, tot_ref, w_ref, g_ref, xhat_ref, y_ref, v_ref):
    step = pl.program_id(0)
    tile = w_ref.shape[0]
    batch = emb_ref.shape[0]

    @pl.when(step == 0)
    def _():
        xwide, _ = unit_rows(emb_ref[...].astype(jnp.float32))
        xhat = xwide.astype(jnp.bfloat16)
        xhat_ref[...] = xhat
        total = tot_ref[...]
        y_ref[...] = (xhat.astype(jnp.float32) * column_of(SCALE / total)).astype(jnp.bfloat16)
        v_ref[...] = st_ref[2:3, :] - st_ref[3:4, :] * total

    wwide, w_inv = unit_rows(w_ref[...].astype(jnp.float32))
    what = wwide.astype(jnp.bfloat16)
    cosine = lax.dot_general(what, xhat_ref[...], NT, preferred_element_type=jnp.float32)
    ids = lax.broadcasted_iota(jnp.int32, (tile, batch), 0)
    is_label = ids == lab_ref[...] - (base_ref[0] + step * tile)
    e = jnp.exp2(cosine * (SCALE * LOG2E) - SCALE * LOG2E)
    d = jnp.where(is_label, v_ref[...], e).astype(jnp.bfloat16)
    raw = jnp.dot(d, y_ref[...], preferred_element_type=jnp.float32)
    g_ref[...] = (raw - wwide * jnp.sum(wwide * raw, axis=1, keepdims=True)) * w_inv


def weight_gradient(base, emb, labels, stats, totals, weights):
    batch, width = emb.shape
    classes = weights.shape[0]
    tile = math.gcd(classes, 1024)
    whole = lambda i: (0, 0)
    return pl.pallas_call(
        weight_kernel,
        grid=(classes // tile,),
        in_specs=[
            pl.BlockSpec(memory_space=pltpu.SMEM),
            pl.BlockSpec((batch, width), whole),
            pl.BlockSpec((1, batch), whole),
            pl.BlockSpec((8, batch), whole),
            pl.BlockSpec((1, batch), whole),
            pl.BlockSpec((tile, width), lambda i: (i, 0)),
        ],
        out_specs=pl.BlockSpec((tile, width), lambda i: (i, 0)),
        out_shape=jax.ShapeDtypeStruct((classes, width), jnp.float32),
        scratch_shapes=[
            pltpu.VMEM((batch, width), jnp.bfloat16),
            pltpu.VMEM((batch, width), jnp.bfloat16),
            pltpu.VMEM((1, batch), jnp.float32),
        ],
        compiler_params=pltpu.CompilerParams(
            dimension_semantics=("arbitrary",), vmem_limit_bytes=VMEM_BYTES
        ),
        cost_estimate=pl.CostEstimate(
            flops=4 * batch * classes * width,
            bytes_accessed=classes * width * 6,
            transcendentals=batch * classes,
        ),
        name="weight_gradient",
    )(base, emb, labels.reshape(1, batch), stats, totals.reshape(1, batch), weights)


def refresh_kernel(slot_ref, rows_ref, w_ref, o_ref, stage_ref, held_ref):
    step = pl.program_id(0)
    parts = pl.num_programs(0) // 2
    tile = rows_ref.shape[0]

    @pl.when(step < parts)
    def _():
        unit, _ = unit_rows(rows_ref[...].astype(jnp.float32))
        stage_ref[0] = unit[:, :128]
        stage_ref[1] = unit[:, 128:]
        first = step * tile

        def place(j, carry):
            for u in range(16):
                row = j * 16 + u
                slot = slot_ref[first + row]
                held_ref[0, pl.ds(slot, 1), :] = stage_ref[0, pl.ds(row, 1), :]
                held_ref[1, pl.ds(slot, 1), :] = stage_ref[1, pl.ds(row, 1), :]
            return carry

        lax.fori_loop(0, tile // 16, place, 0)

    @pl.when(step >= parts)
    def _():
        wwide, _ = unit_rows(w_ref[...].astype(jnp.float32))
        at = pl.ds(pl.multiple_of((step - parts) * tile, tile), tile)
        low = wwide[:, :128] + held_ref[0, at, :]
        high = wwide[:, 128:] + held_ref[1, at, :]
        square = jnp.sum(low * low + high * high, axis=1, keepdims=True)
        inv = lax.rsqrt(square + 1e-06)
        o_ref[:, :128] = (low * inv).astype(jnp.bfloat16)
        o_ref[:, 128:] = (high * inv).astype(jnp.bfloat16)


def refresh(slots, rows, weights):
    classes, width = weights.shape
    tile = math.gcd(classes, 1024)
    parts = classes // tile
    return pl.pallas_call(
        refresh_kernel,
        grid=(2 * parts,),
        in_specs=[
            pl.BlockSpec(memory_space=pltpu.SMEM),
            pl.BlockSpec((tile, width), lambda i: (jnp.minimum(i, parts - 1), 0)),
            pl.BlockSpec((tile, width), lambda i: (jnp.maximum(i - parts, 0), 0)),
        ],
        out_specs=pl.BlockSpec((tile, width), lambda i: (jnp.maximum(i - parts, 0), 0)),
        out_shape=jax.ShapeDtypeStruct((classes, width), jnp.bfloat16),
        scratch_shapes=[
            pltpu.VMEM((2, tile, 128), jnp.float32),
            pltpu.VMEM((2, classes, 128), jnp.float32),
        ],
        compiler_params=pltpu.CompilerParams(
            dimension_semantics=("arbitrary",), vmem_limit_bytes=VMEM_BYTES
        ),
        cost_estimate=pl.CostEstimate(
            flops=10 * classes * width, bytes_accessed=classes * width * 6, transcendentals=classes
        ),
        name="refresh",
    )(slots, rows, weights)


def shifted(value, axis, shift):
    size = lax.axis_size(axis)
    return lax.ppermute(value, axis, [(i, (i + shift) % size) for i in range(size)])


def sum_over(value, axis):
    return sum((shifted(value, axis, s) for s in range(1, lax.axis_size(axis))), value)


def scatter_sum(blocks, axis):
    size, me = lax.axis_size(axis), lax.axis_index(axis)
    total = lax.dynamic_index_in_dim(blocks, me, 0, keepdims=False)
    for s in range(1, size):
        total = total + shifted(
            lax.dynamic_index_in_dim(blocks, (me + s) % size, 0, keepdims=False), axis, s
        )
    return total


def gather_blocks(block, axis):
    size, me = lax.axis_size(axis), lax.axis_index(axis)
    stack = jnp.stack([block] + [shifted(block, axis, s) for s in range(1, size)])
    return stack[(me - jnp.arange(size)) % size]


def shards(embeddings, labels, class_weights, centroids, centroid_class):
    rows_local, width = embeddings.shape
    classes = class_weights.shape[0]
    groups, reps = lax.axis_size("grp"), lax.axis_size("rep")
    peers = groups * reps
    batch = rows_local * reps
    per_peer = classes // peers
    share = rows_local // groups
    grp, rep = lax.axis_index("grp"), lax.axis_index("rep")
    base = ((rep * groups + grp) * classes).astype(jnp.int32).reshape(1)

    slots = centroid_class.reshape(peers, per_peer)
    digits = jnp.concatenate([slots // 128, slots % 128], axis=1).astype(jnp.bfloat16)
    digit_rows = -(-2 * per_peer // width)
    digits = jnp.pad(digits, ((0, 0), (0, digit_rows * width - 2 * per_peer)))
    mine = lax.dynamic_slice_in_dim(embeddings, grp * share, share, 0)
    head = jnp.concatenate(
        [jnp.broadcast_to(mine[None], (peers, share, width)), digits.reshape(peers, digit_rows, width)],
        axis=1,
    )
    head = lax.all_to_all(head, ALL, 0, 0, tiled=True)
    emb = head[:, :share].reshape(batch, width)
    digits = head[:, share:].reshape(peers, digit_rows * width).astype(jnp.int32)
    slots_got = (digits[:, :per_peer] * 128 + digits[:, per_peer : 2 * per_peer]).reshape(-1)
    rows_got = lax.all_to_all(centroids.reshape(peers, per_peer, width), ALL, 0, 0, tiled=True)

    a, b, stats = forward(base, emb, labels, class_weights)
    totals = sum_over(sum_over(stats[:2], "grp"), "rep")
    total, target = totals[0], totals[1]
    weight_grad = weight_gradient(base, emb, labels, stats, total, class_weights)
    loss = lax.dynamic_slice_in_dim(SCALE + jnp.log(total) - target, rep * rows_local, rows_local, 0)
    grad = a / total[:, None] - b
    blocks = grad.reshape(reps, groups, share, width).transpose(1, 0, 2, 3)
    own = scatter_sum(scatter_sum(blocks, "grp"), "rep")
    embedding_gradient = gather_blocks(own, "grp").reshape(rows_local, width)
    refreshed = refresh(slots_got, rows_got.reshape(classes, width), class_weights)
    return (loss, embedding_gradient, weight_grad, refreshed)


def solution(mesh):
    in_specs = (
        P("rep", None),
        P(),
        P(("rep", "grp"), None),
        P(("grp", "rep"), None),
        P(("grp", "rep")),
    )
    out_specs = (P("rep"), P("rep", None), P(("rep", "grp"), None), P(("rep", "grp"), None))
    return jax.shard_map(shards, mesh=mesh, in_specs=in_specs, out_specs=out_specs, check_vma=False)
```

```python
import functools
import math

import jax
import jax.numpy as jnp
from jax import lax
from jax.experimental import pallas as pl
from jax.experimental.pallas import tpu as pltpu
from jax.sharding import PartitionSpec as P

SCALE = 32.0
MARGIN = 0.2
SIN_FLOOR = 0.09
LOG2E = math.log2(math.e)
ALL = ("rep", "grp")
VMEM_BYTES = 28 * 1024 * 1024
GROUPS = 4

NT = (((1,), (1,)), ((), ()))


def unit_rows(wide):
    inv = lax.rsqrt(jnp.sum(wide * wide, axis=1, keepdims=True) + 1e-06)
    return wide * inv, inv


def column_of(row):
    lanes = row.shape[1]
    return jnp.transpose(jnp.broadcast_to(row, (128, lanes)))[:, :1]


def forward_kernel(base_ref, emb_ref, lab_ref, w_ref, a_ref, b_ref, st_ref, xhat_ref, sum_ref, *, classes):
    step = pl.program_id(0)
    tile = w_ref.shape[0]
    batch = emb_ref.shape[0]

    @pl.when(step == 0)
    def _():
        xwide, _ = unit_rows(emb_ref[...].astype(jnp.float32))
        xhat_ref[...] = xwide.astype(jnp.bfloat16)
        sum_ref[...] = jnp.zeros_like(sum_ref)
        a_ref[...] = jnp.zeros_like(a_ref)
        b_ref[...] = jnp.zeros_like(b_ref)

    wwide, _ = unit_rows(w_ref[...].astype(jnp.float32))
    what = wwide.astype(jnp.bfloat16)
    cosine = lax.dot_general(xhat_ref[...], what, NT, preferred_element_type=jnp.float32)
    ids = lax.broadcasted_iota(jnp.int32, (batch, tile), 1)
    is_label = ids == lab_ref[...] - (base_ref[0] + step * tile)
    e = jnp.where(is_label, 0.0, jnp.exp2(cosine * (SCALE * LOG2E) - SCALE * LOG2E))
    partial = e[:, :128]
    for c in range(1, tile // 128):
        partial = partial + e[:, c * 128 : (c + 1) * 128]
    sum_ref[...] += partial
    onehot = jnp.where(is_label, 1.0, 0.0).astype(jnp.bfloat16)
    a_ref[...] += jnp.dot(e.astype(jnp.bfloat16), what, preferred_element_type=jnp.float32)
    b_ref[...] += jnp.dot(onehot, what, preferred_element_type=jnp.float32)

    @pl.when(step == pl.num_programs(0) - 1)
    def _():
        xwide, x_inv = unit_rows(emb_ref[...].astype(jnp.float32))
        label_row = b_ref[...]
        c = jnp.sum(xhat_ref[...].astype(jnp.float32) * label_row, axis=1, keepdims=True)
        offset = lab_ref[...] - base_ref[0]
        has = jnp.where((offset >= 0) & (offset < classes), 1.0, 0.0)
        q = 1.0 - c * c
        sine = jnp.sqrt(jnp.maximum(q, SIN_FLOOR))
        margined = c * math.cos(MARGIN) - sine * math.sin(MARGIN)
        slope = math.cos(MARGIN) + jnp.where(q > SIN_FLOOR, c * math.sin(MARGIN) / sine, 0.0)
        slope = slope * has
        label_e = jnp.exp(SCALE * margined - SCALE) * has
        total = jnp.sum(sum_ref[...], axis=1, keepdims=True) + label_e
        target = SCALE * margined * has
        b = slope * label_row
        a = a_ref[...] + label_e * b
        gain = SCALE * x_inv
        a_ref[...] = (a - xwide * jnp.sum(xwide * a, axis=1, keepdims=True)) * gain
        b_ref[...] = (b - xwide * jnp.sum(xwide * b, axis=1, keepdims=True)) * gain
        lane = lax.broadcasted_iota(jnp.int32, (batch, 128), 1)
        stats = jnp.where(lane == 0, total, 0.0)
        stats = jnp.where(lane == 1, target, stats)
        stats = jnp.where(lane == 2, label_e * slope, stats)
        stats = jnp.where(lane == 3, slope, stats)
        st_ref[...] = jnp.transpose(stats)[:8, :]


def forward(base, emb, labels, weights):
    batch, width = emb.shape
    classes = weights.shape[0]
    tile = math.gcd(classes, 1024)
    whole = lambda i: (0, 0)
    return pl.pallas_call(
        functools.partial(forward_kernel, classes=classes),
        grid=(classes // tile,),
        in_specs=[
            pl.BlockSpec(memory_space=pltpu.SMEM),
            pl.BlockSpec((batch, width), whole),
            pl.BlockSpec((batch, 1), whole),
            pl.BlockSpec((tile, width), lambda i: (i, 0)),
        ],
        out_specs=[
            pl.BlockSpec((batch, width), whole),
            pl.BlockSpec((batch, width), whole),
            pl.BlockSpec((8, batch), whole),
        ],
        out_shape=[
            jax.ShapeDtypeStruct((batch, width), jnp.float32),
            jax.ShapeDtypeStruct((batch, width), jnp.float32),
            jax.ShapeDtypeStruct((8, batch), jnp.float32),
        ],
        scratch_shapes=[pltpu.VMEM((batch, width), jnp.bfloat16), pltpu.VMEM((batch, 128), jnp.float32)],
        compiler_params=pltpu.CompilerParams(
            dimension_semantics=("arbitrary",), vmem_limit_bytes=VMEM_BYTES
        ),
        cost_estimate=pl.CostEstimate(
            flops=6 * batch * classes * width,
            bytes_accessed=classes * width * 2,
            transcendentals=batch * classes,
        ),
        name="forward_sums",
    )(base, emb, labels.reshape(batch, 1), weights)


def weight_kernel(base_ref, emb_ref, lab_ref, st_ref, tot_ref, w_ref, g_ref, xhat_ref, y_ref, v_ref):
    step = pl.program_id(0)
    tile = w_ref.shape[0]
    batch = emb_ref.shape[0]

    @pl.when(step == 0)
    def _():
        xwide, _ = unit_rows(emb_ref[...].astype(jnp.float32))
        xhat = xwide.astype(jnp.bfloat16)
        xhat_ref[...] = xhat
        total = tot_ref[...]
        y_ref[...] = (xhat.astype(jnp.float32) * column_of(SCALE / total)).astype(jnp.bfloat16)
        v_ref[...] = st_ref[2:3, :] - st_ref[3:4, :] * total

    wwide, w_inv = unit_rows(w_ref[...].astype(jnp.float32))
    what = wwide.astype(jnp.bfloat16)
    cosine = lax.dot_general(what, xhat_ref[...], NT, preferred_element_type=jnp.float32)
    ids = lax.broadcasted_iota(jnp.int32, (tile, batch), 0)
    is_label = ids == lab_ref[...] - (base_ref[0] + step * tile)
    e = jnp.exp2(cosine * (SCALE * LOG2E) - SCALE * LOG2E)
    d = jnp.where(is_label, v_ref[...], e).astype(jnp.bfloat16)
    raw = jnp.dot(d, y_ref[...], preferred_element_type=jnp.float32)
    g_ref[...] = (raw - wwide * jnp.sum(wwide * raw, axis=1, keepdims=True)) * w_inv


def weight_gradient(base, emb, labels, stats, totals, weights):
    batch, width = emb.shape
    classes = weights.shape[0]
    tile = math.gcd(classes, 1024)
    whole = lambda i: (0, 0)
    return pl.pallas_call(
        weight_kernel,
        grid=(classes // tile,),
        in_specs=[
            pl.BlockSpec(memory_space=pltpu.SMEM),
            pl.BlockSpec((batch, width), whole),
            pl.BlockSpec((1, batch), whole),
            pl.BlockSpec((8, batch), whole),
            pl.BlockSpec((1, batch), whole),
            pl.BlockSpec((tile, width), lambda i: (i, 0)),
        ],
        out_specs=pl.BlockSpec((tile, width), lambda i: (i, 0)),
        out_shape=jax.ShapeDtypeStruct((classes, width), jnp.float32),
        scratch_shapes=[
            pltpu.VMEM((batch, width), jnp.bfloat16),
            pltpu.VMEM((batch, width), jnp.bfloat16),
            pltpu.VMEM((1, batch), jnp.float32),
        ],
        compiler_params=pltpu.CompilerParams(
            dimension_semantics=("arbitrary",), vmem_limit_bytes=VMEM_BYTES
        ),
        cost_estimate=pl.CostEstimate(
            flops=4 * batch * classes * width,
            bytes_accessed=classes * width * 6,
            transcendentals=batch * classes,
        ),
        name="weight_gradient",
    )(base, emb, labels.reshape(1, batch), stats, totals.reshape(1, batch), weights)


def place_kernel(*refs, sources, started):
    me_ref, slot_ref = refs[:2]
    rows = refs[2 : 2 + len(sources)]
    held_ref, stage_ref = refs[-2:]
    run = rows[0].shape[0]
    for u, (k, row_ref) in enumerate(zip(sources, rows)):
        unit, _ = unit_rows(row_ref[...].astype(jnp.float32))
        stage_ref[pl.ds(u * 2 * run, run, stride=2), :] = unit[:, :128]
        stage_ref[pl.ds(u * 2 * run + 1, run, stride=2), :] = unit[:, 128:]
        first = (me_ref[0] ^ k) * run

        def place(j, carry, u=u, first=first):
            for v in range(16):
                row = j * 16 + v
                slot = slot_ref[first + row]
                held_ref[pl.ds(slot * 2, 2), :] = stage_ref[pl.ds((u * run + row) * 2, 2), :]
            return carry

        lax.fori_loop(0, run // 16, place, 0)


def place_rows(me, slots, rows, sources, held, classes):
    run, width = rows[0].shape
    smem = pl.BlockSpec(memory_space=pltpu.SMEM)
    vmem = pl.BlockSpec(memory_space=pltpu.VMEM)
    started = held is not None
    operands = [me, slots, *rows] + ([held] if started else [])
    return pl.pallas_call(
        functools.partial(place_kernel, sources=tuple(sources), started=started),
        in_specs=[smem, smem] + [vmem] * (len(operands) - 2),
        out_specs=vmem,
        out_shape=jax.ShapeDtypeStruct((2 * classes, 128), jnp.float32),
        input_output_aliases={len(operands) - 1: 0} if started else {},
        scratch_shapes=[pltpu.VMEM((2 * run * len(sources), 128), jnp.float32)],
        compiler_params=pltpu.CompilerParams(vmem_limit_bytes=VMEM_BYTES),
        cost_estimate=pl.CostEstimate(
            flops=10 * len(sources) * run * width,
            bytes_accessed=16 * len(sources) * run * width,
            transcendentals=0,
        ),
        name="place_rows",
    )(*operands)


def blend_kernel(w_ref, held_ref, o_ref):
    wwide, _ = unit_rows(w_ref[...].astype(jnp.float32))
    tile = w_ref.shape[0]
    low = wwide[:, :128] + held_ref[pl.ds(0, tile, stride=2), :]
    high = wwide[:, 128:] + held_ref[pl.ds(1, tile, stride=2), :]
    square = jnp.sum(low * low + high * high, axis=1, keepdims=True)
    inv = lax.rsqrt(square + 1e-06)
    o_ref[:, :128] = (low * inv).astype(jnp.bfloat16)
    o_ref[:, 128:] = (high * inv).astype(jnp.bfloat16)


def blend(weights, held):
    classes, width = weights.shape
    tile = math.gcd(classes, 1024)
    return pl.pallas_call(
        blend_kernel,
        grid=(classes // tile,),
        in_specs=[
            pl.BlockSpec((tile, width), lambda i: (i, 0)),
            pl.BlockSpec((2 * tile, 128), lambda i: (i, 0)),
        ],
        out_specs=pl.BlockSpec((tile, width), lambda i: (i, 0)),
        out_shape=jax.ShapeDtypeStruct((classes, width), jnp.bfloat16),
        compiler_params=pltpu.CompilerParams(
            dimension_semantics=("arbitrary",), vmem_limit_bytes=VMEM_BYTES
        ),
        cost_estimate=pl.CostEstimate(
            flops=10 * classes * width, bytes_accessed=classes * width * 8, transcendentals=classes
        ),
        name="blend",
    )(weights, held)


def shards(embeddings, labels, class_weights, centroids, centroid_class):
    rows_local, width = embeddings.shape
    classes = class_weights.shape[0]
    groups, reps = lax.axis_size("grp"), lax.axis_size("rep")
    peers = groups * reps
    batch = rows_local * reps
    per_peer = classes // peers
    share = rows_local // groups
    grp, rep = lax.axis_index("grp"), lax.axis_index("rep")
    base = ((rep * groups + grp) * classes).astype(jnp.int32).reshape(1)

    slots = centroid_class.reshape(peers, per_peer)
    digits = jnp.concatenate([slots // 128, slots % 128], axis=1).astype(jnp.bfloat16)
    digit_rows = -(-2 * per_peer // width)
    digits = jnp.pad(digits, ((0, 0), (0, digit_rows * width - 2 * per_peer)))
    mine = lax.dynamic_slice_in_dim(embeddings, grp * share, share, 0)
    head = jnp.concatenate(
        [jnp.broadcast_to(mine[None], (peers, share, width)), digits.reshape(peers, digit_rows, width)],
        axis=1,
    )
    head = lax.all_to_all(head, ALL, 0, 0, tiled=True)
    emb = head[:, :share].reshape(batch, width)
    digits = head[:, share:].reshape(peers, digit_rows * width).astype(jnp.int32)
    slots_got = (digits[:, :per_peer] * 128 + digits[:, per_peer : 2 * per_peer]).reshape(-1)
    me = (rep * groups + grp).astype(jnp.int32)
    crossing, near = list(range(peers // 2, peers)), list(range(1, peers // 2))
    order = [k for pair in zip(crossing, near + [0]) for k in pair]
    at = lambda d: d % groups * reps + d // groups
    runs = {}
    for k in order:
        run = lax.dynamic_slice_in_dim(centroids, (me ^ k) * per_peer, per_peer, 0)
        pairs = [(at(d), at(d ^ k)) for d in range(peers)]
        runs[k] = lax.ppermute(run, ("grp", "rep"), pairs) if k else run

    a, b, stats = forward(base, emb, labels, class_weights)
    sums = jnp.broadcast_to(stats[:2].reshape(1, -1, 128), (peers, 2 * batch // 128, 128))
    sums = lax.all_to_all(sums, ALL, 0, 0, tiled=True)
    totals = jnp.sum(sums, axis=0).reshape(2, batch)
    total, target = totals[0], totals[1]
    weight_grad = weight_gradient(base, emb, labels, stats, total, class_weights)
    loss = lax.dynamic_slice_in_dim(SCALE + jnp.log(total) - target, rep * rows_local, rows_local, 0)
    grad = a / total[:, None] - b
    parts = lax.all_to_all(grad.reshape(peers, share, width), ALL, 0, 0, tiled=True)
    own = jnp.sum(parts, axis=0)
    embedding_gradient = lax.all_to_all(
        jnp.broadcast_to(own[None], (groups, share, width)), "grp", 0, 0, tiled=True
    ).reshape(rows_local, width)

    held = None
    step = max(1, peers // GROUPS)
    for first in range(0, peers, step):
        sources = order[first : first + step]
        held = place_rows(me.reshape(1), slots_got, [runs[k] for k in sources], sources, held, classes)
    return (loss, embedding_gradient, weight_grad, blend(class_weights, held))


def solution(mesh):
    in_specs = (
        P("rep", None),
        P(),
        P(("rep", "grp"), None),
        P(("grp", "rep"), None),
        P(("grp", "rep")),
    )
    out_specs = (P("rep"), P("rep", None), P(("rep", "grp"), None), P(("rep", "grp"), None))
    return jax.shard_map(shards, mesh=mesh, in_specs=in_specs, out_specs=out_specs, check_vma=False)
```

```python
import functools
import math

import jax
import jax.numpy as jnp
from jax import lax
from jax.experimental import pallas as pl
from jax.experimental.pallas import tpu as pltpu
from jax.sharding import PartitionSpec as P

SCALE = 32.0
MARGIN = 0.2
SIN_FLOOR = 0.09
LOG2E = math.log2(math.e)
ALL = ("rep", "grp")
VMEM_BYTES = 28 * 1024 * 1024

NT = (((1,), (1,)), ((), ()))


def unit_rows(wide):
    inv = lax.rsqrt(jnp.sum(wide * wide, axis=1, keepdims=True) + 1e-06)
    return wide * inv, inv


def column_of(row):
    lanes = row.shape[1]
    return jnp.transpose(jnp.broadcast_to(row, (128, lanes)))[:, :1]


def forward_kernel(base_ref, rep_ref, lab_ref, w_ref, *refs, classes, reps):
    blocks = refs[:reps]
    emb_ref, a_ref, b_ref, st_ref, xhat_ref, sum_ref = refs[reps:]
    step = pl.program_id(0)
    tile = w_ref.shape[0]
    batch = emb_ref.shape[0]

    @pl.when(step == 0)
    def _():
        for k, block_ref in enumerate(blocks):
            rows = block_ref.shape[0]
            first = pl.multiple_of((rep_ref[0] ^ k) * rows, rows)
            emb_ref[pl.ds(first, rows), :] = block_ref[...]
        xwide, _ = unit_rows(emb_ref[...].astype(jnp.float32))
        xhat_ref[...] = xwide.astype(jnp.bfloat16)
        sum_ref[...] = jnp.zeros_like(sum_ref)
        a_ref[...] = jnp.zeros_like(a_ref)
        b_ref[...] = jnp.zeros_like(b_ref)

    wwide, _ = unit_rows(w_ref[...].astype(jnp.float32))
    what = wwide.astype(jnp.bfloat16)
    cosine = lax.dot_general(xhat_ref[...], what, NT, preferred_element_type=jnp.float32)
    ids = lax.broadcasted_iota(jnp.int32, (batch, tile), 1)
    is_label = ids == lab_ref[...] - (base_ref[0] + step * tile)
    e = jnp.where(is_label, 0.0, jnp.exp2(cosine * (SCALE * LOG2E) - SCALE * LOG2E))
    partial = e[:, :128]
    for c in range(1, tile // 128):
        partial = partial + e[:, c * 128 : (c + 1) * 128]
    sum_ref[...] += partial
    onehot = jnp.where(is_label, 1.0, 0.0).astype(jnp.bfloat16)
    a_ref[...] += jnp.dot(e.astype(jnp.bfloat16), what, preferred_element_type=jnp.float32)
    b_ref[...] += jnp.dot(onehot, what, preferred_element_type=jnp.float32)

    @pl.when(step == pl.num_programs(0) - 1)
    def _():
        xwide, x_inv = unit_rows(emb_ref[...].astype(jnp.float32))
        label_row = b_ref[...]
        c = jnp.sum(xhat_ref[...].astype(jnp.float32) * label_row, axis=1, keepdims=True)
        offset = lab_ref[...] - base_ref[0]
        has = jnp.where((offset >= 0) & (offset < classes), 1.0, 0.0)
        q = 1.0 - c * c
        sine = jnp.sqrt(jnp.maximum(q, SIN_FLOOR))
        margined = c * math.cos(MARGIN) - sine * math.sin(MARGIN)
        slope = math.cos(MARGIN) + jnp.where(q > SIN_FLOOR, c * math.sin(MARGIN) / sine, 0.0)
        slope = slope * has
        label_e = jnp.exp(SCALE * margined - SCALE) * has
        total = jnp.sum(sum_ref[...], axis=1, keepdims=True) + label_e
        target = SCALE * margined * has
        b = slope * label_row
        a = a_ref[...] + label_e * b
        gain = SCALE * x_inv
        a_ref[...] = (a - xwide * jnp.sum(xwide * a, axis=1, keepdims=True)) * gain
        b_ref[...] = (b - xwide * jnp.sum(xwide * b, axis=1, keepdims=True)) * gain
        lane = lax.broadcasted_iota(jnp.int32, (batch, 128), 1)
        stats = jnp.where(lane == 0, total, 0.0)
        stats = jnp.where(lane == 1, target, stats)
        stats = jnp.where(lane == 2, label_e * slope, stats)
        stats = jnp.where(lane == 3, slope, stats)
        st_ref[...] = jnp.transpose(stats)[:8, :]


def forward(base, rep, blocks, labels, weights):
    rows, width = blocks[0].shape
    reps = len(blocks)
    batch = rows * reps
    classes = weights.shape[0]
    tile = math.gcd(classes, 1024)
    whole = lambda i: (0, 0)
    smem = pl.BlockSpec(memory_space=pltpu.SMEM)
    return pl.pallas_call(
        functools.partial(forward_kernel, classes=classes, reps=reps),
        grid=(classes // tile,),
        in_specs=[
            smem,
            smem,
            pl.BlockSpec((batch, 1), whole),
            pl.BlockSpec((tile, width), lambda i: (i, 0)),
        ]
        + [pl.BlockSpec((rows, width), whole)] * reps,
        out_specs=[
            pl.BlockSpec((batch, width), whole),
            pl.BlockSpec((batch, width), whole),
            pl.BlockSpec((batch, width), whole),
            pl.BlockSpec((8, batch), whole),
        ],
        out_shape=[
            jax.ShapeDtypeStruct((batch, width), jnp.bfloat16),
            jax.ShapeDtypeStruct((batch, width), jnp.float32),
            jax.ShapeDtypeStruct((batch, width), jnp.float32),
            jax.ShapeDtypeStruct((8, batch), jnp.float32),
        ],
        scratch_shapes=[pltpu.VMEM((batch, width), jnp.bfloat16), pltpu.VMEM((batch, 128), jnp.float32)],
        compiler_params=pltpu.CompilerParams(
            dimension_semantics=("arbitrary",), vmem_limit_bytes=VMEM_BYTES
        ),
        cost_estimate=pl.CostEstimate(
            flops=6 * batch * classes * width,
            bytes_accessed=classes * width * 2,
            transcendentals=batch * classes,
        ),
        name="forward_sums",
    )(base, rep, labels.reshape(batch, 1), weights, *blocks)


def weight_kernel(base_ref, emb_ref, lab_ref, st_ref, tot_ref, w_ref, g_ref, xhat_ref, y_ref, v_ref):
    step = pl.program_id(0)
    tile = w_ref.shape[0]
    batch = emb_ref.shape[0]

    @pl.when(step == 0)
    def _():
        xwide, _ = unit_rows(emb_ref[...].astype(jnp.float32))
        xhat = xwide.astype(jnp.bfloat16)
        xhat_ref[...] = xhat
        total = tot_ref[...]
        y_ref[...] = (xhat.astype(jnp.float32) * column_of(SCALE / total)).astype(jnp.bfloat16)
        v_ref[...] = st_ref[2:3, :] - st_ref[3:4, :] * total

    wwide, w_inv = unit_rows(w_ref[...].astype(jnp.float32))
    what = wwide.astype(jnp.bfloat16)
    cosine = lax.dot_general(what, xhat_ref[...], NT, preferred_element_type=jnp.float32)
    ids = lax.broadcasted_iota(jnp.int32, (tile, batch), 0)
    is_label = ids == lab_ref[...] - (base_ref[0] + step * tile)
    e = jnp.exp2(cosine * (SCALE * LOG2E) - SCALE * LOG2E)
    d = jnp.where(is_label, v_ref[...], e).astype(jnp.bfloat16)
    raw = jnp.dot(d, y_ref[...], preferred_element_type=jnp.float32)
    g_ref[...] = (raw - wwide * jnp.sum(wwide * raw, axis=1, keepdims=True)) * w_inv


def weight_gradient(base, emb, labels, stats, totals, weights):
    batch, width = emb.shape
    classes = weights.shape[0]
    tile = math.gcd(classes, 1024)
    whole = lambda i: (0, 0)
    return pl.pallas_call(
        weight_kernel,
        grid=(classes // tile,),
        in_specs=[
            pl.BlockSpec(memory_space=pltpu.SMEM),
            pl.BlockSpec((batch, width), whole),
            pl.BlockSpec((1, batch), whole),
            pl.BlockSpec((8, batch), whole),
            pl.BlockSpec((1, batch), whole),
            pl.BlockSpec((tile, width), lambda i: (i, 0)),
        ],
        out_specs=pl.BlockSpec((tile, width), lambda i: (i, 0)),
        out_shape=jax.ShapeDtypeStruct((classes, width), jnp.float32),
        scratch_shapes=[
            pltpu.VMEM((batch, width), jnp.bfloat16),
            pltpu.VMEM((batch, width), jnp.bfloat16),
            pltpu.VMEM((1, batch), jnp.float32),
        ],
        compiler_params=pltpu.CompilerParams(
            dimension_semantics=("arbitrary",), vmem_limit_bytes=VMEM_BYTES
        ),
        cost_estimate=pl.CostEstimate(
            flops=4 * batch * classes * width,
            bytes_accessed=classes * width * 6,
            transcendentals=batch * classes,
        ),
        name="weight_gradient",
    )(base, emb, labels.reshape(1, batch), stats, totals.reshape(1, batch), weights)


def fetch_kernel(me_ref, rows_ref, *refs, sources, tokens):
    outs, sem = refs[tokens : tokens + len(sources)], refs[-1]
    copies = []
    for u, (k, out_ref) in enumerate(zip(sources, outs)):
        run = out_ref.shape[0]
        first = pl.multiple_of((me_ref[0] ^ k) * run, run)
        copies.append(pltpu.make_async_copy(rows_ref.at[pl.ds(first, run), :], out_ref, sem.at[u]))
    for copy in copies:
        copy.start()
    for copy in copies:
        copy.wait()


def fetch_runs(me, rows, run, sources, tokens):
    anywhere = pl.BlockSpec(memory_space=pl.ANY)
    return pl.pallas_call(
        functools.partial(fetch_kernel, sources=tuple(sources), tokens=len(tokens)),
        in_specs=[pl.BlockSpec(memory_space=pltpu.SMEM)] + [anywhere] * (1 + len(tokens)),
        out_specs=[anywhere] * len(sources),
        out_shape=[jax.ShapeDtypeStruct((run, rows.shape[1]), rows.dtype)] * len(sources),
        scratch_shapes=[pltpu.SemaphoreType.DMA((len(sources),))],
        cost_estimate=pl.CostEstimate(
            flops=0, bytes_accessed=4 * len(sources) * run * rows.shape[1], transcendentals=0
        ),
        name="fetch_runs",
    )(me, rows, *tokens)


def place_kernel(*refs, sources):
    me_ref, slot_ref = refs[:2]
    rows = refs[2 : 2 + len(sources)]
    held_ref, token_ref, stage_ref = refs[-3:]
    run = rows[0].shape[0]
    batch = math.gcd(run, 32)
    token_ref[...] = jnp.zeros_like(token_ref)
    for u, (k, row_ref) in enumerate(zip(sources, rows)):
        unit, _ = unit_rows(row_ref[...].astype(jnp.float32))
        stage_ref[pl.ds(u * 2 * run, run, stride=2), :] = unit[:, :128]
        stage_ref[pl.ds(u * 2 * run + 1, run, stride=2), :] = unit[:, 128:]
        first = (me_ref[0] ^ k) * run

        def place(j, carry, u=u, first=first):
            at = j * batch
            slots = [slot_ref[first + at + v] for v in range(batch)]
            values = [stage_ref[pl.ds((u * run + at + v) * 2, 2), :] for v in range(batch)]
            for slot, value in zip(slots, values):
                held_ref[pl.ds(slot * 2, 2), :] = value
            return carry

        lax.fori_loop(0, run // batch, place, 0)


def place_rows(me, slots, rows, sources, held, classes):
    run, width = rows[0].shape
    smem = pl.BlockSpec(memory_space=pltpu.SMEM)
    vmem = pl.BlockSpec(memory_space=pltpu.VMEM)
    operands = [me, slots, *rows] + ([] if held is None else [held])
    return pl.pallas_call(
        functools.partial(place_kernel, sources=tuple(sources)),
        in_specs=[smem, smem] + [vmem] * (len(operands) - 2),
        out_specs=[vmem, vmem],
        out_shape=[
            jax.ShapeDtypeStruct((2 * classes, 128), jnp.float32),
            jax.ShapeDtypeStruct((8, 128), jnp.float32),
        ],
        input_output_aliases={} if held is None else {len(operands) - 1: 0},
        scratch_shapes=[pltpu.VMEM((2 * run * len(sources), 128), jnp.float32)],
        compiler_params=pltpu.CompilerParams(vmem_limit_bytes=VMEM_BYTES),
        cost_estimate=pl.CostEstimate(
            flops=10 * len(sources) * run * width,
            bytes_accessed=16 * len(sources) * run * width,
            transcendentals=0,
        ),
        name="place_rows",
    )(*operands)


def blend_kernel(w_ref, held_ref, o_ref):
    wwide, _ = unit_rows(w_ref[...].astype(jnp.float32))
    tile = w_ref.shape[0]
    first = pl.multiple_of(pl.program_id(0) * 2 * tile, 2 * tile)
    low = wwide[:, :128] + held_ref[pl.ds(first, tile, stride=2), :]
    high = wwide[:, 128:] + held_ref[pl.ds(first + 1, tile, stride=2), :]
    square = jnp.sum(low * low + high * high, axis=1, keepdims=True)
    inv = lax.rsqrt(square + 1e-06)
    o_ref[:, :128] = (low * inv).astype(jnp.bfloat16)
    o_ref[:, 128:] = (high * inv).astype(jnp.bfloat16)


def blend(weights, held):
    classes, width = weights.shape
    tile = math.gcd(classes, 1024)
    return pl.pallas_call(
        blend_kernel,
        grid=(classes // tile,),
        in_specs=[
            pl.BlockSpec((tile, width), lambda i: (i, 0)),
            pl.BlockSpec(memory_space=pltpu.VMEM),
        ],
        out_specs=pl.BlockSpec((tile, width), lambda i: (i, 0)),
        out_shape=jax.ShapeDtypeStruct((classes, width), jnp.bfloat16),
        compiler_params=pltpu.CompilerParams(
            dimension_semantics=("arbitrary",), vmem_limit_bytes=VMEM_BYTES
        ),
        cost_estimate=pl.CostEstimate(
            flops=10 * classes * width, bytes_accessed=classes * width * 8, transcendentals=classes
        ),
        name="blend",
    )(weights, held)


def shards(embeddings, labels, class_weights, centroids, centroid_class):
    rows_local, width = embeddings.shape
    classes = class_weights.shape[0]
    groups, reps = lax.axis_size("grp"), lax.axis_size("rep")
    peers = groups * reps
    batch = rows_local * reps
    run = classes // peers
    share = rows_local // groups
    grp, rep = lax.axis_index("grp").astype(jnp.int32), lax.axis_index("rep").astype(jnp.int32)
    me = rep * groups + grp
    base, me = (me * classes).reshape(1), me.reshape(1)
    at = lambda d: d % groups * reps + d // groups

    def exchange(value, k):
        return lax.ppermute(value, ("grp", "rep"), [(at(d), at(d ^ k)) for d in range(peers)])

    blocks = [embeddings] + [
        lax.ppermute(embeddings, "rep", [(i, i ^ k) for i in range(reps)]) for k in range(1, reps)
    ]
    far, near = list(range(peers // 2, peers)), list(range(1, peers // 2))
    order = [k for pair in zip(far, near) for k in pair] + far[len(near) :]
    cuts = [0] + [round(len(order) * c / 31) for c in (5, 12, 19, 26, 31)]
    plan = [order[i:j] for i, j in zip(cuts, cuts[1:])]

    def send(group, tokens):
        fetched = fetch_runs(me, centroids, run, plan[group], tokens)
        return [exchange(value, k) for value, k in zip(fetched, plan[group])]

    got = [send(0, [])]
    emb, a, b, stats = forward(base, rep.reshape(1), blocks, labels, class_weights)
    got.append(send(1, [stats]))

    flat = [
        jnp.broadcast_to(stats[0][None], (peers, batch)),
        centroid_class.reshape(peers, run).astype(jnp.float32),
        jnp.repeat(stats[1].reshape(reps, rows_local), groups, axis=0),
    ]
    size = batch + run + rows_local
    pad = -size % 1024
    flat = jnp.pad(jnp.concatenate(flat, axis=1), ((0, 0), (0, pad)))
    flat = lax.all_to_all(flat.reshape(peers, -1, 128), ALL, 0, 0, tiled=True).reshape(peers, -1)
    total = jnp.sum(flat[:, :batch], axis=0)
    slots = flat[:, batch : batch + run].reshape(-1).astype(jnp.int32)
    target = jnp.sum(flat[:, batch + run : size], axis=0)
    own_total = lax.dynamic_slice_in_dim(total, rep * rows_local, rows_local, 0)
    loss = SCALE + jnp.log(own_total) - target

    grad = a / total[:, None] - b
    parts = lax.all_to_all(grad.reshape(peers, share, width), ALL, 0, 0, tiled=True)
    own = jnp.sum(parts, axis=0)
    embedding_gradient = lax.all_to_all(
        jnp.broadcast_to(own[None], (groups, share, width)), "grp", 0, 0, tiled=True
    ).reshape(rows_local, width)

    weight_grad = weight_gradient(base, emb, labels, stats, total, class_weights)
    mine = list(fetch_runs(me, centroids, run, [0], [stats]))
    held, token = place_rows(me, slots, got[0] + mine, plan[0] + [0], None, classes)
    tokens = [token, weight_grad]
    for group in range(1, len(plan)):
        if group + 1 < len(plan):
            got.append(send(group + 1, tokens))
        held, token = place_rows(me, slots, got[group], plan[group], held, classes)
        tokens = [token]
    return (loss, embedding_gradient, weight_grad, blend(class_weights, held))


def solution(mesh):
    in_specs = (
        P("rep", None),
        P(),
        P(("rep", "grp"), None),
        P(("grp", "rep"), None),
        P(("grp", "rep")),
    )
    out_specs = (P("rep"), P("rep", None), P(("rep", "grp"), None), P(("rep", "grp"), None))
    return jax.shard_map(shards, mesh=mesh, in_specs=in_specs, out_specs=out_specs, check_vma=False)
```

```python
import functools
import math

import jax
import jax.numpy as jnp
from jax import lax
from jax.experimental import pallas as pl
from jax.experimental.pallas import tpu as pltpu
from jax.sharding import PartitionSpec as P

SCALE = 32.0
MARGIN = 0.2
SIN_FLOOR = 0.09
LOG2E = math.log2(math.e)
ALL = ("rep", "grp")
MIB = 1024 * 1024
COST = pl.CostEstimate(flops=1, bytes_accessed=1, transcendentals=0)

NT = (((1,), (1,)), ((), ()))


def unit_rows(wide):
    inv = lax.rsqrt(jnp.sum(wide * wide, axis=1, keepdims=True) + 1e-06)
    return wide * inv, inv


def column_of(row):
    lanes = row.shape[1]
    return jnp.transpose(jnp.broadcast_to(row, (128, lanes)))[:, :1]


def forward_kernel(base_ref, rep_ref, lab_ref, w_ref, *refs, classes, reps):
    blocks = refs[:reps]
    emb_ref, a_ref, b_ref, st_ref, xhat_ref, sum_ref = refs[reps:]
    step = pl.program_id(0)
    tile = w_ref.shape[0]
    batch = emb_ref.shape[0]

    @pl.when(step == 0)
    def _():
        for k, block_ref in enumerate(blocks):
            rows = block_ref.shape[0]
            first = pl.multiple_of((rep_ref[0] ^ k) * rows, rows)
            emb_ref[pl.ds(first, rows), :] = block_ref[...]
        xwide, _ = unit_rows(emb_ref[...].astype(jnp.float32))
        xhat_ref[...] = xwide.astype(jnp.bfloat16)
        sum_ref[...] = jnp.zeros_like(sum_ref)
        a_ref[...] = jnp.zeros_like(a_ref)
        b_ref[...] = jnp.zeros_like(b_ref)

    wwide, _ = unit_rows(w_ref[...].astype(jnp.float32))
    what = wwide.astype(jnp.bfloat16)
    cosine = lax.dot_general(xhat_ref[...], what, NT, preferred_element_type=jnp.float32)
    ids = lax.broadcasted_iota(jnp.int32, (batch, tile), 1)
    is_label = ids == lab_ref[...] - (base_ref[0] + step * tile)
    e = jnp.where(is_label, 0.0, jnp.exp2(cosine * (SCALE * LOG2E) - SCALE * LOG2E))
    partial = e[:, :128]
    for c in range(1, tile // 128):
        partial = partial + e[:, c * 128 : (c + 1) * 128]
    sum_ref[...] += partial
    onehot = jnp.where(is_label, 1.0, 0.0).astype(jnp.bfloat16)
    a_ref[...] += jnp.dot(e.astype(jnp.bfloat16), what, preferred_element_type=jnp.float32)
    b_ref[...] += jnp.dot(onehot, what, preferred_element_type=jnp.float32)

    @pl.when(step == pl.num_programs(0) - 1)
    def _():
        xwide, x_inv = unit_rows(emb_ref[...].astype(jnp.float32))
        label_row = b_ref[...]
        c = jnp.sum(xhat_ref[...].astype(jnp.float32) * label_row, axis=1, keepdims=True)
        offset = lab_ref[...] - base_ref[0]
        has = jnp.where((offset >= 0) & (offset < classes), 1.0, 0.0)
        q = 1.0 - c * c
        sine = jnp.sqrt(jnp.maximum(q, SIN_FLOOR))
        margined = c * math.cos(MARGIN) - sine * math.sin(MARGIN)
        slope = math.cos(MARGIN) + jnp.where(q > SIN_FLOOR, c * math.sin(MARGIN) / sine, 0.0)
        slope = slope * has
        label_e = jnp.exp(SCALE * margined - SCALE) * has
        total = jnp.sum(sum_ref[...], axis=1, keepdims=True) + label_e
        target = SCALE * margined * has
        b = slope * label_row
        a = a_ref[...] + label_e * b
        gain = SCALE * x_inv
        a_ref[...] = (a - xwide * jnp.sum(xwide * a, axis=1, keepdims=True)) * gain
        b_ref[...] = (b - xwide * jnp.sum(xwide * b, axis=1, keepdims=True)) * gain
        lane = lax.broadcasted_iota(jnp.int32, (batch, 128), 1)
        stats = jnp.where(lane == 0, total, 0.0)
        stats = jnp.where(lane == 1, target, stats)
        stats = jnp.where(lane == 2, label_e * slope, stats)
        stats = jnp.where(lane == 3, slope, stats)
        st_ref[...] = jnp.transpose(stats)[:8, :]


def forward(base, rep, blocks, labels, weights):
    rows, width = blocks[0].shape
    reps = len(blocks)
    batch = rows * reps
    classes = weights.shape[0]
    tile = math.gcd(classes, 1024)
    whole = lambda i: (0, 0)
    smem = pl.BlockSpec(memory_space=pltpu.SMEM)
    return pl.pallas_call(
        functools.partial(forward_kernel, classes=classes, reps=reps),
        grid=(classes // tile,),
        in_specs=[
            smem,
            smem,
            pl.BlockSpec((batch, 1), whole),
            pl.BlockSpec((tile, width), lambda i: (i, 0)),
        ]
        + [pl.BlockSpec((rows, width), whole)] * reps,
        out_specs=[
            pl.BlockSpec((batch, width), whole),
            pl.BlockSpec((batch, width), whole),
            pl.BlockSpec((batch, width), whole),
            pl.BlockSpec((8, batch), whole),
        ],
        out_shape=[
            jax.ShapeDtypeStruct((batch, width), jnp.bfloat16),
            jax.ShapeDtypeStruct((batch, width), jnp.float32),
            jax.ShapeDtypeStruct((batch, width), jnp.float32),
            jax.ShapeDtypeStruct((8, batch), jnp.float32),
        ],
        scratch_shapes=[pltpu.VMEM((batch, width), jnp.bfloat16), pltpu.VMEM((batch, 128), jnp.float32)],
        compiler_params=pltpu.CompilerParams(
            dimension_semantics=("arbitrary",), vmem_limit_bytes=20 * MIB
        ),
        cost_estimate=pl.CostEstimate(
            flops=12 * batch * classes * width, bytes_accessed=classes * width * 2, transcendentals=0
        ),
        name="forward_sums",
    )(base, rep, labels.reshape(batch, 1), weights, *blocks)


def weight_kernel(base_ref, emb_ref, lab_ref, st_ref, tot_ref, w_ref, g_ref, xhat_ref, y_ref, v_ref):
    step = pl.program_id(0)
    tile = w_ref.shape[0]
    batch = emb_ref.shape[0]

    @pl.when(step == 0)
    def _():
        xwide, _ = unit_rows(emb_ref[...].astype(jnp.float32))
        xhat = xwide.astype(jnp.bfloat16)
        xhat_ref[...] = xhat
        total = tot_ref[...]
        y_ref[...] = (xhat.astype(jnp.float32) * column_of(SCALE / total)).astype(jnp.bfloat16)
        v_ref[...] = st_ref[2:3, :] - st_ref[3:4, :] * total

    wwide, w_inv = unit_rows(w_ref[...].astype(jnp.float32))
    what = wwide.astype(jnp.bfloat16)
    cosine = lax.dot_general(what, xhat_ref[...], NT, preferred_element_type=jnp.float32)
    ids = lax.broadcasted_iota(jnp.int32, (tile, batch), 0)
    is_label = ids == lab_ref[...] - (base_ref[0] + step * tile)
    e = jnp.exp2(cosine * (SCALE * LOG2E) - SCALE * LOG2E)
    d = jnp.where(is_label, v_ref[...], e).astype(jnp.bfloat16)
    raw = jnp.dot(d, y_ref[...], preferred_element_type=jnp.float32)
    g_ref[...] = (raw - wwide * jnp.sum(wwide * raw, axis=1, keepdims=True)) * w_inv


def weight_gradient(base, emb, labels, stats, totals, weights):
    batch, width = emb.shape
    classes = weights.shape[0]
    tile = math.gcd(classes, 1024)
    whole = lambda i: (0, 0)
    return pl.pallas_call(
        weight_kernel,
        grid=(classes // tile,),
        in_specs=[
            pl.BlockSpec(memory_space=pltpu.SMEM),
            pl.BlockSpec((batch, width), whole),
            pl.BlockSpec((1, batch), whole),
            pl.BlockSpec((8, batch), whole),
            pl.BlockSpec((1, batch), whole),
            pl.BlockSpec((tile, width), lambda i: (i, 0)),
        ],
        out_specs=pl.BlockSpec((tile, width), lambda i: (i, 0)),
        out_shape=jax.ShapeDtypeStruct((classes, width), jnp.float32),
        scratch_shapes=[
            pltpu.VMEM((batch, width), jnp.bfloat16),
            pltpu.VMEM((batch, width), jnp.bfloat16),
            pltpu.VMEM((1, batch), jnp.float32),
        ],
        compiler_params=pltpu.CompilerParams(
            dimension_semantics=("arbitrary",), vmem_limit_bytes=20 * MIB
        ),
        cost_estimate=pl.CostEstimate(
            flops=12 * batch * classes * width, bytes_accessed=classes * width * 6, transcendentals=0
        ),
        name="weight_gradient",
    )(base, emb, labels.reshape(1, batch), stats, totals.reshape(1, batch), weights)


def fetch_kernel(me_ref, rows_ref, *refs, picks, tokens):
    outs, sem = refs[tokens : tokens + len(picks)], refs[-1]
    copies = []
    for u, (k, out_ref) in enumerate(zip(picks, outs)):
        size = out_ref.shape[0]
        first = pl.multiple_of((me_ref[0] ^ k) * size, size)
        copies.append(pltpu.make_async_copy(rows_ref.at[pl.ds(first, size), :], out_ref, sem.at[u]))
    for copy in copies:
        copy.start()
    for copy in copies:
        copy.wait()


def fetch(me, rows, size, picks, tokens):
    anywhere = pl.BlockSpec(memory_space=pl.ANY)
    return pl.pallas_call(
        functools.partial(fetch_kernel, picks=tuple(picks), tokens=len(tokens)),
        in_specs=[pl.BlockSpec(memory_space=pltpu.SMEM)] + [anywhere] * (1 + len(tokens)),
        out_specs=[pl.BlockSpec(memory_space=pltpu.VMEM)] * len(picks),
        out_shape=[jax.ShapeDtypeStruct((size, rows.shape[1]), rows.dtype)] * len(picks),
        scratch_shapes=[pltpu.SemaphoreType.DMA((len(picks),))],
        compiler_params=pltpu.CompilerParams(vmem_limit_bytes=4 * MIB),
        cost_estimate=COST,
        name="fetch",
    )(me, rows, *tokens)


def tie_kernel(value_ref, *refs):
    refs[-1][...] = value_ref[...]


def tie(value, tokens):
    anywhere = pl.BlockSpec(memory_space=pl.ANY)
    vmem = pl.BlockSpec(memory_space=pltpu.VMEM)
    return pl.pallas_call(
        tie_kernel,
        in_specs=[vmem] + [anywhere] * len(tokens),
        out_specs=vmem,
        out_shape=jax.ShapeDtypeStruct(value.shape, value.dtype),
        compiler_params=pltpu.CompilerParams(vmem_limit_bytes=2 * MIB),
        cost_estimate=COST,
        name="tie",
    )(value, *tokens)


def place_runs(info_ref, slot_ref, row_refs, origins, groups, held_ref, stage_ref):
    run = stage_ref.shape[0] // 2
    batch = math.gcd(run, 32)
    parts = [(ref, u) for ref in row_refs for u in range(ref.shape[0] // run)]
    for (row_ref, u), (rep_flip, grp_flip, grp_from) in zip(parts, origins):
        unit, _ = unit_rows(row_ref[u * run : (u + 1) * run, :].astype(jnp.float32))
        stage_ref[pl.ds(0, run, stride=2), :] = unit[:, :128]
        stage_ref[pl.ds(1, run, stride=2), :] = unit[:, 128:]
        grp = info_ref[1] ^ grp_flip if grp_from is None else grp_from
        first = ((info_ref[0] ^ rep_flip) * groups + grp) * run

        def place(j, carry, first=first):
            at = j * batch
            slots = [slot_ref[first + at + v] for v in range(batch)]
            values = [stage_ref[pl.ds((at + v) * 2, 2), :] for v in range(batch)]
            for slot, value in zip(slots, values):
                held_ref[pl.ds(slot * 2, 2), :] = value
            return carry

        lax.fori_loop(0, run // batch, place, 0)


def place_kernel(info_ref, slot_ref, *refs, origins, groups, arrays):
    held_ref, token_ref, stage_ref = refs[-3:]
    token_ref[...] = jnp.zeros_like(token_ref)
    place_runs(info_ref, slot_ref, refs[:arrays], origins, groups, held_ref, stage_ref)


def place_rows(info, slots, arrays, origins, groups, held, classes, run):
    smem = pl.BlockSpec(memory_space=pltpu.SMEM)
    vmem = pl.BlockSpec(memory_space=pltpu.VMEM)
    operands = [info, slots, *arrays] + ([] if held is None else [held])
    return pl.pallas_call(
        functools.partial(
            place_kernel, origins=tuple(origins), groups=groups, arrays=len(arrays)
        ),
        in_specs=[smem, smem] + [vmem] * (len(operands) - 2),
        out_specs=[vmem, vmem],
        out_shape=[
            jax.ShapeDtypeStruct((2 * classes, 128), jnp.float32),
            jax.ShapeDtypeStruct((8, 128), jnp.float32),
        ],
        input_output_aliases={} if held is None else {len(operands) - 1: 0},
        scratch_shapes=[pltpu.VMEM((2 * run, 128), jnp.float32)],
        compiler_params=pltpu.CompilerParams(vmem_limit_bytes=4 * MIB),
        cost_estimate=COST,
        name="place_rows",
    )(*operands)


def blend_kernel(info_ref, slot_ref, w_ref, *refs, origins, groups, arrays):
    o_ref, held_ref, stage_ref = refs[-3:]
    step = pl.program_id(0)
    tile = w_ref.shape[0]

    @pl.when(step == 0)
    def _():
        place_runs(info_ref, slot_ref, refs[:arrays], origins, groups, held_ref, stage_ref)

    wwide, _ = unit_rows(w_ref[...].astype(jnp.float32))
    first = pl.multiple_of(step * 2 * tile, 2 * tile)
    low = wwide[:, :128] + held_ref[pl.ds(first, tile, stride=2), :]
    high = wwide[:, 128:] + held_ref[pl.ds(first + 1, tile, stride=2), :]
    square = jnp.sum(low * low + high * high, axis=1, keepdims=True)
    inv = lax.rsqrt(square + 1e-06)
    o_ref[:, :128] = (low * inv).astype(jnp.bfloat16)
    o_ref[:, 128:] = (high * inv).astype(jnp.bfloat16)


def place_and_blend(info, slots, arrays, origins, groups, held, weights, run):
    classes, width = weights.shape
    tile = math.gcd(classes, 1024)
    smem = pl.BlockSpec(memory_space=pltpu.SMEM)
    vmem = pl.BlockSpec(memory_space=pltpu.VMEM)
    tiles = pl.BlockSpec((tile, width), lambda i: (i, 0))
    refreshed, _ = pl.pallas_call(
        functools.partial(
            blend_kernel, origins=tuple(origins), groups=groups, arrays=len(arrays)
        ),
        grid=(classes // tile,),
        in_specs=[smem, smem, tiles] + [vmem] * (len(arrays) + 1),
        out_specs=[tiles, vmem],
        out_shape=[
            jax.ShapeDtypeStruct((classes, width), jnp.bfloat16),
            jax.ShapeDtypeStruct(held.shape, held.dtype),
        ],
        input_output_aliases={3 + len(arrays): 1},
        scratch_shapes=[pltpu.VMEM((2 * run, 128), jnp.float32)],
        compiler_params=pltpu.CompilerParams(
            dimension_semantics=("arbitrary",), vmem_limit_bytes=10 * MIB
        ),
        cost_estimate=COST,
        name="place_and_blend",
    )(info, slots, weights, *arrays, held)
    return refreshed


def shards(embeddings, labels, class_weights, centroids, centroid_class):
    rows_local, width = embeddings.shape
    classes = class_weights.shape[0]
    groups, reps = lax.axis_size("grp"), lax.axis_size("rep")
    peers = groups * reps
    batch = rows_local * reps
    run = classes // peers
    share = rows_local // groups
    grp, rep = lax.axis_index("grp").astype(jnp.int32), lax.axis_index("rep").astype(jnp.int32)
    me = rep * groups + grp
    base, me = (me * classes).reshape(1), me.reshape(1)
    info = jnp.stack([rep, grp])
    at = lambda d: d % groups * reps + d // groups

    def over_rep(value, k):
        return lax.ppermute(value, "rep", [(i, i ^ k) for i in range(reps)])

    def over_all(value, k):
        return lax.ppermute(value, ("grp", "rep"), [(at(d), at(d ^ k)) for d in range(peers)])

    def hop(picks, tokens):
        fetched = fetch(rep.reshape(1), centroids, groups * run, picks, tokens)
        return {k: over_rep(value, k) if k else value for k, value in zip(picks, fetched)}

    def spread(held_rows, picks):
        parts = [held_rows[k].reshape(groups, run, width) for k in picks]
        parts = lax.all_to_all(jnp.concatenate(parts, axis=1), "grp", 0, 0, tiled=True)
        origins = [(k, 0, g) for g in range(groups) for k in picks]
        return parts.reshape(-1, width), origins

    def direct(picks, tokens):
        fetched = fetch(me, centroids, run, picks, tokens)
        rows = [over_all(value, k) for k, value in zip(picks, fetched)]
        return rows, [(k // groups, k % groups, None) for k in picks]

    half = reps // 2
    far, near = list(range(peers // 2, peers)), list(range(1, half))
    cuts = [round(len(far) * c / 16) for c in (0, 5, 9, 13, 16)]
    plan = [far[i:j] for i, j in zip(cuts, cuts[1:])]

    blocks = [embeddings] + [over_rep(embeddings, k) for k in range(1, reps)]
    rows0, from0 = direct(plan[0], [blocks[1]])
    emb, a, b, stats = forward(base, rep.reshape(1), blocks, labels, class_weights)
    moved = hop(near, [stats])
    moved |= hop([0], [stats])
    rows1, from1 = direct(plan[1], [stats])

    tied = tie(stats, rows0[:3])
    flat = [
        jnp.broadcast_to(tied[0][None], (peers, batch)),
        centroid_class.reshape(peers, run).astype(jnp.float32),
        jnp.repeat(tied[1].reshape(reps, rows_local), groups, axis=0),
    ]
    size = batch + run + rows_local
    flat = jnp.pad(jnp.concatenate(flat, axis=1), ((0, 0), (0, -size % 1024)))
    flat = lax.all_to_all(flat.reshape(peers, -1, 128), ALL, 0, 0, tiled=True).reshape(peers, -1)
    total = jnp.sum(flat[:, :batch], axis=0)
    slots = flat[:, batch : batch + run].reshape(-1).astype(jnp.int32)
    target = jnp.sum(flat[:, batch + run : size], axis=0)
    own_total = lax.dynamic_slice_in_dim(total, rep * rows_local, rows_local, 0)
    loss = SCALE + jnp.log(own_total) - target

    weight_grad = weight_gradient(base, emb, labels, stats, total, class_weights)
    rows2, from2 = direct(plan[2], [weight_grad])

    grad = a / total[:, None] - b
    parts = lax.all_to_all(grad.reshape(peers, share, width), ALL, 0, 0, tiled=True)
    own = jnp.sum(parts, axis=0)
    embedding_gradient = lax.all_to_all(
        jnp.broadcast_to(own[None], (groups, share, width)), "grp", 0, 0, tiled=True
    ).reshape(rows_local, width)

    held, token = place_rows(info, slots, rows0 + rows1, from0 + from1, groups, None, classes, run)
    rows3, from3 = direct(plan[3], [token])
    rows, origins = spread(moved, [0] + near)
    held, _ = place_rows(
        info, slots, [rows, *rows2], origins + from2, groups, held, classes, run
    )
    refreshed = place_and_blend(info, slots, rows3, from3, groups, held, class_weights, run)
    return (loss, embedding_gradient, weight_grad, refreshed)


def solution(mesh):
    in_specs = (
        P("rep", None),
        P(),
        P(("rep", "grp"), None),
        P(("grp", "rep"), None),
        P(("grp", "rep")),
    )
    out_specs = (P("rep"), P("rep", None), P(("rep", "grp"), None), P(("rep", "grp"), None))
    return jax.shard_map(shards, mesh=mesh, in_specs=in_specs, out_specs=out_specs, check_vma=False)
```

```python
import functools
import math

import jax
import jax.numpy as jnp
from jax import lax
from jax.experimental import pallas as pl
from jax.experimental.pallas import tpu as pltpu
from jax.sharding import PartitionSpec as P

SCALE = 32.0
MARGIN = 0.2
SIN_FLOOR = 0.09
LOG2E = math.log2(math.e)
ALL = ("rep", "grp")
MIB = 1024 * 1024
COST = pl.CostEstimate(flops=1, bytes_accessed=1, transcendentals=0)

NT = (((1,), (1,)), ((), ()))


def unit_rows(wide):
    inv = lax.rsqrt(jnp.sum(wide * wide, axis=1, keepdims=True) + 1e-06)
    return wide * inv, inv


def column_of(row):
    lanes = row.shape[1]
    return jnp.transpose(jnp.broadcast_to(row, (128, lanes)))[:, :1]


def forward_kernel(base_ref, rep_ref, lab_ref, w_ref, *refs, classes, reps):
    blocks = refs[:reps]
    emb_ref, a_ref, b_ref, st_ref, xhat_ref, sum_ref = refs[reps:]
    step = pl.program_id(0)
    tile = w_ref.shape[0]
    batch = emb_ref.shape[0]

    @pl.when(step == 0)
    def _():
        for k, block_ref in enumerate(blocks):
            rows = block_ref.shape[0]
            first = pl.multiple_of((rep_ref[0] ^ k) * rows, rows)
            emb_ref[pl.ds(first, rows), :] = block_ref[...]
        xwide, _ = unit_rows(emb_ref[...].astype(jnp.float32))
        xhat_ref[...] = xwide.astype(jnp.bfloat16)
        sum_ref[...] = jnp.zeros_like(sum_ref)
        a_ref[...] = jnp.zeros_like(a_ref)
        b_ref[...] = jnp.zeros_like(b_ref)

    wwide, _ = unit_rows(w_ref[...].astype(jnp.float32))
    what = wwide.astype(jnp.bfloat16)
    cosine = lax.dot_general(xhat_ref[...], what, NT, preferred_element_type=jnp.float32)
    ids = lax.broadcasted_iota(jnp.int32, (batch, tile), 1)
    is_label = ids == lab_ref[...] - (base_ref[0] + step * tile)
    e = jnp.where(is_label, 0.0, jnp.exp2(cosine * (SCALE * LOG2E) - SCALE * LOG2E))
    partial = e[:, :128]
    for c in range(1, tile // 128):
        partial = partial + e[:, c * 128 : (c + 1) * 128]
    sum_ref[...] += partial
    onehot = jnp.where(is_label, 1.0, 0.0).astype(jnp.bfloat16)
    a_ref[...] += jnp.dot(e.astype(jnp.bfloat16), what, preferred_element_type=jnp.float32)
    b_ref[...] += jnp.dot(onehot, what, preferred_element_type=jnp.float32)

    @pl.when(step == pl.num_programs(0) - 1)
    def _():
        xwide, x_inv = unit_rows(emb_ref[...].astype(jnp.float32))
        label_row = b_ref[...]
        c = jnp.sum(xhat_ref[...].astype(jnp.float32) * label_row, axis=1, keepdims=True)
        offset = lab_ref[...] - base_ref[0]
        has = jnp.where((offset >= 0) & (offset < classes), 1.0, 0.0)
        q = 1.0 - c * c
        sine = jnp.sqrt(jnp.maximum(q, SIN_FLOOR))
        margined = c * math.cos(MARGIN) - sine * math.sin(MARGIN)
        slope = math.cos(MARGIN) + jnp.where(q > SIN_FLOOR, c * math.sin(MARGIN) / sine, 0.0)
        slope = slope * has
        label_e = jnp.exp(SCALE * margined - SCALE) * has
        total = jnp.sum(sum_ref[...], axis=1, keepdims=True) + label_e
        target = SCALE * margined * has
        b = slope * label_row
        a = a_ref[...] + label_e * b
        gain = SCALE * x_inv
        a_ref[...] = (a - xwide * jnp.sum(xwide * a, axis=1, keepdims=True)) * gain
        b_ref[...] = (b - xwide * jnp.sum(xwide * b, axis=1, keepdims=True)) * gain
        lane = lax.broadcasted_iota(jnp.int32, (batch, 128), 1)
        stats = jnp.where(lane == 0, total, 0.0)
        stats = jnp.where(lane == 1, target, stats)
        stats = jnp.where(lane == 2, label_e * slope, stats)
        stats = jnp.where(lane == 3, slope, stats)
        st_ref[...] = jnp.transpose(stats)[:8, :]


def forward(base, rep, blocks, labels, weights):
    rows, width = blocks[0].shape
    reps = len(blocks)
    batch = rows * reps
    classes = weights.shape[0]
    tile = math.gcd(classes, 1024)
    whole = lambda i: (0, 0)
    smem = pl.BlockSpec(memory_space=pltpu.SMEM)
    return pl.pallas_call(
        functools.partial(forward_kernel, classes=classes, reps=reps),
        grid=(classes // tile,),
        in_specs=[
            smem,
            smem,
            pl.BlockSpec((batch, 1), whole),
            pl.BlockSpec((tile, width), lambda i: (i, 0)),
        ]
        + [pl.BlockSpec((rows, width), whole)] * reps,
        out_specs=[
            pl.BlockSpec((batch, width), whole),
            pl.BlockSpec((batch, width), whole),
            pl.BlockSpec((batch, width), whole),
            pl.BlockSpec((8, batch), whole),
        ],
        out_shape=[
            jax.ShapeDtypeStruct((batch, width), jnp.bfloat16),
            jax.ShapeDtypeStruct((batch, width), jnp.float32),
            jax.ShapeDtypeStruct((batch, width), jnp.float32),
            jax.ShapeDtypeStruct((8, batch), jnp.float32),
        ],
        scratch_shapes=[pltpu.VMEM((batch, width), jnp.bfloat16), pltpu.VMEM((batch, 128), jnp.float32)],
        compiler_params=pltpu.CompilerParams(
            dimension_semantics=("arbitrary",), vmem_limit_bytes=20 * MIB
        ),
        cost_estimate=pl.CostEstimate(
            flops=12 * batch * classes * width, bytes_accessed=classes * width * 2, transcendentals=0
        ),
        name="forward_sums",
    )(base, rep, labels.reshape(batch, 1), weights, *blocks)


def weight_kernel(base_ref, emb_ref, lab_ref, st_ref, tot_ref, w_ref, g_ref, xhat_ref, y_ref, v_ref):
    step = pl.program_id(0)
    tile = w_ref.shape[0]
    batch = emb_ref.shape[0]

    @pl.when(step == 0)
    def _():
        xwide, _ = unit_rows(emb_ref[...].astype(jnp.float32))
        xhat = xwide.astype(jnp.bfloat16)
        xhat_ref[...] = xhat
        total = tot_ref[...]
        y_ref[...] = (xhat.astype(jnp.float32) * column_of(SCALE / total)).astype(jnp.bfloat16)
        v_ref[...] = st_ref[2:3, :] - st_ref[3:4, :] * total

    wwide, w_inv = unit_rows(w_ref[...].astype(jnp.float32))
    what = wwide.astype(jnp.bfloat16)
    cosine = lax.dot_general(what, xhat_ref[...], NT, preferred_element_type=jnp.float32)
    ids = lax.broadcasted_iota(jnp.int32, (tile, batch), 0)
    is_label = ids == lab_ref[...] - (base_ref[0] + step * tile)
    e = jnp.exp2(cosine * (SCALE * LOG2E) - SCALE * LOG2E)
    d = jnp.where(is_label, v_ref[...], e).astype(jnp.bfloat16)
    raw = jnp.dot(d, y_ref[...], preferred_element_type=jnp.float32)
    g_ref[...] = (raw - wwide * jnp.sum(wwide * raw, axis=1, keepdims=True)) * w_inv


def weight_gradient(base, emb, labels, stats, totals, weights):
    batch, width = emb.shape
    classes = weights.shape[0]
    tile = math.gcd(classes, 1024)
    whole = lambda i: (0, 0)
    return pl.pallas_call(
        weight_kernel,
        grid=(classes // tile,),
        in_specs=[
            pl.BlockSpec(memory_space=pltpu.SMEM),
            pl.BlockSpec((batch, width), whole),
            pl.BlockSpec((1, batch), whole),
            pl.BlockSpec((8, batch), whole),
            pl.BlockSpec((1, batch), whole),
            pl.BlockSpec((tile, width), lambda i: (i, 0)),
        ],
        out_specs=pl.BlockSpec((tile, width), lambda i: (i, 0)),
        out_shape=jax.ShapeDtypeStruct((classes, width), jnp.float32),
        scratch_shapes=[
            pltpu.VMEM((batch, width), jnp.bfloat16),
            pltpu.VMEM((batch, width), jnp.bfloat16),
            pltpu.VMEM((1, batch), jnp.float32),
        ],
        compiler_params=pltpu.CompilerParams(
            dimension_semantics=("arbitrary",), vmem_limit_bytes=20 * MIB
        ),
        cost_estimate=pl.CostEstimate(
            flops=12 * batch * classes * width, bytes_accessed=classes * width * 6, transcendentals=0
        ),
        name="weight_gradient",
    )(base, emb, labels.reshape(1, batch), stats, totals.reshape(1, batch), weights)


def fetch_kernel(me_ref, rows_ref, *refs, picks, tokens):
    outs, sem = refs[tokens : tokens + len(picks)], refs[-1]
    copies = []
    for u, (k, out_ref) in enumerate(zip(picks, outs)):
        size = out_ref.shape[0]
        first = pl.multiple_of((me_ref[0] ^ k) * size, size)
        copies.append(pltpu.make_async_copy(rows_ref.at[pl.ds(first, size), :], out_ref, sem.at[u]))
    for copy in copies:
        copy.start()
    for copy in copies:
        copy.wait()


def fetch(me, rows, size, picks, tokens):
    anywhere = pl.BlockSpec(memory_space=pl.ANY)
    return pl.pallas_call(
        functools.partial(fetch_kernel, picks=tuple(picks), tokens=len(tokens)),
        in_specs=[pl.BlockSpec(memory_space=pltpu.SMEM)] + [anywhere] * (1 + len(tokens)),
        out_specs=[pl.BlockSpec(memory_space=pltpu.VMEM)] * len(picks),
        out_shape=[jax.ShapeDtypeStruct((size, rows.shape[1]), rows.dtype)] * len(picks),
        scratch_shapes=[pltpu.SemaphoreType.DMA((len(picks),))],
        compiler_params=pltpu.CompilerParams(vmem_limit_bytes=4 * MIB),
        cost_estimate=COST,
        name="fetch",
    )(me, rows, *tokens)


def tie_kernel(value_ref, *refs):
    refs[-1][...] = value_ref[...]


def tie(value, tokens):
    anywhere = pl.BlockSpec(memory_space=pl.ANY)
    vmem = pl.BlockSpec(memory_space=pltpu.VMEM)
    return pl.pallas_call(
        tie_kernel,
        in_specs=[vmem] + [anywhere] * len(tokens),
        out_specs=vmem,
        out_shape=jax.ShapeDtypeStruct(value.shape, value.dtype),
        compiler_params=pltpu.CompilerParams(vmem_limit_bytes=2 * MIB),
        cost_estimate=COST,
        name="tie",
    )(value, *tokens)


def place_runs(info_ref, slot_ref, row_refs, origins, groups, held_ref, stage_ref):
    run = stage_ref.shape[0] // 2
    batch = math.gcd(run, 32)
    parts = [(ref, u) for ref in row_refs for u in range(ref.shape[0] // run)]
    for (row_ref, u), (rep_flip, grp_flip, grp_from) in zip(parts, origins):
        unit, _ = unit_rows(row_ref[u * run : (u + 1) * run, :].astype(jnp.float32))
        stage_ref[pl.ds(0, run, stride=2), :] = unit[:, :128]
        stage_ref[pl.ds(1, run, stride=2), :] = unit[:, 128:]
        grp = info_ref[1] ^ grp_flip if grp_from is None else grp_from
        first = ((info_ref[0] ^ rep_flip) * groups + grp) * run

        def place(j, carry, first=first):
            at = j * batch
            slots = [slot_ref[first + at + v] for v in range(batch)]
            values = [stage_ref[pl.ds((at + v) * 2, 2), :] for v in range(batch)]
            for slot, value in zip(slots, values):
                held_ref[pl.ds(slot * 2, 2), :] = value
            return carry

        lax.fori_loop(0, run // batch, place, 0)


def place_kernel(info_ref, slot_ref, *refs, origins, groups, arrays):
    held_ref, token_ref, stage_ref = refs[-3:]
    token_ref[...] = jnp.zeros_like(token_ref)
    place_runs(info_ref, slot_ref, refs[:arrays], origins, groups, held_ref, stage_ref)


def place_rows(info, slots, arrays, origins, groups, held, classes, run):
    smem = pl.BlockSpec(memory_space=pltpu.SMEM)
    vmem = pl.BlockSpec(memory_space=pltpu.VMEM)
    operands = [info, slots, *arrays] + ([] if held is None else [held])
    return pl.pallas_call(
        functools.partial(
            place_kernel, origins=tuple(origins), groups=groups, arrays=len(arrays)
        ),
        in_specs=[smem, smem] + [vmem] * (len(operands) - 2),
        out_specs=[vmem, vmem],
        out_shape=[
            jax.ShapeDtypeStruct((2 * classes, 128), jnp.float32),
            jax.ShapeDtypeStruct((8, 128), jnp.float32),
        ],
        input_output_aliases={} if held is None else {len(operands) - 1: 0},
        scratch_shapes=[pltpu.VMEM((2 * run, 128), jnp.float32)],
        compiler_params=pltpu.CompilerParams(vmem_limit_bytes=4 * MIB),
        cost_estimate=COST,
        name="place_rows",
    )(*operands)


def blend_kernel(info_ref, slot_ref, w_ref, *refs, origins, groups, arrays):
    o_ref, held_ref, stage_ref = refs[-3:]
    step = pl.program_id(0)
    tile = w_ref.shape[0]

    @pl.when(step == 0)
    def _():
        place_runs(info_ref, slot_ref, refs[:arrays], origins, groups, held_ref, stage_ref)

    wwide, _ = unit_rows(w_ref[...].astype(jnp.float32))
    first = pl.multiple_of(step * 2 * tile, 2 * tile)
    low = wwide[:, :128] + held_ref[pl.ds(first, tile, stride=2), :]
    high = wwide[:, 128:] + held_ref[pl.ds(first + 1, tile, stride=2), :]
    square = jnp.sum(low * low + high * high, axis=1, keepdims=True)
    inv = lax.rsqrt(square + 1e-06)
    o_ref[:, :128] = (low * inv).astype(jnp.bfloat16)
    o_ref[:, 128:] = (high * inv).astype(jnp.bfloat16)


def place_and_blend(info, slots, arrays, origins, groups, held, weights, run):
    classes, width = weights.shape
    tile = math.gcd(classes, 1024)
    smem = pl.BlockSpec(memory_space=pltpu.SMEM)
    vmem = pl.BlockSpec(memory_space=pltpu.VMEM)
    tiles = pl.BlockSpec((tile, width), lambda i: (i, 0))
    refreshed, _ = pl.pallas_call(
        functools.partial(
            blend_kernel, origins=tuple(origins), groups=groups, arrays=len(arrays)
        ),
        grid=(classes // tile,),
        in_specs=[smem, smem, tiles] + [vmem] * (len(arrays) + 1),
        out_specs=[tiles, vmem],
        out_shape=[
            jax.ShapeDtypeStruct((classes, width), jnp.bfloat16),
            jax.ShapeDtypeStruct(held.shape, held.dtype),
        ],
        input_output_aliases={3 + len(arrays): 1},
        scratch_shapes=[pltpu.VMEM((2 * run, 128), jnp.float32)],
        compiler_params=pltpu.CompilerParams(
            dimension_semantics=("arbitrary",), vmem_limit_bytes=10 * MIB
        ),
        cost_estimate=COST,
        name="place_and_blend",
    )(info, slots, weights, *arrays, held)
    return refreshed


def shards(embeddings, labels, class_weights, centroids, centroid_class):
    rows_local, width = embeddings.shape
    classes = class_weights.shape[0]
    groups, reps = lax.axis_size("grp"), lax.axis_size("rep")
    peers = groups * reps
    batch = rows_local * reps
    run = classes // peers
    share = rows_local // groups
    grp, rep = lax.axis_index("grp").astype(jnp.int32), lax.axis_index("rep").astype(jnp.int32)
    me = rep * groups + grp
    base, me = (me * classes).reshape(1), me.reshape(1)
    info = jnp.stack([rep, grp])
    at = lambda d: d % groups * reps + d // groups

    def over_rep(value, k):
        return lax.ppermute(value, "rep", [(i, i ^ k) for i in range(reps)])

    def over_all(value, k):
        return lax.ppermute(value, ("grp", "rep"), [(at(d), at(d ^ k)) for d in range(peers)])

    def hop(picks, tokens):
        fetched = fetch(rep.reshape(1), centroids, groups * run, picks, tokens)
        return {k: over_rep(value, k) if k else value for k, value in zip(picks, fetched)}

    def spread(held_rows, picks):
        parts = [held_rows[k].reshape(groups, run, width) for k in picks]
        parts = lax.all_to_all(jnp.concatenate(parts, axis=1), "grp", 0, 0, tiled=True)
        origins = [(k, 0, g) for g in range(groups) for k in picks]
        return parts.reshape(-1, width), origins

    def direct(picks, tokens):
        fetched = fetch(me, centroids, run, picks, tokens)
        rows = [over_all(value, k) for k, value in zip(picks, fetched)]
        return rows, [(k // groups, k % groups, None) for k in picks]

    half = reps // 2
    far, near = list(range(peers // 2, peers)), list(range(1, half))
    cuts = [len(far) * c // 4 for c in range(5)]
    plan = [far[i:j] for i, j in zip(cuts, cuts[1:])]

    blocks = [embeddings] + [over_rep(embeddings, k) for k in range(1, reps)]
    rows0, from0 = direct(plan[0], [blocks[1]])
    emb, a, b, stats = forward(base, rep.reshape(1), blocks, labels, class_weights)
    rows1, from1 = direct(plan[1], [blocks[1]])

    tied = tie(stats, rows0)
    flat = [
        jnp.broadcast_to(tied[0][None], (peers, batch)),
        centroid_class.reshape(peers, run).astype(jnp.float32),
        jnp.repeat(tied[1].reshape(reps, rows_local), groups, axis=0),
    ]
    size = batch + run + rows_local
    flat = jnp.pad(jnp.concatenate(flat, axis=1), ((0, 0), (0, -size % 1024)))
    flat = lax.all_to_all(flat.reshape(peers, -1, 128), ALL, 0, 0, tiled=True).reshape(peers, -1)
    total = jnp.sum(flat[:, :batch], axis=0)
    slots = flat[:, batch : batch + run].reshape(-1).astype(jnp.int32)
    target = jnp.sum(flat[:, batch + run : size], axis=0)
    own_total = lax.dynamic_slice_in_dim(total, rep * rows_local, rows_local, 0)
    loss = SCALE + jnp.log(own_total) - target

    weight_grad = weight_gradient(base, emb, labels, stats, total, class_weights)
    rows2, from2 = direct(plan[2], [total])

    grad = tie(a / total[:, None] - b, [weight_grad, *rows1])
    parts = lax.all_to_all(grad.reshape(peers, share, width), ALL, 0, 0, tiled=True)
    own = jnp.sum(parts, axis=0)
    embedding_gradient = lax.all_to_all(
        jnp.broadcast_to(own[None], (groups, share, width)), "grp", 0, 0, tiled=True
    ).reshape(rows_local, width)

    held, token = place_rows(info, slots, rows0 + rows1, from0 + from1, groups, None, classes, run)
    rows3, from3 = direct(plan[3], [token])
    moved = hop(near, [weight_grad])
    moved |= hop([0], [weight_grad])
    rows, origins = spread(moved, [0] + near)
    held, _ = place_rows(
        info, slots, [rows, *rows2], origins + from2, groups, held, classes, run
    )
    refreshed = place_and_blend(info, slots, rows3, from3, groups, held, class_weights, run)
    return (loss, embedding_gradient, weight_grad, refreshed)


def solution(mesh):
    in_specs = (
        P("rep", None),
        P(),
        P(("rep", "grp"), None),
        P(("grp", "rep"), None),
        P(("grp", "rep")),
    )
    out_specs = (P("rep"), P("rep", None), P(("rep", "grp"), None), P(("rep", "grp"), None))
    return jax.shard_map(shards, mesh=mesh, in_specs=in_specs, out_specs=out_specs, check_vma=False)
```

```python
import functools
import math

import jax
import jax.numpy as jnp
from jax import lax
from jax.experimental import pallas as pl
from jax.experimental.pallas import tpu as pltpu
from jax.sharding import PartitionSpec as P

SCALE = 32.0
MARGIN = 0.2
SIN_FLOOR = 0.09
LOG2E = math.log2(math.e)
ALL = ("rep", "grp")
MIB = 1024 * 1024
COST = pl.CostEstimate(flops=1, bytes_accessed=1, transcendentals=0)

NT = (((1,), (1,)), ((), ()))


def unit_rows(wide):
    inv = lax.rsqrt(jnp.sum(wide * wide, axis=1, keepdims=True) + 1e-06)
    return wide * inv, inv


def column_of(row):
    lanes = row.shape[1]
    return jnp.transpose(jnp.broadcast_to(row, (128, lanes)))[:, :1]


def forward_kernel(base_ref, rep_ref, lab_ref, w_ref, *refs, classes, reps):
    blocks = refs[:reps]
    emb_ref, a_ref, b_ref, st_ref, xhat_ref, sum_ref = refs[reps:]
    step = pl.program_id(0)
    tile = w_ref.shape[0]
    batch = emb_ref.shape[0]

    @pl.when(step == 0)
    def _():
        for k, block_ref in enumerate(blocks):
            rows = block_ref.shape[0]
            first = pl.multiple_of((rep_ref[0] ^ k) * rows, rows)
            emb_ref[pl.ds(first, rows), :] = block_ref[...]
        xwide, _ = unit_rows(emb_ref[...].astype(jnp.float32))
        xhat_ref[...] = xwide.astype(jnp.bfloat16)
        sum_ref[...] = jnp.zeros_like(sum_ref)
        a_ref[...] = jnp.zeros_like(a_ref)
        b_ref[...] = jnp.zeros_like(b_ref)

    wwide, _ = unit_rows(w_ref[...].astype(jnp.float32))
    what = wwide.astype(jnp.bfloat16)
    cosine = lax.dot_general(xhat_ref[...], what, NT, preferred_element_type=jnp.float32)
    ids = lax.broadcasted_iota(jnp.int32, (batch, tile), 1)
    is_label = ids == lab_ref[...] - (base_ref[0] + step * tile)
    e = jnp.where(is_label, 0.0, jnp.exp2(cosine * (SCALE * LOG2E) - SCALE * LOG2E))
    partial = e[:, :128]
    for c in range(1, tile // 128):
        partial = partial + e[:, c * 128 : (c + 1) * 128]
    sum_ref[...] += partial
    onehot = jnp.where(is_label, 1.0, 0.0).astype(jnp.bfloat16)
    a_ref[...] += jnp.dot(e.astype(jnp.bfloat16), what, preferred_element_type=jnp.float32)
    b_ref[...] += jnp.dot(onehot, what, preferred_element_type=jnp.float32)

    @pl.when(step == pl.num_programs(0) - 1)
    def _():
        xwide, x_inv = unit_rows(emb_ref[...].astype(jnp.float32))
        label_row = b_ref[...]
        c = jnp.sum(xhat_ref[...].astype(jnp.float32) * label_row, axis=1, keepdims=True)
        offset = lab_ref[...] - base_ref[0]
        has = jnp.where((offset >= 0) & (offset < classes), 1.0, 0.0)
        q = 1.0 - c * c
        sine = jnp.sqrt(jnp.maximum(q, SIN_FLOOR))
        margined = c * math.cos(MARGIN) - sine * math.sin(MARGIN)
        slope = math.cos(MARGIN) + jnp.where(q > SIN_FLOOR, c * math.sin(MARGIN) / sine, 0.0)
        slope = slope * has
        label_e = jnp.exp(SCALE * margined - SCALE) * has
        total = jnp.sum(sum_ref[...], axis=1, keepdims=True) + label_e
        target = SCALE * margined * has
        b = slope * label_row
        a = a_ref[...] + label_e * b
        gain = SCALE * x_inv
        a_ref[...] = (a - xwide * jnp.sum(xwide * a, axis=1, keepdims=True)) * gain
        b_ref[...] = (b - xwide * jnp.sum(xwide * b, axis=1, keepdims=True)) * gain
        lane = lax.broadcasted_iota(jnp.int32, (batch, 128), 1)
        stats = jnp.where(lane == 0, total, 0.0)
        stats = jnp.where(lane == 1, target, stats)
        stats = jnp.where(lane == 2, label_e * slope, stats)
        stats = jnp.where(lane == 3, slope, stats)
        st_ref[...] = jnp.transpose(stats)[:8, :]


def forward(base, rep, blocks, labels, weights):
    rows, width = blocks[0].shape
    reps = len(blocks)
    batch = rows * reps
    classes = weights.shape[0]
    tile = math.gcd(classes, 1024)
    whole = lambda i: (0, 0)
    smem = pl.BlockSpec(memory_space=pltpu.SMEM)
    return pl.pallas_call(
        functools.partial(forward_kernel, classes=classes, reps=reps),
        grid=(classes // tile,),
        in_specs=[
            smem,
            smem,
            pl.BlockSpec((batch, 1), whole),
            pl.BlockSpec((tile, width), lambda i: (i, 0)),
        ]
        + [pl.BlockSpec((rows, width), whole)] * reps,
        out_specs=[
            pl.BlockSpec((batch, width), whole),
            pl.BlockSpec((batch, width), whole),
            pl.BlockSpec((batch, width), whole),
            pl.BlockSpec((8, batch), whole),
        ],
        out_shape=[
            jax.ShapeDtypeStruct((batch, width), jnp.bfloat16),
            jax.ShapeDtypeStruct((batch, width), jnp.float32),
            jax.ShapeDtypeStruct((batch, width), jnp.float32),
            jax.ShapeDtypeStruct((8, batch), jnp.float32),
        ],
        scratch_shapes=[pltpu.VMEM((batch, width), jnp.bfloat16), pltpu.VMEM((batch, 128), jnp.float32)],
        compiler_params=pltpu.CompilerParams(
            dimension_semantics=("arbitrary",), vmem_limit_bytes=20 * MIB
        ),
        cost_estimate=pl.CostEstimate(
            flops=12 * batch * classes * width, bytes_accessed=classes * width * 2, transcendentals=0
        ),
        name="forward_sums",
    )(base, rep, labels.reshape(batch, 1), weights, *blocks)


def weight_kernel(base_ref, emb_ref, lab_ref, st_ref, tot_ref, w_ref, g_ref, xhat_ref, y_ref, v_ref):
    step = pl.program_id(0)
    tile = w_ref.shape[0]
    batch = emb_ref.shape[0]

    @pl.when(step == 0)
    def _():
        xwide, _ = unit_rows(emb_ref[...].astype(jnp.float32))
        xhat = xwide.astype(jnp.bfloat16)
        xhat_ref[...] = xhat
        total = tot_ref[...]
        y_ref[...] = (xhat.astype(jnp.float32) * column_of(SCALE / total)).astype(jnp.bfloat16)
        v_ref[...] = st_ref[2:3, :] - st_ref[3:4, :] * total

    wwide, w_inv = unit_rows(w_ref[...].astype(jnp.float32))
    what = wwide.astype(jnp.bfloat16)
    cosine = lax.dot_general(what, xhat_ref[...], NT, preferred_element_type=jnp.float32)
    ids = lax.broadcasted_iota(jnp.int32, (tile, batch), 0)
    is_label = ids == lab_ref[...] - (base_ref[0] + step * tile)
    e = jnp.exp2(cosine * (SCALE * LOG2E) - SCALE * LOG2E)
    d = jnp.where(is_label, v_ref[...], e).astype(jnp.bfloat16)
    raw = jnp.dot(d, y_ref[...], preferred_element_type=jnp.float32)
    g_ref[...] = (raw - wwide * jnp.sum(wwide * raw, axis=1, keepdims=True)) * w_inv


def weight_gradient(base, emb, labels, stats, totals, weights):
    batch, width = emb.shape
    classes = weights.shape[0]
    tile = math.gcd(classes, 1024)
    whole = lambda i: (0, 0)
    return pl.pallas_call(
        weight_kernel,
        grid=(classes // tile,),
        in_specs=[
            pl.BlockSpec(memory_space=pltpu.SMEM),
            pl.BlockSpec((batch, width), whole),
            pl.BlockSpec((1, batch), whole),
            pl.BlockSpec((8, batch), whole),
            pl.BlockSpec((1, batch), whole),
            pl.BlockSpec((tile, width), lambda i: (i, 0)),
        ],
        out_specs=pl.BlockSpec((tile, width), lambda i: (i, 0)),
        out_shape=jax.ShapeDtypeStruct((classes, width), jnp.float32),
        scratch_shapes=[
            pltpu.VMEM((batch, width), jnp.bfloat16),
            pltpu.VMEM((batch, width), jnp.bfloat16),
            pltpu.VMEM((1, batch), jnp.float32),
        ],
        compiler_params=pltpu.CompilerParams(
            dimension_semantics=("arbitrary",), vmem_limit_bytes=20 * MIB
        ),
        cost_estimate=pl.CostEstimate(
            flops=12 * batch * classes * width, bytes_accessed=classes * width * 6, transcendentals=0
        ),
        name="weight_gradient",
    )(base, emb, labels.reshape(1, batch), stats, totals.reshape(1, batch), weights)


def fetch_kernel(rows_ref, *refs, first):
    out_ref, sem = refs[-2:]
    size = out_ref.shape[1]
    copy = pltpu.make_async_copy(rows_ref.at[:, pl.ds(first, size), :], out_ref, sem)
    copy.start()
    copy.wait()


def fetch(runs, first, size, tokens):
    peers, _, width = runs.shape
    anywhere = pl.BlockSpec(memory_space=pl.ANY)
    return pl.pallas_call(
        functools.partial(fetch_kernel, first=first),
        in_specs=[anywhere] * (1 + len(tokens)),
        out_specs=pl.BlockSpec(memory_space=pltpu.VMEM),
        out_shape=jax.ShapeDtypeStruct((peers, size, width), runs.dtype),
        scratch_shapes=[pltpu.SemaphoreType.DMA],
        compiler_params=pltpu.CompilerParams(vmem_limit_bytes=6 * MIB),
        cost_estimate=COST,
        name="fetch",
    )(runs, *tokens)


def tie_kernel(value_ref, *refs):
    refs[-1][...] = value_ref[...]


def tie(value, tokens):
    anywhere = pl.BlockSpec(memory_space=pl.ANY)
    vmem = pl.BlockSpec(memory_space=pltpu.VMEM)
    return pl.pallas_call(
        tie_kernel,
        in_specs=[vmem] + [anywhere] * len(tokens),
        out_specs=vmem,
        out_shape=jax.ShapeDtypeStruct(value.shape, value.dtype),
        compiler_params=pltpu.CompilerParams(vmem_limit_bytes=2 * MIB),
        cost_estimate=COST,
        name="tie",
    )(value, *tokens)


def place_runs(me_ref, slot_ref, row_ref, held_ref, stage_ref, peers, run, first):
    size = stage_ref.shape[0] // 2
    batch = math.gcd(size, 32)
    for source in range(peers):
        rows = row_ref[source * size : (source + 1) * size, :].astype(jnp.float32)
        unit, _ = unit_rows(rows)
        stage_ref[pl.ds(0, size, stride=2), :] = unit[:, :128]
        stage_ref[pl.ds(1, size, stride=2), :] = unit[:, 128:]
        start = (me_ref[0] ^ source) * run + first

        def place(j, carry, start=start):
            at = j * batch
            slots = [slot_ref[start + at + v] for v in range(batch)]
            values = [stage_ref[pl.ds((at + v) * 2, 2), :] for v in range(batch)]
            for slot, value in zip(slots, values):
                held_ref[pl.ds(slot * 2, 2), :] = value
            return carry

        lax.fori_loop(0, size // batch, place, 0)


def place_kernel(me_ref, slot_ref, row_ref, held_ref, token_ref, stage_ref, *, peers, run, first):
    token_ref[...] = jnp.zeros_like(token_ref)
    place_runs(me_ref, slot_ref, row_ref, held_ref, stage_ref, peers, run, first)


def place_rows(me, slots, rows, peers, run, first):
    smem = pl.BlockSpec(memory_space=pltpu.SMEM)
    vmem = pl.BlockSpec(memory_space=pltpu.VMEM)
    return pl.pallas_call(
        functools.partial(place_kernel, peers=peers, run=run, first=first),
        in_specs=[smem, smem, vmem],
        out_specs=[vmem, vmem],
        out_shape=[
            jax.ShapeDtypeStruct((2 * peers * run, 128), jnp.float32),
            jax.ShapeDtypeStruct((8, 128), jnp.float32),
        ],
        scratch_shapes=[pltpu.VMEM((2 * rows.shape[0] // peers, 128), jnp.float32)],
        compiler_params=pltpu.CompilerParams(vmem_limit_bytes=16 * MIB),
        cost_estimate=pl.CostEstimate(
            flops=0, bytes_accessed=16 * rows.shape[0] * rows.shape[1], transcendentals=0
        ),
        name="place_rows",
    )(me, slots, rows)


def blend_kernel(
    me_ref, slot_ref, w_ref, row_ref, _, o_ref, held_ref, stage_ref, *, peers, run, first
):
    step = pl.program_id(0)
    tile = w_ref.shape[0]

    @pl.when(step == 0)
    def _():
        place_runs(me_ref, slot_ref, row_ref, held_ref, stage_ref, peers, run, first)

    wwide, _ = unit_rows(w_ref[...].astype(jnp.float32))
    at = pl.multiple_of(step * 2 * tile, 2 * tile)
    low = wwide[:, :128] + held_ref[pl.ds(at, tile, stride=2), :]
    high = wwide[:, 128:] + held_ref[pl.ds(at + 1, tile, stride=2), :]
    square = jnp.sum(low * low + high * high, axis=1, keepdims=True)
    inv = lax.rsqrt(square + 1e-06)
    o_ref[:, :128] = (low * inv).astype(jnp.bfloat16)
    o_ref[:, 128:] = (high * inv).astype(jnp.bfloat16)


def place_and_blend(me, slots, rows, held, weights, peers, run, first):
    classes, width = weights.shape
    tile = math.gcd(classes, 1024)
    smem = pl.BlockSpec(memory_space=pltpu.SMEM)
    vmem = pl.BlockSpec(memory_space=pltpu.VMEM)
    tiles = pl.BlockSpec((tile, width), lambda i: (i, 0))
    refreshed, _ = pl.pallas_call(
        functools.partial(blend_kernel, peers=peers, run=run, first=first),
        grid=(classes // tile,),
        in_specs=[smem, smem, tiles, vmem, vmem],
        out_specs=[tiles, vmem],
        out_shape=[
            jax.ShapeDtypeStruct((classes, width), jnp.bfloat16),
            jax.ShapeDtypeStruct(held.shape, held.dtype),
        ],
        input_output_aliases={4: 1},
        scratch_shapes=[pltpu.VMEM((2 * rows.shape[0] // peers, 128), jnp.float32)],
        compiler_params=pltpu.CompilerParams(
            dimension_semantics=("arbitrary",), vmem_limit_bytes=16 * MIB
        ),
        cost_estimate=pl.CostEstimate(
            flops=0, bytes_accessed=12 * classes * width, transcendentals=0
        ),
        name="place_and_blend",
    )(me, slots, weights, rows, held)
    return refreshed


def shards(embeddings, labels, class_weights, centroids, centroid_class):
    rows_local, width = embeddings.shape
    classes = class_weights.shape[0]
    groups, reps = lax.axis_size("grp"), lax.axis_size("rep")
    peers = groups * reps
    batch = rows_local * reps
    run = classes // peers
    share = rows_local // groups
    grp, rep = lax.axis_index("grp").astype(jnp.int32), lax.axis_index("rep").astype(jnp.int32)
    me = (rep * groups + grp).reshape(1)
    base = me * classes

    def swap(value, axis, k):
        size = lax.axis_size(axis)
        return lax.ppermute(value, axis, [(i, i ^ k) for i in range(size)]) if k else value

    def pick(value, axis, k, dim):
        return lax.dynamic_index_in_dim(value, lax.axis_index(axis) ^ k, dim, keepdims=False)

    blocks = [swap(embeddings, "rep", k) for k in range(reps)]

    runs = centroids.reshape(peers, run, width)
    cut = run * 5 // 8 // 16 * 16

    def relay(first, size, tokens):
        sent = fetch(runs, first, size, tokens)
        return lax.all_to_all(sent, ALL, 0, 0, tiled=True).reshape(peers * size, width)

    rows_a = relay(0, cut, blocks[1:])
    emb, a, b, stats = forward(base, rep.reshape(1), blocks, labels, class_weights)

    wanted = centroid_class.reshape(reps, groups, run).astype(jnp.float32)
    sums = stats[:2].reshape(-1)
    near = [
        swap(jnp.concatenate([sums, pick(wanted, "grp", j, 1).reshape(-1)]).reshape(-1, 128), "grp", j)
        for j in range(groups)
    ]
    near = jnp.stack(near).reshape(groups, -1)
    sums = jnp.sum(near[:, : 2 * batch], axis=0)
    wanted = near[:, 2 * batch :].reshape(groups, reps, run)
    every = [
        swap(jnp.concatenate([sums, pick(wanted, "rep", k, 1).reshape(-1)]).reshape(-1, 128), "rep", k)
        for k in range(reps)
    ]
    every = jnp.stack(every).reshape(reps, -1)
    sums = jnp.sum(every[:, : 2 * batch], axis=0)
    slots = every[:, 2 * batch :].reshape(-1).astype(jnp.int32)
    total, target = sums[:batch], sums[batch:]
    losses = SCALE + jnp.log(total) - target
    loss = lax.dynamic_slice_in_dim(losses, rep * rows_local, rows_local, 0)

    rows_b = relay(cut, run - cut, [total])
    weight_grad = weight_gradient(base, emb, labels, stats, total, class_weights)
    held, token = place_rows(me, slots, rows_a, peers, run, 0)

    grad = tie(a / total[:, None] - b, [weight_grad, token])
    grad = grad.reshape(reps, groups, share, width)
    grad = sum(swap(pick(grad, "grp", j, 1), "grp", j) for j in range(groups))
    own = sum(swap(pick(grad, "rep", k, 0), "rep", k) for k in range(reps))
    shares = jnp.stack([swap(own, "grp", j) for j in range(groups)])
    embedding_gradient = shares[grp ^ jnp.arange(groups)].reshape(rows_local, width)

    refreshed = place_and_blend(me, slots, rows_b, held, class_weights, peers, run, cut)
    return (loss, embedding_gradient, weight_grad, refreshed)


def solution(mesh):
    in_specs = (
        P("rep", None),
        P(),
        P(("rep", "grp"), None),
        P(("grp", "rep"), None),
        P(("grp", "rep")),
    )
    out_specs = (P("rep"), P("rep", None), P(("rep", "grp"), None), P(("rep", "grp"), None))
    return jax.shard_map(shards, mesh=mesh, in_specs=in_specs, out_specs=out_specs, check_vma=False)
```

```python
import functools
import math

import jax
import jax.numpy as jnp
from jax import lax
from jax.experimental import pallas as pl
from jax.experimental.pallas import tpu as pltpu
from jax.sharding import PartitionSpec as P

SCALE = 32.0
MARGIN = 0.2
SIN_FLOOR = 0.09
LOG2E = math.log2(math.e)
ALL = ("rep", "grp")
MIB = 1024 * 1024
COST = pl.CostEstimate(flops=1, bytes_accessed=1, transcendentals=0)

NT = (((1,), (1,)), ((), ()))


def in_hbm(value):
    return pltpu.with_memory_space_constraint(value, pltpu.HBM)


def unit_rows(wide):
    inv = lax.rsqrt(jnp.sum(wide * wide, axis=1, keepdims=True) + 1e-06)
    return wide * inv, inv


def column_of(row):
    lanes = row.shape[1]
    return jnp.transpose(jnp.broadcast_to(row, (128, lanes)))[:, :1]


def forward_kernel(base_ref, rep_ref, lab_ref, w_ref, _, *refs, classes, reps):
    blocks = refs[:reps]
    emb_ref, a_ref, b_ref, st_ref, wide_ref, xhat_ref, sum_ref = refs[reps:]
    step = pl.program_id(0)
    tile = w_ref.shape[0]
    batch = emb_ref.shape[0]

    @pl.when(step == 0)
    def _():
        for k, block_ref in enumerate(blocks):
            rows = block_ref.shape[0]
            first = pl.multiple_of((rep_ref[0] ^ k) * rows, rows)
            emb_ref[pl.ds(first, rows), :] = block_ref[...]
        xwide, _ = unit_rows(emb_ref[...].astype(jnp.float32))
        xhat_ref[...] = xwide.astype(jnp.bfloat16)
        sum_ref[...] = jnp.zeros_like(sum_ref)
        a_ref[...] = jnp.zeros_like(a_ref)
        b_ref[...] = jnp.zeros_like(b_ref)

    wwide, _ = unit_rows(w_ref[...].astype(jnp.float32))
    wide_ref[pl.ds(0, tile, stride=2), :] = wwide[:, :128]
    wide_ref[pl.ds(1, tile, stride=2), :] = wwide[:, 128:]
    what = wwide.astype(jnp.bfloat16)
    cosine = lax.dot_general(xhat_ref[...], what, NT, preferred_element_type=jnp.float32)
    ids = lax.broadcasted_iota(jnp.int32, (batch, tile), 1)
    is_label = ids == lab_ref[...] - (base_ref[0] + step * tile)
    e = jnp.where(is_label, 0.0, jnp.exp2(cosine * (SCALE * LOG2E) - SCALE * LOG2E))
    partial = e[:, :128]
    for c in range(1, tile // 128):
        partial = partial + e[:, c * 128 : (c + 1) * 128]
    sum_ref[...] += partial
    onehot = jnp.where(is_label, 1.0, 0.0).astype(jnp.bfloat16)
    a_ref[...] += jnp.dot(e.astype(jnp.bfloat16), what, preferred_element_type=jnp.float32)
    b_ref[...] += jnp.dot(onehot, what, preferred_element_type=jnp.float32)

    @pl.when(step == pl.num_programs(0) - 1)
    def _():
        xwide, x_inv = unit_rows(emb_ref[...].astype(jnp.float32))
        label_row = b_ref[...]
        c = jnp.sum(xhat_ref[...].astype(jnp.float32) * label_row, axis=1, keepdims=True)
        offset = lab_ref[...] - base_ref[0]
        has = jnp.where((offset >= 0) & (offset < classes), 1.0, 0.0)
        q = 1.0 - c * c
        sine = jnp.sqrt(jnp.maximum(q, SIN_FLOOR))
        margined = c * math.cos(MARGIN) - sine * math.sin(MARGIN)
        slope = math.cos(MARGIN) + jnp.where(q > SIN_FLOOR, c * math.sin(MARGIN) / sine, 0.0)
        slope = slope * has
        label_e = jnp.exp(SCALE * margined - SCALE) * has
        total = jnp.sum(sum_ref[...], axis=1, keepdims=True) + label_e
        target = SCALE * margined * has
        b = slope * label_row
        a = a_ref[...] + label_e * b
        gain = SCALE * x_inv
        a_ref[...] = (a - xwide * jnp.sum(xwide * a, axis=1, keepdims=True)) * gain
        b_ref[...] = (b - xwide * jnp.sum(xwide * b, axis=1, keepdims=True)) * gain
        lane = lax.broadcasted_iota(jnp.int32, (batch, 128), 1)
        stats = jnp.where(lane == 0, total, 0.0)
        stats = jnp.where(lane == 1, target, stats)
        stats = jnp.where(lane == 2, label_e * slope, stats)
        stats = jnp.where(lane == 3, slope, stats)
        st_ref[...] = jnp.transpose(stats)[:8, :]


def forward(base, rep, blocks, labels, weights, after):
    rows, width = blocks[0].shape
    reps = len(blocks)
    batch = rows * reps
    classes = weights.shape[0]
    tile = math.gcd(classes, 1024)
    whole = lambda i: (0, 0)
    smem = pl.BlockSpec(memory_space=pltpu.SMEM)
    return pl.pallas_call(
        functools.partial(forward_kernel, classes=classes, reps=reps),
        grid=(classes // tile,),
        in_specs=[
            smem,
            smem,
            pl.BlockSpec((batch, 1), whole),
            pl.BlockSpec((tile, width), lambda i: (i, 0)),
            pl.BlockSpec(memory_space=pl.ANY),
        ]
        + [pl.BlockSpec((rows, width), whole)] * reps,
        out_specs=[
            pl.BlockSpec((batch, width), whole),
            pl.BlockSpec((batch, width), whole),
            pl.BlockSpec((batch, width), whole),
            pl.BlockSpec((8, batch), whole),
            pl.BlockSpec((2 * tile, 128), lambda i: (i, 0)),
        ],
        out_shape=[
            jax.ShapeDtypeStruct((batch, width), jnp.bfloat16),
            jax.ShapeDtypeStruct((batch, width), jnp.float32),
            jax.ShapeDtypeStruct((batch, width), jnp.float32),
            jax.ShapeDtypeStruct((8, batch), jnp.float32),
            pltpu.HBM((2 * classes, 128), jnp.float32),
        ],
        scratch_shapes=[pltpu.VMEM((batch, width), jnp.bfloat16), pltpu.VMEM((batch, 128), jnp.float32)],
        compiler_params=pltpu.CompilerParams(
            dimension_semantics=("arbitrary",), vmem_limit_bytes=20 * MIB
        ),
        cost_estimate=pl.CostEstimate(
            flops=12 * batch * classes * width, bytes_accessed=classes * width * 2, transcendentals=0
        ),
        name="forward_sums",
    )(base, rep, labels.reshape(batch, 1), weights, after, *blocks)


def weight_kernel(base_ref, emb_ref, lab_ref, st_ref, tot_ref, w_ref, g_ref, xhat_ref, y_ref, v_ref):
    step = pl.program_id(0)
    tile = w_ref.shape[0]
    batch = emb_ref.shape[0]

    @pl.when(step == 0)
    def _():
        xwide, _ = unit_rows(emb_ref[...].astype(jnp.float32))
        xhat = xwide.astype(jnp.bfloat16)
        xhat_ref[...] = xhat
        total = tot_ref[...]
        y_ref[...] = (xhat.astype(jnp.float32) * column_of(SCALE / total)).astype(jnp.bfloat16)
        v_ref[...] = st_ref[2:3, :] - st_ref[3:4, :] * total

    wwide, w_inv = unit_rows(w_ref[...].astype(jnp.float32))
    what = wwide.astype(jnp.bfloat16)
    cosine = lax.dot_general(what, xhat_ref[...], NT, preferred_element_type=jnp.float32)
    ids = lax.broadcasted_iota(jnp.int32, (tile, batch), 0)
    is_label = ids == lab_ref[...] - (base_ref[0] + step * tile)
    e = jnp.exp2(cosine * (SCALE * LOG2E) - SCALE * LOG2E)
    d = jnp.where(is_label, v_ref[...], e).astype(jnp.bfloat16)
    raw = jnp.dot(d, y_ref[...], preferred_element_type=jnp.float32)
    g_ref[...] = (raw - wwide * jnp.sum(wwide * raw, axis=1, keepdims=True)) * w_inv


def weight_gradient(base, emb, labels, stats, totals, weights):
    batch, width = emb.shape
    classes = weights.shape[0]
    tile = math.gcd(classes, 1024)
    whole = lambda i: (0, 0)
    return pl.pallas_call(
        weight_kernel,
        grid=(classes // tile,),
        in_specs=[
            pl.BlockSpec(memory_space=pltpu.SMEM),
            pl.BlockSpec((batch, width), whole),
            pl.BlockSpec((1, batch), whole),
            pl.BlockSpec((8, batch), whole),
            pl.BlockSpec((1, batch), whole),
            pl.BlockSpec((tile, width), lambda i: (i, 0)),
        ],
        out_specs=pl.BlockSpec((tile, width), lambda i: (i, 0)),
        out_shape=pltpu.HBM((classes, width), jnp.float32),
        scratch_shapes=[
            pltpu.VMEM((batch, width), jnp.bfloat16),
            pltpu.VMEM((batch, width), jnp.bfloat16),
            pltpu.VMEM((1, batch), jnp.float32),
        ],
        compiler_params=pltpu.CompilerParams(
            dimension_semantics=("arbitrary",), vmem_limit_bytes=20 * MIB
        ),
        cost_estimate=pl.CostEstimate(
            flops=12 * batch * classes * width, bytes_accessed=classes * width * 6, transcendentals=0
        ),
        name="weight_gradient",
    )(base, emb, labels.reshape(1, batch), stats, totals.reshape(1, batch), weights)


def fetch_kernel(rows_ref, *refs, first):
    out_ref, sem = refs[-2:]
    size = out_ref.shape[1]
    copy = pltpu.make_async_copy(rows_ref.at[:, pl.ds(first, size), :], out_ref, sem)
    copy.start()
    copy.wait()


def fetch(runs, first, size, tokens):
    peers, _, width = runs.shape
    hbm = pl.BlockSpec(memory_space=pltpu.HBM)
    anywhere = pl.BlockSpec(memory_space=pl.ANY)
    return pl.pallas_call(
        functools.partial(fetch_kernel, first=first),
        in_specs=[hbm] + [anywhere] * len(tokens),
        out_specs=pl.BlockSpec(memory_space=pltpu.VMEM),
        out_shape=jax.ShapeDtypeStruct((peers, size, width), runs.dtype),
        scratch_shapes=[pltpu.SemaphoreType.DMA],
        compiler_params=pltpu.CompilerParams(vmem_limit_bytes=6 * MIB),
        cost_estimate=COST,
        name="fetch",
    )(runs, *tokens)


def tie_kernel(value_ref, *refs):
    refs[-1][...] = value_ref[...]


def tie(value, tokens):
    anywhere = pl.BlockSpec(memory_space=pl.ANY)
    vmem = pl.BlockSpec(memory_space=pltpu.VMEM)
    return pl.pallas_call(
        tie_kernel,
        in_specs=[vmem] + [anywhere] * len(tokens),
        out_specs=vmem,
        out_shape=jax.ShapeDtypeStruct(value.shape, value.dtype),
        compiler_params=pltpu.CompilerParams(vmem_limit_bytes=2 * MIB),
        cost_estimate=COST,
        name="tie",
    )(value, *tokens)


def place_runs(me_ref, slot_ref, row_ref, held_ref, stage_ref, held_copy, peers, run, first):
    size = row_ref.shape[0] // peers
    batch = math.gcd(size, 32)

    def prepare(source, carry):
        at = pl.multiple_of(source * size, size)
        unit, _ = unit_rows(row_ref[pl.ds(at, size), :].astype(jnp.float32))
        at = pl.multiple_of(source * 2 * size, 2 * size)
        stage_ref[pl.ds(at, size, stride=2), :] = unit[:, :128]
        stage_ref[pl.ds(at + 1, size, stride=2), :] = unit[:, 128:]
        return carry

    lax.fori_loop(0, peers, prepare, 0)
    held_copy.wait()

    def place(j, carry):
        source = j // (size // batch)
        at = (j - source * (size // batch)) * batch
        start = (me_ref[0] ^ source) * run + first + at
        at = (source * size + at) * 2
        slots = [slot_ref[start + v] for v in range(batch)]
        values = [
            stage_ref[pl.ds(at + 2 * v, 2), :] + held_ref[pl.ds(slot, 2), :]
            for v, slot in enumerate(slots)
        ]
        for slot, value in zip(slots, values):
            held_ref[pl.ds(slot, 2), :] = value
        return carry

    lax.fori_loop(0, peers * size // batch, place, 0)


def place_kernel(
    me_ref, slot_ref, row_ref, in_ref, _, out_ref, token_ref, held_ref, stage_ref, sem,
    *, peers, run, first,
):
    token_ref[...] = jnp.zeros_like(token_ref)
    load = pltpu.make_async_copy(in_ref, held_ref, sem.at[0])
    load.start()
    place_runs(me_ref, slot_ref, row_ref, held_ref, stage_ref, load, peers, run, first)
    store = pltpu.make_async_copy(held_ref, out_ref, sem.at[1])
    store.start()
    store.wait()


def place_rows(me, slots, rows, held, after, peers, run, first):
    smem = pl.BlockSpec(memory_space=pltpu.SMEM)
    vmem = pl.BlockSpec(memory_space=pltpu.VMEM)
    anywhere = pl.BlockSpec(memory_space=pltpu.HBM)
    return pl.pallas_call(
        functools.partial(place_kernel, peers=peers, run=run, first=first),
        in_specs=[smem, smem, vmem, anywhere, anywhere],
        out_specs=[anywhere, vmem],
        out_shape=[
            pltpu.HBM(held.shape, jnp.float32),
            jax.ShapeDtypeStruct((8, 128), jnp.float32),
        ],
        scratch_shapes=[
            pltpu.VMEM(held.shape, jnp.float32),
            pltpu.VMEM((2 * rows.shape[0], 128), jnp.float32),
            pltpu.SemaphoreType.DMA((2,)),
        ],
        compiler_params=pltpu.CompilerParams(vmem_limit_bytes=32 * MIB),
        cost_estimate=pl.CostEstimate(
            flops=0, bytes_accessed=16 * rows.shape[0] * rows.shape[1], transcendentals=0
        ),
        name="place_rows",
    )(me, slots, rows, held, after)


def blend_kernel(
    me_ref, slot_ref, row_ref, in_ref, o_ref, held_ref, stage_ref, sem, *, peers, run, first
):
    step = pl.program_id(0)
    tile = o_ref.shape[0]

    @pl.when(step == 0)
    def _():
        load = pltpu.make_async_copy(in_ref, held_ref, sem)
        load.start()
        place_runs(me_ref, slot_ref, row_ref, held_ref, stage_ref, load, peers, run, first)

    at = pl.multiple_of(step * 2 * tile, 2 * tile)
    low = held_ref[pl.ds(at, tile, stride=2), :]
    high = held_ref[pl.ds(at + 1, tile, stride=2), :]
    square = jnp.sum(low * low + high * high, axis=1, keepdims=True)
    inv = lax.rsqrt(square + 1e-06)
    o_ref[:, :128] = (low * inv).astype(jnp.bfloat16)
    o_ref[:, 128:] = (high * inv).astype(jnp.bfloat16)


def place_and_blend(me, slots, rows, held, peers, run, first):
    classes, width = peers * run, rows.shape[1]
    tile = math.gcd(classes, 1024)
    smem = pl.BlockSpec(memory_space=pltpu.SMEM)
    vmem = pl.BlockSpec(memory_space=pltpu.VMEM)
    return pl.pallas_call(
        functools.partial(blend_kernel, peers=peers, run=run, first=first),
        grid=(classes // tile,),
        in_specs=[smem, smem, vmem, pl.BlockSpec(memory_space=pltpu.HBM)],
        out_specs=pl.BlockSpec((tile, width), lambda i: (i, 0)),
        out_shape=pltpu.HBM((classes, width), jnp.bfloat16),
        scratch_shapes=[
            pltpu.VMEM(held.shape, jnp.float32),
            pltpu.VMEM((2 * rows.shape[0], 128), jnp.float32),
            pltpu.SemaphoreType.DMA,
        ],
        compiler_params=pltpu.CompilerParams(
            dimension_semantics=("arbitrary",), vmem_limit_bytes=32 * MIB
        ),
        cost_estimate=pl.CostEstimate(
            flops=0, bytes_accessed=12 * classes * width, transcendentals=0
        ),
        name="place_and_blend",
    )(me, slots, rows, held)


def shards(embeddings, labels, class_weights, centroids, centroid_class):
    rows_local, width = embeddings.shape
    classes = class_weights.shape[0]
    groups, reps = lax.axis_size("grp"), lax.axis_size("rep")
    peers = groups * reps
    batch = rows_local * reps
    run = classes // peers
    share = rows_local // groups
    grp, rep = lax.axis_index("grp").astype(jnp.int32), lax.axis_index("rep").astype(jnp.int32)
    me = (rep * groups + grp).reshape(1)
    base = me * classes

    def swap(value, axis, k):
        size = lax.axis_size(axis)
        return lax.ppermute(value, axis, [(i, i ^ k) for i in range(size)]) if k else value

    def pick(value, axis, k, dim):
        return lax.dynamic_index_in_dim(value, lax.axis_index(axis) ^ k, dim, keepdims=False)

    blocks = [swap(embeddings, "rep", k) for k in range(reps)]

    weights = in_hbm(class_weights)
    runs = in_hbm(centroids.reshape(peers, run, width))
    cut = run * 5 // 8 // 16 * 16

    def relay(sent):
        return lax.all_to_all(sent, ALL, 0, 0, tiled=True).reshape(-1, width)

    sent = fetch(runs, 0, cut, blocks[1:])
    rows_a = relay(sent)
    emb, a, b, stats, wide = forward(base, rep.reshape(1), blocks, labels, weights, sent)

    wanted = centroid_class.reshape(reps, groups, run).astype(jnp.float32)
    sums = stats[:2].reshape(-1)
    near = [
        swap(jnp.concatenate([sums, pick(wanted, "grp", j, 1).reshape(-1)]).reshape(-1, 128), "grp", j)
        for j in range(groups)
    ]
    near = jnp.stack(near).reshape(groups, -1)
    sums = jnp.sum(near[:, : 2 * batch], axis=0)
    wanted = near[:, 2 * batch :].reshape(groups, reps, run)
    every = [
        swap(jnp.concatenate([sums, pick(wanted, "rep", k, 1).reshape(-1)]).reshape(-1, 128), "rep", k)
        for k in range(reps)
    ]
    every = jnp.stack(every).reshape(reps, -1)
    sums = jnp.sum(every[:, : 2 * batch], axis=0)
    slots = every[:, 2 * batch :].reshape(-1).astype(jnp.int32) * 2
    total, target = sums[:batch], sums[batch:]
    losses = SCALE + jnp.log(total) - target
    loss = lax.dynamic_slice_in_dim(losses, rep * rows_local, rows_local, 0)

    rows_b = relay(fetch(runs, cut, run - cut, [total]))
    weight_grad = weight_gradient(base, emb, labels, stats, total, weights)
    done = in_hbm(weight_grad)
    held, token = place_rows(me, slots, rows_a, in_hbm(wide), done, peers, run, 0)

    grad = (a / total[:, None] - b).reshape(reps, groups, share, width)
    grad = sum(swap(pick(grad, "grp", j, 1), "grp", j) for j in range(groups))
    grad = tie(grad, [done])
    own = sum(swap(pick(grad, "rep", k, 0), "rep", k) for k in range(reps))
    own = tie(own, [token])
    shares = jnp.stack([swap(own, "grp", j) for j in range(groups)])
    embedding_gradient = shares[grp ^ jnp.arange(groups)].reshape(rows_local, width)

    refreshed = place_and_blend(me, slots, rows_b, in_hbm(held), peers, run, cut)
    return (loss, embedding_gradient, weight_grad, refreshed)


def solution(mesh):
    in_specs = (
        P("rep", None),
        P(),
        P(("rep", "grp"), None),
        P(("grp", "rep"), None),
        P(("grp", "rep")),
    )
    out_specs = (P("rep"), P("rep", None), P(("rep", "grp"), None), P(("rep", "grp"), None))
    return jax.shard_map(shards, mesh=mesh, in_specs=in_specs, out_specs=out_specs, check_vma=False)
```

```python
import functools
import math

import jax
import jax.numpy as jnp
from jax import lax
from jax.experimental import pallas as pl
from jax.experimental.pallas import tpu as pltpu
from jax.sharding import PartitionSpec as P

SCALE = 32.0
MARGIN = 0.2
SIN_FLOOR = 0.09
LOG2E = math.log2(math.e)
ALL = ("rep", "grp")
MIB = 1024 * 1024
COST = pl.CostEstimate(flops=1, bytes_accessed=1, transcendentals=0)

NT = (((1,), (1,)), ((), ()))


def in_hbm(value):
    return pltpu.with_memory_space_constraint(value, pltpu.HBM)


def row_sums(values):
    folded = values[:, :128]
    for c in range(1, values.shape[1] // 128):
        folded = folded + values[:, c * 128 : (c + 1) * 128]
    ones = jnp.ones((128, 128), jnp.bfloat16)
    high = folded.astype(jnp.bfloat16)
    low = (folded - high.astype(jnp.float32)).astype(jnp.bfloat16)
    total = jnp.dot(high, ones, preferred_element_type=jnp.float32)
    return total + jnp.dot(low, ones, preferred_element_type=jnp.float32)


def scale_rows(values, factor):
    parts = [values[:, c : c + 128] * factor for c in range(0, values.shape[1], 128)]
    return jnp.concatenate(parts, axis=1)


def unit_rows(wide):
    inv = lax.rsqrt(row_sums(wide * wide) + 1e-06)
    return scale_rows(wide, inv), inv


def column_of(row):
    lanes = row.shape[1]
    return jnp.transpose(jnp.broadcast_to(row, (128, lanes)))[:, :1]


def forward_kernel(
    base_ref, rep_ref, lab_ref, w_ref, mixed_ref, emb_ref, a_ref, b_ref, st_ref, xhat_ref, sum_ref,
    *, classes, reps,
):
    step = pl.program_id(0)
    tile = w_ref.shape[0]
    batch = emb_ref.shape[0]

    @pl.when(step == 0)
    def _():
        rows = batch // reps
        for k in range(reps):
            first = pl.multiple_of((rep_ref[0] ^ k) * rows, rows)
            emb_ref[pl.ds(first, rows), :] = mixed_ref[k * rows : (k + 1) * rows, :]
        xwide, _ = unit_rows(emb_ref[...].astype(jnp.float32))
        xhat_ref[...] = xwide.astype(jnp.bfloat16)
        sum_ref[...] = jnp.zeros_like(sum_ref)
        a_ref[...] = jnp.zeros_like(a_ref)
        b_ref[...] = jnp.zeros_like(b_ref)

    wwide, _ = unit_rows(w_ref[...].astype(jnp.float32))
    what = wwide.astype(jnp.bfloat16)
    cosine = lax.dot_general(xhat_ref[...], what, NT, preferred_element_type=jnp.float32)
    ids = lax.broadcasted_iota(jnp.int32, (batch, tile), 1)
    is_label = ids == lab_ref[...] - (base_ref[0] + step * tile)
    e = jnp.where(is_label, 0.0, jnp.exp2(cosine * (SCALE * LOG2E) - SCALE * LOG2E))
    partial = e[:, :128]
    for c in range(1, tile // 128):
        partial = partial + e[:, c * 128 : (c + 1) * 128]
    sum_ref[...] += partial
    onehot = jnp.where(is_label, 1.0, 0.0).astype(jnp.bfloat16)
    a_ref[...] += jnp.dot(e.astype(jnp.bfloat16), what, preferred_element_type=jnp.float32)
    b_ref[...] += jnp.dot(onehot, what, preferred_element_type=jnp.float32)

    @pl.when(step == pl.num_programs(0) - 1)
    def _():
        xwide, x_inv = unit_rows(emb_ref[...].astype(jnp.float32))
        label_row = b_ref[...]
        c = jnp.sum(xhat_ref[...].astype(jnp.float32) * label_row, axis=1, keepdims=True)
        offset = lab_ref[...] - base_ref[0]
        has = jnp.where((offset >= 0) & (offset < classes), 1.0, 0.0)
        q = 1.0 - c * c
        sine = jnp.sqrt(jnp.maximum(q, SIN_FLOOR))
        margined = c * math.cos(MARGIN) - sine * math.sin(MARGIN)
        slope = math.cos(MARGIN) + jnp.where(q > SIN_FLOOR, c * math.sin(MARGIN) / sine, 0.0)
        slope = slope * has
        label_e = jnp.exp(SCALE * margined - SCALE) * has
        total = jnp.sum(sum_ref[...], axis=1, keepdims=True) + label_e
        target = SCALE * margined * has
        b = slope * label_row
        a = a_ref[...] + label_e * b
        gain = SCALE * x_inv
        a_ref[...] = scale_rows(a - scale_rows(xwide, row_sums(xwide * a)), gain)
        b_ref[...] = scale_rows(b - scale_rows(xwide, row_sums(xwide * b)), gain)
        lane = lax.broadcasted_iota(jnp.int32, (batch, 128), 1)
        stats = jnp.where(lane == 0, total, 0.0)
        stats = jnp.where(lane == 1, target, stats)
        stats = jnp.where(lane == 2, label_e * slope, stats)
        stats = jnp.where(lane == 3, slope, stats)
        st_ref[...] = jnp.transpose(stats)[:8, :]


def forward(base, rep, mixed, reps, labels, weights):
    batch, width = mixed.shape
    classes = weights.shape[0]
    tile = math.gcd(classes, 1024)
    whole = lambda i: (0, 0)
    smem = pl.BlockSpec(memory_space=pltpu.SMEM)
    return pl.pallas_call(
        functools.partial(forward_kernel, classes=classes, reps=reps),
        grid=(classes // tile,),
        in_specs=[
            smem,
            smem,
            pl.BlockSpec((batch, 1), whole),
            pl.BlockSpec((tile, width), lambda i: (i, 0)),
            pl.BlockSpec((batch, width), whole),
        ],
        out_specs=[
            pl.BlockSpec((batch, width), whole),
            pl.BlockSpec((batch, width), whole),
            pl.BlockSpec((batch, width), whole),
            pl.BlockSpec((8, batch), whole),
        ],
        out_shape=[
            jax.ShapeDtypeStruct((batch, width), jnp.bfloat16),
            jax.ShapeDtypeStruct((batch, width), jnp.float32),
            jax.ShapeDtypeStruct((batch, width), jnp.float32),
            jax.ShapeDtypeStruct((8, batch), jnp.float32),
        ],
        scratch_shapes=[pltpu.VMEM((batch, width), jnp.bfloat16), pltpu.VMEM((batch, 128), jnp.float32)],
        compiler_params=pltpu.CompilerParams(
            dimension_semantics=("arbitrary",), vmem_limit_bytes=20 * MIB
        ),
        cost_estimate=pl.CostEstimate(
            flops=12 * batch * classes * width, bytes_accessed=classes * width * 2, transcendentals=0
        ),
        name="forward_sums",
    )(base, rep, labels.reshape(batch, 1), weights, mixed)


def weight_kernel(base_ref, emb_ref, lab_ref, st_ref, tot_ref, w_ref, g_ref, xhat_ref, y_ref, v_ref):
    step = pl.program_id(0)
    tile = w_ref.shape[0]
    batch = emb_ref.shape[0]

    @pl.when(step == 0)
    def _():
        xwide, _ = unit_rows(emb_ref[...].astype(jnp.float32))
        xhat = xwide.astype(jnp.bfloat16)
        xhat_ref[...] = xhat
        total = tot_ref[...]
        y_ref[...] = (xhat.astype(jnp.float32) * column_of(SCALE / total)).astype(jnp.bfloat16)
        v_ref[...] = st_ref[2:3, :] - st_ref[3:4, :] * total

    wwide, w_inv = unit_rows(w_ref[...].astype(jnp.float32))
    what = wwide.astype(jnp.bfloat16)
    cosine = lax.dot_general(what, xhat_ref[...], NT, preferred_element_type=jnp.float32)
    ids = lax.broadcasted_iota(jnp.int32, (tile, batch), 0)
    is_label = ids == lab_ref[...] - (base_ref[0] + step * tile)
    e = jnp.exp2(cosine * (SCALE * LOG2E) - SCALE * LOG2E)
    d = jnp.where(is_label, v_ref[...], e).astype(jnp.bfloat16)
    raw = jnp.dot(d, y_ref[...], preferred_element_type=jnp.float32)
    g_ref[...] = scale_rows(raw - scale_rows(wwide, row_sums(wwide * raw)), w_inv)


def weight_gradient(base, emb, labels, stats, totals, weights):
    batch, width = emb.shape
    classes = weights.shape[0]
    tile = math.gcd(classes, 1024)
    whole = lambda i: (0, 0)
    return pl.pallas_call(
        weight_kernel,
        grid=(classes // tile,),
        in_specs=[
            pl.BlockSpec(memory_space=pltpu.SMEM),
            pl.BlockSpec((batch, width), whole),
            pl.BlockSpec((1, batch), whole),
            pl.BlockSpec((8, batch), whole),
            pl.BlockSpec((1, batch), whole),
            pl.BlockSpec((tile, width), lambda i: (i, 0)),
        ],
        out_specs=pl.BlockSpec((tile, width), lambda i: (i, 0)),
        out_shape=pltpu.HBM((classes, width), jnp.float32),
        scratch_shapes=[
            pltpu.VMEM((batch, width), jnp.bfloat16),
            pltpu.VMEM((batch, width), jnp.bfloat16),
            pltpu.VMEM((1, batch), jnp.float32),
        ],
        compiler_params=pltpu.CompilerParams(
            dimension_semantics=("arbitrary",), vmem_limit_bytes=20 * MIB
        ),
        cost_estimate=pl.CostEstimate(
            flops=12 * batch * classes * width, bytes_accessed=classes * width * 6, transcendentals=0
        ),
        name="weight_gradient",
    )(base, emb, labels.reshape(1, batch), stats, totals.reshape(1, batch), weights)


def fetch_kernel(rows_ref, *refs, first):
    out_ref, sem = refs[-2:]
    size = out_ref.shape[1]
    copy = pltpu.make_async_copy(rows_ref.at[:, pl.ds(first, size), :], out_ref, sem)
    copy.start()
    copy.wait()


def fetch(runs, first, size, tokens):
    peers, _, width = runs.shape
    hbm = pl.BlockSpec(memory_space=pltpu.HBM)
    anywhere = pl.BlockSpec(memory_space=pl.ANY)
    return pl.pallas_call(
        functools.partial(fetch_kernel, first=first),
        in_specs=[hbm] + [anywhere] * len(tokens),
        out_specs=pl.BlockSpec(memory_space=pltpu.VMEM),
        out_shape=jax.ShapeDtypeStruct((peers, size, width), runs.dtype),
        scratch_shapes=[pltpu.SemaphoreType.DMA],
        compiler_params=pltpu.CompilerParams(vmem_limit_bytes=6 * MIB),
        cost_estimate=COST,
        name="fetch",
    )(runs, *tokens)


def tie_kernel(value_ref, *refs):
    refs[-1][...] = value_ref[...]


def tie(value, tokens):
    anywhere = pl.BlockSpec(memory_space=pl.ANY)
    vmem = pl.BlockSpec(memory_space=pltpu.VMEM)
    return pl.pallas_call(
        tie_kernel,
        in_specs=[vmem] + [anywhere] * len(tokens),
        out_specs=vmem,
        out_shape=jax.ShapeDtypeStruct(value.shape, value.dtype),
        compiler_params=pltpu.CompilerParams(vmem_limit_bytes=2 * MIB),
        cost_estimate=COST,
        name="tie",
    )(value, *tokens)


def place_runs(me_ref, slot_ref, row_ref, held_ref, stage_ref, held_copy, peers, run, first):
    size = row_ref.shape[0] // peers
    batch = math.gcd(size, 32)

    def prepare(source, carry):
        at = pl.multiple_of(source * size, size)
        unit, _ = unit_rows(row_ref[pl.ds(at, size), :].astype(jnp.float32))
        at = pl.multiple_of(source * 2 * size, 2 * size)
        stage_ref[pl.ds(at, size, stride=2), :] = unit[:, :128]
        stage_ref[pl.ds(at + 1, size, stride=2), :] = unit[:, 128:]
        return carry

    lax.fori_loop(0, peers, prepare, 0)
    if held_copy is not None:
        held_copy.wait()

    def place(source, carry):
        start = (me_ref[0] ^ source) * run + first
        at = source * size * 2
        for block in range(0, size, batch):
            slots = [slot_ref[start + block + v] for v in range(batch)]
            values = [stage_ref[pl.ds(at + 2 * (block + v), 2), :] for v in range(batch)]
            for slot, value in zip(slots, values):
                held_ref[pl.ds(slot, 2), :] = value
        return carry

    lax.fori_loop(0, peers, place, 0)


def place_kernel(
    me_ref, slot_ref, row_ref, _, out_ref, token_ref, held_ref, stage_ref, sem, *, peers, run, first
):
    token_ref[...] = jnp.zeros_like(token_ref)
    place_runs(me_ref, slot_ref, row_ref, held_ref, stage_ref, None, peers, run, first)
    store = pltpu.make_async_copy(held_ref, out_ref, sem)
    store.start()
    store.wait()


def place_rows(me, slots, rows, after, peers, run, first):
    smem = pl.BlockSpec(memory_space=pltpu.SMEM)
    vmem = pl.BlockSpec(memory_space=pltpu.VMEM)
    anywhere = pl.BlockSpec(memory_space=pl.ANY)
    held = (2 * peers * run, 128)
    return pl.pallas_call(
        functools.partial(place_kernel, peers=peers, run=run, first=first),
        in_specs=[smem, smem, vmem, anywhere],
        out_specs=[anywhere, vmem],
        out_shape=[pltpu.HBM(held, jnp.float32), jax.ShapeDtypeStruct((8, 128), jnp.float32)],
        scratch_shapes=[
            pltpu.VMEM(held, jnp.float32),
            pltpu.VMEM((2 * rows.shape[0], 128), jnp.float32),
            pltpu.SemaphoreType.DMA,
        ],
        compiler_params=pltpu.CompilerParams(vmem_limit_bytes=32 * MIB),
        cost_estimate=pl.CostEstimate(
            flops=0, bytes_accessed=16 * rows.shape[0] * rows.shape[1], transcendentals=0
        ),
        name="place_rows",
    )(me, slots, rows, after)


def blend_kernel(
    me_ref, slot_ref, w_ref, row_ref, in_ref, o_ref, held_ref, stage_ref, sem, *, peers, run, first
):
    step = pl.program_id(0)
    tile = o_ref.shape[0]

    @pl.when(step == 0)
    def _():
        load = pltpu.make_async_copy(in_ref, held_ref, sem)
        load.start()
        place_runs(me_ref, slot_ref, row_ref, held_ref, stage_ref, load, peers, run, first)

    wwide, _ = unit_rows(w_ref[...].astype(jnp.float32))
    at = pl.multiple_of(step * 2 * tile, 2 * tile)
    low = wwide[:, :128] + held_ref[pl.ds(at, tile, stride=2), :]
    high = wwide[:, 128:] + held_ref[pl.ds(at + 1, tile, stride=2), :]
    inv = lax.rsqrt(row_sums(low * low + high * high) + 1e-06)
    o_ref[:, :128] = (low * inv).astype(jnp.bfloat16)
    o_ref[:, 128:] = (high * inv).astype(jnp.bfloat16)


def place_and_blend(me, slots, rows, held, weights, peers, run, first):
    classes, width = weights.shape
    tile = math.gcd(classes, 1024)
    smem = pl.BlockSpec(memory_space=pltpu.SMEM)
    vmem = pl.BlockSpec(memory_space=pltpu.VMEM)
    tiles = pl.BlockSpec((tile, width), lambda i: (i, 0))
    return pl.pallas_call(
        functools.partial(blend_kernel, peers=peers, run=run, first=first),
        grid=(classes // tile,),
        in_specs=[smem, smem, tiles, vmem, pl.BlockSpec(memory_space=pl.ANY)],
        out_specs=tiles,
        out_shape=pltpu.HBM((classes, width), jnp.bfloat16),
        scratch_shapes=[
            pltpu.VMEM(held.shape, jnp.float32),
            pltpu.VMEM((2 * rows.shape[0], 128), jnp.float32),
            pltpu.SemaphoreType.DMA,
        ],
        compiler_params=pltpu.CompilerParams(
            dimension_semantics=("arbitrary",), vmem_limit_bytes=32 * MIB
        ),
        cost_estimate=pl.CostEstimate(
            flops=0, bytes_accessed=12 * classes * width, transcendentals=0
        ),
        name="place_and_blend",
    )(me, slots, weights, rows, held)


def shards(embeddings, labels, class_weights, centroids, centroid_class):
    rows_local, width = embeddings.shape
    classes = class_weights.shape[0]
    groups, reps = lax.axis_size("grp"), lax.axis_size("rep")
    peers = groups * reps
    batch = rows_local * reps
    run = classes // peers
    share = rows_local // groups
    grp, rep = lax.axis_index("grp").astype(jnp.int32), lax.axis_index("rep").astype(jnp.int32)
    me = (rep * groups + grp).reshape(1)
    base = me * classes

    def swap(value, axis, k):
        size = lax.axis_size(axis)
        return lax.ppermute(value, axis, [(i, i ^ k) for i in range(size)]) if k else value

    def released(value, tokens):
        return lax.dynamic_update_slice(value, tie(value[:1, :16], tokens), (0, 0, 0))

    def relay(sent):
        return lax.all_to_all(sent, ALL, 0, 0, tiled=True).reshape(-1, width)

    weights = in_hbm(class_weights)
    runs = in_hbm(centroids.reshape(peers, run, width))
    cut = run * 5 // 8 // 16 * 16
    mixed = jnp.concatenate([swap(embeddings, "rep", k) for k in range(reps)])
    rows_a = relay(released(fetch(runs, 0, cut, []), [mixed]))
    emb, a, b, stats = forward(base, rep.reshape(1), mixed, reps, labels, weights)

    half = reps // 2
    core, deep = rep % 2, rep // 2
    index = lax.dynamic_index_in_dim

    def share_out(sums, wanted, axis, flips):
        got = []
        for flip, asked in zip(flips, wanted):
            sent = jnp.concatenate([sums, asked.reshape(-1)]).reshape(-1, 128)
            got.append(swap(sent, axis, flip).reshape(-1))
        got = jnp.stack(got)
        return jnp.sum(got[:, : 2 * batch], axis=0), got[:, 2 * batch :]

    wanted = centroid_class.reshape(half, 2, groups, run).astype(jnp.float32)
    wanted = [index(wanted, grp ^ j, 2, False) for j in range(groups)]
    sums, wanted = share_out(stats[:2].reshape(-1), wanted, "grp", range(groups))
    wanted = wanted.reshape(groups, half, 2, run)
    wanted = [index(wanted, core ^ c, 2, False) for c in range(2)]
    sums, wanted = share_out(sums, wanted, "rep", range(2))
    sent_b = fetch(runs, cut, run - cut, [stats])
    sums = tie(sums.reshape(-1, 128), [sent_b]).reshape(-1)
    wanted = wanted.reshape(2, groups, half, run)
    wanted = [index(wanted, deep ^ z, 2, False) for z in range(half)]
    sums, slots = share_out(sums, wanted, "rep", range(0, reps, 2))
    slots = slots.reshape(-1).astype(jnp.int32) * 2
    total, target = sums[:batch], sums[batch:]
    losses = SCALE + jnp.log(total) - target
    loss = lax.dynamic_slice_in_dim(losses, rep * rows_local, rows_local, 0)

    rows_b = relay(released(sent_b, [total]))
    weight_grad = weight_gradient(base, emb, labels, stats, total, weights)
    done = in_hbm(weight_grad)
    held, token = place_rows(me, slots, rows_a, done, peers, run, 0)

    grad = (a / total[:, None] - b).reshape(half, 2, groups, share, width)
    grad = sum(swap(index(grad, grp ^ j, 2, False), "grp", j) for j in range(groups))
    grad = tie(grad, [done])
    grad = sum(swap(index(grad, core ^ c, 1, False), "rep", c) for c in range(2))
    own = sum(swap(index(grad, deep ^ z, 0, False), "rep", 2 * z) for z in range(half))
    own = tie(own, [token])
    shares = jnp.stack([swap(own, "grp", j) for j in range(groups)])
    embedding_gradient = shares[grp ^ jnp.arange(groups)].reshape(rows_local, width)

    refreshed = place_and_blend(me, slots, rows_b, in_hbm(held), weights, peers, run, cut)
    return (loss, embedding_gradient, weight_grad, refreshed)


def solution(mesh):
    in_specs = (
        P("rep", None),
        P(),
        P(("rep", "grp"), None),
        P(("grp", "rep"), None),
        P(("grp", "rep")),
    )
    out_specs = (P("rep"), P("rep", None), P(("rep", "grp"), None), P(("rep", "grp"), None))
    return jax.shard_map(shards, mesh=mesh, in_specs=in_specs, out_specs=out_specs, check_vma=False)
```

```python
import functools
import math

import jax
import jax.numpy as jnp
from jax import lax
from jax.experimental import pallas as pl
from jax.experimental.pallas import tpu as pltpu
from jax.sharding import PartitionSpec as P

SCALE = 32.0
MARGIN = 0.2
SIN_FLOOR = 0.09
LOG2E = math.log2(math.e)
ALL = ("rep", "grp")
MIB = 1024 * 1024
COST = pl.CostEstimate(flops=1, bytes_accessed=1, transcendentals=0)

NT = (((1,), (1,)), ((), ()))


def in_hbm(value):
    return pltpu.with_memory_space_constraint(value, pltpu.HBM)


def unit_rows(wide):
    inv = lax.rsqrt(jnp.sum(wide * wide, axis=1, keepdims=True) + 1e-06)
    return wide * inv, inv


def off_axis(values, unit):
    return values - unit * jnp.sum(unit * values, axis=1, keepdims=True)


def column_of(row):
    lanes = row.shape[1]
    return jnp.transpose(jnp.broadcast_to(row, (128, lanes)))[:, :1]


def forward_kernel(
    base_ref, rep_ref, lab_ref, w_ref, mixed_ref, emb_ref, a_ref, b_ref, st_ref, what_ref, xhat_ref,
    sum_ref,
    *, classes, reps,
):
    step = pl.program_id(0)
    tile = w_ref.shape[0]
    batch = emb_ref.shape[0]

    @pl.when(step == 0)
    def _():
        rows = batch // reps
        for k in range(reps):
            first = pl.multiple_of((rep_ref[0] ^ k) * rows, rows)
            emb_ref[pl.ds(first, rows), :] = mixed_ref[k * rows : (k + 1) * rows, :]
        xwide, _ = unit_rows(emb_ref[...].astype(jnp.float32))
        xhat_ref[...] = xwide.astype(jnp.bfloat16)
        sum_ref[...] = jnp.zeros_like(sum_ref)
        a_ref[...] = jnp.zeros_like(a_ref)
        b_ref[...] = jnp.zeros_like(b_ref)

    wwide, _ = unit_rows(w_ref[...].astype(jnp.float32))
    what = wwide.astype(jnp.bfloat16)
    what_ref[...] = what
    cosine = lax.dot_general(xhat_ref[...], what, NT, preferred_element_type=jnp.float32)
    ids = lax.broadcasted_iota(jnp.int32, (batch, tile), 1)
    is_label = ids == lab_ref[...] - (base_ref[0] + step * tile)
    e = jnp.where(is_label, 0.0, jnp.exp2(cosine * (SCALE * LOG2E)))
    partial = e[:, :128]
    for c in range(1, tile // 128):
        partial = partial + e[:, c * 128 : (c + 1) * 128]
    sum_ref[...] += partial
    onehot = jnp.where(is_label, 1.0, 0.0).astype(jnp.bfloat16)
    a_ref[...] += jnp.dot(e.astype(jnp.bfloat16), what, preferred_element_type=jnp.float32)
    b_ref[...] += jnp.dot(onehot, what, preferred_element_type=jnp.float32)

    @pl.when(step == pl.num_programs(0) - 1)
    def _():
        xwide, x_inv = unit_rows(emb_ref[...].astype(jnp.float32))
        label_row = b_ref[...]
        c = jnp.sum(xhat_ref[...].astype(jnp.float32) * label_row, axis=1, keepdims=True)
        offset = lab_ref[...] - base_ref[0]
        has = jnp.where((offset >= 0) & (offset < classes), 1.0, 0.0)
        q = 1.0 - c * c
        sine = jnp.sqrt(jnp.maximum(q, SIN_FLOOR))
        margined = c * math.cos(MARGIN) - sine * math.sin(MARGIN)
        slope = math.cos(MARGIN) + jnp.where(q > SIN_FLOOR, c * math.sin(MARGIN) / sine, 0.0)
        slope = slope * has
        label_e = jnp.exp(SCALE * margined) * has
        total = jnp.sum(sum_ref[...], axis=1, keepdims=True) + label_e
        target = SCALE * margined * has
        b = slope * label_row
        a = a_ref[...] + label_e * b
        gain = SCALE * x_inv
        a_ref[...] = off_axis(a, xwide) * gain
        b_ref[...] = off_axis(b, xwide) * gain
        lane = lax.broadcasted_iota(jnp.int32, (batch, 128), 1)
        stats = jnp.where(lane == 0, total, 0.0)
        stats = jnp.where(lane == 1, target, stats)
        stats = jnp.where(lane == 2, label_e * slope, stats)
        stats = jnp.where(lane == 3, slope, stats)
        st_ref[...] = jnp.transpose(stats)[:8, :]


def forward(base, rep, mixed, reps, labels, weights):
    batch, width = mixed.shape
    classes = weights.shape[0]
    tile = math.gcd(classes, 1024)
    whole = lambda i: (0, 0)
    smem = pl.BlockSpec(memory_space=pltpu.SMEM)
    return pl.pallas_call(
        functools.partial(forward_kernel, classes=classes, reps=reps),
        grid=(classes // tile,),
        in_specs=[
            smem,
            smem,
            pl.BlockSpec((batch, 1), whole),
            pl.BlockSpec((tile, width), lambda i: (i, 0)),
            pl.BlockSpec((batch, width), whole),
        ],
        out_specs=[
            pl.BlockSpec((batch, width), whole),
            pl.BlockSpec((batch, width), whole),
            pl.BlockSpec((batch, width), whole),
            pl.BlockSpec((8, batch), whole),
            pl.BlockSpec((tile, width), lambda i: (i, 0)),
        ],
        out_shape=[
            jax.ShapeDtypeStruct((batch, width), jnp.bfloat16),
            jax.ShapeDtypeStruct((batch, width), jnp.float32),
            jax.ShapeDtypeStruct((batch, width), jnp.float32),
            jax.ShapeDtypeStruct((8, batch), jnp.float32),
            pltpu.HBM((classes, width), jnp.bfloat16),
        ],
        scratch_shapes=[pltpu.VMEM((batch, width), jnp.bfloat16), pltpu.VMEM((batch, 128), jnp.float32)],
        compiler_params=pltpu.CompilerParams(
            dimension_semantics=("arbitrary",), vmem_limit_bytes=20 * MIB
        ),
        cost_estimate=pl.CostEstimate(
            flops=12 * batch * classes * width, bytes_accessed=classes * width * 2, transcendentals=0
        ),
        name="forward_sums",
    )(base, rep, labels.reshape(batch, 1), weights, mixed)


def weight_kernel(base_ref, emb_ref, lab_ref, st_ref, tot_ref, w_ref, g_ref, xhat_ref, y_ref, v_ref):
    step = pl.program_id(0)
    tile = w_ref.shape[0]
    batch = emb_ref.shape[0]

    @pl.when(step == 0)
    def _():
        xwide, _ = unit_rows(emb_ref[...].astype(jnp.float32))
        xhat = xwide.astype(jnp.bfloat16)
        xhat_ref[...] = xhat
        total = tot_ref[...]
        y_ref[...] = (xhat.astype(jnp.float32) * column_of(SCALE / total)).astype(jnp.bfloat16)
        v_ref[...] = st_ref[2:3, :] - st_ref[3:4, :] * total

    wwide, w_inv = unit_rows(w_ref[...].astype(jnp.float32))
    what = wwide.astype(jnp.bfloat16)
    cosine = lax.dot_general(what, xhat_ref[...], NT, preferred_element_type=jnp.float32)
    ids = lax.broadcasted_iota(jnp.int32, (tile, batch), 0)
    is_label = ids == lab_ref[...] - (base_ref[0] + step * tile)
    e = jnp.exp2(cosine * (SCALE * LOG2E))
    d = jnp.where(is_label, v_ref[...], e).astype(jnp.bfloat16)
    raw = jnp.dot(d, y_ref[...], preferred_element_type=jnp.float32)
    g_ref[...] = off_axis(raw, wwide) * w_inv


def weight_gradient(base, emb, labels, stats, totals, weights):
    batch, width = emb.shape
    classes = weights.shape[0]
    tile = math.gcd(classes, 1024)
    whole = lambda i: (0, 0)
    return pl.pallas_call(
        weight_kernel,
        grid=(classes // tile,),
        in_specs=[
            pl.BlockSpec(memory_space=pltpu.SMEM),
            pl.BlockSpec((batch, width), whole),
            pl.BlockSpec((1, batch), whole),
            pl.BlockSpec((8, batch), whole),
            pl.BlockSpec((1, batch), whole),
            pl.BlockSpec((tile, width), lambda i: (i, 0)),
        ],
        out_specs=pl.BlockSpec((tile, width), lambda i: (i, 0)),
        out_shape=pltpu.HBM((classes, width), jnp.float32),
        scratch_shapes=[
            pltpu.VMEM((batch, width), jnp.bfloat16),
            pltpu.VMEM((batch, width), jnp.bfloat16),
            pltpu.VMEM((1, batch), jnp.float32),
        ],
        compiler_params=pltpu.CompilerParams(
            dimension_semantics=("arbitrary",), vmem_limit_bytes=20 * MIB
        ),
        cost_estimate=pl.CostEstimate(
            flops=12 * batch * classes * width, bytes_accessed=classes * width * 6, transcendentals=0
        ),
        name="weight_gradient",
    )(base, emb, labels.reshape(1, batch), stats, totals.reshape(1, batch), weights)


def fetch_kernel(rows_ref, *refs, first):
    out_ref, sem = refs[-2:]
    peers, size, _ = out_ref.shape
    lanes = sem.shape[0]
    part = peers // lanes
    copies = [
        pltpu.make_async_copy(
            rows_ref.at[pl.ds(c * part, part), pl.ds(first, size), :],
            out_ref.at[pl.ds(c * part, part)],
            sem.at[c],
        )
        for c in range(lanes)
    ]
    for copy in copies:
        copy.start()
    for copy in copies:
        copy.wait()


def fetch(runs, first, size, tokens):
    peers, _, width = runs.shape
    hbm = pl.BlockSpec(memory_space=pltpu.HBM)
    anywhere = pl.BlockSpec(memory_space=pl.ANY)
    return pl.pallas_call(
        functools.partial(fetch_kernel, first=first),
        in_specs=[hbm] + [anywhere] * len(tokens),
        out_specs=pl.BlockSpec(memory_space=pltpu.VMEM),
        out_shape=jax.ShapeDtypeStruct((peers, size, width), runs.dtype),
        scratch_shapes=[pltpu.SemaphoreType.DMA((math.gcd(peers, 8),))],
        compiler_params=pltpu.CompilerParams(vmem_limit_bytes=6 * MIB),
        cost_estimate=COST,
        name="fetch",
    )(runs, *tokens)


def tie_kernel(value_ref, *refs):
    refs[-1][...] = value_ref[...]


def tie(value, tokens):
    anywhere = pl.BlockSpec(memory_space=pl.ANY)
    vmem = pl.BlockSpec(memory_space=pltpu.VMEM)
    return pl.pallas_call(
        tie_kernel,
        in_specs=[vmem] + [anywhere] * len(tokens),
        out_specs=vmem,
        out_shape=jax.ShapeDtypeStruct(value.shape, value.dtype),
        compiler_params=pltpu.CompilerParams(vmem_limit_bytes=2 * MIB),
        cost_estimate=COST,
        name="tie",
    )(value, *tokens)


def place_runs(me_ref, slot_ref, row_ref, held_ref, stage_ref, copies, peers, run, first):
    size = row_ref.shape[0] // peers
    batch = math.gcd(size, 32)

    def prepare(source, carry):
        at = pl.multiple_of(source * size, size)
        unit, _ = unit_rows(row_ref[pl.ds(at, size), :].astype(jnp.float32))
        at = pl.multiple_of(source * 2 * size, 2 * size)
        stage_ref[pl.ds(at, size, stride=2), :] = unit[:, :128]
        stage_ref[pl.ds(at + 1, size, stride=2), :] = unit[:, 128:]
        return carry

    lax.fori_loop(0, peers, prepare, 0)
    for copy in copies:
        copy.wait()

    def place(source, carry):
        start = (me_ref[0] ^ source) * run + first
        at = source * size * 2
        for block in range(0, size, batch):
            slots = [slot_ref[start + block + v] for v in range(batch)]
            values = [stage_ref[pl.ds(at + 2 * (block + v), 2), :] for v in range(batch)]
            for slot, value in zip(slots, values):
                held_ref[pl.ds(slot, 2), :] = value
        return carry

    lax.fori_loop(0, peers, place, 0)


def place_kernel(
    me_ref, slot_ref, row_ref, _, held_ref, token_ref, stage_ref, *, peers, run, first
):
    token_ref[...] = jnp.zeros_like(token_ref)
    place_runs(me_ref, slot_ref, row_ref, held_ref, stage_ref, [], peers, run, first)


def place_rows(me, slots, rows, after, peers, run, first):
    smem = pl.BlockSpec(memory_space=pltpu.SMEM)
    vmem = pl.BlockSpec(memory_space=pltpu.VMEM)
    anywhere = pl.BlockSpec(memory_space=pl.ANY)
    return pl.pallas_call(
        functools.partial(place_kernel, peers=peers, run=run, first=first),
        in_specs=[smem, smem, vmem, anywhere],
        out_specs=[vmem, vmem],
        out_shape=[
            jax.ShapeDtypeStruct((2 * peers * run, 128), jnp.float32),
            jax.ShapeDtypeStruct((8, 128), jnp.float32),
        ],
        scratch_shapes=[pltpu.VMEM((2 * rows.shape[0], 128), jnp.float32)],
        compiler_params=pltpu.CompilerParams(vmem_limit_bytes=24 * MIB),
        cost_estimate=pl.CostEstimate(
            flops=0, bytes_accessed=16 * rows.shape[0] * rows.shape[1], transcendentals=0
        ),
        name="place_rows",
    )(me, slots, rows, after)


def blend_kernel(
    me_ref, slot_ref, w_ref, row_ref, in_ref, o_ref, held_ref, stage_ref, sem, *, peers, run, first
):
    step = pl.program_id(0)
    tile = o_ref.shape[0]

    @pl.when(step == 0)
    def _():
        lanes = sem.shape[0]
        part = held_ref.shape[0] // lanes
        parts = [pl.ds(c * part, part) for c in range(lanes)]
        copies = [
            pltpu.make_async_copy(in_ref.at[at, :], held_ref.at[at, :], sem.at[c])
            for c, at in enumerate(parts)
        ]
        for copy in copies:
            copy.start()
        place_runs(me_ref, slot_ref, row_ref, held_ref, stage_ref, copies, peers, run, first)

    wwide = w_ref[...].astype(jnp.float32)
    at = pl.multiple_of(step * 2 * tile, 2 * tile)
    low = wwide[:, :128] + held_ref[pl.ds(at, tile, stride=2), :]
    high = wwide[:, 128:] + held_ref[pl.ds(at + 1, tile, stride=2), :]
    inv = lax.rsqrt(jnp.sum(low * low + high * high, axis=1, keepdims=True) + 1e-06)
    o_ref[:, :128] = (low * inv).astype(jnp.bfloat16)
    o_ref[:, 128:] = (high * inv).astype(jnp.bfloat16)


def place_and_blend(me, slots, rows, held, weights, peers, run, first):
    classes, width = weights.shape
    tile = math.gcd(classes, 1024)
    smem = pl.BlockSpec(memory_space=pltpu.SMEM)
    vmem = pl.BlockSpec(memory_space=pltpu.VMEM)
    tiles = pl.BlockSpec((tile, width), lambda i: (i, 0))
    return pl.pallas_call(
        functools.partial(blend_kernel, peers=peers, run=run, first=first),
        grid=(classes // tile,),
        in_specs=[smem, smem, tiles, vmem, pl.BlockSpec(memory_space=pl.ANY)],
        out_specs=tiles,
        out_shape=pltpu.HBM((classes, width), jnp.bfloat16),
        scratch_shapes=[
            pltpu.VMEM(held.shape, jnp.float32),
            pltpu.VMEM((2 * rows.shape[0], 128), jnp.float32),
            pltpu.SemaphoreType.DMA((4,)),
        ],
        compiler_params=pltpu.CompilerParams(
            dimension_semantics=("arbitrary",), vmem_limit_bytes=32 * MIB
        ),
        cost_estimate=pl.CostEstimate(
            flops=0, bytes_accessed=12 * classes * width, transcendentals=0
        ),
        name="place_and_blend",
    )(me, slots, weights, rows, held)


def shards(embeddings, labels, class_weights, centroids, centroid_class):
    rows_local, width = embeddings.shape
    classes = class_weights.shape[0]
    groups, reps = lax.axis_size("grp"), lax.axis_size("rep")
    peers = groups * reps
    batch = rows_local * reps
    run = classes // peers
    share = rows_local // groups
    grp, rep = lax.axis_index("grp").astype(jnp.int32), lax.axis_index("rep").astype(jnp.int32)
    me = (rep * groups + grp).reshape(1)
    base = me * classes

    def swap(value, axis, k):
        size = lax.axis_size(axis)
        return lax.ppermute(value, axis, [(i, i ^ k) for i in range(size)]) if k else value

    def released(value, tokens):
        return lax.dynamic_update_slice(value, tie(value[:1, :16], tokens), (0, 0, 0))

    def relay(sent):
        return lax.all_to_all(sent, ALL, 0, 0, tiled=True).reshape(-1, width)

    weights = in_hbm(class_weights)
    runs = in_hbm(centroids.reshape(peers, run, width))
    cut = run * 5 // 8 // 16 * 16
    mixed = jnp.concatenate([swap(embeddings, "rep", c) for c in range(2)])
    mixed = jnp.concatenate([swap(mixed, "rep", 2 * z) for z in range(reps // 2)])
    rows_a = relay(released(fetch(runs, 0, cut, []), [mixed]))
    emb, a, b, stats, what = forward(base, rep.reshape(1), mixed, reps, labels, weights)

    half = reps // 2
    core, deep = rep % 2, rep // 2
    index = lax.dynamic_index_in_dim

    def share_out(sums, wanted, axis, flips):
        got = []
        for flip, asked in zip(flips, wanted):
            sent = jnp.concatenate([sums, asked.reshape(-1)]).reshape(-1, 128)
            got.append(swap(sent, axis, flip).reshape(-1))
        got = jnp.stack(got)
        return jnp.sum(got[:, : 2 * batch], axis=0), got[:, 2 * batch :]

    wanted = centroid_class.reshape(half, 2, groups, run).astype(jnp.float32)
    wanted = [index(wanted, grp ^ j, 2, False) for j in range(groups)]
    sums, wanted = share_out(stats[:2].reshape(-1), wanted, "grp", range(groups))
    wanted = wanted.reshape(groups, half, 2, run)
    wanted = [index(wanted, core ^ c, 2, False) for c in range(2)]
    sums, wanted = share_out(sums, wanted, "rep", range(2))
    sent_b = fetch(runs, cut, run - cut, [stats])
    sums = tie(sums.reshape(-1, 128), [sent_b]).reshape(-1)
    wanted = wanted.reshape(2, groups, half, run)
    wanted = [index(wanted, deep ^ z, 2, False) for z in range(half)]
    sums, slots = share_out(sums, wanted, "rep", range(0, reps, 2))
    slots = slots.reshape(-1).astype(jnp.int32) * 2
    total, target = sums[:batch], sums[batch:]
    losses = jnp.log(total) - target
    loss = lax.dynamic_slice_in_dim(losses, rep * rows_local, rows_local, 0)

    rows_b = relay(released(sent_b, [total]))
    weight_grad = weight_gradient(base, emb, labels, stats, total, weights)
    done = in_hbm(weight_grad)
    held, token = place_rows(me, slots, rows_a, done, peers, run, 0)

    grad = (a / total[:, None] - b).reshape(half, 2, groups, share, width)
    grad = sum(swap(index(grad, grp ^ j, 2, False), "grp", j) for j in range(groups))
    grad = tie(grad, [done])
    grad = sum(swap(index(grad, core ^ c, 1, False), "rep", c) for c in range(2))
    grad = tie(grad, [token])
    own = sum(swap(index(grad, deep ^ z, 0, False), "rep", 2 * z) for z in range(half))
    shares = jnp.stack([swap(own, "grp", j) for j in range(groups)])
    embedding_gradient = shares[grp ^ jnp.arange(groups)].reshape(rows_local, width)

    refreshed = place_and_blend(me, slots, rows_b, in_hbm(held), in_hbm(what), peers, run, cut)
    return (loss, embedding_gradient, weight_grad, refreshed)


def solution(mesh):
    in_specs = (
        P("rep", None),
        P(),
        P(("rep", "grp"), None),
        P(("grp", "rep"), None),
        P(("grp", "rep")),
    )
    out_specs = (P("rep"), P("rep", None), P(("rep", "grp"), None), P(("rep", "grp"), None))
    return jax.shard_map(shards, mesh=mesh, in_specs=in_specs, out_specs=out_specs, check_vma=False)
```

```python
import functools
import math

import jax
import jax.numpy as jnp
from jax import lax
from jax.experimental import pallas as pl
from jax.experimental.pallas import tpu as pltpu
from jax.sharding import PartitionSpec as P

SCALE = 32.0
MARGIN = 0.2
SIN_FLOOR = 0.09
LOG2E = math.log2(math.e)
ALL = ("rep", "grp")
MIB = 1024 * 1024
COST = pl.CostEstimate(flops=1, bytes_accessed=1, transcendentals=0)

NT = (((1,), (1,)), ((), ()))


def in_hbm(value):
    return pltpu.with_memory_space_constraint(value, pltpu.HBM)


def unit_rows(wide):
    inv = lax.rsqrt(jnp.sum(wide * wide, axis=1, keepdims=True) + 1e-06)
    return wide * inv, inv


def off_axis(values, unit):
    return values - unit * jnp.sum(unit * values, axis=1, keepdims=True)


def column_of(row):
    lanes = row.shape[1]
    return jnp.transpose(jnp.broadcast_to(row, (128, lanes)))[:, :1]


def forward_kernel(
    base_ref, rep_ref, lab_ref, w_ref, mixed_ref, emb_ref, a_ref, b_ref, st_ref, what_ref, xhat_ref,
    sum_ref,
    *, classes, reps,
):
    step = pl.program_id(0)
    tile = w_ref.shape[0]
    batch = emb_ref.shape[0]

    @pl.when(step == 0)
    def _():
        rows = batch // reps
        for k in range(reps):
            first = pl.multiple_of((rep_ref[0] ^ k) * rows, rows)
            emb_ref[pl.ds(first, rows), :] = mixed_ref[k * rows : (k + 1) * rows, :]
        xwide, _ = unit_rows(emb_ref[...].astype(jnp.float32))
        xhat_ref[...] = xwide.astype(jnp.bfloat16)
        sum_ref[...] = jnp.zeros_like(sum_ref)
        a_ref[...] = jnp.zeros_like(a_ref)
        b_ref[...] = jnp.zeros_like(b_ref)

    wwide, _ = unit_rows(w_ref[...].astype(jnp.float32))
    what = wwide.astype(jnp.bfloat16)
    what_ref[...] = what
    cosine = lax.dot_general(xhat_ref[...], what, NT, preferred_element_type=jnp.float32)
    ids = lax.broadcasted_iota(jnp.int32, (batch, tile), 1)
    is_label = ids == lab_ref[...] - (base_ref[0] + step * tile)
    e = jnp.where(is_label, 0.0, jnp.exp2(cosine * (SCALE * LOG2E)))
    partial = e[:, :128]
    for c in range(1, tile // 128):
        partial = partial + e[:, c * 128 : (c + 1) * 128]
    sum_ref[...] += partial
    onehot = jnp.where(is_label, 1.0, 0.0).astype(jnp.bfloat16)
    a_ref[...] += jnp.dot(e.astype(jnp.bfloat16), what, preferred_element_type=jnp.float32)
    b_ref[...] += jnp.dot(onehot, what, preferred_element_type=jnp.float32)

    @pl.when(step == pl.num_programs(0) - 1)
    def _():
        xwide, x_inv = unit_rows(emb_ref[...].astype(jnp.float32))
        label_row = b_ref[...]
        c = jnp.sum(xhat_ref[...].astype(jnp.float32) * label_row, axis=1, keepdims=True)
        offset = lab_ref[...] - base_ref[0]
        has = jnp.where((offset >= 0) & (offset < classes), 1.0, 0.0)
        q = 1.0 - c * c
        sine = jnp.sqrt(jnp.maximum(q, SIN_FLOOR))
        margined = c * math.cos(MARGIN) - sine * math.sin(MARGIN)
        slope = math.cos(MARGIN) + jnp.where(q > SIN_FLOOR, c * math.sin(MARGIN) / sine, 0.0)
        slope = slope * has
        label_e = jnp.exp(SCALE * margined) * has
        total = jnp.sum(sum_ref[...], axis=1, keepdims=True) + label_e
        target = SCALE * margined * has
        b = slope * label_row
        a = a_ref[...] + label_e * b
        gain = SCALE * x_inv
        a_ref[...] = off_axis(a, xwide) * gain
        b_ref[...] = off_axis(b, xwide) * gain
        lane = lax.broadcasted_iota(jnp.int32, (batch, 128), 1)
        stats = jnp.where(lane == 0, total, 0.0)
        stats = jnp.where(lane == 1, target, stats)
        stats = jnp.where(lane == 2, label_e * slope, stats)
        stats = jnp.where(lane == 3, slope, stats)
        st_ref[...] = jnp.transpose(stats)[:8, :]


def forward(base, rep, mixed, reps, labels, weights):
    batch, width = mixed.shape
    classes = weights.shape[0]
    tile = math.gcd(classes, 1024)
    whole = lambda i: (0, 0)
    smem = pl.BlockSpec(memory_space=pltpu.SMEM)
    return pl.pallas_call(
        functools.partial(forward_kernel, classes=classes, reps=reps),
        grid=(classes // tile,),
        in_specs=[
            smem,
            smem,
            pl.BlockSpec((batch, 1), whole),
            pl.BlockSpec((tile, width), lambda i: (i, 0)),
            pl.BlockSpec((batch, width), whole),
        ],
        out_specs=[
            pl.BlockSpec((batch, width), whole),
            pl.BlockSpec((batch, width), whole),
            pl.BlockSpec((batch, width), whole),
            pl.BlockSpec((8, batch), whole),
            pl.BlockSpec((tile, width), lambda i: (i, 0)),
        ],
        out_shape=[
            jax.ShapeDtypeStruct((batch, width), jnp.bfloat16),
            jax.ShapeDtypeStruct((batch, width), jnp.float32),
            jax.ShapeDtypeStruct((batch, width), jnp.float32),
            jax.ShapeDtypeStruct((8, batch), jnp.float32),
            pltpu.HBM((classes, width), jnp.bfloat16),
        ],
        scratch_shapes=[pltpu.VMEM((batch, width), jnp.bfloat16), pltpu.VMEM((batch, 128), jnp.float32)],
        compiler_params=pltpu.CompilerParams(
            dimension_semantics=("arbitrary",), vmem_limit_bytes=20 * MIB
        ),
        cost_estimate=pl.CostEstimate(
            flops=12 * batch * classes * width, bytes_accessed=classes * width * 2, transcendentals=0
        ),
        name="forward_sums",
    )(base, rep, labels.reshape(batch, 1), weights, mixed)


def weight_kernel(base_ref, emb_ref, lab_ref, st_ref, tot_ref, w_ref, g_ref, xhat_ref, y_ref, v_ref):
    step = pl.program_id(0)
    tile = w_ref.shape[0]
    batch = emb_ref.shape[0]

    @pl.when(step == 0)
    def _():
        xwide, _ = unit_rows(emb_ref[...].astype(jnp.float32))
        xhat = xwide.astype(jnp.bfloat16)
        xhat_ref[...] = xhat
        total = tot_ref[...]
        y_ref[...] = (xhat.astype(jnp.float32) * column_of(SCALE / total)).astype(jnp.bfloat16)
        v_ref[...] = st_ref[2:3, :] - st_ref[3:4, :] * total

    block = math.gcd(tile, 256)
    for first in range(0, tile, block):
        at = pl.ds(first, block)
        wwide, w_inv = unit_rows(w_ref[at, :].astype(jnp.float32))
        what = wwide.astype(jnp.bfloat16)
        cosine = lax.dot_general(what, xhat_ref[...], NT, preferred_element_type=jnp.float32)
        ids = lax.broadcasted_iota(jnp.int32, (block, batch), 0)
        is_label = ids == lab_ref[...] - (base_ref[0] + step * tile + first)
        e = jnp.exp2(cosine * (SCALE * LOG2E))
        d = jnp.where(is_label, v_ref[...], e).astype(jnp.bfloat16)
        raw = jnp.dot(d, y_ref[...], preferred_element_type=jnp.float32)
        g_ref[at, :] = off_axis(raw, wwide) * w_inv


def weight_gradient(base, emb, labels, stats, totals, weights):
    batch, width = emb.shape
    classes = weights.shape[0]
    tile = math.gcd(classes, 1024)
    whole = lambda i: (0, 0)
    return pl.pallas_call(
        weight_kernel,
        grid=(classes // tile,),
        in_specs=[
            pl.BlockSpec(memory_space=pltpu.SMEM),
            pl.BlockSpec((batch, width), whole),
            pl.BlockSpec((1, batch), whole),
            pl.BlockSpec((8, batch), whole),
            pl.BlockSpec((1, batch), whole),
            pl.BlockSpec((tile, width), lambda i: (i, 0)),
        ],
        out_specs=pl.BlockSpec((tile, width), lambda i: (i, 0)),
        out_shape=pltpu.HBM((classes, width), jnp.float32),
        scratch_shapes=[
            pltpu.VMEM((batch, width), jnp.bfloat16),
            pltpu.VMEM((batch, width), jnp.bfloat16),
            pltpu.VMEM((1, batch), jnp.float32),
        ],
        compiler_params=pltpu.CompilerParams(
            dimension_semantics=("arbitrary",), vmem_limit_bytes=20 * MIB
        ),
        cost_estimate=pl.CostEstimate(
            flops=12 * batch * classes * width, bytes_accessed=classes * width * 6, transcendentals=0
        ),
        name="weight_gradient",
    )(base, emb, labels.reshape(1, batch), stats, totals.reshape(1, batch), weights)


def fetch_kernel(rows_ref, *refs, first):
    out_ref, sem = refs[-2:]
    peers, size, _ = out_ref.shape
    lanes = sem.shape[0]
    part = peers // lanes
    copies = [
        pltpu.make_async_copy(
            rows_ref.at[pl.ds(c * part, part), pl.ds(first, size), :],
            out_ref.at[pl.ds(c * part, part)],
            sem.at[c],
        )
        for c in range(lanes)
    ]
    for copy in copies:
        copy.start()
    for copy in copies:
        copy.wait()


def fetch(runs, first, size, tokens):
    peers, _, width = runs.shape
    hbm = pl.BlockSpec(memory_space=pltpu.HBM)
    anywhere = pl.BlockSpec(memory_space=pl.ANY)
    return pl.pallas_call(
        functools.partial(fetch_kernel, first=first),
        in_specs=[hbm] + [anywhere] * len(tokens),
        out_specs=pl.BlockSpec(memory_space=pltpu.VMEM),
        out_shape=jax.ShapeDtypeStruct((peers, size, width), runs.dtype),
        scratch_shapes=[pltpu.SemaphoreType.DMA((math.gcd(peers, 8),))],
        compiler_params=pltpu.CompilerParams(vmem_limit_bytes=6 * MIB),
        cost_estimate=pl.CostEstimate(
            flops=0, bytes_accessed=8 * peers * size * width, transcendentals=0
        ),
        name="fetch",
    )(runs, *tokens)


def tie_kernel(value_ref, *refs):
    refs[-1][...] = value_ref[...]


def tie(value, tokens):
    anywhere = pl.BlockSpec(memory_space=pl.ANY)
    vmem = pl.BlockSpec(memory_space=pltpu.VMEM)
    return pl.pallas_call(
        tie_kernel,
        in_specs=[vmem] + [anywhere] * len(tokens),
        out_specs=vmem,
        out_shape=jax.ShapeDtypeStruct(value.shape, value.dtype),
        compiler_params=pltpu.CompilerParams(vmem_limit_bytes=2 * MIB),
        cost_estimate=COST,
        name="tie",
    )(value, *tokens)


def place_runs(me_ref, slot_ref, row_ref, held_ref, stage_ref, copies, peers, run, first):
    size = row_ref.shape[0] // peers
    batch = max(n for n in range(1, 49) if size % n == 0)
    chunk = max(n for n in range(16, 49, 16) if size % n == 0)

    def prepare(source, carry):
        for block in range(0, size, chunk):
            at = pl.multiple_of(source * size + block, chunk)
            unit, _ = unit_rows(row_ref[pl.ds(at, chunk), :].astype(jnp.float32))
            stage_ref[pl.ds(2 * at, chunk, stride=2), :] = unit[:, :128]
            stage_ref[pl.ds(2 * at + 1, chunk, stride=2), :] = unit[:, 128:]
        return carry

    lax.fori_loop(0, peers, prepare, 0)
    for copy in copies:
        copy.wait()

    def place(source, carry):
        start = (me_ref[0] ^ source) * run + first
        at = source * size * 2
        for block in range(0, size, batch):
            slots = [slot_ref[start + block + v] for v in range(batch)]
            values = [stage_ref[pl.ds(at + 2 * (block + v), 2), :] for v in range(batch)]
            for slot, value in zip(slots, values):
                held_ref[pl.ds(slot, 2), :] = value
        return carry

    lax.fori_loop(0, peers, place, 0)


def place_kernel(
    me_ref, slot_ref, row_ref, _, held_ref, token_ref, stage_ref, *, peers, run, first
):
    token_ref[...] = jnp.zeros_like(token_ref)
    place_runs(me_ref, slot_ref, row_ref, held_ref, stage_ref, [], peers, run, first)


def place_rows(me, slots, rows, after, peers, run, first):
    smem = pl.BlockSpec(memory_space=pltpu.SMEM)
    vmem = pl.BlockSpec(memory_space=pltpu.VMEM)
    anywhere = pl.BlockSpec(memory_space=pl.ANY)
    return pl.pallas_call(
        functools.partial(place_kernel, peers=peers, run=run, first=first),
        in_specs=[smem, smem, vmem, anywhere],
        out_specs=[vmem, vmem],
        out_shape=[
            jax.ShapeDtypeStruct((2 * peers * run, 128), jnp.float32),
            jax.ShapeDtypeStruct((8, 128), jnp.float32),
        ],
        scratch_shapes=[pltpu.VMEM((2 * rows.shape[0], 128), jnp.float32)],
        compiler_params=pltpu.CompilerParams(vmem_limit_bytes=24 * MIB),
        cost_estimate=pl.CostEstimate(
            flops=0, bytes_accessed=16 * rows.shape[0] * rows.shape[1], transcendentals=0
        ),
        name="place_rows",
    )(me, slots, rows, after)


def blend_kernel(
    me_ref, slot_ref, w_ref, row_ref, in_ref, o_ref, held_ref, stage_ref, sem, *, peers, run, first
):
    step = pl.program_id(0)
    tile = o_ref.shape[0]

    @pl.when(step == 0)
    def _():
        lanes = sem.shape[0]
        part = held_ref.shape[0] // lanes
        parts = [pl.ds(c * part, part) for c in range(lanes)]
        copies = [
            pltpu.make_async_copy(in_ref.at[at, :], held_ref.at[at, :], sem.at[c])
            for c, at in enumerate(parts)
        ]
        for copy in copies:
            copy.start()
        place_runs(me_ref, slot_ref, row_ref, held_ref, stage_ref, copies, peers, run, first)

    block = math.gcd(tile, 64)
    for begin in range(0, tile, block):
        rows = pl.ds(begin, block)
        at = pl.multiple_of((step * tile + begin) * 2, 2 * block)
        low = w_ref[rows, :128].astype(jnp.float32) + held_ref[pl.ds(at, block, stride=2), :]
        high = w_ref[rows, 128:].astype(jnp.float32) + held_ref[pl.ds(at + 1, block, stride=2), :]
        inv = lax.rsqrt(jnp.sum(low * low + high * high, axis=1, keepdims=True) + 1e-06)
        o_ref[rows, :128] = (low * inv).astype(jnp.bfloat16)
        o_ref[rows, 128:] = (high * inv).astype(jnp.bfloat16)


def place_and_blend(me, slots, rows, held, weights, peers, run, first):
    classes, width = weights.shape
    tile = math.gcd(classes, 1024)
    smem = pl.BlockSpec(memory_space=pltpu.SMEM)
    vmem = pl.BlockSpec(memory_space=pltpu.VMEM)
    tiles = pl.BlockSpec((tile, width), lambda i: (i, 0))
    return pl.pallas_call(
        functools.partial(blend_kernel, peers=peers, run=run, first=first),
        grid=(classes // tile,),
        in_specs=[smem, smem, tiles, vmem, pl.BlockSpec(memory_space=pl.ANY)],
        out_specs=tiles,
        out_shape=pltpu.HBM((classes, width), jnp.bfloat16),
        scratch_shapes=[
            pltpu.VMEM(held.shape, jnp.float32),
            pltpu.VMEM((2 * rows.shape[0], 128), jnp.float32),
            pltpu.SemaphoreType.DMA((4,)),
        ],
        compiler_params=pltpu.CompilerParams(
            dimension_semantics=("arbitrary",), vmem_limit_bytes=32 * MIB
        ),
        cost_estimate=pl.CostEstimate(
            flops=0, bytes_accessed=12 * classes * width, transcendentals=0
        ),
        name="place_and_blend",
    )(me, slots, weights, rows, held)


def shards(embeddings, labels, class_weights, centroids, centroid_class):
    rows_local, width = embeddings.shape
    classes = class_weights.shape[0]
    groups, reps = lax.axis_size("grp"), lax.axis_size("rep")
    peers = groups * reps
    batch = rows_local * reps
    run = classes // peers
    share = rows_local // groups
    grp, rep = lax.axis_index("grp").astype(jnp.int32), lax.axis_index("rep").astype(jnp.int32)
    me = (rep * groups + grp).reshape(1)
    base = me * classes

    def swap(value, axis, k):
        size = lax.axis_size(axis)
        return lax.ppermute(value, axis, [(i, i ^ k) for i in range(size)]) if k else value

    def released(value, tokens):
        return lax.dynamic_update_slice(value, tie(value[:1, :16], tokens), (0, 0, 0))

    def relay(sent):
        return lax.all_to_all(sent, ALL, 0, 0, tiled=True).reshape(-1, width)

    weights = in_hbm(class_weights)
    runs = in_hbm(centroids.reshape(peers, run, width))
    cut = run * 9 // 16 // 16 * 16
    mixed = jnp.concatenate([swap(embeddings, "rep", c) for c in range(2)])
    mixed = jnp.concatenate([swap(mixed, "rep", 2 * z) for z in range(reps // 2)])
    rows_a = relay(released(fetch(runs, 0, cut, []), [mixed]))
    emb, a, b, stats, what = forward(base, rep.reshape(1), mixed, reps, labels, weights)

    half = reps // 2
    core, deep = rep % 2, rep // 2
    index = lax.dynamic_index_in_dim

    def share_out(sums, wanted, axis, flips):
        got = []
        for flip, asked in zip(flips, wanted):
            sent = jnp.concatenate([sums, asked.reshape(-1)]).reshape(-1, 128)
            got.append(swap(sent, axis, flip).reshape(-1))
        got = jnp.stack(got)
        return jnp.sum(got[:, : 2 * batch], axis=0), got[:, 2 * batch :]

    wanted = centroid_class.reshape(half, 2, groups, run).astype(jnp.float32)
    wanted = [index(wanted, grp ^ j, 2, False) for j in range(groups)]
    sums, wanted = share_out(stats[:2].reshape(-1), wanted, "grp", range(groups))
    wanted = wanted.reshape(groups, half, 2, run)
    wanted = [index(wanted, core ^ c, 2, False) for c in range(2)]
    sums, wanted = share_out(sums, wanted, "rep", range(2))
    sent_b = fetch(runs, cut, run - cut, [stats])
    sums = tie(sums.reshape(-1, 128), [sent_b]).reshape(-1)
    wanted = wanted.reshape(2, groups, half, run)
    wanted = [index(wanted, deep ^ z, 2, False) for z in range(half)]
    sums, slots = share_out(sums, wanted, "rep", range(0, reps, 2))
    slots = slots.reshape(-1).astype(jnp.int32) * 2
    total, target = sums[:batch], sums[batch:]
    losses = jnp.log(total) - target
    loss = lax.dynamic_slice_in_dim(losses, rep * rows_local, rows_local, 0)

    rows_b = relay(released(sent_b, [total]))
    weight_grad = weight_gradient(base, emb, labels, stats, total, weights)
    done = in_hbm(weight_grad)
    held, token = place_rows(me, slots, rows_a, done, peers, run, 0)

    grad = (a / total[:, None] - b).reshape(half, 2, groups, share, width)
    grad = sum(swap(index(grad, grp ^ j, 2, False), "grp", j) for j in range(groups))
    grad = tie(grad, [done])
    grad = sum(swap(index(grad, core ^ c, 1, False), "rep", c) for c in range(2))
    grad = tie(grad, [token, loss])
    own = sum(swap(index(grad, deep ^ z, 0, False), "rep", 2 * z) for z in range(half))
    shares = [swap(own, "grp", j) for j in range(groups)]
    bit = 1
    while bit < groups:
        flip = (grp & bit) != 0
        shares = [jnp.where(flip, shares[j ^ bit], shares[j]) for j in range(groups)]
        bit *= 2
    embedding_gradient = jnp.concatenate(shares)

    refreshed = place_and_blend(me, slots, rows_b, in_hbm(held), in_hbm(what), peers, run, cut)
    return (loss, embedding_gradient, weight_grad, refreshed)


def solution(mesh):
    in_specs = (
        P("rep", None),
        P(),
        P(("rep", "grp"), None),
        P(("grp", "rep"), None),
        P(("grp", "rep")),
    )
    out_specs = (P("rep"), P("rep", None), P(("rep", "grp"), None), P(("rep", "grp"), None))
    return jax.shard_map(shards, mesh=mesh, in_specs=in_specs, out_specs=out_specs, check_vma=False)
```

```python
import functools
import math

import jax
import jax.numpy as jnp
from jax import lax
from jax.experimental import pallas as pl
from jax.experimental.pallas import tpu as pltpu
from jax.sharding import PartitionSpec as P

SCALE = 32.0
MARGIN = 0.2
SIN_FLOOR = 0.09
LOG2E = math.log2(math.e)
ALL = ("rep", "grp")
MIB = 1024 * 1024
COST = pl.CostEstimate(flops=1, bytes_accessed=1, transcendentals=0)

NT = (((1,), (1,)), ((), ()))


def in_hbm(value):
    return pltpu.with_memory_space_constraint(value, pltpu.HBM)


def unit_rows(wide):
    inv = lax.rsqrt(jnp.sum(wide * wide, axis=1, keepdims=True) + 1e-06)
    return wide * inv, inv


def off_axis(values, unit):
    return values - unit * jnp.sum(unit * values, axis=1, keepdims=True)


def column_of(row):
    lanes = row.shape[1]
    return jnp.transpose(jnp.broadcast_to(row, (128, lanes)))[:, :1]


def forward_kernel(
    base_ref, rep_ref, lab_ref, w_ref, mixed_ref, emb_ref, a_ref, b_ref, st_ref, what_ref, xhat_ref,
    sum_ref,
    *, classes, reps,
):
    step = pl.program_id(0)
    tile = w_ref.shape[0]
    batch = emb_ref.shape[0]

    @pl.when(step == 0)
    def _():
        rows = batch // reps
        for k in range(reps):
            first = pl.multiple_of((rep_ref[0] ^ k) * rows, rows)
            emb_ref[pl.ds(first, rows), :] = mixed_ref[k * rows : (k + 1) * rows, :]
        xwide, _ = unit_rows(emb_ref[...].astype(jnp.float32))
        xhat_ref[...] = xwide.astype(jnp.bfloat16)
        sum_ref[...] = jnp.zeros_like(sum_ref)
        a_ref[...] = jnp.zeros_like(a_ref)
        b_ref[...] = jnp.zeros_like(b_ref)

    wwide, _ = unit_rows(w_ref[...].astype(jnp.float32))
    what = wwide.astype(jnp.bfloat16)
    what_ref[...] = what
    cosine = lax.dot_general(xhat_ref[...], what, NT, preferred_element_type=jnp.float32)
    ids = lax.broadcasted_iota(jnp.int32, (batch, tile), 1)
    is_label = ids == lab_ref[...] - (base_ref[0] + step * tile)
    e = jnp.where(is_label, 0.0, jnp.exp2(cosine * (SCALE * LOG2E)))
    partial = e[:, :128]
    for c in range(1, tile // 128):
        partial = partial + e[:, c * 128 : (c + 1) * 128]
    sum_ref[...] += partial
    onehot = jnp.where(is_label, 1.0, 0.0).astype(jnp.bfloat16)
    a_ref[...] += jnp.dot(e.astype(jnp.bfloat16), what, preferred_element_type=jnp.float32)
    b_ref[...] += jnp.dot(onehot, what, preferred_element_type=jnp.float32)

    @pl.when(step == pl.num_programs(0) - 1)
    def _():
        xwide, x_inv = unit_rows(emb_ref[...].astype(jnp.float32))
        label_row = b_ref[...]
        c = jnp.sum(xhat_ref[...].astype(jnp.float32) * label_row, axis=1, keepdims=True)
        offset = lab_ref[...] - base_ref[0]
        has = jnp.where((offset >= 0) & (offset < classes), 1.0, 0.0)
        q = 1.0 - c * c
        sine = jnp.sqrt(jnp.maximum(q, SIN_FLOOR))
        margined = c * math.cos(MARGIN) - sine * math.sin(MARGIN)
        slope = math.cos(MARGIN) + jnp.where(q > SIN_FLOOR, c * math.sin(MARGIN) / sine, 0.0)
        slope = slope * has
        label_e = jnp.exp(SCALE * margined) * has
        total = jnp.sum(sum_ref[...], axis=1, keepdims=True) + label_e
        target = SCALE * margined * has
        b = slope * label_row
        a = a_ref[...] + label_e * b
        gain = SCALE * x_inv
        a_ref[...] = off_axis(a, xwide) * gain
        b_ref[...] = off_axis(b, xwide) * gain
        lane = lax.broadcasted_iota(jnp.int32, (batch, 128), 1)
        stats = jnp.where(lane == 0, total, 0.0)
        stats = jnp.where(lane == 1, target, stats)
        stats = jnp.where(lane == 2, label_e * slope, stats)
        stats = jnp.where(lane == 3, slope, stats)
        st_ref[...] = jnp.transpose(stats)[:8, :]


def forward(base, rep, mixed, reps, labels, weights):
    batch, width = mixed.shape
    classes = weights.shape[0]
    tile = math.gcd(classes, 1024)
    whole = lambda i: (0, 0)
    smem = pl.BlockSpec(memory_space=pltpu.SMEM)
    return pl.pallas_call(
        functools.partial(forward_kernel, classes=classes, reps=reps),
        grid=(classes // tile,),
        in_specs=[
            smem,
            smem,
            pl.BlockSpec((batch, 1), whole),
            pl.BlockSpec((tile, width), lambda i: (i, 0)),
            pl.BlockSpec((batch, width), whole),
        ],
        out_specs=[
            pl.BlockSpec((batch, width), whole),
            pl.BlockSpec((batch, width), whole),
            pl.BlockSpec((batch, width), whole),
            pl.BlockSpec((8, batch), whole),
            pl.BlockSpec((tile, width), lambda i: (i, 0)),
        ],
        out_shape=[
            jax.ShapeDtypeStruct((batch, width), jnp.bfloat16),
            jax.ShapeDtypeStruct((batch, width), jnp.float32),
            jax.ShapeDtypeStruct((batch, width), jnp.float32),
            jax.ShapeDtypeStruct((8, batch), jnp.float32),
            pltpu.HBM((classes, width), jnp.bfloat16),
        ],
        scratch_shapes=[pltpu.VMEM((batch, width), jnp.bfloat16), pltpu.VMEM((batch, 128), jnp.float32)],
        compiler_params=pltpu.CompilerParams(
            dimension_semantics=("arbitrary",), vmem_limit_bytes=20 * MIB
        ),
        cost_estimate=pl.CostEstimate(
            flops=12 * batch * classes * width, bytes_accessed=classes * width * 2, transcendentals=0
        ),
        name="forward_sums",
    )(base, rep, labels.reshape(batch, 1), weights, mixed)


def weight_kernel(base_ref, emb_ref, lab_ref, st_ref, tot_ref, w_ref, g_ref, xhat_ref, y_ref, v_ref):
    step = pl.program_id(0)
    tile = w_ref.shape[0]
    batch = emb_ref.shape[0]

    @pl.when(step == 0)
    def _():
        xwide, _ = unit_rows(emb_ref[...].astype(jnp.float32))
        xhat = xwide.astype(jnp.bfloat16)
        xhat_ref[...] = xhat
        total = tot_ref[...]
        y_ref[...] = (xhat.astype(jnp.float32) * column_of(SCALE / total)).astype(jnp.bfloat16)
        v_ref[...] = st_ref[2:3, :] - st_ref[3:4, :] * total

    block = math.gcd(tile, 256)
    for first in range(0, tile, block):
        at = pl.ds(first, block)
        wwide, w_inv = unit_rows(w_ref[at, :].astype(jnp.float32))
        what = wwide.astype(jnp.bfloat16)
        cosine = lax.dot_general(what, xhat_ref[...], NT, preferred_element_type=jnp.float32)
        ids = lax.broadcasted_iota(jnp.int32, (block, batch), 0)
        is_label = ids == lab_ref[...] - (base_ref[0] + step * tile + first)
        e = jnp.exp2(cosine * (SCALE * LOG2E))
        d = jnp.where(is_label, v_ref[...], e).astype(jnp.bfloat16)
        raw = jnp.dot(d, y_ref[...], preferred_element_type=jnp.float32)
        g_ref[at, :] = off_axis(raw, wwide) * w_inv


def weight_gradient(base, emb, labels, stats, totals, weights):
    batch, width = emb.shape
    classes = weights.shape[0]
    tile = math.gcd(classes, 1024)
    whole = lambda i: (0, 0)
    return pl.pallas_call(
        weight_kernel,
        grid=(classes // tile,),
        in_specs=[
            pl.BlockSpec(memory_space=pltpu.SMEM),
            pl.BlockSpec((batch, width), whole),
            pl.BlockSpec((1, batch), whole),
            pl.BlockSpec((8, batch), whole),
            pl.BlockSpec((1, batch), whole),
            pl.BlockSpec((tile, width), lambda i: (i, 0)),
        ],
        out_specs=pl.BlockSpec((tile, width), lambda i: (i, 0)),
        out_shape=pltpu.HBM((classes, width), jnp.float32),
        scratch_shapes=[
            pltpu.VMEM((batch, width), jnp.bfloat16),
            pltpu.VMEM((batch, width), jnp.bfloat16),
            pltpu.VMEM((1, batch), jnp.float32),
        ],
        compiler_params=pltpu.CompilerParams(
            dimension_semantics=("arbitrary",), vmem_limit_bytes=20 * MIB
        ),
        cost_estimate=pl.CostEstimate(
            flops=12 * batch * classes * width, bytes_accessed=classes * width * 6, transcendentals=0
        ),
        name="weight_gradient",
    )(base, emb, labels.reshape(1, batch), stats, totals.reshape(1, batch), weights)


def fetch_kernel(rows_ref, *refs, first):
    out_ref, sem = refs[-2:]
    peers, size, _ = out_ref.shape
    lanes = sem.shape[0]
    part = peers // lanes
    copies = [
        pltpu.make_async_copy(
            rows_ref.at[pl.ds(c * part, part), pl.ds(first, size), :],
            out_ref.at[pl.ds(c * part, part)],
            sem.at[c],
        )
        for c in range(lanes)
    ]
    for copy in copies:
        copy.start()
    for copy in copies:
        copy.wait()


def fetch(runs, first, size, tokens):
    peers, _, width = runs.shape
    hbm = pl.BlockSpec(memory_space=pltpu.HBM)
    anywhere = pl.BlockSpec(memory_space=pl.ANY)
    return pl.pallas_call(
        functools.partial(fetch_kernel, first=first),
        in_specs=[hbm] + [anywhere] * len(tokens),
        out_specs=pl.BlockSpec(memory_space=pltpu.VMEM),
        out_shape=jax.ShapeDtypeStruct((peers, size, width), runs.dtype),
        scratch_shapes=[pltpu.SemaphoreType.DMA((math.gcd(peers, 8),))],
        compiler_params=pltpu.CompilerParams(vmem_limit_bytes=6 * MIB),
        cost_estimate=pl.CostEstimate(
            flops=0, bytes_accessed=8 * peers * size * width, transcendentals=0
        ),
        name="fetch",
    )(runs, *tokens)


def tie_kernel(value_ref, *refs):
    refs[-1][...] = value_ref[...]


def tie(value, tokens):
    anywhere = pl.BlockSpec(memory_space=pl.ANY)
    vmem = pl.BlockSpec(memory_space=pltpu.VMEM)
    return pl.pallas_call(
        tie_kernel,
        in_specs=[vmem] + [anywhere] * len(tokens),
        out_specs=vmem,
        out_shape=jax.ShapeDtypeStruct(value.shape, value.dtype),
        compiler_params=pltpu.CompilerParams(vmem_limit_bytes=2 * MIB),
        cost_estimate=COST,
        name="tie",
    )(value, *tokens)


def release_kernel(*refs):
    pass


def released(value, tokens):
    anywhere = pl.BlockSpec(memory_space=pl.ANY)
    return pl.pallas_call(
        release_kernel,
        in_specs=[anywhere] * (1 + len(tokens)),
        out_specs=anywhere,
        out_shape=jax.ShapeDtypeStruct(value.shape, value.dtype),
        input_output_aliases={0: 0},
        cost_estimate=COST,
        name="release",
    )(value, *tokens)


def place_runs(me_ref, slot_ref, row_ref, held_ref, stage_ref, copies, peers, run, first):
    size = row_ref.shape[0] // peers
    batch = max(n for n in range(1, 49) if size % n == 0)
    chunk = max(n for n in range(16, 49, 16) if size % n == 0)

    def prepare(source, carry):
        for block in range(0, size, chunk):
            at = pl.multiple_of(source * size + block, chunk)
            unit, _ = unit_rows(row_ref[pl.ds(at, chunk), :].astype(jnp.float32))
            stage_ref[pl.ds(2 * at, chunk, stride=2), :] = unit[:, :128]
            stage_ref[pl.ds(2 * at + 1, chunk, stride=2), :] = unit[:, 128:]
        return carry

    lax.fori_loop(0, peers, prepare, 0)
    for copy in copies:
        copy.wait()

    def place(source, carry):
        start = (me_ref[0] ^ source) * run + first
        at = source * size * 2
        for block in range(0, size, batch):
            slots = [slot_ref[start + block + v] for v in range(batch)]
            values = [stage_ref[pl.ds(at + 2 * (block + v), 2), :] for v in range(batch)]
            for slot, value in zip(slots, values):
                held_ref[pl.ds(slot, 2), :] = value
        return carry

    lax.fori_loop(0, peers, place, 0)


def place_kernel(
    me_ref, slot_ref, row_ref, _, held_ref, token_ref, stage_ref, *, peers, run, first
):
    token_ref[...] = jnp.zeros_like(token_ref)
    place_runs(me_ref, slot_ref, row_ref, held_ref, stage_ref, [], peers, run, first)


def place_rows(me, slots, rows, after, peers, run, first):
    smem = pl.BlockSpec(memory_space=pltpu.SMEM)
    vmem = pl.BlockSpec(memory_space=pltpu.VMEM)
    anywhere = pl.BlockSpec(memory_space=pl.ANY)
    return pl.pallas_call(
        functools.partial(place_kernel, peers=peers, run=run, first=first),
        in_specs=[smem, smem, vmem, anywhere],
        out_specs=[vmem, vmem],
        out_shape=[
            jax.ShapeDtypeStruct((2 * peers * run, 128), jnp.float32),
            jax.ShapeDtypeStruct((8, 128), jnp.float32),
        ],
        scratch_shapes=[pltpu.VMEM((2 * rows.shape[0], 128), jnp.float32)],
        compiler_params=pltpu.CompilerParams(vmem_limit_bytes=24 * MIB),
        cost_estimate=pl.CostEstimate(
            flops=0, bytes_accessed=16 * rows.shape[0] * rows.shape[1], transcendentals=0
        ),
        name="place_rows",
    )(me, slots, rows, after)


def blend_kernel(
    me_ref, slot_ref, w_ref, row_ref, in_ref, o_ref, held_ref, stage_ref, sem, *, peers, run, first
):
    step = pl.program_id(0)
    tile = o_ref.shape[0]

    @pl.when(step == 0)
    def _():
        lanes = sem.shape[0]
        part = held_ref.shape[0] // lanes
        parts = [pl.ds(c * part, part) for c in range(lanes)]
        copies = [
            pltpu.make_async_copy(in_ref.at[at, :], held_ref.at[at, :], sem.at[c])
            for c, at in enumerate(parts)
        ]
        for copy in copies:
            copy.start()
        place_runs(me_ref, slot_ref, row_ref, held_ref, stage_ref, copies, peers, run, first)

    block = math.gcd(tile, 64)
    for begin in range(0, tile, block):
        rows = pl.ds(begin, block)
        at = pl.multiple_of((step * tile + begin) * 2, 2 * block)
        low = w_ref[rows, :128].astype(jnp.float32) + held_ref[pl.ds(at, block, stride=2), :]
        high = w_ref[rows, 128:].astype(jnp.float32) + held_ref[pl.ds(at + 1, block, stride=2), :]
        inv = lax.rsqrt(jnp.sum(low * low + high * high, axis=1, keepdims=True) + 1e-06)
        o_ref[rows, :128] = (low * inv).astype(jnp.bfloat16)
        o_ref[rows, 128:] = (high * inv).astype(jnp.bfloat16)


def place_and_blend(me, slots, rows, held, weights, peers, run, first):
    classes, width = weights.shape
    tile = math.gcd(classes, 1024)
    smem = pl.BlockSpec(memory_space=pltpu.SMEM)
    vmem = pl.BlockSpec(memory_space=pltpu.VMEM)
    tiles = pl.BlockSpec((tile, width), lambda i: (i, 0))
    return pl.pallas_call(
        functools.partial(blend_kernel, peers=peers, run=run, first=first),
        grid=(classes // tile,),
        in_specs=[smem, smem, tiles, vmem, pl.BlockSpec(memory_space=pl.ANY)],
        out_specs=tiles,
        out_shape=pltpu.HBM((classes, width), jnp.bfloat16),
        scratch_shapes=[
            pltpu.VMEM(held.shape, jnp.float32),
            pltpu.VMEM((2 * rows.shape[0], 128), jnp.float32),
            pltpu.SemaphoreType.DMA((4,)),
        ],
        compiler_params=pltpu.CompilerParams(
            dimension_semantics=("arbitrary",), vmem_limit_bytes=32 * MIB
        ),
        cost_estimate=pl.CostEstimate(
            flops=0, bytes_accessed=12 * classes * width, transcendentals=0
        ),
        name="place_and_blend",
    )(me, slots, weights, rows, held)


def shards(embeddings, labels, class_weights, centroids, centroid_class):
    rows_local, width = embeddings.shape
    classes = class_weights.shape[0]
    groups, reps = lax.axis_size("grp"), lax.axis_size("rep")
    peers = groups * reps
    batch = rows_local * reps
    run = classes // peers
    grp, rep = lax.axis_index("grp").astype(jnp.int32), lax.axis_index("rep").astype(jnp.int32)
    me = (rep * groups + grp).reshape(1)
    base = me * classes

    def swap(value, axis, k):
        size = lax.axis_size(axis)
        return lax.ppermute(value, axis, [(i, i ^ k) for i in range(size)]) if k else value

    def relay(sent):
        return lax.all_to_all(sent, ALL, 0, 0, tiled=True).reshape(-1, width)

    weights = in_hbm(class_weights)
    runs = in_hbm(centroids.reshape(peers, run, width))
    cut = run * 5 // 8 // 16 * 16
    mixed = jnp.concatenate([swap(embeddings, "rep", c) for c in range(2)])
    mixed = jnp.concatenate([swap(mixed, "rep", 2 * z) for z in range(reps // 2)])
    rows_a = relay(released(fetch(runs, 0, cut, []), [mixed]))
    emb, a, b, stats, what = forward(base, rep.reshape(1), mixed, reps, labels, weights)

    half = reps // 2
    core, deep = rep % 2, rep // 2
    index = lax.dynamic_index_in_dim

    def share_out(sums, wanted, axis, flips):
        got = []
        for flip, asked in zip(flips, wanted):
            sent = jnp.concatenate([sums, asked.reshape(-1)]).reshape(-1, 128)
            got.append(swap(sent, axis, flip).reshape(-1))
        got = jnp.stack(got)
        return jnp.sum(got[:, : 2 * batch], axis=0), got[:, 2 * batch :]

    wanted = centroid_class.reshape(half, 2, groups, run).astype(jnp.float32)
    wanted = [index(wanted, grp ^ j, 2, False) for j in range(groups)]
    sums, wanted = share_out(stats[:2].reshape(-1), wanted, "grp", range(groups))
    wanted = wanted.reshape(groups, half, 2, run)
    wanted = [index(wanted, core ^ c, 2, False) for c in range(2)]
    sums, wanted = share_out(sums, wanted, "rep", range(2))
    sent_b = fetch(runs, cut, run - cut, [stats])
    sums = tie(sums.reshape(-1, 128), [sent_b]).reshape(-1)
    wanted = wanted.reshape(2, groups, half, run)
    wanted = [index(wanted, deep ^ z, 2, False) for z in range(half)]
    sums, slots = share_out(sums, wanted, "rep", range(0, reps, 2))
    slots = slots.reshape(-1).astype(jnp.int32) * 2
    total, target = sums[:batch], sums[batch:]
    losses = jnp.log(total) - target
    loss = lax.dynamic_slice_in_dim(losses, rep * rows_local, rows_local, 0)

    rows_b = relay(released(sent_b, [total]))
    weight_grad = weight_gradient(base, emb, labels, stats, total, weights)
    done = in_hbm(weight_grad)
    held, token = place_rows(me, slots, rows_a, done, peers, run, 0)

    grad = (a / total[:, None] - b).reshape(half, 2, rows_local, width)
    grad = sum(swap(index(grad, core ^ c, 1, False), "rep", c) for c in range(2))
    grad = tie(grad, [done])
    grad = sum(swap(grad, "grp", j) for j in range(groups))
    grad = tie(grad, [token, loss])
    embedding_gradient = sum(
        swap(index(grad, deep ^ z, 0, False), "rep", 2 * z) for z in range(half)
    )

    refreshed = place_and_blend(me, slots, rows_b, in_hbm(held), in_hbm(what), peers, run, cut)
    return (loss, embedding_gradient, weight_grad, refreshed)


def solution(mesh):
    in_specs = (
        P("rep", None),
        P(),
        P(("rep", "grp"), None),
        P(("grp", "rep"), None),
        P(("grp", "rep")),
    )
    out_specs = (P("rep"), P("rep", None), P(("rep", "grp"), None), P(("rep", "grp"), None))
    return jax.shard_map(shards, mesh=mesh, in_specs=in_specs, out_specs=out_specs, check_vma=False)
```

```python
import functools
import math

import jax
import jax.numpy as jnp
from jax import lax
from jax.experimental import pallas as pl
from jax.experimental.pallas import tpu as pltpu
from jax.sharding import PartitionSpec as P

SCALE = 32.0
MARGIN = 0.2
SIN_FLOOR = 0.09
LOG2E = math.log2(math.e)
ALL = ("rep", "grp")
MIB = 1024 * 1024
COST = pl.CostEstimate(flops=1, bytes_accessed=1, transcendentals=0)

NT = (((1,), (1,)), ((), ()))


def in_hbm(value):
    return pltpu.with_memory_space_constraint(value, pltpu.HBM)


def unit_rows(wide):
    inv = lax.rsqrt(jnp.sum(wide * wide, axis=1, keepdims=True) + 1e-06)
    return wide * inv, inv


def off_axis(values, unit):
    return values - unit * jnp.sum(unit * values, axis=1, keepdims=True)


def column_of(row):
    lanes = row.shape[1]
    return jnp.transpose(jnp.broadcast_to(row, (128, lanes)))[:, :1]


def forward_kernel(
    base_ref, rep_ref, lab_ref, w_ref, mixed_ref, emb_ref, a_ref, b_ref, st_ref, what_ref, xhat_ref,
    sum_ref,
    *, classes, reps,
):
    step = pl.program_id(0)
    tile = w_ref.shape[0]
    batch = emb_ref.shape[0]

    @pl.when(step == 0)
    def _():
        rows = batch // reps
        for k in range(reps):
            first = pl.multiple_of((rep_ref[0] ^ k) * rows, rows)
            emb_ref[pl.ds(first, rows), :] = mixed_ref[k * rows : (k + 1) * rows, :]
        xwide, _ = unit_rows(emb_ref[...].astype(jnp.float32))
        xhat_ref[...] = xwide.astype(jnp.bfloat16)
        sum_ref[...] = jnp.zeros_like(sum_ref)
        a_ref[...] = jnp.zeros_like(a_ref)
        b_ref[...] = jnp.zeros_like(b_ref)

    wwide, _ = unit_rows(w_ref[...].astype(jnp.float32))
    what = wwide.astype(jnp.bfloat16)
    what_ref[...] = what
    cosine = lax.dot_general(xhat_ref[...], what, NT, preferred_element_type=jnp.float32)
    ids = lax.broadcasted_iota(jnp.int32, (batch, tile), 1)
    is_label = ids == lab_ref[...] - (base_ref[0] + step * tile)
    e = jnp.where(is_label, 0.0, jnp.exp2(cosine * (SCALE * LOG2E)))
    partial = e[:, :128]
    for c in range(1, tile // 128):
        partial = partial + e[:, c * 128 : (c + 1) * 128]
    sum_ref[...] += partial
    onehot = jnp.where(is_label, 1.0, 0.0).astype(jnp.bfloat16)
    a_ref[...] += jnp.dot(e.astype(jnp.bfloat16), what, preferred_element_type=jnp.float32)
    b_ref[...] += jnp.dot(onehot, what, preferred_element_type=jnp.float32)

    @pl.when(step == pl.num_programs(0) - 1)
    def _():
        xwide, x_inv = unit_rows(emb_ref[...].astype(jnp.float32))
        label_row = b_ref[...]
        c = jnp.sum(xhat_ref[...].astype(jnp.float32) * label_row, axis=1, keepdims=True)
        offset = lab_ref[...] - base_ref[0]
        has = jnp.where((offset >= 0) & (offset < classes), 1.0, 0.0)
        q = 1.0 - c * c
        sine = jnp.sqrt(jnp.maximum(q, SIN_FLOOR))
        margined = c * math.cos(MARGIN) - sine * math.sin(MARGIN)
        slope = math.cos(MARGIN) + jnp.where(q > SIN_FLOOR, c * math.sin(MARGIN) / sine, 0.0)
        slope = slope * has
        label_e = jnp.exp(SCALE * margined) * has
        total = jnp.sum(sum_ref[...], axis=1, keepdims=True) + label_e
        target = SCALE * margined * has
        b = slope * label_row
        a = a_ref[...] + label_e * b
        gain = SCALE * x_inv
        a_ref[...] = off_axis(a, xwide) * gain
        b_ref[...] = off_axis(b, xwide) * gain
        lane = lax.broadcasted_iota(jnp.int32, (batch, 128), 1)
        stats = jnp.where(lane == 0, total, 0.0)
        stats = jnp.where(lane == 1, target, stats)
        stats = jnp.where(lane == 2, label_e * slope, stats)
        stats = jnp.where(lane == 3, slope, stats)
        st_ref[...] = jnp.transpose(stats)[:8, :]


def forward(base, rep, mixed, reps, labels, weights):
    batch, width = mixed.shape
    classes = weights.shape[0]
    tile = math.gcd(classes, 1024)
    whole = lambda i: (0, 0)
    smem = pl.BlockSpec(memory_space=pltpu.SMEM)
    return pl.pallas_call(
        functools.partial(forward_kernel, classes=classes, reps=reps),
        grid=(classes // tile,),
        in_specs=[
            smem,
            smem,
            pl.BlockSpec((batch, 1), whole),
            pl.BlockSpec((tile, width), lambda i: (i, 0)),
            pl.BlockSpec((batch, width), whole),
        ],
        out_specs=[
            pl.BlockSpec((batch, width), whole),
            pl.BlockSpec((batch, width), whole),
            pl.BlockSpec((batch, width), whole),
            pl.BlockSpec((8, batch), whole),
            pl.BlockSpec((tile, width), lambda i: (i, 0)),
        ],
        out_shape=[
            jax.ShapeDtypeStruct((batch, width), jnp.bfloat16),
            jax.ShapeDtypeStruct((batch, width), jnp.float32),
            jax.ShapeDtypeStruct((batch, width), jnp.float32),
            jax.ShapeDtypeStruct((8, batch), jnp.float32),
            pltpu.HBM((classes, width), jnp.bfloat16),
        ],
        scratch_shapes=[pltpu.VMEM((batch, width), jnp.bfloat16), pltpu.VMEM((batch, 128), jnp.float32)],
        compiler_params=pltpu.CompilerParams(
            dimension_semantics=("arbitrary",), vmem_limit_bytes=20 * MIB
        ),
        cost_estimate=pl.CostEstimate(
            flops=12 * batch * classes * width, bytes_accessed=classes * width * 2, transcendentals=0
        ),
        name="forward_sums",
    )(base, rep, labels.reshape(batch, 1), weights, mixed)


def weight_kernel(base_ref, emb_ref, lab_ref, st_ref, tot_ref, w_ref, g_ref, xhat_ref, y_ref, v_ref):
    step = pl.program_id(0)
    tile = w_ref.shape[0]
    batch = emb_ref.shape[0]

    @pl.when(step == 0)
    def _():
        xwide, _ = unit_rows(emb_ref[...].astype(jnp.float32))
        xhat = xwide.astype(jnp.bfloat16)
        xhat_ref[...] = xhat
        total = tot_ref[...]
        y_ref[...] = (xhat.astype(jnp.float32) * column_of(SCALE / total)).astype(jnp.bfloat16)
        v_ref[...] = st_ref[2:3, :] - st_ref[3:4, :] * total

    block = math.gcd(tile, 256)
    for first in range(0, tile, block):
        at = pl.ds(first, block)
        wwide, w_inv = unit_rows(w_ref[at, :].astype(jnp.float32))
        what = wwide.astype(jnp.bfloat16)
        cosine = lax.dot_general(what, xhat_ref[...], NT, preferred_element_type=jnp.float32)
        ids = lax.broadcasted_iota(jnp.int32, (block, batch), 0)
        is_label = ids == lab_ref[...] - (base_ref[0] + step * tile + first)
        e = jnp.exp2(cosine * (SCALE * LOG2E))
        d = jnp.where(is_label, v_ref[...], e).astype(jnp.bfloat16)
        raw = jnp.dot(d, y_ref[...], preferred_element_type=jnp.float32)
        g_ref[at, :] = off_axis(raw, wwide) * w_inv


def weight_gradient(base, emb, labels, stats, totals, weights):
    batch, width = emb.shape
    classes = weights.shape[0]
    tile = math.gcd(classes, 1024)
    whole = lambda i: (0, 0)
    return pl.pallas_call(
        weight_kernel,
        grid=(classes // tile,),
        in_specs=[
            pl.BlockSpec(memory_space=pltpu.SMEM),
            pl.BlockSpec((batch, width), whole),
            pl.BlockSpec((1, batch), whole),
            pl.BlockSpec((8, batch), whole),
            pl.BlockSpec((1, batch), whole),
            pl.BlockSpec((tile, width), lambda i: (i, 0)),
        ],
        out_specs=pl.BlockSpec((tile, width), lambda i: (i, 0)),
        out_shape=pltpu.HBM((classes, width), jnp.float32),
        scratch_shapes=[
            pltpu.VMEM((batch, width), jnp.bfloat16),
            pltpu.VMEM((batch, width), jnp.bfloat16),
            pltpu.VMEM((1, batch), jnp.float32),
        ],
        compiler_params=pltpu.CompilerParams(
            dimension_semantics=("arbitrary",), vmem_limit_bytes=20 * MIB
        ),
        cost_estimate=pl.CostEstimate(
            flops=12 * batch * classes * width, bytes_accessed=classes * width * 6, transcendentals=0
        ),
        name="weight_gradient",
    )(base, emb, labels.reshape(1, batch), stats, totals.reshape(1, batch), weights)


def fetch_kernel(rows_ref, *refs, first):
    out_ref, sem = refs[-2:]
    peers, size, _ = out_ref.shape
    lanes = sem.shape[0]
    part = peers // lanes
    copies = [
        pltpu.make_async_copy(
            rows_ref.at[pl.ds(c * part, part), pl.ds(first, size), :],
            out_ref.at[pl.ds(c * part, part)],
            sem.at[c],
        )
        for c in range(lanes)
    ]
    for copy in copies:
        copy.start()
    for copy in copies:
        copy.wait()


def fetch(runs, first, size, tokens):
    peers, _, width = runs.shape
    hbm = pl.BlockSpec(memory_space=pltpu.HBM)
    anywhere = pl.BlockSpec(memory_space=pl.ANY)
    return pl.pallas_call(
        functools.partial(fetch_kernel, first=first),
        in_specs=[hbm] + [anywhere] * len(tokens),
        out_specs=pl.BlockSpec(memory_space=pltpu.VMEM),
        out_shape=jax.ShapeDtypeStruct((peers, size, width), runs.dtype),
        scratch_shapes=[pltpu.SemaphoreType.DMA((math.gcd(peers, 8),))],
        compiler_params=pltpu.CompilerParams(vmem_limit_bytes=6 * MIB),
        cost_estimate=pl.CostEstimate(
            flops=0, bytes_accessed=8 * peers * size * width, transcendentals=0
        ),
        name="fetch",
    )(runs, *tokens)


def join_kernel(*refs, count):
    total = refs[0][...]
    for ref in refs[1:count]:
        total = total + ref[...]
    refs[-1][...] = total


def join(values, tokens):
    anywhere = pl.BlockSpec(memory_space=pl.ANY)
    vmem = pl.BlockSpec(memory_space=pltpu.VMEM)
    return pl.pallas_call(
        functools.partial(join_kernel, count=len(values)),
        in_specs=[vmem] * len(values) + [anywhere] * len(tokens),
        out_specs=vmem,
        out_shape=jax.ShapeDtypeStruct(values[0].shape, values[0].dtype),
        compiler_params=pltpu.CompilerParams(vmem_limit_bytes=6 * MIB),
        cost_estimate=COST,
        name="join",
    )(*values, *tokens)


def release_kernel(*refs):
    pass


def released(value, tokens):
    anywhere = pl.BlockSpec(memory_space=pl.ANY)
    return pl.pallas_call(
        release_kernel,
        in_specs=[anywhere] * (1 + len(tokens)),
        out_specs=anywhere,
        out_shape=jax.ShapeDtypeStruct(value.shape, value.dtype),
        input_output_aliases={0: 0},
        cost_estimate=COST,
        name="release",
    )(value, *tokens)


def place_runs(me_ref, slot_ref, row_ref, held_ref, stage_ref, copies, peers, run, first):
    size = row_ref.shape[0] // peers
    batch = max(n for n in range(1, 49) if size % n == 0)
    chunk = max(n for n in range(16, 49, 16) if size % n == 0)

    def prepare(source, carry):
        for block in range(0, size, chunk):
            at = pl.multiple_of(source * size + block, chunk)
            unit, _ = unit_rows(row_ref[pl.ds(at, chunk), :].astype(jnp.float32))
            stage_ref[pl.ds(2 * at, chunk, stride=2), :] = unit[:, :128]
            stage_ref[pl.ds(2 * at + 1, chunk, stride=2), :] = unit[:, 128:]
        return carry

    lax.fori_loop(0, peers, prepare, 0)
    for copy in copies:
        copy.wait()

    def place(source, carry):
        start = (me_ref[0] ^ source) * run + first
        at = source * size * 2
        for block in range(0, size, batch):
            slots = [slot_ref[start + block + v] for v in range(batch)]
            values = [stage_ref[pl.ds(at + 2 * (block + v), 2), :] for v in range(batch)]
            for slot, value in zip(slots, values):
                held_ref[pl.ds(slot, 2), :] = value
        return carry

    lax.fori_loop(0, peers, place, 0)


def place_kernel(
    me_ref, slot_ref, row_ref, _, held_ref, token_ref, stage_ref, *, peers, run, first
):
    token_ref[...] = jnp.zeros_like(token_ref)
    place_runs(me_ref, slot_ref, row_ref, held_ref, stage_ref, [], peers, run, first)


def place_rows(me, slots, rows, after, peers, run, first):
    smem = pl.BlockSpec(memory_space=pltpu.SMEM)
    vmem = pl.BlockSpec(memory_space=pltpu.VMEM)
    anywhere = pl.BlockSpec(memory_space=pl.ANY)
    return pl.pallas_call(
        functools.partial(place_kernel, peers=peers, run=run, first=first),
        in_specs=[smem, smem, vmem, anywhere],
        out_specs=[vmem, vmem],
        out_shape=[
            jax.ShapeDtypeStruct((2 * peers * run, 128), jnp.float32),
            jax.ShapeDtypeStruct((8, 128), jnp.float32),
        ],
        scratch_shapes=[pltpu.VMEM((2 * rows.shape[0], 128), jnp.float32)],
        compiler_params=pltpu.CompilerParams(vmem_limit_bytes=24 * MIB),
        cost_estimate=pl.CostEstimate(
            flops=0, bytes_accessed=32 * rows.shape[0] * rows.shape[1], transcendentals=0
        ),
        name="place_rows",
    )(me, slots, rows, after)


def blend_kernel(
    me_ref, slot_ref, w_ref, row_ref, in_ref, o_ref, held_ref, stage_ref, sem, *, peers, run, first
):
    step = pl.program_id(0)
    tile = o_ref.shape[0]

    @pl.when(step == 0)
    def _():
        lanes = sem.shape[0]
        part = held_ref.shape[0] // lanes
        parts = [pl.ds(c * part, part) for c in range(lanes)]
        copies = [
            pltpu.make_async_copy(in_ref.at[at, :], held_ref.at[at, :], sem.at[c])
            for c, at in enumerate(parts)
        ]
        for copy in copies:
            copy.start()
        place_runs(me_ref, slot_ref, row_ref, held_ref, stage_ref, copies, peers, run, first)

    block = math.gcd(tile, 64)
    for begin in range(0, tile, block):
        rows = pl.ds(begin, block)
        at = pl.multiple_of((step * tile + begin) * 2, 2 * block)
        low = w_ref[rows, :128].astype(jnp.float32) + held_ref[pl.ds(at, block, stride=2), :]
        high = w_ref[rows, 128:].astype(jnp.float32) + held_ref[pl.ds(at + 1, block, stride=2), :]
        inv = lax.rsqrt(jnp.sum(low * low + high * high, axis=1, keepdims=True) + 1e-06)
        o_ref[rows, :128] = (low * inv).astype(jnp.bfloat16)
        o_ref[rows, 128:] = (high * inv).astype(jnp.bfloat16)


def place_and_blend(me, slots, rows, held, weights, peers, run, first):
    classes, width = weights.shape
    tile = math.gcd(classes, 1024)
    smem = pl.BlockSpec(memory_space=pltpu.SMEM)
    vmem = pl.BlockSpec(memory_space=pltpu.VMEM)
    tiles = pl.BlockSpec((tile, width), lambda i: (i, 0))
    return pl.pallas_call(
        functools.partial(blend_kernel, peers=peers, run=run, first=first),
        grid=(classes // tile,),
        in_specs=[smem, smem, tiles, vmem, pl.BlockSpec(memory_space=pl.ANY)],
        out_specs=tiles,
        out_shape=pltpu.HBM((classes, width), jnp.bfloat16),
        scratch_shapes=[
            pltpu.VMEM(held.shape, jnp.float32),
            pltpu.VMEM((2 * rows.shape[0], 128), jnp.float32),
            pltpu.SemaphoreType.DMA((4,)),
        ],
        compiler_params=pltpu.CompilerParams(
            dimension_semantics=("arbitrary",), vmem_limit_bytes=32 * MIB
        ),
        cost_estimate=pl.CostEstimate(
            flops=0, bytes_accessed=12 * classes * width, transcendentals=0
        ),
        name="place_and_blend",
    )(me, slots, weights, rows, held)


def shards(embeddings, labels, class_weights, centroids, centroid_class):
    rows_local, width = embeddings.shape
    classes = class_weights.shape[0]
    groups, reps = lax.axis_size("grp"), lax.axis_size("rep")
    peers = groups * reps
    batch = rows_local * reps
    run = classes // peers
    grp, rep = lax.axis_index("grp").astype(jnp.int32), lax.axis_index("rep").astype(jnp.int32)
    me = (rep * groups + grp).reshape(1)
    base = me * classes

    def swap(value, axis, k):
        size = lax.axis_size(axis)
        return lax.ppermute(value, axis, [(i, i ^ k) for i in range(size)]) if k else value

    def relay(sent):
        return lax.all_to_all(sent, ALL, 0, 0, tiled=True).reshape(-1, width)

    weights = in_hbm(class_weights)
    runs = in_hbm(centroids.reshape(peers, run, width))
    cut = run * 5 // 8 // 16 * 16
    mixed = jnp.concatenate([swap(embeddings, "rep", c) for c in range(2)])
    mixed = jnp.concatenate([swap(mixed, "rep", 2 * z) for z in range(reps // 2)])
    rows_a = relay(released(fetch(runs, 0, cut, []), [mixed]))
    emb, a, b, stats, what = forward(base, rep.reshape(1), mixed, reps, labels, weights)

    half = reps // 2
    core, deep = rep % 2, rep // 2
    index = lax.dynamic_index_in_dim

    def share_out(sums, wanted, axis, flips):
        got = []
        for flip, asked in zip(flips, wanted):
            sent = jnp.concatenate([sums, asked.reshape(-1)]).reshape(-1, 128)
            got.append(swap(sent, axis, flip).reshape(-1))
        got = jnp.stack(got)
        return jnp.sum(got[:, : 2 * batch], axis=0), got[:, 2 * batch :]

    wanted = centroid_class.reshape(half, 2, groups, run).astype(jnp.float32)
    wanted = [index(wanted, grp ^ j, 2, False) for j in range(groups)]
    sums, wanted = share_out(stats[:2].reshape(-1), wanted, "grp", range(groups))
    wanted = wanted.reshape(groups, half, 2, run)
    wanted = [index(wanted, core ^ c, 2, False) for c in range(2)]
    sums, wanted = share_out(sums, wanted, "rep", range(2))
    sent_b = fetch(runs, cut, run - cut, [stats])
    sums = join([sums.reshape(-1, 128)], [sent_b]).reshape(-1)
    wanted = wanted.reshape(2, groups, half, run)
    wanted = [index(wanted, deep ^ z, 2, False) for z in range(half)]
    sums, slots = share_out(sums, wanted, "rep", range(0, reps, 2))
    slots = slots.reshape(-1).astype(jnp.int32) * 2
    total, target = sums[:batch], sums[batch:]
    losses = jnp.log(total) - target
    loss = lax.dynamic_slice_in_dim(losses, rep * rows_local, rows_local, 0)

    rows_b = relay(released(sent_b, [total]))
    weight_grad = weight_gradient(base, emb, labels, stats, total, weights)
    done = in_hbm(weight_grad)
    held, token = place_rows(me, slots, rows_a, done, peers, run, 0)

    grad = (a / total[:, None] - b).reshape(half, 2, rows_local, width)
    grad = join([swap(index(grad, core ^ c, 1, False), "rep", c) for c in range(2)], [done])
    grad = join([swap(grad, "grp", j) for j in range(groups)], [token, loss])
    embedding_gradient = sum(
        swap(index(grad, deep ^ z, 0, False), "rep", 2 * z) for z in range(half)
    )

    refreshed = place_and_blend(me, slots, rows_b, in_hbm(held), in_hbm(what), peers, run, cut)
    return (loss, embedding_gradient, weight_grad, refreshed)


def solution(mesh):
    in_specs = (
        P("rep", None),
        P(),
        P(("rep", "grp"), None),
        P(("grp", "rep"), None),
        P(("grp", "rep")),
    )
    out_specs = (P("rep"), P("rep", None), P(("rep", "grp"), None), P(("rep", "grp"), None))
    return jax.shard_map(shards, mesh=mesh, in_specs=in_specs, out_specs=out_specs, check_vma=False)
```

```python
import functools
import math

import jax
import jax.numpy as jnp
from jax import lax
from jax.experimental import pallas as pl
from jax.experimental.pallas import tpu as pltpu
from jax.sharding import PartitionSpec as P

SCALE = 32.0
MARGIN = 0.2
SIN_FLOOR = 0.09
LOG2E = math.log2(math.e)
ALL = ("rep", "grp")
MIB = 1024 * 1024
COST = pl.CostEstimate(flops=1, bytes_accessed=1, transcendentals=0)

NT = (((1,), (1,)), ((), ()))


def in_hbm(value):
    return pltpu.with_memory_space_constraint(value, pltpu.HBM)


def unit_rows(wide):
    inv = lax.rsqrt(jnp.sum(wide * wide, axis=1, keepdims=True) + 1e-06)
    return wide * inv, inv


def off_axis(values, unit):
    return values - unit * jnp.sum(unit * values, axis=1, keepdims=True)


def column_of(row):
    lanes = row.shape[1]
    return jnp.transpose(jnp.broadcast_to(row, (128, lanes)))[:, :1]


def forward_kernel(
    base_ref, rep_ref, lab_ref, w_ref, mixed_ref, emb_ref, a_ref, b_ref, st_ref, what_ref, xhat_ref,
    sum_ref,
    *, classes, reps,
):
    step = pl.program_id(0)
    tile = w_ref.shape[0]
    batch = emb_ref.shape[0]

    @pl.when(step == 0)
    def _():
        rows = batch // reps
        for k in range(reps):
            first = pl.multiple_of((rep_ref[0] ^ k) * rows, rows)
            emb_ref[pl.ds(first, rows), :] = mixed_ref[k * rows : (k + 1) * rows, :]
        xwide, _ = unit_rows(emb_ref[...].astype(jnp.float32))
        xhat_ref[...] = xwide.astype(jnp.bfloat16)
        sum_ref[...] = jnp.zeros_like(sum_ref)
        a_ref[...] = jnp.zeros_like(a_ref)
        b_ref[...] = jnp.zeros_like(b_ref)

    wwide, _ = unit_rows(w_ref[...].astype(jnp.float32))
    what = wwide.astype(jnp.bfloat16)
    what_ref[...] = what
    cosine = lax.dot_general(xhat_ref[...], what, NT, preferred_element_type=jnp.float32)
    ids = lax.broadcasted_iota(jnp.int32, (batch, tile), 1)
    is_label = ids == lab_ref[...] - (base_ref[0] + step * tile)
    e = jnp.where(is_label, 0.0, jnp.exp2(cosine * (SCALE * LOG2E)))
    partial = e[:, :128]
    for c in range(1, tile // 128):
        partial = partial + e[:, c * 128 : (c + 1) * 128]
    sum_ref[...] += partial
    onehot = jnp.where(is_label, 1.0, 0.0).astype(jnp.bfloat16)
    a_ref[...] += jnp.dot(e.astype(jnp.bfloat16), what, preferred_element_type=jnp.float32)
    b_ref[...] += jnp.dot(onehot, what, preferred_element_type=jnp.float32)

    @pl.when(step == pl.num_programs(0) - 1)
    def _():
        xwide, x_inv = unit_rows(emb_ref[...].astype(jnp.float32))
        label_row = b_ref[...]
        c = jnp.sum(xhat_ref[...].astype(jnp.float32) * label_row, axis=1, keepdims=True)
        offset = lab_ref[...] - base_ref[0]
        has = jnp.where((offset >= 0) & (offset < classes), 1.0, 0.0)
        q = 1.0 - c * c
        sine = jnp.sqrt(jnp.maximum(q, SIN_FLOOR))
        margined = c * math.cos(MARGIN) - sine * math.sin(MARGIN)
        slope = math.cos(MARGIN) + jnp.where(q > SIN_FLOOR, c * math.sin(MARGIN) / sine, 0.0)
        slope = slope * has
        label_e = jnp.exp(SCALE * margined) * has
        total = jnp.sum(sum_ref[...], axis=1, keepdims=True) + label_e
        target = SCALE * margined * has
        b = slope * label_row
        a = a_ref[...] + label_e * b
        gain = SCALE * x_inv
        a_ref[...] = off_axis(a, xwide) * gain
        b_ref[...] = off_axis(b, xwide) * gain
        lane = lax.broadcasted_iota(jnp.int32, (batch, 128), 1)
        stats = jnp.where(lane == 0, total, 0.0)
        stats = jnp.where(lane == 1, target, stats)
        stats = jnp.where(lane == 2, label_e * slope, stats)
        stats = jnp.where(lane == 3, slope, stats)
        st_ref[...] = jnp.transpose(stats)[:8, :]


def forward(base, rep, mixed, reps, labels, weights):
    batch, width = mixed.shape
    classes = weights.shape[0]
    tile = math.gcd(classes, 1024)
    whole = lambda i: (0, 0)
    smem = pl.BlockSpec(memory_space=pltpu.SMEM)
    return pl.pallas_call(
        functools.partial(forward_kernel, classes=classes, reps=reps),
        grid=(classes // tile,),
        in_specs=[
            smem,
            smem,
            pl.BlockSpec((batch, 1), whole),
            pl.BlockSpec((tile, width), lambda i: (i, 0)),
            pl.BlockSpec((batch, width), whole),
        ],
        out_specs=[
            pl.BlockSpec((batch, width), whole),
            pl.BlockSpec((batch, width), whole),
            pl.BlockSpec((batch, width), whole),
            pl.BlockSpec((8, batch), whole),
            pl.BlockSpec((tile, width), lambda i: (i, 0)),
        ],
        out_shape=[
            jax.ShapeDtypeStruct((batch, width), jnp.bfloat16),
            jax.ShapeDtypeStruct((batch, width), jnp.float32),
            jax.ShapeDtypeStruct((batch, width), jnp.float32),
            jax.ShapeDtypeStruct((8, batch), jnp.float32),
            pltpu.HBM((classes, width), jnp.bfloat16),
        ],
        scratch_shapes=[pltpu.VMEM((batch, width), jnp.bfloat16), pltpu.VMEM((batch, 128), jnp.float32)],
        compiler_params=pltpu.CompilerParams(
            dimension_semantics=("arbitrary",), vmem_limit_bytes=20 * MIB
        ),
        cost_estimate=pl.CostEstimate(
            flops=12 * batch * classes * width, bytes_accessed=classes * width * 2, transcendentals=0
        ),
        name="forward_sums",
    )(base, rep, labels.reshape(batch, 1), weights, mixed)


def split_copies(source_ref, target_ref, sem):
    lanes = sem.shape[0]
    size = source_ref.shape[0] // lanes
    parts = [pl.ds(c * size, size) for c in range(lanes)]
    return [
        pltpu.make_async_copy(source_ref.at[part, :], target_ref.at[part, :], sem.at[c])
        for c, part in enumerate(parts)
    ]


def place_runs(me_ref, slot_ref, row_ref, held_ref, stage_ref, copies, peers, run, first):
    size = row_ref.shape[0] // peers
    batch = max(n for n in range(1, 49) if size % n == 0)
    chunk = max(n for n in range(16, 49, 16) if size % n == 0)

    def prepare(source, carry):
        for block in range(0, size, chunk):
            at = pl.multiple_of(source * size + block, chunk)
            unit, _ = unit_rows(row_ref[pl.ds(at, chunk), :].astype(jnp.float32))
            stage_ref[pl.ds(2 * at, chunk, stride=2), :] = unit[:, :128]
            stage_ref[pl.ds(2 * at + 1, chunk, stride=2), :] = unit[:, 128:]
        return carry

    lax.fori_loop(0, peers, prepare, 0)
    for copy in copies:
        copy.wait()

    def place(source, carry):
        start = (me_ref[0] ^ source) * run + first
        at = source * size * 2
        for block in range(0, size, batch):
            slots = [slot_ref[start + block + v] for v in range(batch)]
            values = [stage_ref[pl.ds(at + 2 * (block + v), 2), :] for v in range(batch)]
            for slot, value in zip(slots, values):
                held_ref[pl.ds(slot, 2), :] = value
        return carry

    lax.fori_loop(0, peers, place, 0)


def weight_kernel(
    base_ref, me_ref, slot_ref, emb_ref, lab_ref, st_ref, tot_ref, w_ref, *refs, peers, run, starts
):
    row_refs, refs = refs[: len(starts)], refs[len(starts) :]
    g_ref, out_ref, xhat_ref, y_ref, v_ref, held_ref, stage_ref, sem = refs
    copies = split_copies(held_ref, out_ref, sem)
    step = pl.program_id(0)
    tile = w_ref.shape[0]
    batch = emb_ref.shape[0]

    @pl.when(step == 0)
    def _():
        xwide, _ = unit_rows(emb_ref[...].astype(jnp.float32))
        xhat = xwide.astype(jnp.bfloat16)
        xhat_ref[...] = xhat
        total = tot_ref[...]
        y_ref[...] = (xhat.astype(jnp.float32) * column_of(SCALE / total)).astype(jnp.bfloat16)
        v_ref[...] = st_ref[2:3, :] - st_ref[3:4, :] * total
        for row_ref, first in zip(row_refs, starts):
            place_runs(me_ref, slot_ref, row_ref, held_ref, stage_ref, [], peers, run, first)
        for copy in copies:
            copy.start()

    block = math.gcd(tile, 256)
    for first in range(0, tile, block):
        at = pl.ds(first, block)
        wwide, w_inv = unit_rows(w_ref[at, :].astype(jnp.float32))
        what = wwide.astype(jnp.bfloat16)
        cosine = lax.dot_general(what, xhat_ref[...], NT, preferred_element_type=jnp.float32)
        ids = lax.broadcasted_iota(jnp.int32, (block, batch), 0)
        is_label = ids == lab_ref[...] - (base_ref[0] + step * tile + first)
        e = jnp.exp2(cosine * (SCALE * LOG2E))
        d = jnp.where(is_label, v_ref[...], e).astype(jnp.bfloat16)
        raw = jnp.dot(d, y_ref[...], preferred_element_type=jnp.float32)
        g_ref[at, :] = off_axis(raw, wwide) * w_inv

    @pl.when(step == pl.num_programs(0) - 1)
    def _():
        for copy in copies:
            copy.wait()


def weight_gradient(base, me, slots, emb, labels, stats, totals, weights, parts, starts, peers):
    batch, width = emb.shape
    classes = weights.shape[0]
    largest = max(rows.shape[0] for rows in parts)
    smem = pl.BlockSpec(memory_space=pltpu.SMEM)
    vmem = pl.BlockSpec(memory_space=pltpu.VMEM)
    tile = math.gcd(classes, 1024)
    whole = lambda i: (0, 0)
    return pl.pallas_call(
        functools.partial(
            weight_kernel, peers=peers, run=classes // peers, starts=tuple(starts)
        ),
        grid=(classes // tile,),
        in_specs=[
            smem,
            smem,
            smem,
            pl.BlockSpec((batch, width), whole),
            pl.BlockSpec((1, batch), whole),
            pl.BlockSpec((8, batch), whole),
            pl.BlockSpec((1, batch), whole),
            pl.BlockSpec((tile, width), lambda i: (i, 0)),
        ]
        + [vmem] * len(parts),
        out_specs=[
            pl.BlockSpec((tile, width), lambda i: (i, 0)),
            pl.BlockSpec(memory_space=pl.ANY),
        ],
        out_shape=[
            pltpu.HBM((classes, width), jnp.float32),
            pltpu.HBM((2 * classes, 128), jnp.float32),
        ],
        scratch_shapes=[
            pltpu.VMEM((batch, width), jnp.bfloat16),
            pltpu.VMEM((batch, width), jnp.bfloat16),
            pltpu.VMEM((1, batch), jnp.float32),
            pltpu.VMEM((2 * classes, 128), jnp.float32),
            pltpu.VMEM((2 * largest, 128), jnp.float32),
            pltpu.SemaphoreType.DMA((4,)),
        ],
        compiler_params=pltpu.CompilerParams(
            dimension_semantics=("arbitrary",), vmem_limit_bytes=40 * MIB
        ),
        cost_estimate=pl.CostEstimate(
            flops=12 * batch * classes * width, bytes_accessed=classes * width * 6, transcendentals=0
        ),
        name="weight_gradient",
    )(
        base, me, slots, emb, labels.reshape(1, batch), stats, totals.reshape(1, batch), weights,
        *parts,
    )


def fetch_kernel(rows_ref, *refs, first):
    out_ref, sem = refs[-2:]
    peers, size, _ = out_ref.shape
    lanes = sem.shape[0]
    part = peers // lanes
    copies = [
        pltpu.make_async_copy(
            rows_ref.at[pl.ds(c * part, part), pl.ds(first, size), :],
            out_ref.at[pl.ds(c * part, part)],
            sem.at[c],
        )
        for c in range(lanes)
    ]
    for copy in copies:
        copy.start()
    for copy in copies:
        copy.wait()


def fetch(runs, first, size, tokens):
    peers, _, width = runs.shape
    hbm = pl.BlockSpec(memory_space=pltpu.HBM)
    anywhere = pl.BlockSpec(memory_space=pl.ANY)
    return pl.pallas_call(
        functools.partial(fetch_kernel, first=first),
        in_specs=[hbm] + [anywhere] * len(tokens),
        out_specs=pl.BlockSpec(memory_space=pltpu.VMEM),
        out_shape=jax.ShapeDtypeStruct((peers, size, width), runs.dtype),
        scratch_shapes=[pltpu.SemaphoreType.DMA((math.gcd(peers, 8),))],
        compiler_params=pltpu.CompilerParams(vmem_limit_bytes=6 * MIB),
        cost_estimate=pl.CostEstimate(
            flops=0, bytes_accessed=8 * peers * size * width, transcendentals=0
        ),
        name="fetch",
    )(runs, *tokens)


def join_kernel(*refs, count):
    total = refs[0][...]
    for ref in refs[1:count]:
        total = total + ref[...]
    refs[-1][...] = total


def join(values, tokens):
    anywhere = pl.BlockSpec(memory_space=pl.ANY)
    vmem = pl.BlockSpec(memory_space=pltpu.VMEM)
    return pl.pallas_call(
        functools.partial(join_kernel, count=len(values)),
        in_specs=[vmem] * len(values) + [anywhere] * len(tokens),
        out_specs=vmem,
        out_shape=jax.ShapeDtypeStruct(values[0].shape, values[0].dtype),
        compiler_params=pltpu.CompilerParams(vmem_limit_bytes=6 * MIB),
        cost_estimate=COST,
        name="join",
    )(*values, *tokens)


def release_kernel(*refs):
    pass


def released(value, tokens):
    anywhere = pl.BlockSpec(memory_space=pl.ANY)
    return pl.pallas_call(
        release_kernel,
        in_specs=[anywhere] * (1 + len(tokens)),
        out_specs=anywhere,
        out_shape=jax.ShapeDtypeStruct(value.shape, value.dtype),
        input_output_aliases={0: 0},
        cost_estimate=COST,
        name="release",
    )(value, *tokens)


def blend_kernel(
    me_ref, slot_ref, w_ref, row_ref, in_ref, o_ref, held_ref, stage_ref, sem, *, peers, run, first
):
    step = pl.program_id(0)
    tile = o_ref.shape[0]

    @pl.when(step == 0)
    def _():
        copies = split_copies(in_ref, held_ref, sem)
        for copy in copies:
            copy.start()
        place_runs(me_ref, slot_ref, row_ref, held_ref, stage_ref, copies, peers, run, first)

    block = math.gcd(tile, 64)
    for begin in range(0, tile, block):
        rows = pl.ds(begin, block)
        at = pl.multiple_of((step * tile + begin) * 2, 2 * block)
        low = w_ref[rows, :128].astype(jnp.float32) + held_ref[pl.ds(at, block, stride=2), :]
        high = w_ref[rows, 128:].astype(jnp.float32) + held_ref[pl.ds(at + 1, block, stride=2), :]
        inv = lax.rsqrt(jnp.sum(low * low + high * high, axis=1, keepdims=True) + 1e-06)
        o_ref[rows, :128] = (low * inv).astype(jnp.bfloat16)
        o_ref[rows, 128:] = (high * inv).astype(jnp.bfloat16)


def place_and_blend(me, slots, rows, held, weights, peers, run, first):
    classes, width = weights.shape
    tile = math.gcd(classes, 1024)
    smem = pl.BlockSpec(memory_space=pltpu.SMEM)
    vmem = pl.BlockSpec(memory_space=pltpu.VMEM)
    tiles = pl.BlockSpec((tile, width), lambda i: (i, 0))
    return pl.pallas_call(
        functools.partial(blend_kernel, peers=peers, run=run, first=first),
        grid=(classes // tile,),
        in_specs=[smem, smem, tiles, vmem, pl.BlockSpec(memory_space=pl.ANY)],
        out_specs=tiles,
        out_shape=pltpu.HBM((classes, width), jnp.bfloat16),
        scratch_shapes=[
            pltpu.VMEM(held.shape, jnp.float32),
            pltpu.VMEM((2 * rows.shape[0], 128), jnp.float32),
            pltpu.SemaphoreType.DMA((4,)),
        ],
        compiler_params=pltpu.CompilerParams(
            dimension_semantics=("arbitrary",), vmem_limit_bytes=32 * MIB
        ),
        cost_estimate=pl.CostEstimate(
            flops=0, bytes_accessed=12 * classes * width, transcendentals=0
        ),
        name="place_and_blend",
    )(me, slots, weights, rows, held)


def shards(embeddings, labels, class_weights, centroids, centroid_class):
    rows_local, width = embeddings.shape
    classes = class_weights.shape[0]
    groups, reps = lax.axis_size("grp"), lax.axis_size("rep")
    peers = groups * reps
    batch = rows_local * reps
    run = classes // peers
    grp, rep = lax.axis_index("grp").astype(jnp.int32), lax.axis_index("rep").astype(jnp.int32)
    me = (rep * groups + grp).reshape(1)
    base = me * classes

    def swap(value, axis, k):
        size = lax.axis_size(axis)
        return lax.ppermute(value, axis, [(i, i ^ k) for i in range(size)]) if k else value

    def relay(sent):
        return lax.all_to_all(sent, ALL, 0, 0, tiled=True).reshape(-1, width)

    weights = in_hbm(class_weights)
    runs = in_hbm(centroids.reshape(peers, run, width))
    cut_a = max(16, run * 3 // 16 // 16 * 16)
    cut = run - max(16, run * 5 // 16 // 16 * 16)
    rows_a = relay(fetch(runs, 0, cut_a, []))
    mixed = jnp.concatenate([swap(embeddings, "rep", c) for c in range(2)])
    mixed = jnp.concatenate([swap(mixed, "rep", 2 * z) for z in range(reps // 2)])
    rows_b = relay(released(fetch(runs, cut_a, cut - cut_a, []), [mixed, rows_a]))
    emb, a, b, stats, what = forward(base, rep.reshape(1), mixed, reps, labels, weights)

    half = reps // 2
    core, deep = rep % 2, rep // 2
    index = lax.dynamic_index_in_dim

    def share_out(sums, wanted, axis, flips):
        got = []
        for flip, asked in zip(flips, wanted):
            sent = jnp.concatenate([sums, asked.reshape(-1)]).reshape(-1, 128)
            got.append(swap(sent, axis, flip).reshape(-1))
        got = jnp.stack(got)
        return jnp.sum(got[:, : 2 * batch], axis=0), got[:, 2 * batch :]

    wanted = centroid_class.reshape(half, 2, groups, run).astype(jnp.float32)
    wanted = [index(wanted, grp ^ j, 2, False) for j in range(groups)]
    sums, wanted = share_out(stats[:2].reshape(-1), wanted, "grp", range(groups))
    wanted = wanted.reshape(groups, half, 2, run)
    wanted = [index(wanted, core ^ c, 2, False) for c in range(2)]
    sums, wanted = share_out(sums, wanted, "rep", range(2))
    sent = fetch(runs, cut, run - cut, [stats])
    sums = join([sums.reshape(-1, 128)], [sent]).reshape(-1)
    wanted = wanted.reshape(2, groups, half, run)
    wanted = [index(wanted, deep ^ z, 2, False) for z in range(half)]
    sums, slots = share_out(sums, wanted, "rep", range(0, reps, 2))
    slots = slots.reshape(-1).astype(jnp.int32) * 2
    total, target = sums[:batch], sums[batch:]
    losses = jnp.log(total) - target
    loss = lax.dynamic_slice_in_dim(losses, rep * rows_local, rows_local, 0)

    rows_c = relay(released(sent, [total]))
    weight_grad, held = weight_gradient(
        base, me, slots, emb, labels, stats, total, weights, [rows_a, rows_b], [0, cut_a], peers
    )

    grad = (a / total[:, None] - b).reshape(half, 2, rows_local, width)
    grad = sum(swap(index(grad, core ^ c, 1, False), "rep", c) for c in range(2))
    grad = join([swap(grad, "grp", j) for j in range(groups)], [in_hbm(weight_grad), loss])
    embedding_gradient = sum(
        swap(index(grad, deep ^ z, 0, False), "rep", 2 * z) for z in range(half)
    )

    refreshed = place_and_blend(me, slots, rows_c, in_hbm(held), in_hbm(what), peers, run, cut)
    return (loss, embedding_gradient, weight_grad, refreshed)


def solution(mesh):
    in_specs = (
        P("rep", None),
        P(),
        P(("rep", "grp"), None),
        P(("grp", "rep"), None),
        P(("grp", "rep")),
    )
    out_specs = (P("rep"), P("rep", None), P(("rep", "grp"), None), P(("rep", "grp"), None))
    return jax.shard_map(shards, mesh=mesh, in_specs=in_specs, out_specs=out_specs, check_vma=False)
```

```python
import functools
import math

import jax
import jax.numpy as jnp
from jax import lax
from jax.experimental import pallas as pl
from jax.experimental.pallas import tpu as pltpu
from jax.sharding import PartitionSpec as P

SCALE = 32.0
MARGIN = 0.2
SIN_FLOOR = 0.09
LOG2E = math.log2(math.e)
ALL = ("rep", "grp")
MIB = 1024 * 1024
COST = pl.CostEstimate(flops=1, bytes_accessed=1, transcendentals=0)

NT = (((1,), (1,)), ((), ()))


def in_hbm(value):
    return pltpu.with_memory_space_constraint(value, pltpu.HBM)


def unit_rows(wide):
    inv = lax.rsqrt(jnp.sum(wide * wide, axis=1, keepdims=True) + 1e-06)
    return wide * inv, inv


def off_axis(values, unit):
    return values - unit * jnp.sum(unit * values, axis=1, keepdims=True)


def column_of(row):
    lanes = row.shape[1]
    return jnp.transpose(jnp.broadcast_to(row, (128, lanes)))[:, :1]


def forward_kernel(
    base_ref, rep_ref, lab_ref, w_ref, mixed_ref, emb_ref, a_ref, b_ref, st_ref, what_ref, xhat_ref,
    sum_ref,
    *, classes, reps,
):
    step = pl.program_id(0)
    tile = w_ref.shape[0]
    batch = emb_ref.shape[0]

    @pl.when(step == 0)
    def _():
        rows = batch // reps
        for k in range(reps):
            flip = k // (reps // 2) + k % (reps // 2) * 2
            first = pl.multiple_of((rep_ref[0] ^ flip) * rows, rows)
            emb_ref[pl.ds(first, rows), :] = mixed_ref[k * rows : (k + 1) * rows, :]
        xwide, _ = unit_rows(emb_ref[...].astype(jnp.float32))
        xhat_ref[...] = xwide.astype(jnp.bfloat16)
        sum_ref[...] = jnp.zeros_like(sum_ref)
        a_ref[...] = jnp.zeros_like(a_ref)
        b_ref[...] = jnp.zeros_like(b_ref)

    wwide, _ = unit_rows(w_ref[...].astype(jnp.float32))
    what = wwide.astype(jnp.bfloat16)
    what_ref[...] = what
    cosine = lax.dot_general(xhat_ref[...], what, NT, preferred_element_type=jnp.float32)
    ids = lax.broadcasted_iota(jnp.int32, (batch, tile), 1)
    is_label = ids == lab_ref[...] - (base_ref[0] + step * tile)
    e = jnp.where(is_label, 0.0, jnp.exp2(cosine * (SCALE * LOG2E)))
    partial = e[:, :128]
    for c in range(1, tile // 128):
        partial = partial + e[:, c * 128 : (c + 1) * 128]
    sum_ref[...] += partial
    onehot = jnp.where(is_label, 1.0, 0.0).astype(jnp.bfloat16)
    a_ref[...] += jnp.dot(e.astype(jnp.bfloat16), what, preferred_element_type=jnp.float32)
    b_ref[...] += jnp.dot(onehot, what, preferred_element_type=jnp.float32)

    @pl.when(step == pl.num_programs(0) - 1)
    def _():
        xwide, x_inv = unit_rows(emb_ref[...].astype(jnp.float32))
        label_row = b_ref[...]
        c = jnp.sum(xhat_ref[...].astype(jnp.float32) * label_row, axis=1, keepdims=True)
        offset = lab_ref[...] - base_ref[0]
        has = jnp.where((offset >= 0) & (offset < classes), 1.0, 0.0)
        q = 1.0 - c * c
        sine = jnp.sqrt(jnp.maximum(q, SIN_FLOOR))
        margined = c * math.cos(MARGIN) - sine * math.sin(MARGIN)
        slope = math.cos(MARGIN) + jnp.where(q > SIN_FLOOR, c * math.sin(MARGIN) / sine, 0.0)
        slope = slope * has
        label_e = jnp.exp(SCALE * margined) * has
        total = jnp.sum(sum_ref[...], axis=1, keepdims=True) + label_e
        target = SCALE * margined * has
        b = slope * label_row
        a = a_ref[...] + label_e * b
        gain = SCALE * x_inv
        a_ref[...] = off_axis(a, xwide) * gain
        b_ref[...] = off_axis(b, xwide) * gain
        lane = lax.broadcasted_iota(jnp.int32, (batch, 128), 1)
        stats = jnp.where(lane == 0, total, 0.0)
        stats = jnp.where(lane == 1, target, stats)
        stats = jnp.where(lane == 2, label_e * slope, stats)
        stats = jnp.where(lane == 3, slope, stats)
        st_ref[...] = jnp.transpose(stats)[:8, :]


def forward(base, rep, mixed, reps, labels, weights):
    batch, width = mixed.shape
    classes = weights.shape[0]
    tile = math.gcd(classes, 1024)
    whole = lambda i: (0, 0)
    smem = pl.BlockSpec(memory_space=pltpu.SMEM)
    return pl.pallas_call(
        functools.partial(forward_kernel, classes=classes, reps=reps),
        grid=(classes // tile,),
        in_specs=[
            smem,
            smem,
            pl.BlockSpec((batch, 1), whole),
            pl.BlockSpec((tile, width), lambda i: (i, 0)),
            pl.BlockSpec((batch, width), whole),
        ],
        out_specs=[
            pl.BlockSpec((batch, width), whole),
            pl.BlockSpec((batch, width), whole),
            pl.BlockSpec((batch, width), whole),
            pl.BlockSpec((8, batch), whole),
            pl.BlockSpec((tile, width), lambda i: (i, 0)),
        ],
        out_shape=[
            jax.ShapeDtypeStruct((batch, width), jnp.bfloat16),
            jax.ShapeDtypeStruct((batch, width), jnp.float32),
            jax.ShapeDtypeStruct((batch, width), jnp.float32),
            jax.ShapeDtypeStruct((8, batch), jnp.float32),
            pltpu.HBM((classes, width), jnp.bfloat16),
        ],
        scratch_shapes=[pltpu.VMEM((batch, width), jnp.bfloat16), pltpu.VMEM((batch, 128), jnp.float32)],
        compiler_params=pltpu.CompilerParams(
            dimension_semantics=("arbitrary",), vmem_limit_bytes=20 * MIB
        ),
        cost_estimate=pl.CostEstimate(
            flops=12 * batch * classes * width, bytes_accessed=classes * width * 2, transcendentals=0
        ),
        name="forward_sums",
    )(base, rep, labels.reshape(batch, 1), weights, mixed)


def weight_kernel(base_ref, emb_ref, lab_ref, st_ref, tot_ref, w_ref, g_ref, xhat_ref, y_ref, v_ref):
    step = pl.program_id(0)
    tile = w_ref.shape[0]
    batch = emb_ref.shape[0]

    @pl.when(step == 0)
    def _():
        xwide, _ = unit_rows(emb_ref[...].astype(jnp.float32))
        xhat = xwide.astype(jnp.bfloat16)
        xhat_ref[...] = xhat
        total = tot_ref[...]
        y_ref[...] = (xhat.astype(jnp.float32) * column_of(SCALE / total)).astype(jnp.bfloat16)
        v_ref[...] = st_ref[2:3, :] - st_ref[3:4, :] * total

    block = math.gcd(tile, 256)
    for first in range(0, tile, block):
        at = pl.ds(first, block)
        wwide, w_inv = unit_rows(w_ref[at, :].astype(jnp.float32))
        what = wwide.astype(jnp.bfloat16)
        cosine = lax.dot_general(what, xhat_ref[...], NT, preferred_element_type=jnp.float32)
        ids = lax.broadcasted_iota(jnp.int32, (block, batch), 0)
        is_label = ids == lab_ref[...] - (base_ref[0] + step * tile + first)
        e = jnp.exp2(cosine * (SCALE * LOG2E))
        d = jnp.where(is_label, v_ref[...], e).astype(jnp.bfloat16)
        raw = jnp.dot(d, y_ref[...], preferred_element_type=jnp.float32)
        g_ref[at, :] = off_axis(raw, wwide) * w_inv


def weight_gradient(base, emb, labels, stats, totals, weights):
    batch, width = emb.shape
    classes = weights.shape[0]
    tile = math.gcd(classes, 512)
    whole = lambda i: (0, 0)
    return pl.pallas_call(
        weight_kernel,
        grid=(classes // tile,),
        in_specs=[
            pl.BlockSpec(memory_space=pltpu.SMEM),
            pl.BlockSpec((batch, width), whole),
            pl.BlockSpec((1, batch), whole),
            pl.BlockSpec((8, batch), whole),
            pl.BlockSpec((1, batch), whole),
            pl.BlockSpec((tile, width), lambda i: (i, 0)),
        ],
        out_specs=pl.BlockSpec((tile, width), lambda i: (i, 0)),
        out_shape=pltpu.HBM((classes, width), jnp.float32),
        scratch_shapes=[
            pltpu.VMEM((batch, width), jnp.bfloat16),
            pltpu.VMEM((batch, width), jnp.bfloat16),
            pltpu.VMEM((1, batch), jnp.float32),
        ],
        compiler_params=pltpu.CompilerParams(
            dimension_semantics=("arbitrary",), vmem_limit_bytes=20 * MIB
        ),
        cost_estimate=pl.CostEstimate(
            flops=12 * batch * classes * width, bytes_accessed=classes * width * 6, transcendentals=0
        ),
        name="weight_gradient",
    )(base, emb, labels.reshape(1, batch), stats, totals.reshape(1, batch), weights)


def fetch_kernel(rows_ref, *refs, first):
    out_ref, sem = refs[-2:]
    peers, size, _ = out_ref.shape
    lanes = sem.shape[0]
    part = peers // lanes
    copies = [
        pltpu.make_async_copy(
            rows_ref.at[pl.ds(c * part, part), pl.ds(first, size), :],
            out_ref.at[pl.ds(c * part, part)],
            sem.at[c],
        )
        for c in range(lanes)
    ]
    for copy in copies:
        copy.start()
    for copy in copies:
        copy.wait()


def fetch(runs, first, size, tokens):
    peers, _, width = runs.shape
    hbm = pl.BlockSpec(memory_space=pltpu.HBM)
    anywhere = pl.BlockSpec(memory_space=pl.ANY)
    return pl.pallas_call(
        functools.partial(fetch_kernel, first=first),
        in_specs=[hbm] + [anywhere] * len(tokens),
        out_specs=pl.BlockSpec(memory_space=pltpu.VMEM),
        out_shape=jax.ShapeDtypeStruct((peers, size, width), runs.dtype),
        scratch_shapes=[pltpu.SemaphoreType.DMA((math.gcd(peers, 8),))],
        compiler_params=pltpu.CompilerParams(vmem_limit_bytes=6 * MIB),
        cost_estimate=pl.CostEstimate(
            flops=0, bytes_accessed=8 * peers * size * width, transcendentals=0
        ),
        name="fetch",
    )(runs, *tokens)


def join_kernel(*refs, count):
    total = refs[0][...]
    for ref in refs[1:count]:
        total = total + ref[...]
    refs[-1][...] = total


def join(values, tokens):
    anywhere = pl.BlockSpec(memory_space=pl.ANY)
    vmem = pl.BlockSpec(memory_space=pltpu.VMEM)
    return pl.pallas_call(
        functools.partial(join_kernel, count=len(values)),
        in_specs=[vmem] * len(values) + [anywhere] * len(tokens),
        out_specs=vmem,
        out_shape=jax.ShapeDtypeStruct(values[0].shape, values[0].dtype),
        compiler_params=pltpu.CompilerParams(vmem_limit_bytes=6 * MIB),
        cost_estimate=COST,
        name="join",
    )(*values, *tokens)


def release_kernel(*refs):
    pass


def released(value, tokens):
    anywhere = pl.BlockSpec(memory_space=pl.ANY)
    return pl.pallas_call(
        release_kernel,
        in_specs=[anywhere] * (1 + len(tokens)),
        out_specs=anywhere,
        out_shape=jax.ShapeDtypeStruct(value.shape, value.dtype),
        input_output_aliases={0: 0},
        cost_estimate=COST,
        name="release",
    )(value, *tokens)


def place_runs(me_ref, slot_ref, row_ref, held_ref, stage_ref, copies, peers, run, first):
    size = row_ref.shape[0] // peers
    batch = max(n for n in range(1, 49) if size % n == 0)
    chunk = max(n for n in range(16, 49, 16) if size % n == 0)

    def prepare(source, carry):
        for block in range(0, size, chunk):
            at = pl.multiple_of(source * size + block, chunk)
            unit, _ = unit_rows(row_ref[pl.ds(at, chunk), :].astype(jnp.float32))
            stage_ref[pl.ds(2 * at, chunk, stride=2), :] = unit[:, :128]
            stage_ref[pl.ds(2 * at + 1, chunk, stride=2), :] = unit[:, 128:]
        return carry

    lax.fori_loop(0, peers, prepare, 0)
    for copy in copies:
        copy.wait()

    def place(source, carry):
        start = (me_ref[0] ^ source) * run + first
        at = source * size * 2
        for block in range(0, size, batch):
            slots = [slot_ref[start + block + v] for v in range(batch)]
            values = [stage_ref[pl.ds(at + 2 * (block + v), 2), :] for v in range(batch)]
            for slot, value in zip(slots, values):
                held_ref[pl.ds(slot, 2), :] = value
        return carry

    lax.fori_loop(0, peers, place, 0)


def place_kernel(
    me_ref, slot_ref, row_ref, _, held_ref, token_ref, stage_ref, *, peers, run, first
):
    token_ref[...] = jnp.zeros_like(token_ref)
    place_runs(me_ref, slot_ref, row_ref, held_ref, stage_ref, [], peers, run, first)


def place_rows(me, slots, rows, after, peers, run, first):
    smem = pl.BlockSpec(memory_space=pltpu.SMEM)
    vmem = pl.BlockSpec(memory_space=pltpu.VMEM)
    anywhere = pl.BlockSpec(memory_space=pl.ANY)
    return pl.pallas_call(
        functools.partial(place_kernel, peers=peers, run=run, first=first),
        in_specs=[smem, smem, vmem, anywhere],
        out_specs=[vmem, vmem],
        out_shape=[
            jax.ShapeDtypeStruct((2 * peers * run, 128), jnp.float32),
            jax.ShapeDtypeStruct((8, 128), jnp.float32),
        ],
        scratch_shapes=[pltpu.VMEM((2 * rows.shape[0], 128), jnp.float32)],
        compiler_params=pltpu.CompilerParams(vmem_limit_bytes=24 * MIB),
        cost_estimate=pl.CostEstimate(
            flops=0, bytes_accessed=32 * rows.shape[0] * rows.shape[1], transcendentals=0
        ),
        name="place_rows",
    )(me, slots, rows, after)


def blend_kernel(
    me_ref, slot_ref, w_ref, row_ref, in_ref, o_ref, held_ref, stage_ref, sem, *, peers, run, first
):
    step = pl.program_id(0)
    tile = o_ref.shape[0]

    @pl.when(step == 0)
    def _():
        lanes = sem.shape[0]
        part = held_ref.shape[0] // lanes
        parts = [pl.ds(c * part, part) for c in range(lanes)]
        copies = [
            pltpu.make_async_copy(in_ref.at[at, :], held_ref.at[at, :], sem.at[c])
            for c, at in enumerate(parts)
        ]
        for copy in copies:
            copy.start()
        place_runs(me_ref, slot_ref, row_ref, held_ref, stage_ref, copies, peers, run, first)

    block = math.gcd(tile, 64)
    for begin in range(0, tile, block):
        rows = pl.ds(begin, block)
        at = pl.multiple_of((step * tile + begin) * 2, 2 * block)
        low = w_ref[rows, :128].astype(jnp.float32) + held_ref[pl.ds(at, block, stride=2), :]
        high = w_ref[rows, 128:].astype(jnp.float32) + held_ref[pl.ds(at + 1, block, stride=2), :]
        inv = lax.rsqrt(jnp.sum(low * low + high * high, axis=1, keepdims=True) + 1e-06)
        o_ref[rows, :128] = (low * inv).astype(jnp.bfloat16)
        o_ref[rows, 128:] = (high * inv).astype(jnp.bfloat16)


def place_and_blend(me, slots, rows, held, weights, peers, run, first):
    classes, width = weights.shape
    tile = math.gcd(classes, 1024)
    smem = pl.BlockSpec(memory_space=pltpu.SMEM)
    vmem = pl.BlockSpec(memory_space=pltpu.VMEM)
    tiles = pl.BlockSpec((tile, width), lambda i: (i, 0))
    return pl.pallas_call(
        functools.partial(blend_kernel, peers=peers, run=run, first=first),
        grid=(classes // tile,),
        in_specs=[smem, smem, tiles, vmem, pl.BlockSpec(memory_space=pl.ANY)],
        out_specs=tiles,
        out_shape=pltpu.HBM((classes, width), jnp.bfloat16),
        scratch_shapes=[
            pltpu.VMEM(held.shape, jnp.float32),
            pltpu.VMEM((2 * rows.shape[0], 128), jnp.float32),
            pltpu.SemaphoreType.DMA((4,)),
        ],
        compiler_params=pltpu.CompilerParams(
            dimension_semantics=("arbitrary",), vmem_limit_bytes=32 * MIB
        ),
        cost_estimate=pl.CostEstimate(
            flops=0, bytes_accessed=12 * classes * width, transcendentals=0
        ),
        name="place_and_blend",
    )(me, slots, weights, rows, held)


def shards(embeddings, labels, class_weights, centroids, centroid_class):
    rows_local, width = embeddings.shape
    classes = class_weights.shape[0]
    groups, reps = lax.axis_size("grp"), lax.axis_size("rep")
    peers = groups * reps
    batch = rows_local * reps
    run = classes // peers
    grp, rep = lax.axis_index("grp").astype(jnp.int32), lax.axis_index("rep").astype(jnp.int32)
    me = (rep * groups + grp).reshape(1)
    base = me * classes

    def swap(value, axis, k):
        size = lax.axis_size(axis)
        return lax.ppermute(value, axis, [(i, i ^ k) for i in range(size)]) if k else value

    def relay(sent):
        return lax.all_to_all(sent, ALL, 0, 0, tiled=True).reshape(-1, width)

    weights = in_hbm(class_weights)
    runs = in_hbm(centroids.reshape(peers, run, width))
    cut = run * 5 // 8 // 16 * 16
    mixed = jnp.concatenate([swap(embeddings, "rep", 2 * z) for z in range(reps // 2)])
    rows_a = relay(released(fetch(runs, 0, cut, []), [mixed]))
    mixed = jnp.concatenate([swap(mixed, "rep", c) for c in range(2)])
    emb, a, b, stats, what = forward(base, rep.reshape(1), mixed, reps, labels, weights)

    half = reps // 2
    core, deep = rep % 2, rep // 2
    index = lax.dynamic_index_in_dim

    def share_out(sums, wanted, axis, flips):
        got = []
        for flip, asked in zip(flips, wanted):
            sent = jnp.concatenate([sums, asked.reshape(-1)]).reshape(-1, 128)
            got.append(swap(sent, axis, flip).reshape(-1))
        got = jnp.stack(got)
        return jnp.sum(got[:, : 2 * batch], axis=0), got[:, 2 * batch :]

    wanted = centroid_class.reshape(half, 2, groups, run).astype(jnp.float32)
    wanted = [index(wanted, grp ^ j, 2, False) for j in range(groups)]
    sums, wanted = share_out(stats[:2].reshape(-1), wanted, "grp", range(groups))
    wanted = wanted.reshape(groups, half, 2, run)
    wanted = [index(wanted, core ^ c, 2, False) for c in range(2)]
    sums, wanted = share_out(sums, wanted, "rep", range(2))
    sent_b = fetch(runs, cut, run - cut, [stats])
    sums = join([sums.reshape(-1, 128)], [sent_b]).reshape(-1)
    wanted = wanted.reshape(2, groups, half, run)
    wanted = [index(wanted, deep ^ z, 2, False) for z in range(half)]
    sums, slots = share_out(sums, wanted, "rep", range(0, reps, 2))
    slots = slots.reshape(-1).astype(jnp.int32) * 2
    total, target = sums[:batch], sums[batch:]
    losses = jnp.log(total) - target
    loss = lax.dynamic_slice_in_dim(losses, rep * rows_local, rows_local, 0)

    rows_b = relay(released(sent_b, [total]))
    weight_grad = weight_gradient(base, emb, labels, stats, total, weights)
    done = in_hbm(weight_grad)
    held, token = place_rows(me, slots, rows_a, done, peers, run, 0)

    grad = (a / total[:, None] - b).reshape(half, 2, rows_local, width)
    grad = sum(swap(index(grad, core ^ c, 1, False), "rep", c) for c in range(2))
    grad = join([swap(grad, "grp", j) for j in range(groups)], [token, loss])
    embedding_gradient = sum(
        swap(index(grad, deep ^ z, 0, False), "rep", 2 * z) for z in range(half)
    )

    refreshed = place_and_blend(me, slots, rows_b, in_hbm(held), in_hbm(what), peers, run, cut)
    return (loss, embedding_gradient, weight_grad, refreshed)


def solution(mesh):
    in_specs = (
        P("rep", None),
        P(),
        P(("rep", "grp"), None),
        P(("grp", "rep"), None),
        P(("grp", "rep")),
    )
    out_specs = (P("rep"), P("rep", None), P(("rep", "grp"), None), P(("rep", "grp"), None))
    return jax.shard_map(shards, mesh=mesh, in_specs=in_specs, out_specs=out_specs, check_vma=False)
```

```python
import functools
import math

import jax
import jax.numpy as jnp
from jax import lax
from jax.experimental import pallas as pl
from jax.experimental.pallas import tpu as pltpu
from jax.sharding import PartitionSpec as P

SCALE = 32.0
MARGIN = 0.2
SIN_FLOOR = 0.09
LOG2E = math.log2(math.e)
ALL = ("rep", "grp")
MIB = 1024 * 1024
COST = pl.CostEstimate(flops=1, bytes_accessed=1, transcendentals=0)

NT = (((1,), (1,)), ((), ()))


def in_hbm(value):
    return pltpu.with_memory_space_constraint(value, pltpu.HBM)


def unit_rows(wide):
    inv = lax.rsqrt(jnp.sum(wide * wide, axis=1, keepdims=True) + 1e-06)
    return wide * inv, inv


def off_axis(values, unit):
    return values - unit * jnp.sum(unit * values, axis=1, keepdims=True)


def column_of(row):
    lanes = row.shape[1]
    return jnp.transpose(jnp.broadcast_to(row, (128, lanes)))[:, :1]


def forward_kernel(
    base_ref, rep_ref, lab_ref, w_ref, mixed_ref, emb_ref, a_ref, b_ref, st_ref, what_ref, xhat_ref,
    sum_ref,
    *, classes, reps,
):
    step = pl.program_id(0)
    tile = w_ref.shape[0]
    batch = emb_ref.shape[0]

    @pl.when(step == 0)
    def _():
        rows = batch // reps
        for k in range(reps):
            flip = k // (reps // 2) + k % (reps // 2) * 2
            first = pl.multiple_of((rep_ref[0] ^ flip) * rows, rows)
            emb_ref[pl.ds(first, rows), :] = mixed_ref[k * rows : (k + 1) * rows, :]
        xwide, _ = unit_rows(emb_ref[...].astype(jnp.float32))
        xhat_ref[...] = xwide.astype(jnp.bfloat16)
        sum_ref[...] = jnp.zeros_like(sum_ref)
        a_ref[...] = jnp.zeros_like(a_ref)
        b_ref[...] = jnp.zeros_like(b_ref)

    wwide, _ = unit_rows(w_ref[...].astype(jnp.float32))
    what = wwide.astype(jnp.bfloat16)
    what_ref[...] = what
    cosine = lax.dot_general(xhat_ref[...], what, NT, preferred_element_type=jnp.float32)
    ids = lax.broadcasted_iota(jnp.int32, (batch, tile), 1)
    is_label = ids == lab_ref[...] - (base_ref[0] + step * tile)
    e = jnp.where(is_label, 0.0, jnp.exp2(cosine * (SCALE * LOG2E)))
    partial = e[:, :128]
    for c in range(1, tile // 128):
        partial = partial + e[:, c * 128 : (c + 1) * 128]
    sum_ref[...] += partial
    onehot = jnp.where(is_label, 1.0, 0.0).astype(jnp.bfloat16)
    a_ref[...] += jnp.dot(e.astype(jnp.bfloat16), what, preferred_element_type=jnp.float32)
    b_ref[...] += jnp.dot(onehot, what, preferred_element_type=jnp.float32)

    @pl.when(step == pl.num_programs(0) - 1)
    def _():
        xwide, x_inv = unit_rows(emb_ref[...].astype(jnp.float32))
        label_row = b_ref[...]
        c = jnp.sum(xhat_ref[...].astype(jnp.float32) * label_row, axis=1, keepdims=True)
        offset = lab_ref[...] - base_ref[0]
        has = jnp.where((offset >= 0) & (offset < classes), 1.0, 0.0)
        q = 1.0 - c * c
        sine = jnp.sqrt(jnp.maximum(q, SIN_FLOOR))
        margined = c * math.cos(MARGIN) - sine * math.sin(MARGIN)
        slope = math.cos(MARGIN) + jnp.where(q > SIN_FLOOR, c * math.sin(MARGIN) / sine, 0.0)
        slope = slope * has
        label_e = jnp.exp(SCALE * margined) * has
        total = jnp.sum(sum_ref[...], axis=1, keepdims=True) + label_e
        target = SCALE * margined * has
        b = slope * label_row
        a = a_ref[...] + label_e * b
        gain = SCALE * x_inv
        a_ref[...] = off_axis(a, xwide) * gain
        b_ref[...] = off_axis(b, xwide) * gain
        lane = lax.broadcasted_iota(jnp.int32, (batch, 128), 1)
        stats = jnp.where(lane == 0, total, 0.0)
        stats = jnp.where(lane == 1, target, stats)
        stats = jnp.where(lane == 2, label_e * slope, stats)
        stats = jnp.where(lane == 3, slope, stats)
        st_ref[...] = jnp.transpose(stats)[:8, :]


def forward(base, rep, mixed, reps, labels, weights):
    batch, width = mixed.shape
    classes = weights.shape[0]
    tile = math.gcd(classes, 1024)
    whole = lambda i: (0, 0)
    smem = pl.BlockSpec(memory_space=pltpu.SMEM)
    return pl.pallas_call(
        functools.partial(forward_kernel, classes=classes, reps=reps),
        grid=(classes // tile,),
        in_specs=[
            smem,
            smem,
            pl.BlockSpec((batch, 1), whole),
            pl.BlockSpec((tile, width), lambda i: (i, 0)),
            pl.BlockSpec((batch, width), whole),
        ],
        out_specs=[
            pl.BlockSpec((batch, width), whole),
            pl.BlockSpec((batch, width), whole),
            pl.BlockSpec((batch, width), whole),
            pl.BlockSpec((8, batch), whole),
            pl.BlockSpec((tile, width), lambda i: (i, 0)),
        ],
        out_shape=[
            jax.ShapeDtypeStruct((batch, width), jnp.bfloat16),
            jax.ShapeDtypeStruct((batch, width), jnp.float32),
            jax.ShapeDtypeStruct((batch, width), jnp.float32),
            jax.ShapeDtypeStruct((8, batch), jnp.float32),
            pltpu.HBM((classes, width), jnp.bfloat16),
        ],
        scratch_shapes=[pltpu.VMEM((batch, width), jnp.bfloat16), pltpu.VMEM((batch, 128), jnp.float32)],
        compiler_params=pltpu.CompilerParams(
            dimension_semantics=("arbitrary",), vmem_limit_bytes=20 * MIB
        ),
        cost_estimate=pl.CostEstimate(
            flops=12 * batch * classes * width, bytes_accessed=classes * width * 2, transcendentals=0
        ),
        name="forward_sums",
    )(base, rep, labels.reshape(batch, 1), weights, mixed)


def weight_kernel(base_ref, emb_ref, lab_ref, st_ref, tot_ref, w_ref, g_ref, xhat_ref, y_ref, v_ref):
    step = pl.program_id(0)
    tile = w_ref.shape[0]
    batch = emb_ref.shape[0]

    @pl.when(step == 0)
    def _():
        xwide, _ = unit_rows(emb_ref[...].astype(jnp.float32))
        xhat = xwide.astype(jnp.bfloat16)
        xhat_ref[...] = xhat
        total = tot_ref[...]
        y_ref[...] = (xhat.astype(jnp.float32) * column_of(SCALE / total)).astype(jnp.bfloat16)
        v_ref[...] = st_ref[2:3, :] - st_ref[3:4, :] * total

    block = math.gcd(tile, 256)
    for first in range(0, tile, block):
        at = pl.ds(first, block)
        wwide, w_inv = unit_rows(w_ref[at, :].astype(jnp.float32))
        what = wwide.astype(jnp.bfloat16)
        cosine = lax.dot_general(what, xhat_ref[...], NT, preferred_element_type=jnp.float32)
        ids = lax.broadcasted_iota(jnp.int32, (block, batch), 0)
        is_label = ids == lab_ref[...] - (base_ref[0] + step * tile + first)
        e = jnp.exp2(cosine * (SCALE * LOG2E))
        d = jnp.where(is_label, v_ref[...], e).astype(jnp.bfloat16)
        raw = jnp.dot(d, y_ref[...], preferred_element_type=jnp.float32)
        g_ref[at, :] = off_axis(raw, wwide) * w_inv


def weight_gradient(base, emb, labels, stats, totals, weights):
    batch, width = emb.shape
    classes = weights.shape[0]
    tile = math.gcd(classes, 2048)
    whole = lambda i: (0, 0)
    return pl.pallas_call(
        weight_kernel,
        grid=(classes // tile,),
        in_specs=[
            pl.BlockSpec(memory_space=pltpu.SMEM),
            pl.BlockSpec((batch, width), whole),
            pl.BlockSpec((1, batch), whole),
            pl.BlockSpec((8, batch), whole),
            pl.BlockSpec((1, batch), whole),
            pl.BlockSpec((tile, width), lambda i: (i, 0)),
        ],
        out_specs=pl.BlockSpec((tile, width), lambda i: (i, 0)),
        out_shape=pltpu.HBM((classes, width), jnp.float32),
        scratch_shapes=[
            pltpu.VMEM((batch, width), jnp.bfloat16),
            pltpu.VMEM((batch, width), jnp.bfloat16),
            pltpu.VMEM((1, batch), jnp.float32),
        ],
        compiler_params=pltpu.CompilerParams(
            dimension_semantics=("arbitrary",), vmem_limit_bytes=20 * MIB
        ),
        cost_estimate=pl.CostEstimate(
            flops=12 * batch * classes * width, bytes_accessed=classes * width * 6, transcendentals=0
        ),
        name="weight_gradient",
    )(base, emb, labels.reshape(1, batch), stats, totals.reshape(1, batch), weights)


def fetch_kernel(rows_ref, *refs, first):
    out_ref, held_ref, sem = refs[-3:]
    peers, size, _ = out_ref.shape
    lanes = sem.shape[1]
    parts = [pl.ds(c * (peers // lanes), peers // lanes) for c in range(lanes)]
    loads = [
        pltpu.make_async_copy(rows_ref.at[part, pl.ds(first, size), :], held_ref.at[part], sem.at[0, c])
        for c, part in enumerate(parts)
    ]
    stores = [
        pltpu.make_async_copy(held_ref.at[part], out_ref.at[part], sem.at[1, c])
        for c, part in enumerate(parts)
    ]
    for load in loads:
        load.start()
    for load, store in zip(loads, stores):
        load.wait()
        store.start()
    for store in stores:
        store.wait()


def fetch(runs, first, size, tokens):
    peers, _, width = runs.shape
    hbm = pl.BlockSpec(memory_space=pltpu.HBM)
    anywhere = pl.BlockSpec(memory_space=pl.ANY)
    return pl.pallas_call(
        functools.partial(fetch_kernel, first=first),
        in_specs=[hbm] + [anywhere] * len(tokens),
        out_specs=anywhere,
        out_shape=pltpu.HBM((peers, size, width), runs.dtype),
        scratch_shapes=[
            pltpu.VMEM((peers, size, width), runs.dtype),
            pltpu.SemaphoreType.DMA((2, math.gcd(peers, 8))),
        ],
        compiler_params=pltpu.CompilerParams(vmem_limit_bytes=6 * MIB),
        cost_estimate=pl.CostEstimate(
            flops=0, bytes_accessed=8 * peers * size * width, transcendentals=0
        ),
        name="fetch",
    )(runs, *tokens)


def join_kernel(*refs, count):
    total = refs[0][...]
    for ref in refs[1:count]:
        total = total + ref[...]
    refs[-1][...] = total


def join(values, tokens):
    anywhere = pl.BlockSpec(memory_space=pl.ANY)
    vmem = pl.BlockSpec(memory_space=pltpu.VMEM)
    return pl.pallas_call(
        functools.partial(join_kernel, count=len(values)),
        in_specs=[vmem] * len(values) + [anywhere] * len(tokens),
        out_specs=vmem,
        out_shape=jax.ShapeDtypeStruct(values[0].shape, values[0].dtype),
        compiler_params=pltpu.CompilerParams(vmem_limit_bytes=6 * MIB),
        cost_estimate=COST,
        name="join",
    )(*values, *tokens)


def release_kernel(*refs):
    pass


def released(value, tokens):
    anywhere = pl.BlockSpec(memory_space=pl.ANY)
    return pl.pallas_call(
        release_kernel,
        in_specs=[anywhere] * (1 + len(tokens)),
        out_specs=anywhere,
        out_shape=pltpu.HBM(value.shape, value.dtype),
        input_output_aliases={0: 0},
        cost_estimate=COST,
        name="release",
    )(value, *tokens)


def place_runs(me_ref, slot_ref, row_ref, held_ref, stage_ref, copies, peers, run, first):
    size = row_ref.shape[0] // peers
    batch = max(n for n in range(1, 49) if size % n == 0)
    chunk = max(n for n in range(16, 49, 16) if size % n == 0)

    def prepare(source, carry):
        for block in range(0, size, chunk):
            at = pl.multiple_of(source * size + block, chunk)
            unit, _ = unit_rows(row_ref[pl.ds(at, chunk), :].astype(jnp.float32))
            stage_ref[pl.ds(2 * at, chunk, stride=2), :] = unit[:, :128]
            stage_ref[pl.ds(2 * at + 1, chunk, stride=2), :] = unit[:, 128:]
        return carry

    lax.fori_loop(0, peers, prepare, 0)
    for copy in copies:
        copy.wait()

    def place(source, carry):
        start = (me_ref[0] ^ source) * run + first
        at = source * size * 2
        for block in range(0, size, batch):
            slots = [slot_ref[start + block + v] for v in range(batch)]
            values = [stage_ref[pl.ds(at + 2 * (block + v), 2), :] for v in range(batch)]
            for slot, value in zip(slots, values):
                held_ref[pl.ds(slot, 2), :] = value
        return carry

    lax.fori_loop(0, peers, place, 0)


def place_kernel(
    me_ref, slot_ref, row_ref, _, held_ref, token_ref, stage_ref, *, peers, run, first
):
    token_ref[...] = jnp.zeros_like(token_ref)
    place_runs(me_ref, slot_ref, row_ref, held_ref, stage_ref, [], peers, run, first)


def place_rows(me, slots, rows, after, peers, run, first):
    smem = pl.BlockSpec(memory_space=pltpu.SMEM)
    vmem = pl.BlockSpec(memory_space=pltpu.VMEM)
    anywhere = pl.BlockSpec(memory_space=pl.ANY)
    return pl.pallas_call(
        functools.partial(place_kernel, peers=peers, run=run, first=first),
        in_specs=[smem, smem, vmem, anywhere],
        out_specs=[vmem, vmem],
        out_shape=[
            jax.ShapeDtypeStruct((2 * peers * run, 128), jnp.float32),
            jax.ShapeDtypeStruct((8, 128), jnp.float32),
        ],
        scratch_shapes=[pltpu.VMEM((2 * rows.shape[0], 128), jnp.float32)],
        compiler_params=pltpu.CompilerParams(vmem_limit_bytes=24 * MIB),
        cost_estimate=pl.CostEstimate(
            flops=0, bytes_accessed=32 * rows.shape[0] * rows.shape[1], transcendentals=0
        ),
        name="place_rows",
    )(me, slots, rows, after)


def blend_kernel(
    me_ref, slot_ref, w_ref, row_ref, in_ref, o_ref, held_ref, stage_ref, sem, *, peers, run, first
):
    step = pl.program_id(0)
    tile = o_ref.shape[0]

    @pl.when(step == 0)
    def _():
        lanes = sem.shape[0]
        part = held_ref.shape[0] // lanes
        parts = [pl.ds(c * part, part) for c in range(lanes)]
        copies = [
            pltpu.make_async_copy(in_ref.at[at, :], held_ref.at[at, :], sem.at[c])
            for c, at in enumerate(parts)
        ]
        for copy in copies:
            copy.start()
        place_runs(me_ref, slot_ref, row_ref, held_ref, stage_ref, copies, peers, run, first)

    block = math.gcd(tile, 64)
    for begin in range(0, tile, block):
        rows = pl.ds(begin, block)
        at = pl.multiple_of((step * tile + begin) * 2, 2 * block)
        low = w_ref[rows, :128].astype(jnp.float32) + held_ref[pl.ds(at, block, stride=2), :]
        high = w_ref[rows, 128:].astype(jnp.float32) + held_ref[pl.ds(at + 1, block, stride=2), :]
        inv = lax.rsqrt(jnp.sum(low * low + high * high, axis=1, keepdims=True) + 1e-06)
        o_ref[rows, :128] = (low * inv).astype(jnp.bfloat16)
        o_ref[rows, 128:] = (high * inv).astype(jnp.bfloat16)


def place_and_blend(me, slots, rows, held, weights, peers, run, first):
    classes, width = weights.shape
    tile = math.gcd(classes, 2048)
    smem = pl.BlockSpec(memory_space=pltpu.SMEM)
    vmem = pl.BlockSpec(memory_space=pltpu.VMEM)
    tiles = pl.BlockSpec((tile, width), lambda i: (i, 0))
    return pl.pallas_call(
        functools.partial(blend_kernel, peers=peers, run=run, first=first),
        grid=(classes // tile,),
        in_specs=[smem, smem, tiles, vmem, pl.BlockSpec(memory_space=pl.ANY)],
        out_specs=tiles,
        out_shape=pltpu.HBM((classes, width), jnp.bfloat16),
        scratch_shapes=[
            pltpu.VMEM(held.shape, jnp.float32),
            pltpu.VMEM((2 * rows.shape[0], 128), jnp.float32),
            pltpu.SemaphoreType.DMA((4,)),
        ],
        compiler_params=pltpu.CompilerParams(
            dimension_semantics=("arbitrary",), vmem_limit_bytes=32 * MIB
        ),
        cost_estimate=pl.CostEstimate(
            flops=0, bytes_accessed=12 * classes * width, transcendentals=0
        ),
        name="place_and_blend",
    )(me, slots, weights, rows, held)


def shards(embeddings, labels, class_weights, centroids, centroid_class):
    rows_local, width = embeddings.shape
    classes = class_weights.shape[0]
    groups, reps = lax.axis_size("grp"), lax.axis_size("rep")
    peers = groups * reps
    batch = rows_local * reps
    run = classes // peers
    grp, rep = lax.axis_index("grp").astype(jnp.int32), lax.axis_index("rep").astype(jnp.int32)
    me = (rep * groups + grp).reshape(1)
    base = me * classes

    def swap(value, axis, k):
        size = lax.axis_size(axis)
        return lax.ppermute(value, axis, [(i, i ^ k) for i in range(size)]) if k else value

    def relay(sent):
        return lax.all_to_all(sent, ALL, 0, 0, tiled=True).reshape(-1, width)

    weights = in_hbm(class_weights)
    runs = in_hbm(centroids.reshape(peers, run, width))
    cut = run * 5 // 8 // 16 * 16
    mixed = jnp.concatenate([swap(embeddings, "rep", 2 * z) for z in range(reps // 2)])
    rows_a = relay(released(in_hbm(fetch(runs, 0, cut, [])), [mixed]))
    mixed = jnp.concatenate([swap(mixed, "rep", c) for c in range(2)])
    emb, a, b, stats, what = forward(base, rep.reshape(1), mixed, reps, labels, weights)

    half = reps // 2
    core, deep = rep % 2, rep // 2
    index = lax.dynamic_index_in_dim

    def share_out(sums, wanted, axis, flips):
        got = []
        for flip, asked in zip(flips, wanted):
            sent = jnp.concatenate([sums, asked.reshape(-1)]).reshape(-1, 128)
            got.append(swap(sent, axis, flip).reshape(-1))
        got = jnp.stack(got)
        return jnp.sum(got[:, : 2 * batch], axis=0), got[:, 2 * batch :]

    wanted = centroid_class.reshape(half, 2, groups, run).astype(jnp.float32)
    wanted = [index(wanted, grp ^ j, 2, False) for j in range(groups)]
    sums, wanted = share_out(stats[:2].reshape(-1), wanted, "grp", range(groups))
    wanted = wanted.reshape(groups, half, 2, run)
    wanted = [index(wanted, core ^ c, 2, False) for c in range(2)]
    sums, wanted = share_out(sums, wanted, "rep", range(2))
    sent_b = in_hbm(fetch(runs, cut, run - cut, [stats]))
    sums = join([sums.reshape(-1, 128)], [sent_b]).reshape(-1)
    wanted = wanted.reshape(2, groups, half, run)
    wanted = [index(wanted, deep ^ z, 2, False) for z in range(half)]
    sums, slots = share_out(sums, wanted, "rep", range(0, reps, 2))
    slots = slots.reshape(-1).astype(jnp.int32) * 2
    total, target = sums[:batch], sums[batch:]
    losses = jnp.log(total) - target
    loss = lax.dynamic_slice_in_dim(losses, rep * rows_local, rows_local, 0)

    rows_b = relay(released(sent_b, [total]))
    weight_grad = weight_gradient(base, emb, labels, stats, total, weights)
    done = in_hbm(weight_grad)
    held, token = place_rows(me, slots, rows_a, done, peers, run, 0)

    grad = (a / total[:, None] - b).reshape(half, 2, rows_local, width)
    grad = sum(swap(index(grad, core ^ c, 1, False), "rep", c) for c in range(2))
    grad = join([swap(grad, "grp", j) for j in range(groups)], [token, loss])
    embedding_gradient = sum(
        swap(index(grad, deep ^ z, 0, False), "rep", 2 * z) for z in range(half)
    )

    refreshed = place_and_blend(me, slots, rows_b, in_hbm(held), in_hbm(what), peers, run, cut)
    return (loss, embedding_gradient, weight_grad, refreshed)


def solution(mesh):
    in_specs = (
        P("rep", None),
        P(),
        P(("rep", "grp"), None),
        P(("grp", "rep"), None),
        P(("grp", "rep")),
    )
    out_specs = (P("rep"), P("rep", None), P(("rep", "grp"), None), P(("rep", "grp"), None))
    return jax.shard_map(shards, mesh=mesh, in_specs=in_specs, out_specs=out_specs, check_vma=False)
```

```python
import functools
import math

import jax
import jax.numpy as jnp
from jax import lax
from jax.experimental import pallas as pl
from jax.experimental.pallas import tpu as pltpu
from jax.sharding import PartitionSpec as P

SCALE = 32.0
MARGIN = 0.2
SIN_FLOOR = 0.09
LOG2E = math.log2(math.e)
ALL = ("rep", "grp")
MIB = 1024 * 1024
COST = pl.CostEstimate(flops=1, bytes_accessed=1, transcendentals=0)

NT = (((1,), (1,)), ((), ()))


def in_hbm(value):
    return pltpu.with_memory_space_constraint(value, pltpu.HBM)


def unit_rows(wide):
    inv = lax.rsqrt(jnp.sum(wide * wide, axis=1, keepdims=True) + 1e-06)
    return wide * inv, inv


def off_axis(values, unit):
    return values - unit * jnp.sum(unit * values, axis=1, keepdims=True)


def column_of(row):
    lanes = row.shape[1]
    return jnp.transpose(jnp.broadcast_to(row, (128, lanes)))[:, :1]


def forward_kernel(
    base_ref, rep_ref, lab_ref, w_ref, mixed_ref, emb_ref, a_ref, b_ref, st_ref, what_ref, xhat_ref,
    sum_ref,
    *, classes, reps,
):
    step = pl.program_id(0)
    tile = w_ref.shape[0]
    batch = emb_ref.shape[0]

    @pl.when(step == 0)
    def _():
        rows = batch // reps
        for k in range(reps):
            flip = k // (reps // 2) + k % (reps // 2) * 2
            first = pl.multiple_of((rep_ref[0] ^ flip) * rows, rows)
            emb_ref[pl.ds(first, rows), :] = mixed_ref[k * rows : (k + 1) * rows, :]
        xwide, _ = unit_rows(emb_ref[...].astype(jnp.float32))
        xhat_ref[...] = xwide.astype(jnp.bfloat16)
        sum_ref[...] = jnp.zeros_like(sum_ref)
        a_ref[...] = jnp.zeros_like(a_ref)
        b_ref[...] = jnp.zeros_like(b_ref)

    wwide, _ = unit_rows(w_ref[...].astype(jnp.float32))
    what = wwide.astype(jnp.bfloat16)
    what_ref[...] = what
    cosine = lax.dot_general(xhat_ref[...], what, NT, preferred_element_type=jnp.float32)
    ids = lax.broadcasted_iota(jnp.int32, (batch, tile), 1)
    is_label = ids == lab_ref[...] - (base_ref[0] + step * tile)
    e = jnp.where(is_label, 0.0, jnp.exp2(cosine * (SCALE * LOG2E)))
    partial = e[:, :128]
    for c in range(1, tile // 128):
        partial = partial + e[:, c * 128 : (c + 1) * 128]
    sum_ref[...] += partial
    onehot = jnp.where(is_label, 1.0, 0.0).astype(jnp.bfloat16)
    a_ref[...] += jnp.dot(e.astype(jnp.bfloat16), what, preferred_element_type=jnp.float32)
    b_ref[...] += jnp.dot(onehot, what, preferred_element_type=jnp.float32)

    @pl.when(step == pl.num_programs(0) - 1)
    def _():
        xwide, x_inv = unit_rows(emb_ref[...].astype(jnp.float32))
        label_row = b_ref[...]
        c = jnp.sum(xhat_ref[...].astype(jnp.float32) * label_row, axis=1, keepdims=True)
        offset = lab_ref[...] - base_ref[0]
        has = jnp.where((offset >= 0) & (offset < classes), 1.0, 0.0)
        q = 1.0 - c * c
        sine = jnp.sqrt(jnp.maximum(q, SIN_FLOOR))
        margined = c * math.cos(MARGIN) - sine * math.sin(MARGIN)
        slope = math.cos(MARGIN) + jnp.where(q > SIN_FLOOR, c * math.sin(MARGIN) / sine, 0.0)
        slope = slope * has
        label_e = jnp.exp(SCALE * margined) * has
        total = jnp.sum(sum_ref[...], axis=1, keepdims=True) + label_e
        target = SCALE * margined * has
        b = slope * label_row
        a = a_ref[...] + label_e * b
        gain = SCALE * x_inv
        a_ref[...] = off_axis(a, xwide) * gain
        b_ref[...] = off_axis(b, xwide) * gain
        lane = lax.broadcasted_iota(jnp.int32, (batch, 128), 1)
        stats = jnp.where(lane == 0, total, 0.0)
        stats = jnp.where(lane == 1, target, stats)
        stats = jnp.where(lane == 2, label_e * slope, stats)
        stats = jnp.where(lane == 3, slope, stats)
        st_ref[...] = jnp.transpose(stats)[:8, :]


def forward(base, rep, mixed, reps, labels, weights):
    batch, width = mixed.shape
    classes = weights.shape[0]
    tile = math.gcd(classes, 1024)
    whole = lambda i: (0, 0)
    smem = pl.BlockSpec(memory_space=pltpu.SMEM)
    return pl.pallas_call(
        functools.partial(forward_kernel, classes=classes, reps=reps),
        grid=(classes // tile,),
        in_specs=[
            smem,
            smem,
            pl.BlockSpec((batch, 1), whole),
            pl.BlockSpec((tile, width), lambda i: (i, 0)),
            pl.BlockSpec((batch, width), whole),
        ],
        out_specs=[
            pl.BlockSpec((batch, width), whole),
            pl.BlockSpec((batch, width), whole),
            pl.BlockSpec((batch, width), whole),
            pl.BlockSpec((8, batch), whole),
            pl.BlockSpec((tile, width), lambda i: (i, 0)),
        ],
        out_shape=[
            jax.ShapeDtypeStruct((batch, width), jnp.bfloat16),
            jax.ShapeDtypeStruct((batch, width), jnp.float32),
            jax.ShapeDtypeStruct((batch, width), jnp.float32),
            jax.ShapeDtypeStruct((8, batch), jnp.float32),
            pltpu.HBM((classes, width), jnp.bfloat16),
        ],
        scratch_shapes=[pltpu.VMEM((batch, width), jnp.bfloat16), pltpu.VMEM((batch, 128), jnp.float32)],
        compiler_params=pltpu.CompilerParams(
            dimension_semantics=("arbitrary",), vmem_limit_bytes=20 * MIB
        ),
        cost_estimate=pl.CostEstimate(
            flops=12 * batch * classes * width, bytes_accessed=classes * width * 2, transcendentals=0
        ),
        name="forward_sums",
    )(base, rep, labels.reshape(batch, 1), weights, mixed)


def weight_kernel(base_ref, emb_ref, lab_ref, st_ref, tot_ref, w_ref, g_ref, xhat_ref, y_ref, v_ref):
    step = pl.program_id(0)
    tile = w_ref.shape[0]
    batch = emb_ref.shape[0]

    @pl.when(step == 0)
    def _():
        xwide, _ = unit_rows(emb_ref[...].astype(jnp.float32))
        xhat = xwide.astype(jnp.bfloat16)
        xhat_ref[...] = xhat
        total = tot_ref[...]
        y_ref[...] = (xhat.astype(jnp.float32) * column_of(SCALE / total)).astype(jnp.bfloat16)
        v_ref[...] = st_ref[2:3, :] - st_ref[3:4, :] * total

    block = math.gcd(tile, 256)
    for first in range(0, tile, block):
        at = pl.ds(first, block)
        wwide, w_inv = unit_rows(w_ref[at, :].astype(jnp.float32))
        what = wwide.astype(jnp.bfloat16)
        cosine = lax.dot_general(what, xhat_ref[...], NT, preferred_element_type=jnp.float32)
        ids = lax.broadcasted_iota(jnp.int32, (block, batch), 0)
        is_label = ids == lab_ref[...] - (base_ref[0] + step * tile + first)
        e = jnp.exp2(cosine * (SCALE * LOG2E))
        d = jnp.where(is_label, v_ref[...], e).astype(jnp.bfloat16)
        raw = jnp.dot(d, y_ref[...], preferred_element_type=jnp.float32)
        g_ref[at, :] = off_axis(raw, wwide) * w_inv


def weight_gradient(base, emb, labels, stats, totals, weights):
    batch, width = emb.shape
    classes = weights.shape[0]
    tile = math.gcd(classes, 2048)
    whole = lambda i: (0, 0)
    return pl.pallas_call(
        weight_kernel,
        grid=(classes // tile,),
        in_specs=[
            pl.BlockSpec(memory_space=pltpu.SMEM),
            pl.BlockSpec((batch, width), whole),
            pl.BlockSpec((1, batch), whole),
            pl.BlockSpec((8, batch), whole),
            pl.BlockSpec((1, batch), whole),
            pl.BlockSpec((tile, width), lambda i: (i, 0)),
        ],
        out_specs=pl.BlockSpec((tile, width), lambda i: (i, 0)),
        out_shape=pltpu.HBM((classes, width), jnp.float32),
        scratch_shapes=[
            pltpu.VMEM((batch, width), jnp.bfloat16),
            pltpu.VMEM((batch, width), jnp.bfloat16),
            pltpu.VMEM((1, batch), jnp.float32),
        ],
        compiler_params=pltpu.CompilerParams(
            dimension_semantics=("arbitrary",), vmem_limit_bytes=20 * MIB
        ),
        cost_estimate=pl.CostEstimate(
            flops=12 * batch * classes * width, bytes_accessed=classes * width * 6, transcendentals=0
        ),
        name="weight_gradient",
    )(base, emb, labels.reshape(1, batch), stats, totals.reshape(1, batch), weights)


def fetch_kernel(rows_ref, *refs, first):
    out_ref, held_ref, sem = refs[-3:]
    peers, size, _ = out_ref.shape
    lanes = sem.shape[1]
    parts = [pl.ds(c * (peers // lanes), peers // lanes) for c in range(lanes)]
    loads = [
        pltpu.make_async_copy(rows_ref.at[part, pl.ds(first, size), :], held_ref.at[part], sem.at[0, c])
        for c, part in enumerate(parts)
    ]
    stores = [
        pltpu.make_async_copy(held_ref.at[part], out_ref.at[part], sem.at[1, c])
        for c, part in enumerate(parts)
    ]
    for load in loads:
        load.start()
    for load, store in zip(loads, stores):
        load.wait()
        store.start()
    for store in stores:
        store.wait()


def fetch(runs, first, size, tokens):
    peers, _, width = runs.shape
    hbm = pl.BlockSpec(memory_space=pltpu.HBM)
    anywhere = pl.BlockSpec(memory_space=pl.ANY)
    return pl.pallas_call(
        functools.partial(fetch_kernel, first=first),
        in_specs=[hbm] + [anywhere] * len(tokens),
        out_specs=anywhere,
        out_shape=pltpu.HBM((peers, size, width), runs.dtype),
        scratch_shapes=[
            pltpu.VMEM((peers, size, width), runs.dtype),
            pltpu.SemaphoreType.DMA((2, math.gcd(peers, 8))),
        ],
        compiler_params=pltpu.CompilerParams(vmem_limit_bytes=6 * MIB),
        cost_estimate=pl.CostEstimate(
            flops=0, bytes_accessed=8 * peers * size * width, transcendentals=0
        ),
        name="fetch",
    )(runs, *tokens)


def join_kernel(*refs, count):
    total = refs[0][...]
    for ref in refs[1:count]:
        total = total + ref[...]
    refs[-1][...] = total


def join(values, tokens):
    anywhere = pl.BlockSpec(memory_space=pl.ANY)
    vmem = pl.BlockSpec(memory_space=pltpu.VMEM)
    return pl.pallas_call(
        functools.partial(join_kernel, count=len(values)),
        in_specs=[vmem] * len(values) + [anywhere] * len(tokens),
        out_specs=vmem,
        out_shape=jax.ShapeDtypeStruct(values[0].shape, values[0].dtype),
        compiler_params=pltpu.CompilerParams(vmem_limit_bytes=6 * MIB),
        cost_estimate=COST,
        name="join",
    )(*values, *tokens)


def release_kernel(*refs):
    pass


def released(value, tokens):
    anywhere = pl.BlockSpec(memory_space=pl.ANY)
    return pl.pallas_call(
        release_kernel,
        in_specs=[anywhere] * (1 + len(tokens)),
        out_specs=anywhere,
        out_shape=pltpu.HBM(value.shape, value.dtype),
        input_output_aliases={0: 0},
        cost_estimate=COST,
        name="release",
    )(value, *tokens)


def place_runs(me_ref, slot_ref, row_ref, held_ref, stage_ref, copies, peers, run, first):
    size = row_ref.shape[0] // peers
    batch = max(n for n in range(1, 49) if size % n == 0)
    chunk = max(n for n in range(16, 49, 16) if size % n == 0)

    def prepare(source, carry):
        for block in range(0, size, chunk):
            at = pl.multiple_of(source * size + block, chunk)
            unit, _ = unit_rows(row_ref[pl.ds(at, chunk), :].astype(jnp.float32))
            stage_ref[pl.ds(2 * at, chunk, stride=2), :] = unit[:, :128]
            stage_ref[pl.ds(2 * at + 1, chunk, stride=2), :] = unit[:, 128:]
        return carry

    lax.fori_loop(0, peers, prepare, 0)
    for copy in copies:
        copy.wait()

    def place(source, carry):
        start = (me_ref[0] ^ source) * run + first
        at = source * size * 2
        for block in range(0, size, batch):
            slots = [slot_ref[start + block + v] for v in range(batch)]
            values = [stage_ref[pl.ds(at + 2 * (block + v), 2), :] for v in range(batch)]
            for slot, value in zip(slots, values):
                held_ref[pl.ds(slot, 2), :] = value
        return carry

    lax.fori_loop(0, peers, place, 0)


def place_kernel(
    me_ref, slot_ref, row_ref, _, held_ref, token_ref, stage_ref, *, peers, run, first
):
    token_ref[...] = jnp.zeros_like(token_ref)
    place_runs(me_ref, slot_ref, row_ref, held_ref, stage_ref, [], peers, run, first)


def place_rows(me, slots, rows, after, peers, run, first):
    smem = pl.BlockSpec(memory_space=pltpu.SMEM)
    vmem = pl.BlockSpec(memory_space=pltpu.VMEM)
    anywhere = pl.BlockSpec(memory_space=pl.ANY)
    return pl.pallas_call(
        functools.partial(place_kernel, peers=peers, run=run, first=first),
        in_specs=[smem, smem, vmem, anywhere],
        out_specs=[vmem, vmem],
        out_shape=[
            jax.ShapeDtypeStruct((2 * peers * run, 128), jnp.float32),
            jax.ShapeDtypeStruct((8, 128), jnp.float32),
        ],
        scratch_shapes=[pltpu.VMEM((2 * rows.shape[0], 128), jnp.float32)],
        compiler_params=pltpu.CompilerParams(vmem_limit_bytes=24 * MIB),
        cost_estimate=pl.CostEstimate(
            flops=0, bytes_accessed=32 * rows.shape[0] * rows.shape[1], transcendentals=0
        ),
        name="place_rows",
    )(me, slots, rows, after)


def split_copies(source_ref, target_ref, sem):
    lanes = sem.shape[0]
    size = source_ref.shape[0] // lanes
    parts = [pl.ds(c * size, size) for c in range(lanes)]
    return [
        pltpu.make_async_copy(source_ref.at[part, :], target_ref.at[part, :], sem.at[c])
        for c, part in enumerate(parts)
    ]


def blend_kernel(
    me_ref, slot_ref, row_ref, w_ref, in_ref, o_ref, held_ref, stage_ref, what_ref, new_ref,
    held_sem, what_sem, new_sem, *, peers, run, first,
):
    copies = split_copies(in_ref, held_ref, held_sem)
    weights = split_copies(w_ref, what_ref, what_sem)
    for copy in copies + weights:
        copy.start()
    place_runs(me_ref, slot_ref, row_ref, held_ref, stage_ref, copies, peers, run, first)
    for copy in weights:
        copy.wait()
    classes = o_ref.shape[0]
    pieces = new_sem.shape[0]
    piece = classes // pieces
    block = math.gcd(piece, 64)

    def leaving(c):
        part = pl.ds(pl.multiple_of(c * piece, piece), piece)
        return pltpu.make_async_copy(new_ref.at[part, :], o_ref.at[part, :], new_sem.at[c])

    def blend(c, carry):
        for begin in range(0, piece, block):
            start = pl.multiple_of(c * piece + begin, block)
            rows = pl.ds(start, block)
            low = held_ref[pl.ds(start * 2, block, stride=2), :]
            high = held_ref[pl.ds(start * 2 + 1, block, stride=2), :]
            low = low + what_ref[rows, :128].astype(jnp.float32)
            high = high + what_ref[rows, 128:].astype(jnp.float32)
            inv = lax.rsqrt(jnp.sum(low * low + high * high, axis=1, keepdims=True) + 1e-06)
            new_ref[rows, :128] = (low * inv).astype(jnp.bfloat16)
            new_ref[rows, 128:] = (high * inv).astype(jnp.bfloat16)
        leaving(c).start()
        return carry

    lax.fori_loop(0, pieces, blend, 0)
    for c in range(pieces):
        leaving(c).wait()


def place_and_blend(me, slots, rows, held, weights, peers, run, first):
    classes, width = weights.shape
    smem = pl.BlockSpec(memory_space=pltpu.SMEM)
    vmem = pl.BlockSpec(memory_space=pltpu.VMEM)
    anywhere = pl.BlockSpec(memory_space=pl.ANY)
    return pl.pallas_call(
        functools.partial(blend_kernel, peers=peers, run=run, first=first),
        in_specs=[smem, smem, vmem, anywhere, anywhere],
        out_specs=anywhere,
        out_shape=pltpu.HBM((classes, width), jnp.bfloat16),
        scratch_shapes=[
            pltpu.VMEM(held.shape, jnp.float32),
            pltpu.VMEM((2 * rows.shape[0], 128), jnp.float32),
            pltpu.VMEM((classes, width), jnp.bfloat16),
            pltpu.VMEM((classes, width), jnp.bfloat16),
            pltpu.SemaphoreType.DMA((4,)),
            pltpu.SemaphoreType.DMA((2,)),
            pltpu.SemaphoreType.DMA((8,)),
        ],
        compiler_params=pltpu.CompilerParams(vmem_limit_bytes=32 * MIB),
        cost_estimate=pl.CostEstimate(
            flops=0, bytes_accessed=12 * classes * width, transcendentals=0
        ),
        name="place_and_blend",
    )(me, slots, rows, weights, held)


def shards(embeddings, labels, class_weights, centroids, centroid_class):
    rows_local, width = embeddings.shape
    classes = class_weights.shape[0]
    groups, reps = lax.axis_size("grp"), lax.axis_size("rep")
    peers = groups * reps
    batch = rows_local * reps
    run = classes // peers
    grp, rep = lax.axis_index("grp").astype(jnp.int32), lax.axis_index("rep").astype(jnp.int32)
    me = (rep * groups + grp).reshape(1)
    base = me * classes

    def swap(value, axis, k):
        size = lax.axis_size(axis)
        return lax.ppermute(value, axis, [(i, i ^ k) for i in range(size)]) if k else value

    def relay(sent):
        return lax.all_to_all(sent, ALL, 0, 0, tiled=True).reshape(-1, width)

    weights = in_hbm(class_weights)
    runs = in_hbm(centroids.reshape(peers, run, width))
    cut = run * 5 // 8 // 16 * 16
    mixed = jnp.concatenate([swap(embeddings, "rep", 2 * z) for z in range(reps // 2)])
    rows_a = relay(released(in_hbm(fetch(runs, 0, cut, [])), [mixed]))
    mixed = jnp.concatenate([swap(mixed, "rep", c) for c in range(2)])
    emb, a, b, stats, what = forward(base, rep.reshape(1), mixed, reps, labels, weights)

    half = reps // 2
    core, deep = rep % 2, rep // 2
    index = lax.dynamic_index_in_dim

    def share_out(sums, wanted, axis, flips):
        got = []
        for flip, asked in zip(flips, wanted):
            sent = jnp.concatenate([sums, asked.reshape(-1)]).reshape(-1, 128)
            got.append(swap(sent, axis, flip).reshape(-1))
        got = jnp.stack(got)
        return jnp.sum(got[:, : 2 * batch], axis=0), got[:, 2 * batch :]

    wanted = centroid_class.reshape(half, 2, groups, run).astype(jnp.float32)
    wanted = [index(wanted, grp ^ j, 2, False) for j in range(groups)]
    sums, wanted = share_out(stats[:2].reshape(-1), wanted, "grp", range(groups))
    wanted = wanted.reshape(groups, half, 2, run)
    wanted = [index(wanted, core ^ c, 2, False) for c in range(2)]
    sums, wanted = share_out(sums, wanted, "rep", range(2))
    sent_b = in_hbm(fetch(runs, cut, run - cut, [stats]))
    sums = join([sums.reshape(-1, 128)], [sent_b]).reshape(-1)
    wanted = wanted.reshape(2, groups, half, run)
    wanted = [index(wanted, deep ^ z, 2, False) for z in range(half)]
    sums, slots = share_out(sums, wanted, "rep", range(0, reps, 2))
    slots = slots.reshape(-1).astype(jnp.int32) * 2
    total, target = sums[:batch], sums[batch:]
    losses = jnp.log(total) - target
    loss = lax.dynamic_slice_in_dim(losses, rep * rows_local, rows_local, 0)

    rows_b = relay(released(sent_b, [total]))
    weight_grad = weight_gradient(base, emb, labels, stats, total, weights)
    done = in_hbm(weight_grad)
    held, token = place_rows(me, slots, rows_a, done, peers, run, 0)

    grad = (a / total[:, None] - b).reshape(half, 2, rows_local, width)
    grad = sum(swap(index(grad, core ^ c, 1, False), "rep", c) for c in range(2))
    grad = join([swap(grad, "grp", j) for j in range(groups)], [token, loss])
    sent = grad.astype(jnp.bfloat16)
    parts = [swap(index(sent, deep ^ z, 0, False), "rep", 2 * z) for z in range(1, half)]
    embedding_gradient = index(grad, deep, 0, False)
    for part in parts:
        embedding_gradient = embedding_gradient + part.astype(jnp.float32)

    refreshed = place_and_blend(me, slots, rows_b, in_hbm(held), in_hbm(what), peers, run, cut)
    return (loss, embedding_gradient, weight_grad, refreshed)


def solution(mesh):
    in_specs = (
        P("rep", None),
        P(),
        P(("rep", "grp"), None),
        P(("grp", "rep"), None),
        P(("grp", "rep")),
    )
    out_specs = (P("rep"), P("rep", None), P(("rep", "grp"), None), P(("rep", "grp"), None))
    return jax.shard_map(shards, mesh=mesh, in_specs=in_specs, out_specs=out_specs, check_vma=False)
```

```python
import functools
import math

import jax
import jax.numpy as jnp
from jax import lax
from jax.experimental import pallas as pl
from jax.experimental.pallas import tpu as pltpu
from jax.sharding import PartitionSpec as P

SCALE = 32.0
MARGIN = 0.2
SIN_FLOOR = 0.09
LOG2E = math.log2(math.e)
ALL = ("rep", "grp")
MIB = 1024 * 1024
COST = pl.CostEstimate(flops=1, bytes_accessed=1, transcendentals=0)

NT = (((1,), (1,)), ((), ()))


def in_hbm(value):
    return pltpu.with_memory_space_constraint(value, pltpu.HBM)


def unit_rows(wide):
    inv = lax.rsqrt(jnp.sum(wide * wide, axis=1, keepdims=True) + 1e-06)
    return wide * inv, inv


def off_axis(values, unit):
    return values - unit * jnp.sum(unit * values, axis=1, keepdims=True)


def column_of(row):
    lanes = row.shape[1]
    return jnp.transpose(jnp.broadcast_to(row, (128, lanes)))[:, :1]


def forward_kernel(
    base_ref, rep_ref, lab_ref, w_ref, mixed_ref, emb_ref, a_ref, b_ref, st_ref, what_ref, xhat_ref,
    sum_ref,
    *, classes, reps,
):
    step = pl.program_id(0)
    tile = w_ref.shape[0]
    batch = emb_ref.shape[0]

    @pl.when(step == 0)
    def _():
        rows = batch // reps
        for k in range(reps):
            flip = k // (reps // 2) + k % (reps // 2) * 2
            first = pl.multiple_of((rep_ref[0] ^ flip) * rows, rows)
            emb_ref[pl.ds(first, rows), :] = mixed_ref[k * rows : (k + 1) * rows, :]
        xwide, _ = unit_rows(emb_ref[...].astype(jnp.float32))
        xhat_ref[...] = xwide.astype(jnp.bfloat16)
        sum_ref[...] = jnp.zeros_like(sum_ref)
        a_ref[...] = jnp.zeros_like(a_ref)
        b_ref[...] = jnp.zeros_like(b_ref)

    wwide, _ = unit_rows(w_ref[...].astype(jnp.float32))
    what = wwide.astype(jnp.bfloat16)
    what_ref[...] = what
    cosine = lax.dot_general(xhat_ref[...], what, NT, preferred_element_type=jnp.float32)
    ids = lax.broadcasted_iota(jnp.int32, (batch, tile), 1)
    is_label = ids == lab_ref[...] - (base_ref[0] + step * tile)
    e = jnp.where(is_label, 0.0, jnp.exp2(cosine * (SCALE * LOG2E)))
    partial = e[:, :128]
    for c in range(1, tile // 128):
        partial = partial + e[:, c * 128 : (c + 1) * 128]
    sum_ref[...] += partial
    onehot = jnp.where(is_label, 1.0, 0.0).astype(jnp.bfloat16)
    a_ref[...] += jnp.dot(e.astype(jnp.bfloat16), what, preferred_element_type=jnp.float32)
    b_ref[...] += jnp.dot(onehot, what, preferred_element_type=jnp.float32)

    @pl.when(step == pl.num_programs(0) - 1)
    def _():
        xwide, x_inv = unit_rows(emb_ref[...].astype(jnp.float32))
        label_row = b_ref[...]
        c = jnp.sum(xhat_ref[...].astype(jnp.float32) * label_row, axis=1, keepdims=True)
        offset = lab_ref[...] - base_ref[0]
        has = jnp.where((offset >= 0) & (offset < classes), 1.0, 0.0)
        q = 1.0 - c * c
        sine = jnp.sqrt(jnp.maximum(q, SIN_FLOOR))
        margined = c * math.cos(MARGIN) - sine * math.sin(MARGIN)
        slope = math.cos(MARGIN) + jnp.where(q > SIN_FLOOR, c * math.sin(MARGIN) / sine, 0.0)
        slope = slope * has
        label_e = jnp.exp(SCALE * margined) * has
        total = jnp.sum(sum_ref[...], axis=1, keepdims=True) + label_e
        target = SCALE * margined * has
        b = slope * label_row
        a = a_ref[...] + label_e * b
        gain = SCALE * x_inv
        a_ref[...] = off_axis(a, xwide) * gain
        b_ref[...] = off_axis(b, xwide) * gain
        lane = lax.broadcasted_iota(jnp.int32, (batch, 128), 1)
        stats = jnp.where(lane == 0, total, 0.0)
        stats = jnp.where(lane == 1, target, stats)
        stats = jnp.where(lane == 2, label_e * slope, stats)
        stats = jnp.where(lane == 3, slope, stats)
        st_ref[...] = jnp.transpose(stats)[:8, :]


def forward(base, rep, mixed, reps, labels, weights):
    batch, width = mixed.shape
    classes = weights.shape[0]
    tile = math.gcd(classes, 1024)
    whole = lambda i: (0, 0)
    smem = pl.BlockSpec(memory_space=pltpu.SMEM)
    return pl.pallas_call(
        functools.partial(forward_kernel, classes=classes, reps=reps),
        grid=(classes // tile,),
        in_specs=[
            smem,
            smem,
            pl.BlockSpec((batch, 1), whole),
            pl.BlockSpec((tile, width), lambda i: (i, 0)),
            pl.BlockSpec((batch, width), whole),
        ],
        out_specs=[
            pl.BlockSpec((batch, width), whole),
            pl.BlockSpec((batch, width), whole),
            pl.BlockSpec((batch, width), whole),
            pl.BlockSpec((8, batch), whole),
            pl.BlockSpec((tile, width), lambda i: (i, 0)),
        ],
        out_shape=[
            jax.ShapeDtypeStruct((batch, width), jnp.bfloat16),
            jax.ShapeDtypeStruct((batch, width), jnp.float32),
            jax.ShapeDtypeStruct((batch, width), jnp.float32),
            jax.ShapeDtypeStruct((8, batch), jnp.float32),
            pltpu.HBM((classes, width), jnp.bfloat16),
        ],
        scratch_shapes=[pltpu.VMEM((batch, width), jnp.bfloat16), pltpu.VMEM((batch, 128), jnp.float32)],
        compiler_params=pltpu.CompilerParams(
            dimension_semantics=("arbitrary",), vmem_limit_bytes=20 * MIB
        ),
        cost_estimate=pl.CostEstimate(
            flops=12 * batch * classes * width, bytes_accessed=classes * width * 2, transcendentals=0
        ),
        name="forward_sums",
    )(base, rep, labels.reshape(batch, 1), weights, mixed)


def weight_kernel(base_ref, emb_ref, lab_ref, st_ref, tot_ref, w_ref, _, g_ref, xhat_ref, y_ref, v_ref):
    step = pl.program_id(0)
    tile = w_ref.shape[0]
    batch = emb_ref.shape[0]

    @pl.when(step == 0)
    def _():
        xwide, _ = unit_rows(emb_ref[...].astype(jnp.float32))
        xhat = xwide.astype(jnp.bfloat16)
        xhat_ref[...] = xhat
        total = tot_ref[...]
        y_ref[...] = (xhat.astype(jnp.float32) * column_of(SCALE / total)).astype(jnp.bfloat16)
        v_ref[...] = st_ref[2:3, :] - st_ref[3:4, :] * total

    block = math.gcd(tile, 256)
    for first in range(0, tile, block):
        at = pl.ds(first, block)
        wwide, w_inv = unit_rows(w_ref[at, :].astype(jnp.float32))
        what = wwide.astype(jnp.bfloat16)
        cosine = lax.dot_general(what, xhat_ref[...], NT, preferred_element_type=jnp.float32)
        ids = lax.broadcasted_iota(jnp.int32, (block, batch), 0)
        is_label = ids == lab_ref[...] - (base_ref[0] + step * tile + first)
        e = jnp.exp2(cosine * (SCALE * LOG2E))
        d = jnp.where(is_label, v_ref[...], e).astype(jnp.bfloat16)
        raw = jnp.dot(d, y_ref[...], preferred_element_type=jnp.float32)
        g_ref[at, :] = off_axis(raw, wwide) * w_inv


def weight_gradient(base, emb, labels, stats, totals, weights, after):
    batch, width = emb.shape
    classes = weights.shape[0]
    tile = math.gcd(classes, 2048)
    whole = lambda i: (0, 0)
    return pl.pallas_call(
        weight_kernel,
        grid=(classes // tile,),
        in_specs=[
            pl.BlockSpec(memory_space=pltpu.SMEM),
            pl.BlockSpec((batch, width), whole),
            pl.BlockSpec((1, batch), whole),
            pl.BlockSpec((8, batch), whole),
            pl.BlockSpec((1, batch), whole),
            pl.BlockSpec((tile, width), lambda i: (i, 0)),
            pl.BlockSpec(memory_space=pl.ANY),
        ],
        out_specs=pl.BlockSpec((tile, width), lambda i: (i, 0)),
        out_shape=pltpu.HBM((classes, width), jnp.float32),
        scratch_shapes=[
            pltpu.VMEM((batch, width), jnp.bfloat16),
            pltpu.VMEM((batch, width), jnp.bfloat16),
            pltpu.VMEM((1, batch), jnp.float32),
        ],
        compiler_params=pltpu.CompilerParams(
            dimension_semantics=("arbitrary",), vmem_limit_bytes=20 * MIB
        ),
        cost_estimate=pl.CostEstimate(
            flops=12 * batch * classes * width, bytes_accessed=classes * width * 6, transcendentals=0
        ),
        name="weight_gradient",
    )(base, emb, labels.reshape(1, batch), stats, totals.reshape(1, batch), weights, after)


def fetch_kernel(rows_ref, *refs, first):
    out_ref, held_ref, sem = refs[-3:]
    peers, size, _ = out_ref.shape
    lanes = sem.shape[1]
    parts = [pl.ds(c * (peers // lanes), peers // lanes) for c in range(lanes)]
    loads = [
        pltpu.make_async_copy(rows_ref.at[part, pl.ds(first, size), :], held_ref.at[part], sem.at[0, c])
        for c, part in enumerate(parts)
    ]
    stores = [
        pltpu.make_async_copy(held_ref.at[part], out_ref.at[part], sem.at[1, c])
        for c, part in enumerate(parts)
    ]
    for load in loads:
        load.start()
    for load, store in zip(loads, stores):
        load.wait()
        store.start()
    for store in stores:
        store.wait()


def fetch(runs, first, size, tokens):
    peers, _, width = runs.shape
    hbm = pl.BlockSpec(memory_space=pltpu.HBM)
    anywhere = pl.BlockSpec(memory_space=pl.ANY)
    return pl.pallas_call(
        functools.partial(fetch_kernel, first=first),
        in_specs=[hbm] + [anywhere] * len(tokens),
        out_specs=anywhere,
        out_shape=pltpu.HBM((peers, size, width), runs.dtype),
        scratch_shapes=[
            pltpu.VMEM((peers, size, width), runs.dtype),
            pltpu.SemaphoreType.DMA((2, math.gcd(peers, 8))),
        ],
        compiler_params=pltpu.CompilerParams(vmem_limit_bytes=6 * MIB),
        cost_estimate=pl.CostEstimate(
            flops=0, bytes_accessed=8 * peers * size * width, transcendentals=0
        ),
        name="fetch",
    )(runs, *tokens)


def join_kernel(*refs, count):
    total = refs[0][...]
    for ref in refs[1:count]:
        total = total + ref[...]
    refs[-1][...] = total


def join(values, tokens):
    anywhere = pl.BlockSpec(memory_space=pl.ANY)
    vmem = pl.BlockSpec(memory_space=pltpu.VMEM)
    return pl.pallas_call(
        functools.partial(join_kernel, count=len(values)),
        in_specs=[vmem] * len(values) + [anywhere] * len(tokens),
        out_specs=vmem,
        out_shape=jax.ShapeDtypeStruct(values[0].shape, values[0].dtype),
        compiler_params=pltpu.CompilerParams(vmem_limit_bytes=6 * MIB),
        cost_estimate=COST,
        name="join",
    )(*values, *tokens)


def release_kernel(*refs):
    pass


def released(value, tokens):
    anywhere = pl.BlockSpec(memory_space=pl.ANY)
    return pl.pallas_call(
        release_kernel,
        in_specs=[anywhere] * (1 + len(tokens)),
        out_specs=anywhere,
        out_shape=pltpu.HBM(value.shape, value.dtype),
        input_output_aliases={0: 0},
        cost_estimate=COST,
        name="release",
    )(value, *tokens)


def place_runs(me_ref, slot_ref, row_ref, held_ref, stage_ref, copies, peers, run, first):
    size = row_ref.shape[0] // peers
    batch = max(n for n in range(1, 49) if size % n == 0)
    chunk = max(n for n in range(16, 49, 16) if size % n == 0)

    def prepare(source, carry):
        for block in range(0, size, chunk):
            at = pl.multiple_of(source * size + block, chunk)
            unit, _ = unit_rows(row_ref[pl.ds(at, chunk), :].astype(jnp.float32))
            stage_ref[pl.ds(2 * at, chunk, stride=2), :] = unit[:, :128]
            stage_ref[pl.ds(2 * at + 1, chunk, stride=2), :] = unit[:, 128:]
        return carry

    lax.fori_loop(0, peers, prepare, 0)
    for copy in copies:
        copy.wait()

    def place(source, carry):
        start = (me_ref[0] ^ source) * run + first
        at = source * size * 2
        for block in range(0, size, batch):
            slots = [slot_ref[start + block + v] for v in range(batch)]
            values = [stage_ref[pl.ds(at + 2 * (block + v), 2), :] for v in range(batch)]
            for slot, value in zip(slots, values):
                held_ref[pl.ds(slot, 2), :] = value
        return carry

    lax.fori_loop(0, peers, place, 0)


def place_kernel(
    me_ref, slot_ref, row_ref, held_ref, token_ref, stage_ref, *, peers, run, first
):
    token_ref[...] = jnp.zeros_like(token_ref)
    place_runs(me_ref, slot_ref, row_ref, held_ref, stage_ref, [], peers, run, first)


def place_rows(me, slots, rows, peers, run, first):
    smem = pl.BlockSpec(memory_space=pltpu.SMEM)
    vmem = pl.BlockSpec(memory_space=pltpu.VMEM)
    return pl.pallas_call(
        functools.partial(place_kernel, peers=peers, run=run, first=first),
        in_specs=[smem, smem, vmem],
        out_specs=[vmem, vmem],
        out_shape=[
            jax.ShapeDtypeStruct((2 * peers * run, 128), jnp.float32),
            jax.ShapeDtypeStruct((8, 128), jnp.float32),
        ],
        scratch_shapes=[pltpu.VMEM((2 * rows.shape[0], 128), jnp.float32)],
        compiler_params=pltpu.CompilerParams(vmem_limit_bytes=24 * MIB),
        cost_estimate=pl.CostEstimate(
            flops=0, bytes_accessed=32 * rows.shape[0] * rows.shape[1], transcendentals=0
        ),
        name="place_rows",
    )(me, slots, rows)


def split_copies(source_ref, target_ref, sem):
    lanes = sem.shape[0]
    size = source_ref.shape[0] // lanes
    parts = [pl.ds(c * size, size) for c in range(lanes)]
    return [
        pltpu.make_async_copy(source_ref.at[part, :], target_ref.at[part, :], sem.at[c])
        for c, part in enumerate(parts)
    ]


def blend_kernel(
    me_ref, slot_ref, row_ref, w_ref, _, o_ref, held_ref, stage_ref, what_ref, new_ref,
    what_sem, new_sem, *, peers, run, first,
):
    weights = split_copies(w_ref, what_ref, what_sem)
    for copy in weights:
        copy.start()
    place_runs(me_ref, slot_ref, row_ref, held_ref, stage_ref, [], peers, run, first)
    for copy in weights:
        copy.wait()
    classes = o_ref.shape[0]
    pieces = new_sem.shape[0]
    piece = classes // pieces
    block = math.gcd(piece, 64)

    def leaving(c):
        part = pl.ds(pl.multiple_of(c * piece, piece), piece)
        return pltpu.make_async_copy(new_ref.at[part, :], o_ref.at[part, :], new_sem.at[c])

    def blend(c, carry):
        for begin in range(0, piece, block):
            start = pl.multiple_of(c * piece + begin, block)
            rows = pl.ds(start, block)
            low = held_ref[pl.ds(start * 2, block, stride=2), :]
            high = held_ref[pl.ds(start * 2 + 1, block, stride=2), :]
            low = low + what_ref[rows, :128].astype(jnp.float32)
            high = high + what_ref[rows, 128:].astype(jnp.float32)
            inv = lax.rsqrt(jnp.sum(low * low + high * high, axis=1, keepdims=True) + 1e-06)
            new_ref[rows, :128] = (low * inv).astype(jnp.bfloat16)
            new_ref[rows, 128:] = (high * inv).astype(jnp.bfloat16)
        leaving(c).start()
        return carry

    lax.fori_loop(0, pieces, blend, 0)
    for c in range(pieces):
        leaving(c).wait()


def place_and_blend(me, slots, rows, held, weights, peers, run, first):
    classes, width = weights.shape
    smem = pl.BlockSpec(memory_space=pltpu.SMEM)
    vmem = pl.BlockSpec(memory_space=pltpu.VMEM)
    anywhere = pl.BlockSpec(memory_space=pl.ANY)
    refreshed, _ = pl.pallas_call(
        functools.partial(blend_kernel, peers=peers, run=run, first=first),
        in_specs=[smem, smem, vmem, anywhere, vmem],
        out_specs=[anywhere, vmem],
        out_shape=[
            pltpu.HBM((classes, width), jnp.bfloat16),
            jax.ShapeDtypeStruct(held.shape, held.dtype),
        ],
        input_output_aliases={4: 1},
        scratch_shapes=[
            pltpu.VMEM((2 * rows.shape[0], 128), jnp.float32),
            pltpu.VMEM((classes, width), jnp.bfloat16),
            pltpu.VMEM((classes, width), jnp.bfloat16),
            pltpu.SemaphoreType.DMA((2,)),
            pltpu.SemaphoreType.DMA((8,)),
        ],
        compiler_params=pltpu.CompilerParams(vmem_limit_bytes=20 * MIB),
        cost_estimate=pl.CostEstimate(
            flops=0, bytes_accessed=12 * classes * width, transcendentals=0
        ),
        name="place_and_blend",
    )(me, slots, rows, weights, held)
    return refreshed


def shards(embeddings, labels, class_weights, centroids, centroid_class):
    rows_local, width = embeddings.shape
    classes = class_weights.shape[0]
    groups, reps = lax.axis_size("grp"), lax.axis_size("rep")
    peers = groups * reps
    batch = rows_local * reps
    run = classes // peers
    grp, rep = lax.axis_index("grp").astype(jnp.int32), lax.axis_index("rep").astype(jnp.int32)
    me = (rep * groups + grp).reshape(1)
    base = me * classes

    def swap(value, axis, k):
        size = lax.axis_size(axis)
        return lax.ppermute(value, axis, [(i, i ^ k) for i in range(size)]) if k else value

    def relay(sent):
        return lax.all_to_all(sent, ALL, 0, 0, tiled=True).reshape(-1, width)

    weights = in_hbm(class_weights)
    runs = in_hbm(centroids.reshape(peers, run, width))
    cut = run * 5 // 8 // 16 * 16
    mixed = jnp.concatenate([swap(embeddings, "rep", 2 * z) for z in range(reps // 2)])
    rows_a = relay(released(in_hbm(fetch(runs, 0, cut, [])), [mixed]))
    mixed = jnp.concatenate([swap(mixed, "rep", c) for c in range(2)])
    emb, a, b, stats, what = forward(base, rep.reshape(1), mixed, reps, labels, weights)

    half = reps // 2
    core, deep = rep % 2, rep // 2
    index = lax.dynamic_index_in_dim

    def share_out(sums, wanted, axis, flips):
        raw, got = [], []
        for flip, asked in zip(flips, wanted):
            sent = jnp.concatenate([sums, asked.reshape(-1)]).reshape(-1, 128)
            raw.append(swap(sent, axis, flip))
            got.append(raw[-1].reshape(-1))
        got = jnp.stack(got)
        return jnp.sum(got[:, : 2 * batch], axis=0), got[:, 2 * batch :], raw

    wanted = centroid_class.reshape(half, 2, groups, run).astype(jnp.float32)
    wanted = [index(wanted, grp ^ j, 2, False) for j in range(groups)]
    sums, wanted, _ = share_out(stats[:2].reshape(-1), wanted, "grp", range(groups))
    wanted = wanted.reshape(groups, half, 2, run)
    wanted = [index(wanted, core ^ c, 2, False) for c in range(2)]
    sums, wanted, _ = share_out(sums, wanted, "rep", range(2))
    sent_b = in_hbm(fetch(runs, cut, run - cut, [stats]))
    sums = join([sums.reshape(-1, 128)], [sent_b]).reshape(-1)
    wanted = wanted.reshape(2, groups, half, run)
    wanted = [index(wanted, deep ^ z, 2, False) for z in range(half)]
    sums, slots, raw = share_out(sums, wanted, "rep", range(0, reps, 2))
    slots = slots.reshape(-1).astype(jnp.int32) * 2
    total, target = sums[:batch], sums[batch:]
    losses = jnp.log(total) - target
    loss = lax.dynamic_slice_in_dim(losses, rep * rows_local, rows_local, 0)

    rows_b = relay(released(sent_b, raw[1:]))
    held, token = place_rows(me, slots, rows_a, peers, run, 0)
    weight_grad = weight_gradient(base, emb, labels, stats, total, weights, token)

    grad = (a / total[:, None] - b).reshape(half, 2, rows_local, width)
    grad = sum(swap(index(grad, core ^ c, 1, False), "rep", c) for c in range(2))
    grad = join([swap(grad, "grp", j) for j in range(groups)], [in_hbm(weight_grad), loss])
    sent = grad.astype(jnp.bfloat16)
    parts = [swap(index(sent, deep ^ z, 0, False), "rep", 2 * z) for z in range(1, half)]
    embedding_gradient = index(grad, deep, 0, False)
    for part in parts:
        embedding_gradient = embedding_gradient + part.astype(jnp.float32)

    refreshed = place_and_blend(me, slots, rows_b, held, in_hbm(what), peers, run, cut)
    return (loss, embedding_gradient, weight_grad, refreshed)


def solution(mesh):
    in_specs = (
        P("rep", None),
        P(),
        P(("rep", "grp"), None),
        P(("grp", "rep"), None),
        P(("grp", "rep")),
    )
    out_specs = (P("rep"), P("rep", None), P(("rep", "grp"), None), P(("rep", "grp"), None))
    return jax.shard_map(shards, mesh=mesh, in_specs=in_specs, out_specs=out_specs, check_vma=False)
```

```python
import functools
import math

import jax
import jax.numpy as jnp
from jax import lax
from jax.experimental import pallas as pl
from jax.experimental.pallas import tpu as pltpu
from jax.sharding import PartitionSpec as P

SCALE = 32.0
MARGIN = 0.2
SIN_FLOOR = 0.09
LOG2E = math.log2(math.e)
ALL = ("rep", "grp")
MIB = 1024 * 1024
COST = pl.CostEstimate(flops=1, bytes_accessed=1, transcendentals=0)

NT = (((1,), (1,)), ((), ()))


def in_hbm(value):
    return pltpu.with_memory_space_constraint(value, pltpu.HBM)


def unit_rows(wide):
    inv = lax.rsqrt(jnp.sum(wide * wide, axis=1, keepdims=True) + 1e-06)
    return wide * inv, inv


def off_axis(values, unit):
    return values - unit * jnp.sum(unit * values, axis=1, keepdims=True)


def column_of(row):
    lanes = row.shape[1]
    return jnp.transpose(jnp.broadcast_to(row, (128, lanes)))[:, :1]


def forward_kernel(
    base_ref, rep_ref, lab_ref, w_ref, mixed_ref, emb_ref, a_ref, b_ref, st_ref, what_ref, xhat_ref,
    sum_ref,
    *, classes, reps,
):
    step = pl.program_id(0)
    tile = w_ref.shape[0]
    batch = emb_ref.shape[0]

    @pl.when(step == 0)
    def _():
        rows = batch // reps
        for k in range(reps):
            flip = k // (reps // 2) + k % (reps // 2) * 2
            first = pl.multiple_of((rep_ref[0] ^ flip) * rows, rows)
            emb_ref[pl.ds(first, rows), :] = mixed_ref[k * rows : (k + 1) * rows, :]
        xwide, _ = unit_rows(emb_ref[...].astype(jnp.float32))
        xhat_ref[...] = xwide.astype(jnp.bfloat16)
        sum_ref[...] = jnp.zeros_like(sum_ref)
        a_ref[...] = jnp.zeros_like(a_ref)
        b_ref[...] = jnp.zeros_like(b_ref)

    wwide, _ = unit_rows(w_ref[...].astype(jnp.float32))
    what = wwide.astype(jnp.bfloat16)
    what_ref[...] = what
    cosine = lax.dot_general(xhat_ref[...], what, NT, preferred_element_type=jnp.float32)
    ids = lax.broadcasted_iota(jnp.int32, (batch, tile), 1)
    is_label = ids == lab_ref[...] - (base_ref[0] + step * tile)
    e = jnp.where(is_label, 0.0, jnp.exp2(cosine * (SCALE * LOG2E)))
    partial = e[:, :128]
    for c in range(1, tile // 128):
        partial = partial + e[:, c * 128 : (c + 1) * 128]
    sum_ref[...] += partial
    onehot = jnp.where(is_label, 1.0, 0.0).astype(jnp.bfloat16)
    a_ref[...] += jnp.dot(e.astype(jnp.bfloat16), what, preferred_element_type=jnp.float32)
    b_ref[...] += jnp.dot(onehot, what, preferred_element_type=jnp.float32)

    @pl.when(step == pl.num_programs(0) - 1)
    def _():
        xwide, x_inv = unit_rows(emb_ref[...].astype(jnp.float32))
        label_row = b_ref[...]
        c = jnp.sum(xhat_ref[...].astype(jnp.float32) * label_row, axis=1, keepdims=True)
        offset = lab_ref[...] - base_ref[0]
        has = jnp.where((offset >= 0) & (offset < classes), 1.0, 0.0)
        q = 1.0 - c * c
        sine = jnp.sqrt(jnp.maximum(q, SIN_FLOOR))
        margined = c * math.cos(MARGIN) - sine * math.sin(MARGIN)
        slope = math.cos(MARGIN) + jnp.where(q > SIN_FLOOR, c * math.sin(MARGIN) / sine, 0.0)
        slope = slope * has
        label_e = jnp.exp(SCALE * margined) * has
        total = jnp.sum(sum_ref[...], axis=1, keepdims=True) + label_e
        target = SCALE * margined * has
        b = slope * label_row
        a = a_ref[...] + label_e * b
        gain = SCALE * x_inv
        a_ref[...] = off_axis(a, xwide) * gain
        b_ref[...] = off_axis(b, xwide) * gain
        lane = lax.broadcasted_iota(jnp.int32, (batch, 128), 1)
        stats = jnp.where(lane == 0, total, 0.0)
        stats = jnp.where(lane == 1, target, stats)
        stats = jnp.where(lane == 2, label_e * slope, stats)
        stats = jnp.where(lane == 3, slope, stats)
        st_ref[...] = jnp.transpose(stats)[:8, :]


def forward(base, rep, mixed, reps, labels, weights):
    batch, width = mixed.shape
    classes = weights.shape[0]
    tile = math.gcd(classes, 1024)
    whole = lambda i: (0, 0)
    smem = pl.BlockSpec(memory_space=pltpu.SMEM)
    return pl.pallas_call(
        functools.partial(forward_kernel, classes=classes, reps=reps),
        grid=(classes // tile,),
        in_specs=[
            smem,
            smem,
            pl.BlockSpec((batch, 1), whole),
            pl.BlockSpec((tile, width), lambda i: (i, 0)),
            pl.BlockSpec((batch, width), whole),
        ],
        out_specs=[
            pl.BlockSpec((batch, width), whole),
            pl.BlockSpec((batch, width), whole),
            pl.BlockSpec((batch, width), whole),
            pl.BlockSpec((8, batch), whole),
            pl.BlockSpec((tile, width), lambda i: (i, 0)),
        ],
        out_shape=[
            jax.ShapeDtypeStruct((batch, width), jnp.bfloat16),
            jax.ShapeDtypeStruct((batch, width), jnp.float32),
            jax.ShapeDtypeStruct((batch, width), jnp.float32),
            jax.ShapeDtypeStruct((8, batch), jnp.float32),
            pltpu.HBM((classes, width), jnp.bfloat16),
        ],
        scratch_shapes=[pltpu.VMEM((batch, width), jnp.bfloat16), pltpu.VMEM((batch, 128), jnp.float32)],
        compiler_params=pltpu.CompilerParams(
            dimension_semantics=("arbitrary",), vmem_limit_bytes=20 * MIB
        ),
        cost_estimate=pl.CostEstimate(
            flops=12 * batch * classes * width, bytes_accessed=classes * width * 2, transcendentals=0
        ),
        name="forward_sums",
    )(base, rep, labels.reshape(batch, 1), weights, mixed)


def weight_kernel(base_ref, emb_ref, lab_ref, st_ref, tot_ref, w_ref, _, g_ref, xhat_ref, y_ref, v_ref):
    step = pl.program_id(0)
    tile = w_ref.shape[0]
    batch = emb_ref.shape[0]

    @pl.when(step == 0)
    def _():
        xwide, _ = unit_rows(emb_ref[...].astype(jnp.float32))
        xhat = xwide.astype(jnp.bfloat16)
        xhat_ref[...] = xhat
        total = tot_ref[...]
        y_ref[...] = (xhat.astype(jnp.float32) * column_of(SCALE / total)).astype(jnp.bfloat16)
        v_ref[...] = st_ref[2:3, :] - st_ref[3:4, :] * total

    block = math.gcd(tile, 256)
    for first in range(0, tile, block):
        at = pl.ds(first, block)
        wwide, w_inv = unit_rows(w_ref[at, :].astype(jnp.float32))
        what = wwide.astype(jnp.bfloat16)
        cosine = lax.dot_general(what, xhat_ref[...], NT, preferred_element_type=jnp.float32)
        ids = lax.broadcasted_iota(jnp.int32, (block, batch), 0)
        is_label = ids == lab_ref[...] - (base_ref[0] + step * tile + first)
        e = jnp.exp2(cosine * (SCALE * LOG2E))
        d = jnp.where(is_label, v_ref[...], e).astype(jnp.bfloat16)
        raw = jnp.dot(d, y_ref[...], preferred_element_type=jnp.float32)
        g_ref[at, :] = off_axis(raw, wwide) * w_inv


def weight_gradient(base, emb, labels, stats, totals, weights, after):
    batch, width = emb.shape
    classes = weights.shape[0]
    tile = math.gcd(classes, 2048)
    whole = lambda i: (0, 0)
    return pl.pallas_call(
        weight_kernel,
        grid=(classes // tile,),
        in_specs=[
            pl.BlockSpec(memory_space=pltpu.SMEM),
            pl.BlockSpec((batch, width), whole),
            pl.BlockSpec((1, batch), whole),
            pl.BlockSpec((8, batch), whole),
            pl.BlockSpec((1, batch), whole),
            pl.BlockSpec((tile, width), lambda i: (i, 0)),
            pl.BlockSpec(memory_space=pl.ANY),
        ],
        out_specs=pl.BlockSpec((tile, width), lambda i: (i, 0)),
        out_shape=pltpu.HBM((classes, width), jnp.float32),
        scratch_shapes=[
            pltpu.VMEM((batch, width), jnp.bfloat16),
            pltpu.VMEM((batch, width), jnp.bfloat16),
            pltpu.VMEM((1, batch), jnp.float32),
        ],
        compiler_params=pltpu.CompilerParams(
            dimension_semantics=("arbitrary",), vmem_limit_bytes=20 * MIB
        ),
        cost_estimate=pl.CostEstimate(
            flops=12 * batch * classes * width, bytes_accessed=classes * width * 6, transcendentals=0
        ),
        name="weight_gradient",
    )(base, emb, labels.reshape(1, batch), stats, totals.reshape(1, batch), weights, after)


def fetch_kernel(rows_ref, *refs, first):
    out_ref, held_ref, sem = refs[-3:]
    peers, size, _ = out_ref.shape
    lanes = sem.shape[1]
    parts = [pl.ds(c * (peers // lanes), peers // lanes) for c in range(lanes)]
    loads = [
        pltpu.make_async_copy(rows_ref.at[part, pl.ds(first, size), :], held_ref.at[part], sem.at[0, c])
        for c, part in enumerate(parts)
    ]
    stores = [
        pltpu.make_async_copy(held_ref.at[part], out_ref.at[part], sem.at[1, c])
        for c, part in enumerate(parts)
    ]
    for load in loads:
        load.start()
    for load, store in zip(loads, stores):
        load.wait()
        store.start()
    for store in stores:
        store.wait()


def fetch(runs, first, size, tokens):
    peers, _, width = runs.shape
    hbm = pl.BlockSpec(memory_space=pltpu.HBM)
    anywhere = pl.BlockSpec(memory_space=pl.ANY)
    return pl.pallas_call(
        functools.partial(fetch_kernel, first=first),
        in_specs=[hbm] + [anywhere] * len(tokens),
        out_specs=anywhere,
        out_shape=pltpu.HBM((peers, size, width), runs.dtype),
        scratch_shapes=[
            pltpu.VMEM((peers, size, width), runs.dtype),
            pltpu.SemaphoreType.DMA((2, math.gcd(peers, 8))),
        ],
        compiler_params=pltpu.CompilerParams(vmem_limit_bytes=6 * MIB),
        cost_estimate=pl.CostEstimate(
            flops=0, bytes_accessed=8 * peers * size * width, transcendentals=0
        ),
        name="fetch",
    )(runs, *tokens)


def join_kernel(*refs, count):
    total = refs[0][...]
    for ref in refs[1:count]:
        total = total + ref[...].astype(total.dtype)
    refs[-1][...] = total


def join(values, tokens):
    anywhere = pl.BlockSpec(memory_space=pl.ANY)
    vmem = pl.BlockSpec(memory_space=pltpu.VMEM)
    return pl.pallas_call(
        functools.partial(join_kernel, count=len(values)),
        in_specs=[vmem] * len(values) + [anywhere] * len(tokens),
        out_specs=vmem,
        out_shape=jax.ShapeDtypeStruct(values[0].shape, values[0].dtype),
        compiler_params=pltpu.CompilerParams(vmem_limit_bytes=6 * MIB),
        cost_estimate=COST,
        name="join",
    )(*values, *tokens)


def release_kernel(*refs):
    pass


def released(value, tokens):
    anywhere = pl.BlockSpec(memory_space=pl.ANY)
    return pl.pallas_call(
        release_kernel,
        in_specs=[anywhere] * (1 + len(tokens)),
        out_specs=anywhere,
        out_shape=pltpu.HBM(value.shape, value.dtype),
        input_output_aliases={0: 0},
        cost_estimate=COST,
        name="release",
    )(value, *tokens)


def place_runs(me_ref, slot_ref, row_ref, held_ref, stage_ref, copies, peers, run, first):
    size = row_ref.shape[0] // peers
    batch = max(n for n in range(1, 49) if size % n == 0)
    chunk = max(n for n in range(16, 49, 16) if size % n == 0)

    def prepare(source, carry):
        for block in range(0, size, chunk):
            at = pl.multiple_of(source * size + block, chunk)
            unit, _ = unit_rows(row_ref[pl.ds(at, chunk), :].astype(jnp.float32))
            stage_ref[pl.ds(2 * at, chunk, stride=2), :] = unit[:, :128]
            stage_ref[pl.ds(2 * at + 1, chunk, stride=2), :] = unit[:, 128:]
        return carry

    lax.fori_loop(0, peers, prepare, 0)
    for copy in copies:
        copy.wait()

    def place(source, carry):
        start = (me_ref[0] ^ source) * run + first
        at = source * size * 2
        for block in range(0, size, batch):
            slots = [slot_ref[start + block + v] for v in range(batch)]
            values = [stage_ref[pl.ds(at + 2 * (block + v), 2), :] for v in range(batch)]
            for slot, value in zip(slots, values):
                held_ref[pl.ds(slot, 2), :] = value
        return carry

    lax.fori_loop(0, peers, place, 0)


def place_kernel(
    me_ref, slot_ref, row_ref, held_ref, token_ref, stage_ref, *, peers, run, first
):
    token_ref[...] = jnp.zeros_like(token_ref)
    place_runs(me_ref, slot_ref, row_ref, held_ref, stage_ref, [], peers, run, first)


def place_rows(me, slots, rows, peers, run, first):
    smem = pl.BlockSpec(memory_space=pltpu.SMEM)
    vmem = pl.BlockSpec(memory_space=pltpu.VMEM)
    return pl.pallas_call(
        functools.partial(place_kernel, peers=peers, run=run, first=first),
        in_specs=[smem, smem, vmem],
        out_specs=[vmem, vmem],
        out_shape=[
            jax.ShapeDtypeStruct((2 * peers * run, 128), jnp.float32),
            jax.ShapeDtypeStruct((8, 128), jnp.float32),
        ],
        scratch_shapes=[pltpu.VMEM((2 * rows.shape[0], 128), jnp.float32)],
        compiler_params=pltpu.CompilerParams(vmem_limit_bytes=24 * MIB),
        cost_estimate=pl.CostEstimate(
            flops=0, bytes_accessed=32 * rows.shape[0] * rows.shape[1], transcendentals=0
        ),
        name="place_rows",
    )(me, slots, rows)


def split_copies(source_ref, target_ref, sem):
    lanes = sem.shape[0]
    size = source_ref.shape[0] // lanes
    parts = [pl.ds(c * size, size) for c in range(lanes)]
    return [
        pltpu.make_async_copy(source_ref.at[part, :], target_ref.at[part, :], sem.at[c])
        for c, part in enumerate(parts)
    ]


def blend_kernel(
    me_ref, slot_ref, row_ref, w_ref, in_ref, o_ref, held_ref, stage_ref, what_ref, new_ref,
    held_sem, what_sem, new_sem, *, peers, run, first,
):
    copies = split_copies(in_ref, held_ref, held_sem)
    weights = split_copies(w_ref, what_ref, what_sem)
    for copy in copies + weights:
        copy.start()
    place_runs(me_ref, slot_ref, row_ref, held_ref, stage_ref, copies, peers, run, first)
    for copy in weights:
        copy.wait()
    classes = o_ref.shape[0]
    pieces = new_sem.shape[0]
    piece = classes // pieces
    block = math.gcd(piece, 64)

    def leaving(c):
        part = pl.ds(pl.multiple_of(c * piece, piece), piece)
        return pltpu.make_async_copy(new_ref.at[part, :], o_ref.at[part, :], new_sem.at[c])

    def blend(c, carry):
        for begin in range(0, piece, block):
            start = pl.multiple_of(c * piece + begin, block)
            rows = pl.ds(start, block)
            low = held_ref[pl.ds(start * 2, block, stride=2), :]
            high = held_ref[pl.ds(start * 2 + 1, block, stride=2), :]
            low = low + what_ref[rows, :128].astype(jnp.float32)
            high = high + what_ref[rows, 128:].astype(jnp.float32)
            inv = lax.rsqrt(jnp.sum(low * low + high * high, axis=1, keepdims=True) + 1e-06)
            new_ref[rows, :128] = (low * inv).astype(jnp.bfloat16)
            new_ref[rows, 128:] = (high * inv).astype(jnp.bfloat16)
        leaving(c).start()
        return carry

    lax.fori_loop(0, pieces, blend, 0)
    for c in range(pieces):
        leaving(c).wait()


def place_and_blend(me, slots, rows, held, weights, peers, run, first):
    classes, width = weights.shape
    smem = pl.BlockSpec(memory_space=pltpu.SMEM)
    vmem = pl.BlockSpec(memory_space=pltpu.VMEM)
    anywhere = pl.BlockSpec(memory_space=pl.ANY)
    return pl.pallas_call(
        functools.partial(blend_kernel, peers=peers, run=run, first=first),
        in_specs=[smem, smem, vmem, anywhere, anywhere],
        out_specs=anywhere,
        out_shape=pltpu.HBM((classes, width), jnp.bfloat16),
        scratch_shapes=[
            pltpu.VMEM(held.shape, jnp.float32),
            pltpu.VMEM((2 * rows.shape[0], 128), jnp.float32),
            pltpu.VMEM((classes, width), jnp.bfloat16),
            pltpu.VMEM((classes, width), jnp.bfloat16),
            pltpu.SemaphoreType.DMA((4,)),
            pltpu.SemaphoreType.DMA((2,)),
            pltpu.SemaphoreType.DMA((8,)),
        ],
        compiler_params=pltpu.CompilerParams(vmem_limit_bytes=32 * MIB),
        cost_estimate=pl.CostEstimate(
            flops=0, bytes_accessed=12 * classes * width, transcendentals=0
        ),
        name="place_and_blend",
    )(me, slots, rows, weights, held)


def shards(embeddings, labels, class_weights, centroids, centroid_class):
    rows_local, width = embeddings.shape
    classes = class_weights.shape[0]
    groups, reps = lax.axis_size("grp"), lax.axis_size("rep")
    peers = groups * reps
    batch = rows_local * reps
    run = classes // peers
    grp, rep = lax.axis_index("grp").astype(jnp.int32), lax.axis_index("rep").astype(jnp.int32)
    me = (rep * groups + grp).reshape(1)
    base = me * classes

    def swap(value, axis, k):
        size = lax.axis_size(axis)
        return lax.ppermute(value, axis, [(i, i ^ k) for i in range(size)]) if k else value

    def relay(sent):
        return lax.all_to_all(sent, ALL, 0, 0, tiled=True).reshape(-1, width)

    weights = in_hbm(class_weights)
    runs = in_hbm(centroids.reshape(peers, run, width))
    cut = run * 5 // 8 // 16 * 16
    mixed = jnp.concatenate([swap(embeddings, "rep", 2 * z) for z in range(reps // 2)])
    rows_a = relay(released(in_hbm(fetch(runs, 0, cut, [])), [mixed]))
    mixed = jnp.concatenate([swap(mixed, "rep", c) for c in range(2)])
    emb, a, b, stats, what = forward(base, rep.reshape(1), mixed, reps, labels, weights)

    half = reps // 2
    core, deep = rep % 2, rep // 2
    index = lax.dynamic_index_in_dim

    def share_out(sums, wanted, axis, flips):
        got = []
        for flip, asked in zip(flips, wanted):
            sent = jnp.concatenate([sums, asked.reshape(-1)]).reshape(-1, 128)
            got.append(swap(sent, axis, flip).reshape(-1))
        got = jnp.stack(got)
        return jnp.sum(got[:, : 2 * batch], axis=0), got[:, 2 * batch :]

    wanted = centroid_class.reshape(half, 2, groups, run).astype(jnp.float32)
    wanted = [index(wanted, grp ^ j, 2, False) for j in range(groups)]
    sums, wanted = share_out(stats[:2].reshape(-1), wanted, "grp", range(groups))
    wanted = wanted.reshape(groups, half, 2, run)
    wanted = [index(wanted, core ^ c, 2, False) for c in range(2)]
    sums, wanted = share_out(sums, wanted, "rep", range(2))
    sent_b = in_hbm(fetch(runs, cut, run - cut, [stats]))
    sums = join([sums.reshape(-1, 128)], [sent_b]).reshape(-1)
    wanted = wanted.reshape(2, groups, half, run)
    wanted = [index(wanted, deep ^ z, 2, False) for z in range(half)]
    sums, slots = share_out(sums, wanted, "rep", range(0, reps, 2))
    slots = slots.reshape(-1).astype(jnp.int32) * 2
    total, target = sums[:batch], sums[batch:]
    losses = jnp.log(total) - target
    loss = lax.dynamic_slice_in_dim(losses, rep * rows_local, rows_local, 0)

    rows_b = relay(released(sent_b, [total]))
    held, token = place_rows(me, slots, rows_a, peers, run, 0)
    weight_grad = weight_gradient(base, emb, labels, stats, total, weights, token)

    grad = (a / total[:, None] - b).reshape(half, 2, rows_local, width)
    grad = sum(swap(index(grad, core ^ c, 1, False), "rep", c) for c in range(2))
    sent = grad.astype(jnp.bfloat16)
    parts = [swap(sent, "grp", j) for j in range(1, groups)]
    grad = join([grad, *parts], [in_hbm(weight_grad), loss])
    sent = grad.astype(jnp.bfloat16)
    parts = [swap(index(sent, deep ^ z, 0, False), "rep", 2 * z) for z in range(1, half)]
    embedding_gradient = index(grad, deep, 0, False)
    for part in parts:
        embedding_gradient = embedding_gradient + part.astype(jnp.float32)

    refreshed = place_and_blend(me, slots, rows_b, in_hbm(held), in_hbm(what), peers, run, cut)
    return (loss, embedding_gradient, weight_grad, refreshed)


def solution(mesh):
    in_specs = (
        P("rep", None),
        P(),
        P(("rep", "grp"), None),
        P(("grp", "rep"), None),
        P(("grp", "rep")),
    )
    out_specs = (P("rep"), P("rep", None), P(("rep", "grp"), None), P(("rep", "grp"), None))
    return jax.shard_map(shards, mesh=mesh, in_specs=in_specs, out_specs=out_specs, check_vma=False)
```

```python
import functools
import math

import jax
import jax.numpy as jnp
from jax import lax
from jax.experimental import pallas as pl
from jax.experimental.pallas import tpu as pltpu
from jax.sharding import PartitionSpec as P

SCALE = 32.0
MARGIN = 0.2
SIN_FLOOR = 0.09
LOG2E = math.log2(math.e)
ALL = ("rep", "grp")
MIB = 1024 * 1024
COST = pl.CostEstimate(flops=1, bytes_accessed=1, transcendentals=0)

NT = (((1,), (1,)), ((), ()))


def in_hbm(value):
    return pltpu.with_memory_space_constraint(value, pltpu.HBM)


def unit_rows(wide):
    inv = lax.rsqrt(jnp.sum(wide * wide, axis=1, keepdims=True) + 1e-06)
    return wide * inv, inv


def off_axis(values, unit):
    return values - unit * jnp.sum(unit * values, axis=1, keepdims=True)


def column_of(row):
    lanes = row.shape[1]
    return jnp.transpose(jnp.broadcast_to(row, (128, lanes)))[:, :1]


def forward_kernel(
    base_ref, rep_ref, lab_ref, w_ref, mixed_ref, emb_ref, a_ref, b_ref, st_ref, what_ref, xhat_ref,
    sum_ref,
    *, classes, reps,
):
    step = pl.program_id(0)
    tile = w_ref.shape[0]
    batch = emb_ref.shape[0]

    @pl.when(step == 0)
    def _():
        rows = batch // reps
        for k in range(reps):
            flip = k // (reps // 2) + k % (reps // 2) * 2
            first = pl.multiple_of((rep_ref[0] ^ flip) * rows, rows)
            emb_ref[pl.ds(first, rows), :] = mixed_ref[k * rows : (k + 1) * rows, :]
        xwide, _ = unit_rows(emb_ref[...].astype(jnp.float32))
        xhat_ref[...] = xwide.astype(jnp.bfloat16)
        sum_ref[...] = jnp.zeros_like(sum_ref)
        a_ref[...] = jnp.zeros_like(a_ref)
        b_ref[...] = jnp.zeros_like(b_ref)

    wwide, _ = unit_rows(w_ref[...].astype(jnp.float32))
    what = wwide.astype(jnp.bfloat16)
    what_ref[...] = what
    cosine = lax.dot_general(xhat_ref[...], what, NT, preferred_element_type=jnp.float32)
    ids = lax.broadcasted_iota(jnp.int32, (batch, tile), 1)
    is_label = ids == lab_ref[...] - (base_ref[0] + step * tile)
    e = jnp.where(is_label, 0.0, jnp.exp2(cosine * (SCALE * LOG2E)))
    partial = e[:, :128]
    for c in range(1, tile // 128):
        partial = partial + e[:, c * 128 : (c + 1) * 128]
    sum_ref[...] += partial
    onehot = jnp.where(is_label, 1.0, 0.0).astype(jnp.bfloat16)
    a_ref[...] += jnp.dot(e.astype(jnp.bfloat16), what, preferred_element_type=jnp.float32)
    b_ref[...] += jnp.dot(onehot, what, preferred_element_type=jnp.float32)

    @pl.when(step == pl.num_programs(0) - 1)
    def _():
        xwide, x_inv = unit_rows(emb_ref[...].astype(jnp.float32))
        label_row = b_ref[...]
        c = jnp.sum(xhat_ref[...].astype(jnp.float32) * label_row, axis=1, keepdims=True)
        offset = lab_ref[...] - base_ref[0]
        has = jnp.where((offset >= 0) & (offset < classes), 1.0, 0.0)
        q = 1.0 - c * c
        sine = jnp.sqrt(jnp.maximum(q, SIN_FLOOR))
        margined = c * math.cos(MARGIN) - sine * math.sin(MARGIN)
        slope = math.cos(MARGIN) + jnp.where(q > SIN_FLOOR, c * math.sin(MARGIN) / sine, 0.0)
        slope = slope * has
        label_e = jnp.exp(SCALE * margined) * has
        total = jnp.sum(sum_ref[...], axis=1, keepdims=True) + label_e
        target = SCALE * margined * has
        b = slope * label_row
        a = a_ref[...] + label_e * b
        gain = SCALE * x_inv
        a_ref[...] = off_axis(a, xwide) * gain
        b_ref[...] = off_axis(b, xwide) * gain
        lane = lax.broadcasted_iota(jnp.int32, (batch, 128), 1)
        stats = jnp.where(lane == 0, total, 0.0)
        stats = jnp.where(lane == 1, target, stats)
        stats = jnp.where(lane == 2, label_e * slope, stats)
        stats = jnp.where(lane == 3, slope, stats)
        st_ref[...] = jnp.transpose(stats)[:8, :]


def forward(base, rep, mixed, reps, labels, weights):
    batch, width = mixed.shape
    classes = weights.shape[0]
    tile = math.gcd(classes, 1024)
    whole = lambda i: (0, 0)
    smem = pl.BlockSpec(memory_space=pltpu.SMEM)
    return pl.pallas_call(
        functools.partial(forward_kernel, classes=classes, reps=reps),
        grid=(classes // tile,),
        in_specs=[
            smem,
            smem,
            pl.BlockSpec((batch, 1), whole),
            pl.BlockSpec((tile, width), lambda i: (i, 0)),
            pl.BlockSpec((batch, width), whole),
        ],
        out_specs=[
            pl.BlockSpec((batch, width), whole),
            pl.BlockSpec((batch, width), whole),
            pl.BlockSpec((batch, width), whole),
            pl.BlockSpec((8, batch), whole),
            pl.BlockSpec((tile, width), lambda i: (i, 0)),
        ],
        out_shape=[
            jax.ShapeDtypeStruct((batch, width), jnp.bfloat16),
            jax.ShapeDtypeStruct((batch, width), jnp.float32),
            jax.ShapeDtypeStruct((batch, width), jnp.float32),
            jax.ShapeDtypeStruct((8, batch), jnp.float32),
            pltpu.HBM((classes, width), jnp.bfloat16),
        ],
        scratch_shapes=[pltpu.VMEM((batch, width), jnp.bfloat16), pltpu.VMEM((batch, 128), jnp.float32)],
        compiler_params=pltpu.CompilerParams(
            dimension_semantics=("arbitrary",), vmem_limit_bytes=20 * MIB
        ),
        cost_estimate=pl.CostEstimate(
            flops=12 * batch * classes * width, bytes_accessed=classes * width * 2, transcendentals=0
        ),
        name="forward_sums",
    )(base, rep, labels.reshape(batch, 1), weights, mixed)


def weight_kernel(base_ref, emb_ref, lab_ref, st_ref, tot_ref, w_ref, _, g_ref, xhat_ref, y_ref, v_ref):
    step = pl.program_id(0)
    tile = w_ref.shape[0]
    batch = emb_ref.shape[0]

    @pl.when(step == 0)
    def _():
        xwide, _ = unit_rows(emb_ref[...].astype(jnp.float32))
        xhat = xwide.astype(jnp.bfloat16)
        xhat_ref[...] = xhat
        total = tot_ref[...]
        y_ref[...] = (xhat.astype(jnp.float32) * column_of(SCALE / total)).astype(jnp.bfloat16)
        v_ref[...] = st_ref[2:3, :] - st_ref[3:4, :] * total

    block = math.gcd(tile, 256)
    for first in range(0, tile, block):
        at = pl.ds(first, block)
        wwide, w_inv = unit_rows(w_ref[at, :].astype(jnp.float32))
        what = wwide.astype(jnp.bfloat16)
        cosine = lax.dot_general(what, xhat_ref[...], NT, preferred_element_type=jnp.float32)
        ids = lax.broadcasted_iota(jnp.int32, (block, batch), 0)
        is_label = ids == lab_ref[...] - (base_ref[0] + step * tile + first)
        e = jnp.exp2(cosine * (SCALE * LOG2E))
        d = jnp.where(is_label, v_ref[...], e).astype(jnp.bfloat16)
        raw = jnp.dot(d, y_ref[...], preferred_element_type=jnp.float32)
        g_ref[at, :] = off_axis(raw, wwide) * w_inv


def weight_gradient(base, emb, labels, stats, totals, weights, after):
    batch, width = emb.shape
    classes = weights.shape[0]
    tile = math.gcd(classes, 2048)
    whole = lambda i: (0, 0)
    return pl.pallas_call(
        weight_kernel,
        grid=(classes // tile,),
        in_specs=[
            pl.BlockSpec(memory_space=pltpu.SMEM),
            pl.BlockSpec((batch, width), whole),
            pl.BlockSpec((1, batch), whole),
            pl.BlockSpec((8, batch), whole),
            pl.BlockSpec((1, batch), whole),
            pl.BlockSpec((tile, width), lambda i: (i, 0)),
            pl.BlockSpec(memory_space=pl.ANY),
        ],
        out_specs=pl.BlockSpec((tile, width), lambda i: (i, 0)),
        out_shape=pltpu.HBM((classes, width), jnp.float32),
        scratch_shapes=[
            pltpu.VMEM((batch, width), jnp.bfloat16),
            pltpu.VMEM((batch, width), jnp.bfloat16),
            pltpu.VMEM((1, batch), jnp.float32),
        ],
        compiler_params=pltpu.CompilerParams(
            dimension_semantics=("arbitrary",), vmem_limit_bytes=20 * MIB
        ),
        cost_estimate=pl.CostEstimate(
            flops=12 * batch * classes * width, bytes_accessed=classes * width * 6, transcendentals=0
        ),
        name="weight_gradient",
    )(base, emb, labels.reshape(1, batch), stats, totals.reshape(1, batch), weights, after)


def fetch_kernel(rows_ref, *refs, first):
    out_ref, held_ref, sem = refs[-3:]
    peers, size, _ = out_ref.shape
    lanes = sem.shape[1]
    parts = [pl.ds(c * (peers // lanes), peers // lanes) for c in range(lanes)]
    loads = [
        pltpu.make_async_copy(rows_ref.at[part, pl.ds(first, size), :], held_ref.at[part], sem.at[0, c])
        for c, part in enumerate(parts)
    ]
    stores = [
        pltpu.make_async_copy(held_ref.at[part], out_ref.at[part], sem.at[1, c])
        for c, part in enumerate(parts)
    ]
    for load in loads:
        load.start()
    for load, store in zip(loads, stores):
        load.wait()
        store.start()
    for store in stores:
        store.wait()


def fetch(runs, first, size, tokens):
    peers, _, width = runs.shape
    hbm = pl.BlockSpec(memory_space=pltpu.HBM)
    anywhere = pl.BlockSpec(memory_space=pl.ANY)
    return pl.pallas_call(
        functools.partial(fetch_kernel, first=first),
        in_specs=[hbm] + [anywhere] * len(tokens),
        out_specs=anywhere,
        out_shape=pltpu.HBM((peers, size, width), runs.dtype),
        scratch_shapes=[
            pltpu.VMEM((peers, size, width), runs.dtype),
            pltpu.SemaphoreType.DMA((2, math.gcd(peers, 8))),
        ],
        compiler_params=pltpu.CompilerParams(vmem_limit_bytes=6 * MIB),
        cost_estimate=pl.CostEstimate(
            flops=0, bytes_accessed=8 * peers * size * width, transcendentals=0
        ),
        name="fetch",
    )(runs, *tokens)


def join_kernel(*refs, count):
    total = refs[0][...]
    for ref in refs[1:count]:
        total = total + ref[...].astype(total.dtype)
    refs[-1][...] = total


def join(values, tokens):
    anywhere = pl.BlockSpec(memory_space=pl.ANY)
    vmem = pl.BlockSpec(memory_space=pltpu.VMEM)
    return pl.pallas_call(
        functools.partial(join_kernel, count=len(values)),
        in_specs=[vmem] * len(values) + [anywhere] * len(tokens),
        out_specs=vmem,
        out_shape=jax.ShapeDtypeStruct(values[0].shape, values[0].dtype),
        compiler_params=pltpu.CompilerParams(vmem_limit_bytes=6 * MIB),
        cost_estimate=COST,
        name="join",
    )(*values, *tokens)


def release_kernel(*refs):
    pass


def released(value, tokens):
    anywhere = pl.BlockSpec(memory_space=pl.ANY)
    return pl.pallas_call(
        release_kernel,
        in_specs=[anywhere] * (1 + len(tokens)),
        out_specs=anywhere,
        out_shape=pltpu.HBM(value.shape, value.dtype),
        input_output_aliases={0: 0},
        cost_estimate=COST,
        name="release",
    )(value, *tokens)


def place_runs(me_ref, slot_ref, row_ref, held_ref, stage_ref, copies, peers, run, first):
    size = row_ref.shape[0] // peers
    batch = max(n for n in range(1, 49) if size % n == 0)
    chunk = max(n for n in range(16, 49, 16) if size % n == 0)

    def prepare(source, carry):
        for block in range(0, size, chunk):
            at = pl.multiple_of(source * size + block, chunk)
            unit, _ = unit_rows(row_ref[pl.ds(at, chunk), :].astype(jnp.float32))
            stage_ref[pl.ds(2 * at, chunk, stride=2), :] = unit[:, :128]
            stage_ref[pl.ds(2 * at + 1, chunk, stride=2), :] = unit[:, 128:]
        return carry

    lax.fori_loop(0, peers, prepare, 0)
    for copy in copies:
        copy.wait()

    def place(source, carry):
        start = (me_ref[0] ^ source) * run + first
        at = source * size * 2
        for block in range(0, size, batch):
            slots = [slot_ref[start + block + v] for v in range(batch)]
            values = [stage_ref[pl.ds(at + 2 * (block + v), 2), :] for v in range(batch)]
            for slot, value in zip(slots, values):
                held_ref[pl.ds(slot, 2), :] = value
        return carry

    lax.fori_loop(0, peers, place, 0)


def place_kernel(
    me_ref, slot_ref, row_ref, held_ref, token_ref, stage_ref, *, peers, run, first
):
    token_ref[...] = jnp.zeros_like(token_ref)
    place_runs(me_ref, slot_ref, row_ref, held_ref, stage_ref, [], peers, run, first)


def place_rows(me, slots, rows, peers, run, first):
    smem = pl.BlockSpec(memory_space=pltpu.SMEM)
    vmem = pl.BlockSpec(memory_space=pltpu.VMEM)
    return pl.pallas_call(
        functools.partial(place_kernel, peers=peers, run=run, first=first),
        in_specs=[smem, smem, vmem],
        out_specs=[vmem, vmem],
        out_shape=[
            jax.ShapeDtypeStruct((2 * peers * run, 128), jnp.float32),
            jax.ShapeDtypeStruct((8, 128), jnp.float32),
        ],
        scratch_shapes=[pltpu.VMEM((2 * rows.shape[0], 128), jnp.float32)],
        compiler_params=pltpu.CompilerParams(vmem_limit_bytes=24 * MIB),
        cost_estimate=pl.CostEstimate(
            flops=0, bytes_accessed=32 * rows.shape[0] * rows.shape[1], transcendentals=0
        ),
        name="place_rows",
    )(me, slots, rows)


def split_copies(source_ref, target_ref, sem):
    lanes = sem.shape[0]
    size = source_ref.shape[0] // lanes
    parts = [pl.ds(c * size, size) for c in range(lanes)]
    return [
        pltpu.make_async_copy(source_ref.at[part, :], target_ref.at[part, :], sem.at[c])
        for c, part in enumerate(parts)
    ]


def blend_kernel(
    me_ref, slot_ref, row_ref, w_ref, in_ref, o_ref, held_ref, stage_ref, what_ref, new_ref,
    held_sem, what_sem, new_sem, *, peers, run, first,
):
    copies = split_copies(in_ref, held_ref, held_sem)
    weights = split_copies(w_ref, what_ref, what_sem)
    for copy in copies + weights:
        copy.start()
    place_runs(me_ref, slot_ref, row_ref, held_ref, stage_ref, copies, peers, run, first)
    for copy in weights:
        copy.wait()
    classes = o_ref.shape[0]
    pieces = new_sem.shape[0]
    piece = classes // pieces
    block = math.gcd(piece, 64)

    def leaving(c):
        part = pl.ds(pl.multiple_of(c * piece, piece), piece)
        return pltpu.make_async_copy(new_ref.at[part, :], o_ref.at[part, :], new_sem.at[c])

    def blend(c, carry):
        for begin in range(0, piece, block):
            start = pl.multiple_of(c * piece + begin, block)
            rows = pl.ds(start, block)
            low = held_ref[pl.ds(start * 2, block, stride=2), :]
            high = held_ref[pl.ds(start * 2 + 1, block, stride=2), :]
            low = low + what_ref[rows, :128].astype(jnp.float32)
            high = high + what_ref[rows, 128:].astype(jnp.float32)
            inv = lax.rsqrt(jnp.sum(low * low + high * high, axis=1, keepdims=True) + 1e-06)
            new_ref[rows, :128] = (low * inv).astype(jnp.bfloat16)
            new_ref[rows, 128:] = (high * inv).astype(jnp.bfloat16)
        leaving(c).start()
        return carry

    lax.fori_loop(0, pieces, blend, 0)
    for c in range(pieces):
        leaving(c).wait()


def place_and_blend(me, slots, rows, held, weights, peers, run, first):
    classes, width = weights.shape
    smem = pl.BlockSpec(memory_space=pltpu.SMEM)
    vmem = pl.BlockSpec(memory_space=pltpu.VMEM)
    anywhere = pl.BlockSpec(memory_space=pl.ANY)
    return pl.pallas_call(
        functools.partial(blend_kernel, peers=peers, run=run, first=first),
        in_specs=[smem, smem, vmem, anywhere, anywhere],
        out_specs=anywhere,
        out_shape=pltpu.HBM((classes, width), jnp.bfloat16),
        scratch_shapes=[
            pltpu.VMEM(held.shape, jnp.float32),
            pltpu.VMEM((2 * rows.shape[0], 128), jnp.float32),
            pltpu.VMEM((classes, width), jnp.bfloat16),
            pltpu.VMEM((classes, width), jnp.bfloat16),
            pltpu.SemaphoreType.DMA((8,)),
            pltpu.SemaphoreType.DMA((2,)),
            pltpu.SemaphoreType.DMA((8,)),
        ],
        compiler_params=pltpu.CompilerParams(vmem_limit_bytes=32 * MIB),
        cost_estimate=pl.CostEstimate(
            flops=0, bytes_accessed=12 * classes * width, transcendentals=0
        ),
        name="place_and_blend",
    )(me, slots, rows, weights, held)


def shards(embeddings, labels, class_weights, centroids, centroid_class):
    rows_local, width = embeddings.shape
    classes = class_weights.shape[0]
    groups, reps = lax.axis_size("grp"), lax.axis_size("rep")
    peers = groups * reps
    batch = rows_local * reps
    run = classes // peers
    grp, rep = lax.axis_index("grp").astype(jnp.int32), lax.axis_index("rep").astype(jnp.int32)
    me = (rep * groups + grp).reshape(1)
    base = me * classes

    def swap(value, axis, k):
        size = lax.axis_size(axis)
        return lax.ppermute(value, axis, [(i, i ^ k) for i in range(size)]) if k else value

    def relay(sent):
        return lax.all_to_all(sent, ALL, 0, 0, tiled=True).reshape(-1, width)

    weights = in_hbm(class_weights)
    runs = in_hbm(centroids.reshape(peers, run, width))
    cut = run * 11 // 16 // 16 * 16
    mixed = jnp.concatenate([swap(embeddings, "rep", 2 * z) for z in range(reps // 2)])
    rows_a = relay(released(in_hbm(fetch(runs, 0, cut, [])), [mixed]))
    mixed = jnp.concatenate([swap(mixed, "rep", c) for c in range(2)])
    emb, a, b, stats, what = forward(base, rep.reshape(1), mixed, reps, labels, weights)

    half = reps // 2
    core, deep = rep % 2, rep // 2
    index = lax.dynamic_index_in_dim

    def share_out(sums, wanted, axis, flips):
        got = []
        for flip, asked in zip(flips, wanted):
            sent = jnp.concatenate([sums, asked.reshape(-1)]).reshape(-1, 128)
            got.append(swap(sent, axis, flip).reshape(-1))
        got = jnp.stack(got)
        return jnp.sum(got[:, : 2 * batch], axis=0), got[:, 2 * batch :]

    wanted = centroid_class.reshape(half, 2, groups, run).astype(jnp.float32)
    wanted = [index(wanted, grp ^ j, 2, False) for j in range(groups)]
    sums, wanted = share_out(stats[:2].reshape(-1), wanted, "grp", range(groups))
    wanted = wanted.reshape(groups, half, 2, run)
    wanted = [index(wanted, core ^ c, 2, False) for c in range(2)]
    sums, wanted = share_out(sums, wanted, "rep", range(2))
    sent_b = in_hbm(fetch(runs, cut, run - cut, [stats]))
    sums = join([sums.reshape(-1, 128)], [sent_b]).reshape(-1)
    wanted = wanted.reshape(2, groups, half, run)
    wanted = [index(wanted, deep ^ z, 2, False) for z in range(half)]
    sums, slots = share_out(sums, wanted, "rep", range(0, reps, 2))
    slots = slots.reshape(-1).astype(jnp.int32) * 2
    total, target = sums[:batch], sums[batch:]
    losses = jnp.log(total) - target
    loss = lax.dynamic_slice_in_dim(losses, rep * rows_local, rows_local, 0)

    rows_b = relay(released(sent_b, [total]))
    held, token = place_rows(me, slots, rows_a, peers, run, 0)
    weight_grad = weight_gradient(base, emb, labels, stats, total, weights, token)

    grad = (a / total[:, None] - b).reshape(half, 2, rows_local, width)
    grad = sum(swap(index(grad, core ^ c, 1, False), "rep", c) for c in range(2))
    sent = grad.astype(jnp.bfloat16)
    parts = [swap(sent, "grp", j) for j in range(1, groups)]
    grad = join([grad, *parts], [in_hbm(weight_grad), loss])
    sent = grad.astype(jnp.bfloat16)
    parts = [swap(index(sent, deep ^ z, 0, False), "rep", 2 * z) for z in range(1, half)]
    embedding_gradient = index(grad, deep, 0, False)
    for part in parts:
        embedding_gradient = embedding_gradient + part.astype(jnp.float32)

    refreshed = place_and_blend(me, slots, rows_b, in_hbm(held), in_hbm(what), peers, run, cut)
    return (loss, embedding_gradient, weight_grad, refreshed)


def solution(mesh):
    in_specs = (
        P("rep", None),
        P(),
        P(("rep", "grp"), None),
        P(("grp", "rep"), None),
        P(("grp", "rep")),
    )
    out_specs = (P("rep"), P("rep", None), P(("rep", "grp"), None), P(("rep", "grp"), None))
    return jax.shard_map(shards, mesh=mesh, in_specs=in_specs, out_specs=out_specs, check_vma=False)
```

```python
import functools
import math

import jax
import jax.numpy as jnp
from jax import lax
from jax.experimental import pallas as pl
from jax.experimental.pallas import tpu as pltpu
from jax.sharding import PartitionSpec as P

SCALE = 32.0
MARGIN = 0.2
SIN_FLOOR = 0.09
LOG2E = math.log2(math.e)
ALL = ("rep", "grp")
MIB = 1024 * 1024
COST = pl.CostEstimate(flops=1, bytes_accessed=1, transcendentals=0)

NT = (((1,), (1,)), ((), ()))


def in_hbm(value):
    return pltpu.with_memory_space_constraint(value, pltpu.HBM)


def unit_rows(wide):
    inv = lax.rsqrt(jnp.sum(wide * wide, axis=1, keepdims=True) + 1e-06)
    return wide * inv, inv


def off_axis(values, unit):
    return values - unit * jnp.sum(unit * values, axis=1, keepdims=True)


def column_of(row):
    lanes = row.shape[1]
    return jnp.transpose(jnp.broadcast_to(row, (128, lanes)))[:, :1]


def forward_kernel(
    base_ref, rep_ref, lab_ref, w_ref, mixed_ref, emb_ref, a_ref, b_ref, st_ref, what_ref, xhat_ref,
    sum_ref,
    *, classes, reps,
):
    step = pl.program_id(0)
    tile = w_ref.shape[0]
    batch = emb_ref.shape[0]

    @pl.when(step == 0)
    def _():
        rows = batch // reps
        for k in range(reps):
            flip = k // (reps // 2) + k % (reps // 2) * 2
            first = pl.multiple_of((rep_ref[0] ^ flip) * rows, rows)
            emb_ref[pl.ds(first, rows), :] = mixed_ref[k * rows : (k + 1) * rows, :]
        xwide, _ = unit_rows(emb_ref[...].astype(jnp.float32))
        xhat_ref[...] = xwide.astype(jnp.bfloat16)
        sum_ref[...] = jnp.zeros_like(sum_ref)
        a_ref[...] = jnp.zeros_like(a_ref)
        b_ref[...] = jnp.zeros_like(b_ref)

    wwide, _ = unit_rows(w_ref[...].astype(jnp.float32))
    what = wwide.astype(jnp.bfloat16)
    what_ref[...] = what
    cosine = lax.dot_general(xhat_ref[...], what, NT, preferred_element_type=jnp.float32)
    ids = lax.broadcasted_iota(jnp.int32, (batch, tile), 1)
    is_label = ids == lab_ref[...] - (base_ref[0] + step * tile)
    e = jnp.where(is_label, 0.0, jnp.exp2(cosine * (SCALE * LOG2E)))
    partial = e[:, :128]
    for c in range(1, tile // 128):
        partial = partial + e[:, c * 128 : (c + 1) * 128]
    sum_ref[...] += partial
    onehot = jnp.where(is_label, 1.0, 0.0).astype(jnp.bfloat16)
    a_ref[...] += jnp.dot(e.astype(jnp.bfloat16), what, preferred_element_type=jnp.float32)
    b_ref[...] += jnp.dot(onehot, what, preferred_element_type=jnp.float32)

    @pl.when(step == pl.num_programs(0) - 1)
    def _():
        xwide, x_inv = unit_rows(emb_ref[...].astype(jnp.float32))
        label_row = b_ref[...]
        c = jnp.sum(xhat_ref[...].astype(jnp.float32) * label_row, axis=1, keepdims=True)
        offset = lab_ref[...] - base_ref[0]
        has = jnp.where((offset >= 0) & (offset < classes), 1.0, 0.0)
        q = 1.0 - c * c
        sine = jnp.sqrt(jnp.maximum(q, SIN_FLOOR))
        margined = c * math.cos(MARGIN) - sine * math.sin(MARGIN)
        slope = math.cos(MARGIN) + jnp.where(q > SIN_FLOOR, c * math.sin(MARGIN) / sine, 0.0)
        slope = slope * has
        label_e = jnp.exp(SCALE * margined) * has
        total = jnp.sum(sum_ref[...], axis=1, keepdims=True) + label_e
        target = SCALE * margined * has
        b = slope * label_row
        a = a_ref[...] + label_e * b
        gain = SCALE * x_inv
        a_ref[...] = off_axis(a, xwide) * gain
        b_ref[...] = off_axis(b, xwide) * gain
        lane = lax.broadcasted_iota(jnp.int32, (batch, 128), 1)
        stats = jnp.where(lane == 0, total, 0.0)
        stats = jnp.where(lane == 1, target, stats)
        stats = jnp.where(lane == 2, label_e * slope, stats)
        stats = jnp.where(lane == 3, slope, stats)
        st_ref[...] = jnp.transpose(stats)[:8, :]


def forward(base, rep, mixed, reps, labels, weights):
    batch, width = mixed.shape
    classes = weights.shape[0]
    tile = math.gcd(classes, 1024)
    whole = lambda i: (0, 0)
    smem = pl.BlockSpec(memory_space=pltpu.SMEM)
    return pl.pallas_call(
        functools.partial(forward_kernel, classes=classes, reps=reps),
        grid=(classes // tile,),
        in_specs=[
            smem,
            smem,
            pl.BlockSpec((batch, 1), whole),
            pl.BlockSpec((tile, width), lambda i: (i, 0)),
            pl.BlockSpec((batch, width), whole),
        ],
        out_specs=[
            pl.BlockSpec((batch, width), whole),
            pl.BlockSpec((batch, width), whole),
            pl.BlockSpec((batch, width), whole),
            pl.BlockSpec((8, batch), whole),
            pl.BlockSpec((tile, width), lambda i: (i, 0)),
        ],
        out_shape=[
            jax.ShapeDtypeStruct((batch, width), jnp.bfloat16),
            jax.ShapeDtypeStruct((batch, width), jnp.float32),
            jax.ShapeDtypeStruct((batch, width), jnp.float32),
            jax.ShapeDtypeStruct((8, batch), jnp.float32),
            pltpu.HBM((classes, width), jnp.bfloat16),
        ],
        scratch_shapes=[pltpu.VMEM((batch, width), jnp.bfloat16), pltpu.VMEM((batch, 128), jnp.float32)],
        compiler_params=pltpu.CompilerParams(
            dimension_semantics=("arbitrary",), vmem_limit_bytes=20 * MIB
        ),
        cost_estimate=pl.CostEstimate(
            flops=12 * batch * classes * width, bytes_accessed=classes * width * 2, transcendentals=0
        ),
        name="forward_sums",
    )(base, rep, labels.reshape(batch, 1), weights, mixed)


def weight_kernel(base_ref, emb_ref, lab_ref, st_ref, tot_ref, w_ref, _, g_ref, xhat_ref, y_ref, v_ref):
    step = pl.program_id(0)
    tile = w_ref.shape[0]
    batch = emb_ref.shape[0]

    @pl.when(step == 0)
    def _():
        xwide, _ = unit_rows(emb_ref[...].astype(jnp.float32))
        xhat = xwide.astype(jnp.bfloat16)
        xhat_ref[...] = xhat
        total = tot_ref[...]
        y_ref[...] = (xhat.astype(jnp.float32) * column_of(SCALE / total)).astype(jnp.bfloat16)
        v_ref[...] = st_ref[2:3, :] - st_ref[3:4, :] * total

    block = math.gcd(tile, 256)
    for first in range(0, tile, block):
        at = pl.ds(first, block)
        wwide, w_inv = unit_rows(w_ref[at, :].astype(jnp.float32))
        what = wwide.astype(jnp.bfloat16)
        cosine = lax.dot_general(what, xhat_ref[...], NT, preferred_element_type=jnp.float32)
        ids = lax.broadcasted_iota(jnp.int32, (block, batch), 0)
        is_label = ids == lab_ref[...] - (base_ref[0] + step * tile + first)
        e = jnp.exp2(cosine * (SCALE * LOG2E))
        d = jnp.where(is_label, v_ref[...], e).astype(jnp.bfloat16)
        raw = jnp.dot(d, y_ref[...], preferred_element_type=jnp.float32)
        g_ref[at, :] = off_axis(raw, wwide) * w_inv


def weight_gradient(base, emb, labels, stats, totals, weights, after):
    batch, width = emb.shape
    classes = weights.shape[0]
    tile = math.gcd(classes, 2048)
    whole = lambda i: (0, 0)
    return pl.pallas_call(
        weight_kernel,
        grid=(classes // tile,),
        in_specs=[
            pl.BlockSpec(memory_space=pltpu.SMEM),
            pl.BlockSpec((batch, width), whole),
            pl.BlockSpec((1, batch), whole),
            pl.BlockSpec((8, batch), whole),
            pl.BlockSpec((1, batch), whole),
            pl.BlockSpec((tile, width), lambda i: (i, 0)),
            pl.BlockSpec(memory_space=pl.ANY),
        ],
        out_specs=pl.BlockSpec((tile, width), lambda i: (i, 0)),
        out_shape=pltpu.HBM((classes, width), jnp.float32),
        scratch_shapes=[
            pltpu.VMEM((batch, width), jnp.bfloat16),
            pltpu.VMEM((batch, width), jnp.bfloat16),
            pltpu.VMEM((1, batch), jnp.float32),
        ],
        compiler_params=pltpu.CompilerParams(
            dimension_semantics=("arbitrary",), vmem_limit_bytes=20 * MIB
        ),
        cost_estimate=pl.CostEstimate(
            flops=12 * batch * classes * width, bytes_accessed=classes * width * 6, transcendentals=0
        ),
        name="weight_gradient",
    )(base, emb, labels.reshape(1, batch), stats, totals.reshape(1, batch), weights, after)


def fetch_kernel(rows_ref, *refs, first):
    out_ref, held_ref, sem = refs[-3:]
    peers, size, _ = out_ref.shape
    lanes = sem.shape[1]
    parts = [pl.ds(c * (peers // lanes), peers // lanes) for c in range(lanes)]
    loads = [
        pltpu.make_async_copy(rows_ref.at[part, pl.ds(first, size), :], held_ref.at[part], sem.at[0, c])
        for c, part in enumerate(parts)
    ]
    stores = [
        pltpu.make_async_copy(held_ref.at[part], out_ref.at[part], sem.at[1, c])
        for c, part in enumerate(parts)
    ]
    for load in loads:
        load.start()
    for load, store in zip(loads, stores):
        load.wait()
        store.start()
    for store in stores:
        store.wait()


def fetch(runs, first, size, tokens):
    peers, _, width = runs.shape
    hbm = pl.BlockSpec(memory_space=pltpu.HBM)
    anywhere = pl.BlockSpec(memory_space=pl.ANY)
    return pl.pallas_call(
        functools.partial(fetch_kernel, first=first),
        in_specs=[hbm] + [anywhere] * len(tokens),
        out_specs=anywhere,
        out_shape=pltpu.HBM((peers, size, width), runs.dtype),
        scratch_shapes=[
            pltpu.VMEM((peers, size, width), runs.dtype),
            pltpu.SemaphoreType.DMA((2, math.gcd(peers, 8))),
        ],
        compiler_params=pltpu.CompilerParams(vmem_limit_bytes=6 * MIB),
        cost_estimate=pl.CostEstimate(
            flops=0, bytes_accessed=8 * peers * size * width, transcendentals=0
        ),
        name="fetch",
    )(runs, *tokens)


def join_kernel(*refs, count):
    total = refs[0][...]
    for ref in refs[1:count]:
        total = total + ref[...].astype(total.dtype)
    refs[-1][...] = total


def join(values, tokens):
    anywhere = pl.BlockSpec(memory_space=pl.ANY)
    vmem = pl.BlockSpec(memory_space=pltpu.VMEM)
    return pl.pallas_call(
        functools.partial(join_kernel, count=len(values)),
        in_specs=[vmem] * len(values) + [anywhere] * len(tokens),
        out_specs=vmem,
        out_shape=jax.ShapeDtypeStruct(values[0].shape, values[0].dtype),
        compiler_params=pltpu.CompilerParams(vmem_limit_bytes=6 * MIB),
        cost_estimate=COST,
        name="join",
    )(*values, *tokens)


def release_kernel(*refs):
    pass


def released(value, tokens):
    anywhere = pl.BlockSpec(memory_space=pl.ANY)
    return pl.pallas_call(
        release_kernel,
        in_specs=[anywhere] * (1 + len(tokens)),
        out_specs=anywhere,
        out_shape=pltpu.HBM(value.shape, value.dtype),
        input_output_aliases={0: 0},
        cost_estimate=COST,
        name="release",
    )(value, *tokens)


def place_runs(me_ref, slot_ref, row_ref, held_ref, stage_ref, copies, peers, run, first):
    size = row_ref.shape[0] // peers
    batch = max(n for n in range(1, 49) if size % n == 0)
    chunk = max(n for n in range(16, 193, 16) if size % n == 0)

    def prepare(source, carry):
        for block in range(0, size, chunk):
            at = pl.multiple_of(source * size + block, chunk)
            unit, _ = unit_rows(row_ref[pl.ds(at, chunk), :].astype(jnp.float32))
            stage_ref[pl.ds(2 * at, chunk, stride=2), :] = unit[:, :128]
            stage_ref[pl.ds(2 * at + 1, chunk, stride=2), :] = unit[:, 128:]
        return carry

    lax.fori_loop(0, peers, prepare, 0)
    for copy in copies:
        copy.wait()

    def place(source, carry):
        start = (me_ref[0] ^ source) * run + first
        at = source * size * 2
        for block in range(0, size, batch):
            slots = [slot_ref[start + block + v] for v in range(batch)]
            values = [stage_ref[pl.ds(at + 2 * (block + v), 2), :] for v in range(batch)]
            for slot, value in zip(slots, values):
                held_ref[pl.ds(slot, 2), :] = value
        return carry

    lax.fori_loop(0, peers, place, 0)


def place_kernel(
    me_ref, slot_ref, row_ref, held_ref, token_ref, stage_ref, *, peers, run, first
):
    token_ref[...] = jnp.zeros_like(token_ref)
    place_runs(me_ref, slot_ref, row_ref, held_ref, stage_ref, [], peers, run, first)


def place_rows(me, slots, rows, peers, run, first):
    smem = pl.BlockSpec(memory_space=pltpu.SMEM)
    vmem = pl.BlockSpec(memory_space=pltpu.VMEM)
    return pl.pallas_call(
        functools.partial(place_kernel, peers=peers, run=run, first=first),
        in_specs=[smem, smem, vmem],
        out_specs=[vmem, vmem],
        out_shape=[
            jax.ShapeDtypeStruct((2 * peers * run, 128), jnp.float32),
            jax.ShapeDtypeStruct((8, 128), jnp.float32),
        ],
        scratch_shapes=[pltpu.VMEM((2 * rows.shape[0], 128), jnp.float32)],
        compiler_params=pltpu.CompilerParams(vmem_limit_bytes=24 * MIB),
        cost_estimate=pl.CostEstimate(
            flops=0, bytes_accessed=32 * rows.shape[0] * rows.shape[1], transcendentals=0
        ),
        name="place_rows",
    )(me, slots, rows)


def split_copies(source_ref, target_ref, sem):
    lanes = sem.shape[0]
    size = source_ref.shape[0] // lanes
    parts = [pl.ds(c * size, size) for c in range(lanes)]
    return [
        pltpu.make_async_copy(source_ref.at[part, :], target_ref.at[part, :], sem.at[c])
        for c, part in enumerate(parts)
    ]


def blend_kernel(
    me_ref, slot_ref, row_ref, w_ref, in_ref, o_ref, held_ref, stage_ref, what_ref, new_ref,
    held_sem, what_sem, new_sem, *, peers, run, first,
):
    copies = split_copies(in_ref, held_ref, held_sem)
    weights = split_copies(w_ref, what_ref, what_sem)
    for copy in copies + weights:
        copy.start()
    place_runs(me_ref, slot_ref, row_ref, held_ref, stage_ref, copies, peers, run, first)
    for copy in weights:
        copy.wait()
    classes = o_ref.shape[0]
    pieces = new_sem.shape[0]
    piece = classes // pieces
    block = math.gcd(piece, 64)

    def leaving(c):
        part = pl.ds(pl.multiple_of(c * piece, piece), piece)
        return pltpu.make_async_copy(new_ref.at[part, :], o_ref.at[part, :], new_sem.at[c])

    def blend(c, carry):
        for begin in range(0, piece, block):
            start = pl.multiple_of(c * piece + begin, block)
            rows = pl.ds(start, block)
            low = held_ref[pl.ds(start * 2, block, stride=2), :]
            high = held_ref[pl.ds(start * 2 + 1, block, stride=2), :]
            low = low + what_ref[rows, :128].astype(jnp.float32)
            high = high + what_ref[rows, 128:].astype(jnp.float32)
            inv = lax.rsqrt(jnp.sum(low * low + high * high, axis=1, keepdims=True) + 1e-06)
            new_ref[rows, :128] = (low * inv).astype(jnp.bfloat16)
            new_ref[rows, 128:] = (high * inv).astype(jnp.bfloat16)
        leaving(c).start()
        return carry

    lax.fori_loop(0, pieces, blend, 0)
    for c in range(pieces):
        leaving(c).wait()


def place_and_blend(me, slots, rows, held, weights, peers, run, first):
    classes, width = weights.shape
    smem = pl.BlockSpec(memory_space=pltpu.SMEM)
    vmem = pl.BlockSpec(memory_space=pltpu.VMEM)
    anywhere = pl.BlockSpec(memory_space=pl.ANY)
    return pl.pallas_call(
        functools.partial(blend_kernel, peers=peers, run=run, first=first),
        in_specs=[smem, smem, vmem, anywhere, anywhere],
        out_specs=anywhere,
        out_shape=pltpu.HBM((classes, width), jnp.bfloat16),
        scratch_shapes=[
            pltpu.VMEM(held.shape, jnp.float32),
            pltpu.VMEM((2 * rows.shape[0], 128), jnp.float32),
            pltpu.VMEM((classes, width), jnp.bfloat16),
            pltpu.VMEM((classes, width), jnp.bfloat16),
            pltpu.SemaphoreType.DMA((8,)),
            pltpu.SemaphoreType.DMA((2,)),
            pltpu.SemaphoreType.DMA((8,)),
        ],
        compiler_params=pltpu.CompilerParams(vmem_limit_bytes=32 * MIB),
        cost_estimate=pl.CostEstimate(
            flops=0, bytes_accessed=12 * classes * width, transcendentals=0
        ),
        name="place_and_blend",
    )(me, slots, rows, weights, held)


def shards(embeddings, labels, class_weights, centroids, centroid_class):
    rows_local, width = embeddings.shape
    classes = class_weights.shape[0]
    groups, reps = lax.axis_size("grp"), lax.axis_size("rep")
    peers = groups * reps
    batch = rows_local * reps
    run = classes // peers
    grp, rep = lax.axis_index("grp").astype(jnp.int32), lax.axis_index("rep").astype(jnp.int32)
    me = (rep * groups + grp).reshape(1)
    base = me * classes

    def swap(value, axis, k):
        size = lax.axis_size(axis)
        return lax.ppermute(value, axis, [(i, i ^ k) for i in range(size)]) if k else value

    def relay(sent):
        return lax.all_to_all(sent, ALL, 0, 0, tiled=True).reshape(-1, width)

    weights = in_hbm(class_weights)
    runs = in_hbm(centroids.reshape(peers, run, width))
    cut = run * 11 // 16 // 16 * 16
    mixed = jnp.concatenate([swap(embeddings, "rep", 2 * z) for z in range(reps // 2)])
    rows_a = relay(released(in_hbm(fetch(runs, 0, cut, [])), [mixed]))
    mixed = jnp.concatenate([swap(mixed, "rep", c) for c in range(2)])
    emb, a, b, stats, what = forward(base, rep.reshape(1), mixed, reps, labels, weights)

    half = reps // 2
    core, deep = rep % 2, rep // 2
    index = lax.dynamic_index_in_dim

    def share_out(sums, wanted, axis, flips):
        got = []
        for flip, asked in zip(flips, wanted):
            sent = jnp.concatenate([sums, asked.reshape(-1)]).reshape(-1, 128)
            got.append(swap(sent, axis, flip).reshape(-1))
        got = jnp.stack(got)
        return jnp.sum(got[:, : 2 * batch], axis=0), got[:, 2 * batch :]

    wanted = centroid_class.reshape(half, 2, groups, run).astype(jnp.float32)
    wanted = [index(wanted, grp ^ j, 2, False) for j in range(groups)]
    sums, wanted = share_out(stats[:2].reshape(-1), wanted, "grp", range(groups))
    wanted = wanted.reshape(groups, half, 2, run)
    wanted = [index(wanted, core ^ c, 2, False) for c in range(2)]
    sums, wanted = share_out(sums, wanted, "rep", range(2))
    sent_b = in_hbm(fetch(runs, cut, run - cut, [stats]))
    sums = join([sums.reshape(-1, 128)], [sent_b]).reshape(-1)
    wanted = wanted.reshape(2, groups, half, run)
    wanted = [index(wanted, deep ^ z, 2, False) for z in range(half)]
    sums, slots = share_out(sums, wanted, "rep", range(0, reps, 2))
    slots = slots.reshape(-1).astype(jnp.int32) * 2
    total, target = sums[:batch], sums[batch:]
    losses = jnp.log(total) - target
    loss = lax.dynamic_slice_in_dim(losses, rep * rows_local, rows_local, 0)

    rows_b = relay(released(sent_b, [total]))
    held, token = place_rows(me, slots, rows_a, peers, run, 0)
    weight_grad = weight_gradient(base, emb, labels, stats, total, weights, token)

    grad = (a / total[:, None] - b).reshape(half, 2, rows_local, width)
    grad = sum(swap(index(grad, core ^ c, 1, False), "rep", c) for c in range(2))
    sent = grad.astype(jnp.bfloat16)
    parts = [swap(sent, "grp", j) for j in range(1, groups)]
    grad = join([grad, *parts], [in_hbm(weight_grad), loss])
    sent = grad.astype(jnp.bfloat16)
    parts = [swap(index(sent, deep ^ z, 0, False), "rep", 2 * z) for z in range(1, half)]
    embedding_gradient = index(grad, deep, 0, False)
    for part in parts:
        embedding_gradient = embedding_gradient + part.astype(jnp.float32)

    refreshed = place_and_blend(me, slots, rows_b, in_hbm(held), in_hbm(what), peers, run, cut)
    return (loss, embedding_gradient, weight_grad, refreshed)


def solution(mesh):
    in_specs = (
        P("rep", None),
        P(),
        P(("rep", "grp"), None),
        P(("grp", "rep"), None),
        P(("grp", "rep")),
    )
    out_specs = (P("rep"), P("rep", None), P(("rep", "grp"), None), P(("rep", "grp"), None))
    return jax.shard_map(shards, mesh=mesh, in_specs=in_specs, out_specs=out_specs, check_vma=False)
```
